32 devices in a mesh: dp: 8 (over y, x, core), tensor: 4 (over z).
Axes of the slice: x: 2, y: 2, z: 4, core: 2. Of those that a mesh axis runs over, the one named last changes fastest.
Arguments:
- tokens: bfloat16 [16384, 1024], P('dp'), may hold values from -6 to 6
- qkv_weight: bfloat16 [3, 1024, 1024], P(None, None, 'tensor'), may hold values from -0.1875 to 0.1875
- out_weight: bfloat16 [1024, 1024], P('tensor'), may hold values from -3 to 3
- gate_up_weight: bfloat16 [2, 1024, 4096], P(None, None, 'tensor'), may hold values from -0.1875 to 0.1875
- down_weight: bfloat16 [4096, 1024], P('tensor'), may hold values from -0.09375 to 0.09375
- norm_gains: float32 [2, 1024], replicated, may hold values from 0.1 to 1.9
- species_weight: float32 [850], replicated, may hold values from 0.3 to 3
- species_ids: int32 [8], P('dp'), may hold values from 0 to 849
- lengths: int32 [8], P('dp'), may hold values from 256 to 2048, as said below
- cotangent: bfloat16 [16384, 1024], P('dp'), may hold values from -6 to 6
Outputs:
- out: float32 [16384, 1024], P(('dp', 'tensor'))
- grad_tokens: float32 [16384, 1024], P(('dp', 'tensor'))
- grad_qkv: float32 [3, 1024, 1024], P(None, 'dp', 'tensor')
- grad_out_proj: float32 [1024, 1024], P('tensor', 'dp')
- grad_gate_up: float32 [2, 1024, 4096], P(None, 'dp', 'tensor')
- grad_down: float32 [4096, 1024], P('tensor', 'dp')
- grad_gains: float32 [2, 1024], replicated
The draws below stay inside these ranges and needn't reach their ends.
Inputs may be any that keep to these rules, and one draw needn't show every extreme that they name: `lengths`: each window's count of valid leading slots; in every draw some window has 2048 and another 2048 // 8.
All inputs are finite; a program needn't handle non-finite values.
Results may differ from the reference program's by a relative error of at most 0.019.
Values may be sent and summed in bfloat16 or wider, within the bound.
No kernel may reach another device: no remote copies, remote signals or barrier semaphores. Data moves between devices by JAX's collectives and lax.ppermute only.
A program may use at most 192 MiB of HBM per device.

```python
import math
import jax
import jax.numpy as jnp
import numpy as np
from jax import lax

D = 1024
H = 16
HD = 64
FF = 4096
SPECIES = 850
WIN = 2048
WINDOWS = 8
TOKENS = 16384


def draw_lengths(key, part):
    key = jax.random.fold_in(key, 7)
    first_key, second_key = jax.random.split(key)
    drawn = jax.random.randint(first_key, (WINDOWS,), WIN // 8, WIN + 1).astype(jnp.int32)
    chosen = jax.random.randint(second_key, (), 0, WINDOWS).astype(jnp.int32)
    drawn = drawn.at[chosen].set(WIN)
    drawn = drawn.at[(chosen + 1) % WINDOWS].set(WIN // 8)
    return drawn.astype(jnp.int32)


def touch_ends(values, stream_key, least, largest):
    spot = [jax.random.randint(jax.random.fold_in(stream_key, axis), (), 0, length) for axis, length in enumerate(values.shape)]
    widest = values.shape.index(max(values.shape))
    beside = spot[:widest] + [(spot[widest] + 1) % values.shape[widest]] + spot[widest + 1:]
    return values.at[tuple(spot)].set(least).at[tuple(beside)].set(largest)


def level_of(stream_key, dims, cuts, smallest, largest):
    def one(axis_at, blocks):
        heights = jax.random.uniform(jax.random.fold_in(jax.random.fold_in(stream_key, 6), axis_at), (blocks,), jnp.float32, smallest / len(cuts), largest / len(cuts))
        return jnp.repeat(jnp.exp(heights), dims[axis_at] // blocks).reshape((-1,) + (1,) * (len(dims) - axis_at - 1))

    factor_of = one(*cuts[0])
    for cut in cuts[1:]:
        factor_of = factor_of * one(*cut)
    return factor_of


def rank_bounds(amount, lean):
    portions = [(1 << 20) // math.isqrt(standing ** lean) + 1 for standing in range(1, amount + 1)]
    scale = 1 + sum(portions) // (1 << 30)
    return np.cumsum(np.array([max(1, weight // scale) for weight in portions]))


def skewed_ids(own_key, dims, amount, slope):
    grid = rank_bounds(amount, slope)
    lot = jax.random.randint(jax.random.fold_in(own_key, 1), dims, 0, int(grid[amount - 1]))
    standing = jnp.searchsorted(jnp.asarray(grid, jnp.int32), lot, side="right")
    return jax.random.permutation(jax.random.fold_in(own_key, 2), amount)[standing].astype(jnp.int32)


def bell_draw(rng, dims, spread, most, cuts=(), held_as=jnp.bfloat16):
    values = jax.random.normal(rng, dims, jnp.float32) * spread
    if len(cuts) > 0:
        values = level_of(rng, dims, cuts, -0.22, 0.18) * values
    return jnp.clip(values, min=-most, max=most).astype(held_as)


def setup_inputs(seed: int = 0) -> dict:
    key_of = jax.random.split(jax.random.key(seed), 11)
    return {
        "tokens": bell_draw(key_of[0], (TOKENS, D), 1.0, 6.0, ((0, 8),)),
        "qkv_weight": bell_draw(key_of[1], (3, D, D), D ** -0.5, 0.1875, ((2, 4),)),
        "out_weight": bell_draw(key_of[2], (D, D), (max(D // 256, 1)) ** -0.5, 3.0, ((0, 4),)),
        "gate_up_weight": bell_draw(key_of[3], (2, D, FF), D ** -0.5, 0.1875, ((2, 4),)),
        "down_weight": bell_draw(key_of[4], (FF, D), FF ** -0.5, 0.09375, ((0, 4),)),
        "norm_gains": jnp.clip(1.0 + 0.18 * jax.random.normal(key_of[5], (2, D), jnp.float32), 0.1, 1.9),
        "species_weight": jnp.clip(jnp.exp(jax.random.uniform(key_of[6], (SPECIES,), jnp.float32, math.log(0.3), math.log(3.0))), 0.3, 3.0),
        "species_ids": touch_ends(skewed_ids(key_of[7], (WINDOWS,), SPECIES, 2), jax.random.fold_in(key_of[7], 3), 0, SPECIES - 1).astype(jnp.int32),
        "lengths": draw_lengths(jax.random.fold_in(key_of[10], 71), 0),
        "cotangent": bell_draw(key_of[9], (TOKENS, D), 1.0, 6.0, ((0, 8),)),
    }


EPSILON = 1e-05
NEG_FILL = -1e+30

@jax.custom_vjp
def low(v):
    return lax.optimization_barrier(v.astype(jnp.bfloat16)).astype(jnp.float32)

@jax.custom_vjp
def low_back(v):
    return v

def low_keep(v):
    return (low(v), None)

def low_pass(kept, grad):
    return (grad,)

def back_keep(v):
    return (v, None)

def back_low(kept, grad):
    return (low(grad),)
low.defvjp(low_keep, low_pass)
low_back.defvjp(back_keep, back_low)

def rms_factor(values):
    return lax.rsqrt(lax.optimization_barrier(jnp.mean(values * values, axis=-1, keepdims=True)) + EPSILON)

def rotary_tables(length, width):
    position = jnp.arange(length).astype(jnp.float32)
    frequency = jnp.power(jnp.float32(10000.0), -(jnp.arange(width // 2).astype(jnp.float32) * 2.0) / width)
    angles = position[:, None] * frequency[None, :]
    angles = jnp.concatenate([angles, angles], axis=1)
    return (jnp.cos(angles), jnp.sin(angles))

def rotate(values, cosine, sine_part):
    half = values.shape[-1] // 2
    turned = jnp.concatenate([-values[..., half:], values[..., :half]], axis=-1)
    return values * cosine[:, None, :] + turned * sine_part[:, None, :]

def window_layer(xwin, wqkv, wout, wgu, wdown, gains, length):
    top = lax.Precision.HIGHEST
    unit1 = xwin * rms_factor(xwin)
    normed1 = low(unit1 * gains[0])
    qkv = low_back(jnp.einsum('td,cde->cte', normed1, wqkv, precision=top))
    cosine, sine_part = rotary_tables(WIN, HD)
    queries = low(rotate(qkv[0].reshape(WIN, H, HD), cosine, sine_part))
    keys = low(rotate(qkv[1].reshape(WIN, H, HD), cosine, sine_part))
    values = low(qkv[2].reshape(WIN, H, HD))
    scores = jnp.einsum('qhd,khd->hqk', queries, keys, precision=top) * HD ** (-0.5)
    visible = jnp.arange(WIN) < length
    scores = low_back(jnp.where(visible[None, None, :], scores, NEG_FILL))
    peak = lax.optimization_barrier(jnp.max(scores, axis=-1, keepdims=True))
    expo = jnp.exp(scores - peak)
    probs = expo / lax.optimization_barrier(jnp.sum(expo, axis=-1, keepdims=True))
    attended = jnp.einsum('hqk,khd->qhd', low(probs), values, precision=top).reshape(WIN, D)
    attended = low(low_back(attended))
    resid = xwin + low_back(jnp.dot(attended, wout, precision=top))
    unit2 = resid * rms_factor(resid)
    normed2 = low(unit2 * gains[1])
    gate = low_back(jnp.dot(normed2, wgu[0], precision=top))
    upper = low_back(jnp.dot(normed2, wgu[1], precision=top))
    hidden = low(gate * jax.nn.sigmoid(gate) * upper)
    return resid + low_back(jnp.dot(hidden, wdown, precision=top))

def reference(tokens, qkv_weight, out_weight, gate_up_weight, down_weight, norm_gains, species_weight, species_ids, lengths, cotangent):
    xall = tokens.astype(jnp.float32).reshape(WINDOWS, WIN, D)
    weights_in = (qkv_weight.astype(jnp.float32), out_weight.astype(jnp.float32), gate_up_weight.astype(jnp.float32), down_weight.astype(jnp.float32), norm_gains.astype(jnp.float32))

    def forward(xwins, wqkv, wout, wgu, wdown, gains):

        def one_window(item):
            length = item[1]

            def inner(xwin):
                return window_layer(xwin, wqkv, wout, wgu, wdown, gains, length)
            return jax.checkpoint(inner)(item[0])
        return lax.map(one_window, (xwins, lengths))
    result, pullback = jax.vjp(forward, xall, *weights_in)
    picked = species_weight.astype(jnp.float32)[species_ids]
    live = jnp.arange(WIN)[None, :] < lengths[:, None]
    row_weight = jnp.where(live, picked[:, None], jnp.float32(0.0))
    grad_out = cotangent.astype(jnp.float32).reshape(WINDOWS, WIN, D) * row_weight[:, :, None]
    grads = pullback(grad_out)
    return (result.reshape(TOKENS, D), grads[0].reshape(TOKENS, D), grads[1], grads[2], grads[3], grads[4], grads[5])
```

```python
import functools
import math

import jax
import jax.numpy as jnp
import numpy as np
from jax import lax
from jax.experimental import pallas as pl
from jax.experimental.pallas import tpu as pltpu
from jax.sharding import PartitionSpec as P

HD = 64
WIN = 2048
EPSILON = 1e-05
NEG_FILL = -1e30
LOG2E = math.log2(math.e)
LN2 = math.log(2.0)
FACTOR = HD ** (-0.5)
VMEM = 60 * 2**20
F32 = jnp.float32
BF16 = jnp.bfloat16

NN = (((1,), (0,)), ((), ()))
NT = (((1,), (1,)), ((), ()))
TN = (((0,), (0,)), ((), ()))


def dot(a, b, dims=NN):
    return lax.dot_general(a, b, dims, preferred_element_type=F32)


def call(kernel, grid, in_specs, out_specs, out_shape, scratch=(), flops=0, nbytes=0, trans=0):
    return pl.pallas_call(
        kernel,
        grid=grid,
        in_specs=in_specs,
        out_specs=out_specs,
        out_shape=out_shape,
        scratch_shapes=scratch,
        compiler_params=pltpu.CompilerParams(vmem_limit_bytes=VMEM),
        cost_estimate=pl.CostEstimate(flops=flops, bytes_accessed=nbytes, transcendentals=trans),
    )


def whole(shape):
    return pl.BlockSpec(shape, lambda *_: (0,) * len(shape), pipeline_mode=pl.Buffered(1))


def smem():
    return pl.BlockSpec(memory_space=pltpu.SMEM)


def sds(shape, dtype):
    return jax.ShapeDtypeStruct(shape, dtype)


def rotary_tables():
    position = np.arange(WIN, dtype=np.float64)
    frequency = 10000.0 ** (-2.0 * np.arange(HD // 2, dtype=np.float64) / HD)
    angles = position[:, None] * frequency[None, :]
    cosine = np.cos(angles)
    sine = np.sin(angles)
    cos_full = np.tile(np.concatenate([cosine, cosine], axis=1), (1, 2))
    sin_full = np.tile(np.concatenate([-sine, sine], axis=1), (1, 2))
    return cos_full.astype(np.float32), sin_full.astype(np.float32)


def swap_halves(v):
    lane = lax.broadcasted_iota(jnp.int32, v.shape, 1)
    return jnp.where(lane % HD < HD // 2, pltpu.roll(v, 96, 1), pltpu.roll(v, 32, 1))


def rms(x):
    return lax.rsqrt(jnp.mean(x * x, axis=-1, keepdims=True) + EPSILON)


def split3(v):
    hi = v.astype(BF16)
    rest = v - hi.astype(F32)
    mid = rest.astype(BF16)
    low = (rest - mid.astype(F32)).astype(BF16)
    return hi, mid, low


def qkv_kernel(len_ref, x_ref, w_ref, gain_ref, cos_ref, sin_ref, q_ref, k_ref, v_ref):
    rows = x_ref.shape[0]
    x = x_ref[...].astype(F32)
    normed = (x * rms(x) * gain_ref[0:1, :]).astype(BF16)
    cosine = cos_ref[...]
    sine = sin_ref[...]
    lane = lax.broadcasted_iota(jnp.int32, (rows, 128), 1)
    slot = lax.broadcasted_iota(jnp.int32, (rows, 128), 0) + pl.program_id(0) * rows
    masked = jnp.where(slot < len_ref[0], 0.0, NEG_FILL).astype(BF16)
    one = jnp.ones((rows, 128), BF16)
    zero = jnp.zeros((rows, 128), BF16)
    pairs = w_ref.shape[2] // 128
    for c in range(3):
        y = dot(normed, w_ref[c])
        for j in range(pairs):
            v = y[:, 128 * j : 128 * (j + 1)]
            if c < 2:
                v = v * cosine + swap_halves(v) * sine
            if c == 0:
                v = v * (FACTOR * LOG2E)
            v = v.astype(BF16)
            for s in range(2):
                first = HD * (1 - s)
                own = (lane >= HD * s) & (lane < HD * (s + 1))
                if c == 0:
                    q_ref[2 * j + s] = jnp.where(own, v, jnp.where(lane == first, one, zero))
                elif c == 1:
                    tail = jnp.where(
                        lane == first, masked, jnp.where(lane < first + 4, one, zero)
                    )
                    tail = jnp.where(lane < first, zero, tail)
                    k_ref[2 * j + s] = jnp.where(own, v, tail)
                else:
                    v_ref[2 * j + s] = jnp.where(own, v, one)


def project(lengths, tokens, qkv_weight, gains, cosine, sine, block=512):
    rows, width = tokens.shape
    local = qkv_weight.shape[2]
    heads = local // HD
    spec = pl.BlockSpec((heads, block, 128), lambda i: (0, i, 0))
    return call(
        qkv_kernel,
        (rows // block,),
        [
            smem(),
            pl.BlockSpec((block, width), lambda i: (i, 0)),
            whole(qkv_weight.shape),
            whole(gains.shape),
            pl.BlockSpec((block, 128), lambda i: (i, 0)),
            pl.BlockSpec((block, 128), lambda i: (i, 0)),
        ],
        [spec] * 3,
        [sds((heads, rows, 128), BF16)] * 3,
        flops=2 * rows * width * 3 * local,
        nbytes=rows * width * 2 + 3 * heads * rows * 256,
    )(lengths, tokens, qkv_weight, gains, cosine, sine)


def attend_kernel(sub, q_ref, k_ref, v_ref, o_ref, qb_ref):
    rows = q_ref.shape[1]
    lane = lax.broadcasted_iota(jnp.int32, (sub, 128), 1)
    for r in range(rows // sub):
        part = slice(r * sub, (r + 1) * sub)
        outs = []
        for s in range(2):
            q = q_ref[s, part, :]
            scores = dot(q, k_ref[s], NT)
            peak = jnp.max(scores, axis=1, keepdims=True)
            expo = jnp.exp2(scores - peak).astype(BF16)
            acc = dot(expo, v_ref[s])
            outs.append(acc / pltpu.roll(acc, HD, 1))
            first = HD * (1 - s)
            total = jnp.where((lane >= first) & (lane < first + HD), acc, 1.0)
            hi, mid, low = split3(-(peak + jnp.log2(total)))
            tail = jnp.where(lane == first + 3, low, q)
            tail = jnp.where(lane == first + 2, mid, tail)
            qb_ref[s, part, :] = jnp.where(lane == first + 1, hi, tail)
        o_ref[part, :] = jnp.where(lane < HD, outs[0], outs[1]).astype(BF16)


def attend(q, k, v, block=512, sub=256):
    heads, rows, _ = q.shape
    keys = k.shape[1]
    return call(
        functools.partial(attend_kernel, sub),
        (heads // 2, rows // block),
        [
            pl.BlockSpec((2, block, 128), lambda j, i: (j, i, 0)),
            pl.BlockSpec((2, keys, 128), lambda j, i: (j, 0, 0)),
            pl.BlockSpec((2, keys, 128), lambda j, i: (j, 0, 0)),
        ],
        [
            pl.BlockSpec((block, 128), lambda j, i: (i, j)),
            pl.BlockSpec((2, block, 128), lambda j, i: (j, i, 0)),
        ],
        [sds((rows, heads * HD), BF16), sds((heads, rows, 128), BF16)],
        flops=heads * rows * keys * 128 * 4,
        nbytes=heads * (2 * rows + 2 * keys) * 256,
        trans=heads * rows * keys,
    )(q, k, v)


def ffn_kernel(
    len_ref, weight_ref, att_ref, x_ref, cot_ref, ow_ref, gu_ref, dw_ref, gain_ref,
    resid_ref, n2_ref, ffn_ref, gn2_ref, hid_ref, gg_ref, gup_ref, go_ref,
):
    rows = x_ref.shape[0]
    parts, _, local = att_ref.shape
    resid = x_ref[...].astype(F32)
    for z in range(parts):
        resid = resid + dot(att_ref[z], ow_ref[local * z : local * (z + 1), :])
    resid_ref[...] = resid
    normed = (resid * rms(resid) * gain_ref[1:2, :]).astype(BF16)
    n2_ref[...] = normed
    slot = lax.broadcasted_iota(jnp.int32, (rows, 1), 0) + pl.program_id(0) * rows
    row_weight = jnp.where(slot < len_ref[0], weight_ref[0], 0.0)
    go = (cot_ref[...].astype(F32) * row_weight).astype(BF16)
    go_ref[...] = go
    gate = dot(normed, gu_ref[0])
    upper = dot(normed, gu_ref[1])
    sigma = jax.nn.sigmoid(gate)
    act = gate * sigma
    hidden = (act * upper).astype(BF16)
    hid_ref[...] = hidden
    ffn_ref[...] = dot(hidden, dw_ref[...]).astype(BF16)
    grad_hidden = dot(go, dw_ref[...], NT)
    grad_up = (grad_hidden * act).astype(BF16)
    grad_gate = (grad_hidden * upper * (sigma + act * (1.0 - sigma))).astype(BF16)
    gup_ref[...] = grad_up
    gg_ref[...] = grad_gate
    gn2_ref[...] = (dot(grad_gate, gu_ref[0], NT) + dot(grad_up, gu_ref[1], NT)).astype(BF16)


def feed_forward(lengths, picked, att_all, tokens, cotangent, out_full, gate_up, down, gains, block=512):
    rows, width = tokens.shape
    parts, _, local = att_all.shape
    hidden = gate_up.shape[2]
    row = lambda n: pl.BlockSpec((block, n), lambda i: (i, 0))
    return call(
        ffn_kernel,
        (rows // block,),
        [
            smem(), smem(),
            pl.BlockSpec((parts, block, local), lambda i: (0, i, 0)),
            row(width), row(width),
            whole(out_full.shape), whole(gate_up.shape), whole(down.shape), whole(gains.shape),
        ],
        [row(width), row(width), row(width), row(width), row(hidden), row(hidden), row(hidden), row(width)],
        [
            sds((rows, width), F32), sds((rows, width), BF16), sds((rows, width), BF16),
            sds((rows, width), BF16), sds((rows, hidden), BF16), sds((rows, hidden), BF16),
            sds((rows, hidden), BF16), sds((rows, width), BF16),
        ],
        flops=2 * rows * width * (width + 6 * hidden),
        nbytes=rows * width * 20 + 8 * width * hidden,
        trans=rows * hidden,
    )(lengths, picked, att_all, tokens, cotangent, out_full, gate_up, down, gains)


def ffn_grad_kernel(n2_ref, hid_ref, gg_ref, gup_ref, go_ref, gu_ref, gain_ref, out_ref, sum_ref, acc):
    step = pl.program_id(0)

    @pl.when(step == 0)
    def _():
        acc[...] = jnp.zeros_like(acc)

    n2 = n2_ref[...]
    acc[0] += dot(n2, gg_ref[...], TN)
    acc[1] += dot(n2, gup_ref[...], TN)
    acc[2] += dot(go_ref[...], hid_ref[...], TN)

    @pl.when(step == pl.num_programs(0) - 1)
    def _():
        width = acc.shape[1]
        shares = out_ref.shape[0]
        part = width // shares
        for c in range(3):
            for d in range(shares):
                out_ref[d, c * part : (c + 1) * part, :] = acc[c, d * part : (d + 1) * part, :].astype(BF16)
        total = jnp.sum(
            acc[0] * gu_ref[0].astype(F32) + acc[1] * gu_ref[1].astype(F32), axis=1, keepdims=True
        )
        sum_ref[...] = jnp.broadcast_to(total, sum_ref.shape)


def ffn_grads(n2, hid, gg, gup, go, gate_up, gains, shares, block=512):
    rows, width = n2.shape
    hidden = hid.shape[1]
    row = lambda n: pl.BlockSpec((block, n), lambda i: (i, 0))
    return call(
        ffn_grad_kernel,
        (rows // block,),
        [row(width), row(hidden), row(hidden), row(hidden), row(width), whole(gate_up.shape), whole(gains.shape)],
        [whole((shares, 3 * width // shares, hidden)), whole((width, 128))],
        [sds((shares, 3 * width // shares, hidden), BF16), sds((width, 128), F32)],
        scratch=[pltpu.VMEM((3, width, hidden), F32)],
        flops=6 * rows * width * hidden,
        nbytes=rows * (2 * width + 3 * hidden) * 2,
    )(n2, hid, gg, gup, go, gate_up, gains)


def attend_back_kernel(gr_ref, ow_ref, q_ref, k_ref, v_ref, att_ref, dq_ref, dk_ref, dv_ref):
    rows = q_ref.shape[1]
    lane = lax.broadcasted_iota(jnp.int32, (rows, 128), 1)

    @pl.when(pl.program_id(1) == 0)
    def _():
        dk_ref[...] = jnp.zeros_like(dk_ref)
        dv_ref[...] = jnp.zeros_like(dv_ref)

    grad = dot(gr_ref[...], ow_ref[...], NT).astype(BF16)
    prod = grad.astype(F32) * att_ref[...].astype(F32)
    zero = jnp.zeros((rows, 128), BF16)
    dqs = []
    for s in range(2):
        first = HD * (1 - s)
        own = (lane >= HD * s) & (lane < HD * (s + 1))
        delta = jnp.sum(jnp.where(own, prod, 0.0), axis=1, keepdims=True)
        hi, mid, low = split3(-delta)
        grad_own = jnp.where(own, grad, zero)
        grad_aug = jnp.where(lane == first + 2, low, grad_own)
        grad_aug = jnp.where(lane == first + 1, mid, grad_aug)
        grad_aug = jnp.where(lane == first, hi, grad_aug)
        q = q_ref[s]
        probs = jnp.exp2(dot(k_ref[s], q, NT))
        scores_grad = (probs * dot(v_ref[s], grad_aug, NT)).astype(BF16)
        dv_ref[...] += dot(probs.astype(BF16), grad_own)
        dk_ref[...] += dot(scores_grad, jnp.where(own, q, zero))
        dqs.append(dot(k_ref[s], scores_grad, TN).T)
    dq_ref[...] = jnp.where(lane < HD, dqs[0], dqs[1])


def attend_back(grad_low, out_weight, q, k, v, att, block=512):
    heads, rows, _ = q.shape
    width = grad_low.shape[1]
    local = heads * HD
    return call(
        attend_back_kernel,
        (heads // 2, rows // block),
        [
            pl.BlockSpec((block, width), lambda j, i: (i, 0)),
            pl.BlockSpec((128, width), lambda j, i: (j, 0)),
            pl.BlockSpec((2, block, 128), lambda j, i: (j, i, 0)),
            pl.BlockSpec((2, rows, 128), lambda j, i: (j, 0, 0)),
            pl.BlockSpec((2, rows, 128), lambda j, i: (j, 0, 0)),
            pl.BlockSpec((block, 128), lambda j, i: (i, j)),
        ],
        [
            pl.BlockSpec((block, 128), lambda j, i: (i, j)),
            pl.BlockSpec((rows, 128), lambda j, i: (0, j)),
            pl.BlockSpec((rows, 128), lambda j, i: (0, j)),
        ],
        [sds((rows, local), F32)] * 3,
        flops=heads * rows * rows * 128 * 10 + 2 * rows * width * local,
        nbytes=heads * rows * 256 * 6,
        trans=heads * rows * rows,
    )(grad_low, out_weight, q, k, v, att)


def project_back_kernel(
    x_ref, dq_ref, dk_ref, dv_ref, gr_ref, att_ref, w_ref, gain_ref, cos_ref, sin_ref,
    gn1_ref, wg_ref, sum_ref, acc,
):
    step = pl.program_id(0)

    @pl.when(step == 0)
    def _():
        acc[...] = jnp.zeros_like(acc)

    x = x_ref[...].astype(F32)
    normed = (x * rms(x) * gain_ref[0:1, :]).astype(BF16)
    local = dq_ref.shape[1]
    cosine = cos_ref[...]
    sine = sin_ref[...]

    def back(g, scale):
        cols = []
        for j in range(local // 128):
            v = g[:, 128 * j : 128 * (j + 1)]
            cols.append((v * cosine - swap_halves(v) * sine) * scale)
        return jnp.concatenate(cols, axis=1).astype(BF16)

    acts = [back(dq_ref[...], FACTOR), back(dk_ref[...], LN2), dv_ref[...].astype(BF16)]
    total = dot(acts[0], w_ref[0], NT) + dot(acts[1], w_ref[1], NT) + dot(acts[2], w_ref[2], NT)
    gn1_ref[...] = total.astype(BF16)
    acc[:, : 3 * local] += dot(normed, jnp.concatenate(acts, axis=1), TN)
    acc[:, 3 * local :] += dot(gr_ref[...], att_ref[...], TN)

    @pl.when(step == pl.num_programs(0) - 1)
    def _():
        shares = wg_ref.shape[0]
        part = acc.shape[0] // shares
        for d in range(shares):
            wg_ref[d] = acc[d * part : (d + 1) * part, :].astype(BF16)
        gain_sum = acc[:, :local] * w_ref[0].astype(F32)
        for c in (1, 2):
            gain_sum += acc[:, c * local : (c + 1) * local] * w_ref[c].astype(F32)
        sum_ref[...] = jnp.broadcast_to(jnp.sum(gain_sum, axis=1, keepdims=True), sum_ref.shape)


def project_back(tokens, dq, dk, dv, grad_low, att, qkv_weight, gains, cosine, sine, shares, block=512):
    rows, width = tokens.shape
    local = dq.shape[1]
    row = lambda n: pl.BlockSpec((block, n), lambda i: (i, 0))
    return call(
        project_back_kernel,
        (rows // block,),
        [
            row(width), row(local), row(local), row(local), row(width), row(local),
            whole(qkv_weight.shape), whole(gains.shape), row(128), row(128),
        ],
        [row(width), whole((shares, width // shares, 4 * local)), whole((width, 128))],
        [
            sds((rows, width), BF16),
            sds((shares, width // shares, 4 * local), BF16),
            sds((width, 128), F32),
        ],
        scratch=[pltpu.VMEM((width, 4 * local), F32)],
        flops=2 * rows * width * 7 * local,
        nbytes=rows * width * 8,
    )(tokens, dq, dk, dv, grad_low, att, qkv_weight, gains, cosine, sine)


def norm_back(grad_normed, gain, unit, factor):
    scaled = grad_normed * gain
    return factor * (scaled - unit * jnp.mean(scaled * unit, axis=-1, keepdims=True))


def body(
    tokens, qkv_weight, out_weight, gate_up_weight, down_weight, norm_gains,
    species_weight, species_ids, lengths, cotangent,
):
    rows, width = tokens.shape
    local = out_weight.shape[0]
    hidden = down_weight.shape[0]
    parts = lax.axis_size("tensor")
    shares = lax.axis_size("dp")
    share = rows // parts
    offset = lax.axis_index("tensor") * share
    own = lambda a: lax.dynamic_slice_in_dim(a, offset, share, 0)
    cosine, sine = (jnp.asarray(t) for t in rotary_tables())

    matches = species_ids[:, None] == jnp.arange(species_weight.shape[0])[None, :]
    picked = jnp.sum(jnp.where(matches, species_weight[None, :], F32(0.0)), axis=1)

    out_full = lax.all_gather(out_weight, "tensor", axis=0, tiled=True)
    q, k, v = project(lengths, tokens, qkv_weight, norm_gains, cosine, sine)
    att, q_back = attend(q, k, v)
    att_all = lax.all_gather(att, "tensor", axis=0)
    resid, n2, ffn, gn2, hid, gg, gup, go = feed_forward(
        lengths, picked, att_all, tokens, cotangent, out_full, gate_up_weight, down_weight, norm_gains
    )
    gn2_own = lax.psum_scatter(gn2, "tensor", scatter_dimension=0, tiled=True).astype(F32)
    ffn_wg, gain_two = ffn_grads(n2, hid, gg, gup, go, gate_up_weight, norm_gains, shares)

    resid_own = own(resid)
    scale_two = rms(resid_own)
    unit_two = resid_own * scale_two
    slot = offset + jnp.arange(share)
    row_weight = jnp.where(slot < lengths[0], picked[0], F32(0.0))
    go_own = own(cotangent).astype(F32) * row_weight[:, None]
    grad_resid = go_own + norm_back(gn2_own, norm_gains[1], unit_two, scale_two)
    grad_low = lax.all_gather(grad_resid.astype(BF16), "tensor", axis=0, tiled=True)

    dq, dk, dv = attend_back(grad_low, out_weight, q_back, k, v, att)
    gn1, attn_wg, gain_one = project_back(
        tokens, dq, dk, dv, grad_low, att, qkv_weight, norm_gains, cosine, sine, shares
    )
    gn1_own = lax.psum_scatter(gn1, "tensor", scatter_dimension=0, tiled=True).astype(F32)
    ffn_own = lax.psum_scatter(ffn, "tensor", scatter_dimension=0, tiled=True).astype(F32)
    out = resid_own + ffn_own

    tok_own = own(tokens).astype(F32)
    scale_one = rms(tok_own)
    grad_tok = grad_resid + norm_back(gn1_own, norm_gains[0], tok_own * scale_one, scale_one)

    gains_grad = jnp.stack([gain_one[:, 0], gain_two[:, 0]]) / norm_gains
    gains_grad = lax.psum(gains_grad, ("dp", "tensor"))

    part = width // shares
    ffn_sum = lax.psum_scatter(ffn_wg, "dp", scatter_dimension=0, tiled=True)[0].astype(F32)
    attn_sum = lax.psum_scatter(attn_wg, "dp", scatter_dimension=0, tiled=True)[0].astype(F32)
    grad_gu = ffn_sum[: 2 * part].reshape(2, part, hidden)
    grad_down = ffn_sum[2 * part :].T
    grad_qkv = jnp.stack([attn_sum[:, c * local : (c + 1) * local] for c in range(3)])
    grad_op = attn_sum[:, 3 * local :].T
    return (out, grad_tok, grad_qkv, grad_op, grad_gu, grad_down, gains_grad)


def solution(mesh):
    in_specs = (
        P("dp", None),
        P(None, None, "tensor"),
        P("tensor", None),
        P(None, None, "tensor"),
        P("tensor", None),
        P(),
        P(),
        P("dp"),
        P("dp"),
        P("dp", None),
    )
    out_specs = (
        P(("dp", "tensor"), None),
        P(("dp", "tensor"), None),
        P(None, "dp", "tensor"),
        P("tensor", "dp"),
        P(None, "dp", "tensor"),
        P("tensor", "dp"),
        P(),
    )
    return jax.shard_map(body, mesh=mesh, in_specs=in_specs, out_specs=out_specs, check_vma=False)
```

```python
import functools
import math

import jax
import jax.numpy as jnp
import numpy as np
from jax import lax
from jax.experimental import pallas as pl
from jax.experimental.pallas import tpu as pltpu
from jax.sharding import PartitionSpec as P

HD = 64
WIN = 2048
EPSILON = 1e-05
NEG_FILL = -1e30
LOG2E = math.log2(math.e)
LN2 = math.log(2.0)
FACTOR = HD ** (-0.5)
VMEM = 60 * 2**20
F32 = jnp.float32
BF16 = jnp.bfloat16

NN = (((1,), (0,)), ((), ()))
NT = (((1,), (1,)), ((), ()))
TN = (((0,), (0,)), ((), ()))


def dot(a, b, dims=NN):
    return lax.dot_general(a, b, dims, preferred_element_type=F32)


def call(kernel, grid, in_specs, out_specs, out_shape, scratch=(), flops=0, nbytes=0, trans=0, prefetch=0):
    return pl.pallas_call(
        kernel,
        grid_spec=pltpu.PrefetchScalarGridSpec(
            num_scalar_prefetch=prefetch,
            grid=grid,
            in_specs=in_specs,
            out_specs=out_specs,
            scratch_shapes=list(scratch),
        ),
        out_shape=out_shape,
        compiler_params=pltpu.CompilerParams(vmem_limit_bytes=VMEM),
        cost_estimate=pl.CostEstimate(flops=flops, bytes_accessed=nbytes, transcendentals=trans),
    )


def whole(shape):
    return pl.BlockSpec(shape, lambda *_: (0,) * len(shape), pipeline_mode=pl.Buffered(1))


def smem():
    return pl.BlockSpec(memory_space=pltpu.SMEM)


def sds(shape, dtype):
    return jax.ShapeDtypeStruct(shape, dtype)


def rotary_tables():
    position = np.arange(WIN, dtype=np.float64)
    frequency = 10000.0 ** (-2.0 * np.arange(HD // 2, dtype=np.float64) / HD)
    angles = position[:, None] * frequency[None, :]
    cosine = np.cos(angles)
    sine = np.sin(angles)
    cos_full = np.tile(np.concatenate([cosine, cosine], axis=1), (1, 2))
    sin_full = np.tile(np.concatenate([-sine, sine], axis=1), (1, 2))
    return cos_full.astype(np.float32), sin_full.astype(np.float32)


def swap_halves(v):
    lane = lax.broadcasted_iota(jnp.int32, v.shape, 1)
    return jnp.where(lane % HD < HD // 2, pltpu.roll(v, 96, 1), pltpu.roll(v, 32, 1))


def rms(x):
    return lax.rsqrt(jnp.mean(x * x, axis=-1, keepdims=True) + EPSILON)


def split3(v):
    hi = v.astype(BF16)
    rest = v - hi.astype(F32)
    mid = rest.astype(BF16)
    low = (rest - mid.astype(F32)).astype(BF16)
    return hi, mid, low


def norm_back(grad_normed, gain, unit, factor):
    scaled = grad_normed * gain
    return factor * (scaled - unit * jnp.mean(scaled * unit, axis=-1, keepdims=True))


def qkv_kernel(len_ref, x_ref, w_ref, gain_ref, cos_ref, sin_ref, q_ref, k_ref, v_ref):
    rows = x_ref.shape[0]
    x = x_ref[...].astype(F32)
    normed = (x * rms(x) * gain_ref[0:1, :]).astype(BF16)
    cosine = cos_ref[...]
    sine = sin_ref[...]
    lane = lax.broadcasted_iota(jnp.int32, (rows, 128), 1)
    slot = lax.broadcasted_iota(jnp.int32, (rows, 128), 0) + pl.program_id(0) * rows
    masked = jnp.where(slot < len_ref[0], 0.0, NEG_FILL).astype(BF16)
    one = jnp.ones((rows, 128), BF16)
    zero = jnp.zeros((rows, 128), BF16)
    pairs = w_ref.shape[2] // 128
    for c in range(3):
        y = dot(normed, w_ref[c])
        for j in range(pairs):
            v = y[:, 128 * j : 128 * (j + 1)]
            if c < 2:
                v = v * cosine + swap_halves(v) * sine
            if c == 0:
                v = v * (FACTOR * LOG2E)
            v = v.astype(BF16)
            for s in range(2):
                first = HD * (1 - s)
                own = (lane >= HD * s) & (lane < HD * (s + 1))
                if c == 0:
                    q_ref[2 * j + s] = jnp.where(own, v, jnp.where(lane == first, one, zero))
                elif c == 1:
                    tail = jnp.where(
                        lane == first, masked, jnp.where(lane < first + 4, one, zero)
                    )
                    tail = jnp.where(lane < first, zero, tail)
                    k_ref[2 * j + s] = jnp.where(own, v, tail)
                else:
                    v_ref[2 * j + s] = jnp.where(own, v, one)


def project(lengths, tokens, qkv_weight, gains, cosine, sine, block=512):
    rows, width = tokens.shape
    local = qkv_weight.shape[2]
    heads = local // HD
    spec = pl.BlockSpec((heads, block, 128), lambda i: (0, i, 0))
    return call(
        qkv_kernel,
        (rows // block,),
        [
            smem(),
            pl.BlockSpec((block, width), lambda i: (i, 0)),
            whole(qkv_weight.shape),
            whole(gains.shape),
            pl.BlockSpec((block, 128), lambda i: (i, 0)),
            pl.BlockSpec((block, 128), lambda i: (i, 0)),
        ],
        [spec] * 3,
        [sds((heads, rows, 128), BF16)] * 3,
        flops=2 * rows * width * 3 * local,
        nbytes=rows * width * 2 + 3 * heads * rows * 256,
    )(lengths, tokens, qkv_weight, gains, cosine, sine)


def attend_kernel(sub, q_ref, k_ref, v_ref, o_ref, qb_ref):
    rows = q_ref.shape[1]
    lane = lax.broadcasted_iota(jnp.int32, (sub, 128), 1)
    for r in range(rows // sub):
        part = slice(r * sub, (r + 1) * sub)
        outs = []
        for s in range(2):
            q = q_ref[s, part, :]
            scores = dot(q, k_ref[s], NT)
            peak = jnp.max(scores, axis=1, keepdims=True)
            expo = jnp.exp2(scores - peak).astype(BF16)
            acc = dot(expo, v_ref[s])
            outs.append(acc / pltpu.roll(acc, HD, 1))
            first = HD * (1 - s)
            total = jnp.where((lane >= first) & (lane < first + HD), acc, 1.0)
            hi, mid, low = split3(-(peak + jnp.log2(total)))
            tail = jnp.where(lane == first + 3, low, q)
            tail = jnp.where(lane == first + 2, mid, tail)
            qb_ref[s, part, :] = jnp.where(lane == first + 1, hi, tail)
        o_ref[part, :] = jnp.where(lane < HD, outs[0], outs[1]).astype(BF16)


def attend(q, k, v, block=512, sub=256):
    heads, rows, _ = q.shape
    keys = k.shape[1]
    return call(
        functools.partial(attend_kernel, sub),
        (heads // 2, rows // block),
        [
            pl.BlockSpec((2, block, 128), lambda j, i: (j, i, 0)),
            pl.BlockSpec((2, keys, 128), lambda j, i: (j, 0, 0)),
            pl.BlockSpec((2, keys, 128), lambda j, i: (j, 0, 0)),
        ],
        [
            pl.BlockSpec((block, 128), lambda j, i: (i, j)),
            pl.BlockSpec((2, block, 128), lambda j, i: (j, i, 0)),
        ],
        [sds((rows, heads * HD), BF16), sds((heads, rows, 128), BF16)],
        flops=heads * rows * keys * 128 * 4,
        nbytes=heads * (2 * rows + 2 * keys) * 256,
        trans=heads * rows * keys,
    )(q, k, v)


def shard_weights(gu_ref, dt_ref, pb_ref, shard):
    width = gu_ref.shape[1]
    if shard == 0:
        return gu_ref[0], gu_ref[1], dt_ref[...]
    hidden = pb_ref.shape[2]
    part = pb_ref.shape[1] // 3
    return tuple(pb_ref[:, c * part : (c + 1) * part, :].reshape(width, hidden) for c in range(3))


def ffn_kernel(parts, idx_ref, len_ref, weight_ref, x_ref, cot_ref, ow_ref, gu_ref, dt_ref, pb_ref, gain_ref, *refs):
    att_refs = refs[:parts]
    resid_ref, n2_ref, ffn_ref, gn2_ref, hid_ref, gg_ref, gup_ref, go_ref = refs[parts:]
    rows, width = x_ref.shape
    local = att_refs[0].shape[1]
    hidden_units = gu_ref.shape[2]
    me = idx_ref[0]
    resid = x_ref[...].astype(F32)
    for d in range(parts):
        block = ow_ref[:, me ^ d].reshape(local, width)
        resid = resid + dot(att_refs[d][...], block)
    resid_ref[...] = resid
    normed = (resid * rms(resid) * gain_ref[1:2, :]).astype(BF16)
    n2_ref[...] = normed
    first = (idx_ref[1] * pl.num_programs(0) + pl.program_id(0)) * rows
    slot = lax.broadcasted_iota(jnp.int32, (rows, 1), 0) + first
    row_weight = jnp.where(slot < len_ref[0], weight_ref[0], 0.0)
    go = (cot_ref[...].astype(F32) * row_weight).astype(BF16)
    go_ref[...] = go
    ffn = jnp.zeros((rows, width), F32)
    gn2 = jnp.zeros((rows, width), F32)
    for shard in range(2):
        gate_w, up_w, down_t = shard_weights(gu_ref, dt_ref, pb_ref, shard)
        cols = slice(shard * hidden_units, (shard + 1) * hidden_units)
        gate = dot(normed, gate_w)
        upper = dot(normed, up_w)
        sigma = jax.nn.sigmoid(gate)
        act = gate * sigma
        hidden = (act * upper).astype(BF16)
        hid_ref[:, cols] = hidden
        ffn = ffn + dot(hidden, down_t, NT)
        grad_hidden = dot(go, down_t)
        grad_up = (grad_hidden * act).astype(BF16)
        grad_gate = (grad_hidden * upper * (sigma + act * (1.0 - sigma))).astype(BF16)
        gup_ref[:, cols] = grad_up
        gg_ref[:, cols] = grad_gate
        gn2 = gn2 + dot(grad_gate, gate_w, NT) + dot(grad_up, up_w, NT)
    ffn_ref[...] = ffn.astype(BF16)
    gn2_ref[...] = gn2.astype(BF16)


def feed_forward(index, lengths, picked, atts, tokens, cotangent, out_full, gate_up, down_t, partner, gains, block=256):
    width = tokens.shape[1]
    parts = len(atts)
    rows = tokens.shape[0] // 2
    local = atts[0].shape[1]
    hidden = 2 * gate_up.shape[2]
    steps = rows // block
    row = lambda n: pl.BlockSpec((block, n), lambda i, idx: (i, 0))
    half = lambda n: pl.BlockSpec((block, n), lambda i, idx: (idx[1] * steps + i, 0))
    att_specs = [half(local)] + [row(local)] * (parts - 1)
    return call(
        functools.partial(ffn_kernel, parts),
        (steps,),
        [
            smem(), smem(), half(width), half(width),
            whole(out_full.shape), whole(gate_up.shape), whole(down_t.shape), whole(partner.shape), whole(gains.shape),
        ]
        + att_specs,
        [row(width), row(width), row(width), row(width), row(hidden), row(hidden), row(hidden), row(width)],
        [
            sds((rows, width), F32), sds((rows, width), BF16), sds((rows, width), BF16),
            sds((rows, width), BF16), sds((rows, hidden), BF16), sds((rows, hidden), BF16),
            sds((rows, hidden), BF16), sds((rows, width), BF16),
        ],
        flops=2 * rows * width * (width + 6 * hidden),
        nbytes=rows * width * 30 + 8 * width * hidden,
        trans=rows * hidden,
        prefetch=1,
    )(index, lengths, picked, tokens, cotangent, out_full, gate_up, down_t, partner, gains, *atts)


def ffn_grad_kernel(n2_ref, hid_ref, gg_ref, gup_ref, go_ref, gu_ref, dt_ref, pb_ref, out_ref, sum_ref, acc):
    shard = pl.program_id(0)
    step = pl.program_id(1)

    @pl.when(step == 0)
    def _():
        acc[...] = jnp.zeros_like(acc)

    n2 = n2_ref[...]
    acc[0] += dot(n2, gg_ref[...], TN)
    acc[1] += dot(n2, gup_ref[...], TN)
    acc[2] += dot(go_ref[...], hid_ref[...], TN)

    def gain_sum(which):
        gate_w, up_w, _ = shard_weights(gu_ref, dt_ref, pb_ref, which)
        total = jnp.sum(acc[0] * gate_w.astype(F32) + acc[1] * up_w.astype(F32), axis=1, keepdims=True)
        return jnp.broadcast_to(total, sum_ref.shape)

    @pl.when(step == pl.num_programs(1) - 1)
    def _():
        width = acc.shape[1]
        shares = out_ref.shape[0]
        part = width // shares
        for c in range(3):
            for d in range(shares):
                out_ref[d, 0, c * part : (c + 1) * part, :] = acc[c, d * part : (d + 1) * part, :].astype(BF16)

        @pl.when(shard == 0)
        def _():
            sum_ref[...] = gain_sum(0)

        @pl.when(shard == 1)
        def _():
            sum_ref[...] += gain_sum(1)


def ffn_grads(n2, hid, gg, gup, go, gate_up, down_t, partner, shares, block=512):
    rows, width = n2.shape
    hidden = hid.shape[1] // 2
    row = lambda n: pl.BlockSpec((block, n), lambda s, i: (i, 0))
    col = lambda n: pl.BlockSpec((block, n), lambda s, i: (i, s))
    part = width // shares
    return call(
        ffn_grad_kernel,
        (2, rows // block),
        [row(width), col(hidden), col(hidden), col(hidden), row(width),
         whole(gate_up.shape), whole(down_t.shape), whole(partner.shape)],
        [pl.BlockSpec((shares, 1, 3 * part, hidden), lambda s, i: (0, s, 0, 0)), whole((width, 128))],
        [sds((shares, 2, 3 * part, hidden), BF16), sds((width, 128), F32)],
        scratch=[pltpu.VMEM((3, width, hidden), F32)],
        flops=12 * rows * width * hidden,
        nbytes=rows * (2 * width + 3 * hidden) * 4 + 12 * width * hidden,
    )(n2, hid, gg, gup, go, gate_up, down_t, partner)


def resid_kernel(parts, members, idx_ref, len_ref, weight_ref, cot_ref, resid_ref, gn2_ref, ow_ref, gain_ref, *refs):
    gn2_refs = refs[: members - 1]
    att_refs = refs[members - 1 : members - 1 + parts]
    gr_ref, wg_ref, acc = refs[members - 1 + parts], refs[members + parts], refs[-1]
    g_refs = refs[members + parts + 1 : -1]
    rows, width = cot_ref.shape
    local = att_refs[0].shape[1]
    me = idx_ref[0]
    step = pl.program_id(0)
    first = me * rows * pl.num_programs(0) + step * rows
    slot = lax.broadcasted_iota(jnp.int32, (rows, 1), 0) + first
    row_weight = jnp.where(slot < len_ref[0], weight_ref[0], 0.0)
    gn2 = gn2_ref[...].astype(F32)
    for ref in gn2_refs:
        gn2 = gn2 + ref[...].astype(F32)
    resid = resid_ref[...]
    factor = rms(resid)
    grad = cot_ref[...].astype(F32) * row_weight + norm_back(gn2, gain_ref[1:2, :], resid * factor, factor)
    gr_ref[...] = grad
    low = grad.astype(BF16)

    @pl.when(step == 0)
    def _():
        acc[...] = jnp.zeros_like(acc)

    for d in range(parts):
        block = ow_ref[:, me ^ d].reshape(local, width)
        g_refs[d][...] = dot(low, block, NT).astype(BF16)
        acc[:, d * local : (d + 1) * local] += dot(low, att_refs[d][...], TN)

    @pl.when(step == pl.num_programs(0) - 1)
    def _():
        shares, part, _ = wg_ref.shape
        for d in range(shares):
            wg_ref[d] = acc[d * part : (d + 1) * part, :].astype(BF16)


def resid_back(index, lengths, picked, cotangent, resid, gn2, gn2_others, out_full, gains, atts, share, shares, block=256):
    width = cotangent.shape[1]
    parts = len(atts)
    local = atts[0].shape[1]
    members = len(gn2_others) + 1
    steps = share // block
    row = lambda n: pl.BlockSpec((block, n), lambda i, idx: (i, 0))
    full = lambda n: pl.BlockSpec((block, n), lambda i, idx: (idx[0] * steps + i, 0))
    half = lambda n: pl.BlockSpec((block, n), lambda i, idx: (idx[2] * steps + i, 0))
    return call(
        functools.partial(resid_kernel, parts, members),
        (steps,),
        [smem(), smem(), full(width), half(width), half(width), whole(out_full.shape), whole(gains.shape)]
        + [row(width)] * (members - 1)
        + [full(local)] + [half(local)] * (parts - 1),
        [row(width), whole((shares, width // shares, parts * local))] + [row(local)] * parts,
        [sds((share, width), F32), sds((shares, width // shares, parts * local), BF16)]
        + [sds((share, local), BF16)] * parts,
        scratch=[pltpu.VMEM((width, parts * local), F32)],
        flops=4 * share * width * width,
        nbytes=share * width * 20,
        prefetch=1,
    )(index, lengths, picked, cotangent, resid, gn2, out_full, gains, *gn2_others, *atts)


def attend_back_kernel(parts, idx_ref, g_ref, q_ref, k_ref, v_ref, att_ref, cos_ref, sin_ref, *refs):
    outs = refs[:parts]
    dk_acc, dv_acc = refs[parts:]
    rows = q_ref.shape[1]
    step = pl.program_id(0)
    me = idx_ref[0]
    lane = lax.broadcasted_iota(jnp.int32, (rows, 128), 1)

    def table(ref, d):
        return ref[pl.ds(pl.multiple_of((me ^ d) * rows, rows), rows), :]

    def back(v, d, scale):
        return ((v * table(cos_ref, d) - swap_halves(v) * table(sin_ref, d)) * scale).astype(BF16)

    @pl.when(step == 0)
    def _():
        dk_acc[...] = jnp.zeros_like(dk_acc)
        dv_acc[...] = jnp.zeros_like(dv_acc)

    grad = g_ref[0]
    prod = grad.astype(F32) * att_ref[...].astype(F32)
    zero = jnp.zeros((rows, 128), BF16)
    dqs = []
    for s in range(2):
        first = HD * (1 - s)
        own = (lane >= HD * s) & (lane < HD * (s + 1))
        delta = jnp.sum(jnp.where(own, prod, 0.0), axis=1, keepdims=True)
        hi, mid, low = split3(-delta)
        grad_own = jnp.where(own, grad, zero)
        grad_aug = jnp.where(lane == first + 2, low, grad_own)
        grad_aug = jnp.where(lane == first + 1, mid, grad_aug)
        grad_aug = jnp.where(lane == first, hi, grad_aug)
        q = q_ref[s]
        probs = jnp.exp2(dot(k_ref[s], q, NT))
        scores_grad = (probs * dot(v_ref[s], grad_aug, NT)).astype(BF16)
        dv_acc[...] += dot(probs.astype(BF16), grad_own)
        dk_acc[...] += dot(scores_grad, jnp.where(own, q, zero))
        dqs.append(dot(k_ref[s], scores_grad, TN).T)
    dq = jnp.where(lane < HD, dqs[0], dqs[1])
    for d in range(parts):

        @pl.when(step == d)
        def _():
            outs[d][0] = back(dq, d, FACTOR)

    @pl.when(step == parts - 1)
    def _():
        for d in range(parts):
            outs[d][1] = back(table(dk_acc, d), d, LN2)
            outs[d][2] = table(dv_acc, d).astype(BF16)


def attend_back(index, grads, q, k, v, att, cosine, sine, pair):
    parts, share, _ = grads.shape
    rows = q.shape[1]
    keys = pl.BlockSpec((2, rows, 128), lambda i, idx: (pair, 0, 0), pipeline_mode=pl.Buffered(1))
    return call(
        functools.partial(attend_back_kernel, parts),
        (parts,),
        [
            pl.BlockSpec((1, share, 128), lambda i, idx: (i, 0, pair)),
            pl.BlockSpec((2, share, 128), lambda i, idx: (pair, idx[0] ^ i, 0)),
            keys,
            keys,
            pl.BlockSpec((share, 128), lambda i, idx: (idx[0] ^ i, pair)),
            whole(cosine.shape),
            whole(sine.shape),
        ],
        [whole((3, share, 128))] * parts,
        [sds((3, share, 128), BF16)] * parts,
        scratch=[pltpu.VMEM((rows, 128), F32)] * 2,
        flops=2 * rows * rows * 128 * 10,
        nbytes=rows * 256 * 16,
        trans=2 * rows * rows,
        prefetch=1,
    )(index, grads, q, k, v, att, cosine, sine)


def project_grad_kernel(parts, pairs, idx_ref, x_ref, w_ref, gain_ref, *refs):
    act_refs = refs[: parts * pairs]
    wg_ref, sum_ref, acc = refs[parts * pairs :]
    step = pl.program_id(0)

    @pl.when(step == 0)
    def _():
        acc[...] = jnp.zeros_like(acc)

    x = x_ref[...].astype(F32)
    normed = (x * rms(x) * gain_ref[0:1, :]).astype(BF16)
    for d in range(parts):

        @pl.when(step == d)
        def _():
            acts = [act_refs[j * parts + d][c] for c in range(3) for j in range(pairs)]
            acc[...] += dot(normed, jnp.concatenate(acts, axis=1), TN)

    @pl.when(step == pl.num_programs(0) - 1)
    def _():
        shares, part, _ = wg_ref.shape
        local = w_ref.shape[2]
        for d in range(shares):
            wg_ref[d] = acc[d * part : (d + 1) * part, :].astype(BF16)
        gain_sum = acc[:, :local] * w_ref[0].astype(F32)
        for c in (1, 2):
            gain_sum += acc[:, c * local : (c + 1) * local] * w_ref[c].astype(F32)
        sum_ref[...] = jnp.broadcast_to(jnp.sum(gain_sum, axis=1, keepdims=True), sum_ref.shape)


def project_grads(index, tokens, acts, qkv_weight, gains, shares):
    width = tokens.shape[1]
    local = qkv_weight.shape[2]
    pairs, parts = len(acts), len(acts[0])
    share = acts[0][0].shape[1]
    flat = [a for group in acts for a in group]
    return call(
        functools.partial(project_grad_kernel, parts, pairs),
        (parts,),
        [
            pl.BlockSpec((share, width), lambda i, idx: (idx[0] ^ i, 0)),
            whole(qkv_weight.shape),
            whole(gains.shape),
        ]
        + [whole(a.shape) for a in flat],
        [whole((shares, width // shares, 3 * local)), whole((width, 128))],
        [sds((shares, width // shares, 3 * local), BF16), sds((width, 128), F32)],
        scratch=[pltpu.VMEM((width, 3 * local), F32)],
        flops=2 * tokens.shape[0] * width * 3 * local,
        nbytes=tokens.size * 2 + 8 * width * local * 3,
        prefetch=1,
    )(index, tokens, qkv_weight, gains, *flat)


def token_grad_kernel(parts, pairs, idx_ref, x_ref, gr_ref, w_ref, gain_ref, *refs):
    act_refs = refs[: parts * pairs]
    out_ref = refs[-1]
    me = idx_ref[0]
    width = x_ref.shape[1]
    local = 128 * pairs
    grad = jnp.zeros(x_ref.shape, F32)
    for d in range(parts):
        for c in range(3):
            act = jnp.concatenate([act_refs[j * parts + d][c] for j in range(pairs)], axis=1)
            grad = grad + dot(act, w_ref[:, me ^ d, c].reshape(width, local), NT)
    x = x_ref[...].astype(F32)
    factor = rms(x)
    out_ref[...] = gr_ref[...] + norm_back(grad, gain_ref[0:1, :], x * factor, factor)


def token_grad(index, tokens, grad_resid, qkv_full, gains, acts, block=256):
    share, width = grad_resid.shape
    pairs, parts = len(acts), len(acts[0])
    flat = [a for group in acts for a in group]
    steps = share // block
    return call(
        functools.partial(token_grad_kernel, parts, pairs),
        (steps,),
        [
            pl.BlockSpec((block, width), lambda i, idx: (idx[0] * steps + i, 0)),
            pl.BlockSpec((block, width), lambda i, idx: (i, 0)),
            whole(qkv_full.shape),
            whole(gains.shape),
        ]
        + [pl.BlockSpec((3, block, 128), lambda i, idx: (0, i, 0))] * len(flat),
        pl.BlockSpec((block, width), lambda i, idx: (i, 0)),
        sds((share, width), F32),
        flops=2 * share * width * width * 3,
        nbytes=share * width * 10 + 6 * width * width,
        prefetch=1,
    )(index, tokens, grad_resid, qkv_full, gains, *flat)


def body(
    tokens, qkv_weight, out_weight, gate_up_weight, down_weight, norm_gains,
    species_weight, species_ids, lengths, cotangent,
):
    rows, width = tokens.shape
    local = out_weight.shape[0]
    hidden = down_weight.shape[0]
    parts = lax.axis_size("tensor")
    members = parts // 2
    shares = lax.axis_size("dp")
    part = width // shares
    share = rows // parts
    me = lax.axis_index("tensor")
    dp = lax.axis_index("dp")
    half = me // members
    seat = me % members
    index = jnp.stack([me, half, seat]).astype(jnp.int32)
    cosine, sine = (jnp.asarray(t) for t in rotary_tables())
    pairs = local // 128

    def swap(a, d):
        return lax.ppermute(a, "tensor", [(i, i ^ d) for i in range(parts)])

    def cut(a, start, size, axis=0):
        return lax.dynamic_slice_in_dim(a, start, size, axis)

    def spread(a):
        stacked = [a] + [swap(a, d) for d in range(1, parts)]
        order = [lax.dynamic_index_in_dim(jnp.stack(stacked), me ^ d, 0, keepdims=False) for d in range(parts)]
        return lax.all_gather(jnp.stack(order), "dp", axis=0)

    matches = species_ids[:, None] == jnp.arange(species_weight.shape[0])[None, :]
    picked = jnp.sum(jnp.where(matches, species_weight[None, :], F32(0.0)), axis=1)

    down_t = down_weight.T
    out_full = spread(cut(out_weight, dp * (local // shares), local // shares))
    mine = jnp.concatenate(
        [cut(gate_up_weight[0], dp * part, part), cut(gate_up_weight[1], dp * part, part), cut(down_t, dp * part, part)]
    )
    partner = lax.all_gather(swap(mine, members), "dp", axis=0)
    qkv_full = spread(cut(qkv_weight, dp * part, part, 1))

    q, k, v = project(lengths, tokens, qkv_weight, norm_gains, cosine, sine)
    att, q_back = attend(q, k, v)
    near = cut(att, half * (rows // 2), rows // 2)
    far = cut(att, (1 - half) * (rows // 2), rows // 2)
    atts = [att] + [swap(near if d < members else far, d) for d in range(1, parts)]

    resid, n2, ffn, gn2, hid, gg, gup, go = feed_forward(
        index, lengths, picked, atts, tokens, cotangent, out_full, gate_up_weight, down_t, partner, norm_gains
    )
    gn2_others = [swap(cut(gn2, (seat ^ d) * share, share), d) for d in range(1, members)]
    ffn_wg, gain_two = ffn_grads(n2, hid, gg, gup, go, gate_up_weight, down_t, partner, shares)
    grad_resid, op_wg, *grads = resid_back(
        index, lengths, picked, cotangent, resid, gn2, gn2_others, out_full, norm_gains, atts, share, shares
    )
    grads = jnp.stack([grads[0]] + [swap(grads[d], d) for d in range(1, parts)])

    acts, got = [], []
    for j in range(pairs):
        group = attend_back(index, grads, q_back, k, v, att, cosine, sine, j)
        acts.append(group)
        got.append([group[0]] + [swap(group[d], d) for d in range(1, parts)])
    qkv_wg, gain_one = project_grads(index, tokens, acts, qkv_weight, norm_gains, shares)
    grad_tok = token_grad(index, tokens, grad_resid, qkv_full, norm_gains, got)

    ffn_own = cut(ffn, seat * share, share).astype(F32)
    for d in range(1, members):
        ffn_own = ffn_own + swap(cut(ffn, (seat ^ d) * share, share), d).astype(F32)
    out = cut(resid, seat * share, share) + ffn_own

    gains_grad = jnp.stack([gain_one[:, 0], gain_two[:, 0]]) / norm_gains
    for name, size in (("dp", shares), ("tensor", parts)):
        d = 1
        while d < size:
            gains_grad = gains_grad + lax.ppermute(gains_grad, name, [(i, i ^ d) for i in range(size)])
            d *= 2

    ffn_sum = lax.psum_scatter(ffn_wg, "dp", scatter_dimension=0, tiled=True)[0]
    ffn_sum = ffn_sum[0].astype(F32) + swap(ffn_sum[1], members).astype(F32)
    op_sum = lax.psum_scatter(op_wg, "dp", scatter_dimension=0, tiled=True)[0]
    grad_op = op_sum[:, :local].astype(F32)
    for d in range(1, parts):
        grad_op = grad_op + swap(op_sum[:, d * local : (d + 1) * local], d).astype(F32)
    qkv_sum = lax.psum_scatter(qkv_wg, "dp", scatter_dimension=0, tiled=True)[0].astype(F32)

    grad_gu = ffn_sum[: 2 * part].reshape(2, part, hidden)
    grad_down = ffn_sum[2 * part :].T
    grad_qkv = jnp.stack([qkv_sum[:, c * local : (c + 1) * local] for c in range(3)])
    return (out, grad_tok, grad_qkv, grad_op.T, grad_gu, grad_down, gains_grad)


def solution(mesh):
    in_specs = (
        P("dp", None),
        P(None, None, "tensor"),
        P("tensor", None),
        P(None, None, "tensor"),
        P("tensor", None),
        P(),
        P(),
        P("dp"),
        P("dp"),
        P("dp", None),
    )
    out_specs = (
        P(("dp", "tensor"), None),
        P(("dp", "tensor"), None),
        P(None, "dp", "tensor"),
        P("tensor", "dp"),
        P(None, "dp", "tensor"),
        P("tensor", "dp"),
        P(),
    )
    return jax.shard_map(body, mesh=mesh, in_specs=in_specs, out_specs=out_specs, check_vma=False)
```

```python
import functools
import math

import jax
import jax.numpy as jnp
import numpy as np
from jax import lax
from jax.experimental import pallas as pl
from jax.experimental.pallas import tpu as pltpu
from jax.sharding import PartitionSpec as P

HD = 64
WIN = 2048
EPSILON = 1e-05
NEG_FILL = -1e30
LOG2E = math.log2(math.e)
LN2 = math.log(2.0)
FACTOR = HD ** (-0.5)
VMEM = 60 * 2**20
F32 = jnp.float32
BF16 = jnp.bfloat16

NN = (((1,), (0,)), ((), ()))
NT = (((1,), (1,)), ((), ()))
TN = (((0,), (0,)), ((), ()))


def dot(a, b, dims=NN):
    return lax.dot_general(a, b, dims, preferred_element_type=F32)


def call(kernel, grid, in_specs, out_specs, out_shape, scratch=(), flops=0, nbytes=0, trans=0, prefetch=0):
    return pl.pallas_call(
        kernel,
        grid_spec=pltpu.PrefetchScalarGridSpec(
            num_scalar_prefetch=prefetch,
            grid=grid,
            in_specs=in_specs,
            out_specs=out_specs,
            scratch_shapes=list(scratch),
        ),
        out_shape=out_shape,
        compiler_params=pltpu.CompilerParams(vmem_limit_bytes=VMEM),
        cost_estimate=pl.CostEstimate(flops=flops, bytes_accessed=nbytes, transcendentals=trans),
    )


def whole(shape):
    return pl.BlockSpec(shape, lambda *_: (0,) * len(shape), pipeline_mode=pl.Buffered(1))


def smem():
    return pl.BlockSpec(memory_space=pltpu.SMEM)


def sds(shape, dtype):
    return jax.ShapeDtypeStruct(shape, dtype)


def rotary_tables():
    position = np.arange(WIN, dtype=np.float64)
    frequency = 10000.0 ** (-2.0 * np.arange(HD // 2, dtype=np.float64) / HD)
    angles = position[:, None] * frequency[None, :]
    cosine = np.cos(angles)
    sine = np.sin(angles)
    cos_full = np.tile(np.concatenate([cosine, cosine], axis=1), (1, 2))
    sin_full = np.tile(np.concatenate([-sine, sine], axis=1), (1, 2))
    return cos_full.astype(np.float32), sin_full.astype(np.float32)


def swap_halves(v):
    lane = lax.broadcasted_iota(jnp.int32, v.shape, 1)
    return jnp.where(lane % HD < HD // 2, pltpu.roll(v, 96, 1), pltpu.roll(v, 32, 1))


def rms(x):
    return lax.rsqrt(jnp.mean(x * x, axis=-1, keepdims=True) + EPSILON)


def split3(v):
    hi = v.astype(BF16)
    rest = v - hi.astype(F32)
    mid = rest.astype(BF16)
    low = (rest - mid.astype(F32)).astype(BF16)
    return hi, mid, low


def norm_back(grad_normed, gain, unit, factor):
    scaled = grad_normed * gain
    return factor * (scaled - unit * jnp.mean(scaled * unit, axis=-1, keepdims=True))


def qkv_kernel(len_ref, x_ref, w_ref, gain_ref, cos_ref, sin_ref, q_ref, k_ref, v_ref):
    rows = x_ref.shape[0]
    x = x_ref[...].astype(F32)
    normed = (x * rms(x) * gain_ref[0:1, :]).astype(BF16)
    cosine = cos_ref[...]
    sine = sin_ref[...]
    lane = lax.broadcasted_iota(jnp.int32, (rows, 128), 1)
    slot = lax.broadcasted_iota(jnp.int32, (rows, 128), 0) + pl.program_id(0) * rows
    masked = jnp.where(slot < len_ref[0], 0.0, NEG_FILL).astype(BF16)
    one = jnp.ones((rows, 128), BF16)
    zero = jnp.zeros((rows, 128), BF16)
    pairs = w_ref.shape[2] // 128
    for c in range(3):
        y = dot(normed, w_ref[c])
        for j in range(pairs):
            v = y[:, 128 * j : 128 * (j + 1)]
            if c < 2:
                v = v * cosine + swap_halves(v) * sine
            if c == 0:
                v = v * (FACTOR * LOG2E)
            v = v.astype(BF16)
            for s in range(2):
                first = HD * (1 - s)
                own = (lane >= HD * s) & (lane < HD * (s + 1))
                if c == 0:
                    q_ref[2 * j + s] = jnp.where(own, v, jnp.where(lane == first, one, zero))
                elif c == 1:
                    tail = jnp.where(
                        lane == first, masked, jnp.where(lane < first + 4, one, zero)
                    )
                    tail = jnp.where(lane < first, zero, tail)
                    k_ref[2 * j + s] = jnp.where(own, v, tail)
                else:
                    v_ref[2 * j + s] = jnp.where(own, v, one)


def project(lengths, tokens, qkv_weight, gains, cosine, sine, block=512):
    rows, width = tokens.shape
    local = qkv_weight.shape[2]
    heads = local // HD
    spec = pl.BlockSpec((heads, block, 128), lambda i: (0, i, 0))
    return call(
        qkv_kernel,
        (rows // block,),
        [
            smem(),
            pl.BlockSpec((block, width), lambda i: (i, 0)),
            whole(qkv_weight.shape),
            whole(gains.shape),
            pl.BlockSpec((block, 128), lambda i: (i, 0)),
            pl.BlockSpec((block, 128), lambda i: (i, 0)),
        ],
        [spec] * 3,
        [sds((heads, rows, 128), BF16)] * 3,
        flops=2 * rows * width * 3 * local,
        nbytes=rows * width * 2 + 3 * heads * rows * 256,
    )(lengths, tokens, qkv_weight, gains, cosine, sine)


def attend_kernel(sub, parts, idx_ref, q_ref, k_ref, v_ref, *refs):
    o_refs = refs[:parts]
    nat_ref, qb_ref = refs[parts:]
    rows = q_ref.shape[1]
    lane = lax.broadcasted_iota(jnp.int32, (sub, 128), 1)
    for r in range(rows // sub):
        part = slice(r * sub, (r + 1) * sub)
        outs = []
        for s in range(2):
            q = q_ref[s, part, :]
            scores = dot(q, k_ref[s], NT)
            peak = jnp.max(scores, axis=1, keepdims=True)
            expo = jnp.exp2(scores - peak).astype(BF16)
            acc = dot(expo, v_ref[s])
            outs.append(acc / pltpu.roll(acc, HD, 1))
            first = HD * (1 - s)
            total = jnp.where((lane >= first) & (lane < first + HD), acc, 1.0)
            hi, mid, low = split3(-(peak + jnp.log2(total)))
            tail = jnp.where(lane == first + 3, low, q)
            tail = jnp.where(lane == first + 2, mid, tail)
            qb_ref[s, part, :] = jnp.where(lane == first + 1, hi, tail)
        nat_ref[part, :] = jnp.where(lane < HD, outs[0], outs[1]).astype(BF16)
    for d in range(parts):

        @pl.when(pl.program_id(1) == d)
        def _():
            o_refs[d][...] = nat_ref[...]


def attend(index, q, k, v, parts, sub=256):
    heads, rows, _ = q.shape
    keys = k.shape[1]
    share = rows // parts
    local = heads * HD
    return call(
        functools.partial(attend_kernel, min(sub, share), parts),
        (heads // 2, parts),
        [
            pl.BlockSpec((2, share, 128), lambda j, i, idx: (j, idx[0] ^ i, 0)),
            pl.BlockSpec((2, keys, 128), lambda j, i, idx: (j, 0, 0)),
            pl.BlockSpec((2, keys, 128), lambda j, i, idx: (j, 0, 0)),
        ],
        [pl.BlockSpec((share, 128), lambda j, i, idx: (0, j))] * parts
        + [
            pl.BlockSpec((share, 128), lambda j, i, idx: (idx[0] ^ i, j)),
            pl.BlockSpec((2, share, 128), lambda j, i, idx: (j, idx[0] ^ i, 0)),
        ],
        [sds((share, local), BF16)] * parts + [sds((rows, local), BF16), sds((heads, rows, 128), BF16)],
        flops=heads * rows * keys * 128 * 4,
        nbytes=heads * (2 * rows + 2 * keys) * 256,
        trans=heads * rows * keys,
        prefetch=1,
    )(index, q, k, v)


def cut_kernel(idx_ref, gu_ref, dw_ref, first_ref, second_ref):
    part = gu_ref.shape[1]
    half = part // 2
    first_ref[:part, :] = gu_ref[0]
    first_ref[part:, :] = gu_ref[1, :half, :]
    second_ref[:half, :] = gu_ref[1, half:, :]
    second_ref[half:, :] = dw_ref[...].T


def cut_weights(dp, gate_up, down, shares):
    _, width, hidden = gate_up.shape
    part = width // shares
    if part % 128:
        down = lax.dynamic_slice_in_dim(down, dp[0] * part, part, 1)
        spec = whole(down.shape)
    else:
        spec = pl.BlockSpec((hidden, part), lambda i, idx: (0, idx[0]))
    chunk = (3 * part // 2, hidden)
    return call(
        cut_kernel,
        (1,),
        [pl.BlockSpec((2, part, hidden), lambda i, idx: (0, idx[0], 0)), spec],
        [whole(chunk)] * 2,
        [sds(chunk, BF16)] * 2,
        nbytes=12 * part * hidden,
        prefetch=1,
    )(dp, gate_up, down)


def ffn_kernel(parts, shares, slot, idx_ref, len_ref, weight_ref, gain_ref, x_h, cot_h, ow_h, gu_h, dw_h, *refs):
    own = slot == 0
    att_h = refs[:parts]
    pieces_h = refs[parts : parts + 2 * shares]
    refs = refs[parts + 2 * shares :]
    count = 5 if own else 4
    outs, scratch = refs[:count], refs[count:]
    x_v, cot_v, att_v, ow_v, gu_v, dw_v, pb_v, left_v, act_v, ffn_v, gn2_v, low_v, sem_in, sem_out = scratch
    rows, width = x_v.shape
    local = att_v.shape[2]
    hidden_units = gu_v.shape[2]
    part = pb_v.shape[1] // 3
    row0 = pl.multiple_of((idx_ref[0] ^ slot) * rows, rows)
    mine = pl.ds(row0, rows)

    def fetch(src, dst, i):
        copy = pltpu.make_async_copy(src, dst, sem_in.at[i])
        copy.start()
        return copy

    pending = []

    def store(src, dst, i):
        copy = pltpu.make_async_copy(src, dst, sem_out.at[i])
        copy.start()
        pending.append(copy)

    get_x = fetch(x_h.at[mine], x_v, 0)
    get_ow = fetch(ow_h, ow_v, 1)
    get_att = [fetch(att_h[d], att_v.at[d], 2 + d) for d in range(parts)]
    get_cot = fetch(cot_h.at[mine], cot_v, 2 + parts)
    get_gu = fetch(gu_h, gu_v, 3 + parts)
    get_dw = fetch(dw_h, dw_v, 4 + parts)
    chunk = pb_v.shape[1] // 2
    get_pb = []
    for c in range(2):
        for x in range(shares):
            rows_at = pl.ds(c * chunk, chunk)
            get_pb.append(fetch(pieces_h[c * shares + x], pb_v.at[idx_ref[3] ^ x, rows_at], 5 + parts + len(get_pb)))

    get_x.wait()
    get_ow.wait()
    resid = x_v[...].astype(F32)
    for d in range(parts):
        get_att[d].wait()
        resid = resid + dot(att_v[d], ow_v[:, d].reshape(local, width))
    if own:
        ffn_v[...] = resid
        store(ffn_v, outs[4], 4)
    normed = (resid * rms(resid) * gain_ref[1:2, :]).astype(BF16)
    left_v[0] = normed
    position = lax.broadcasted_iota(jnp.int32, (rows, 1), 0) + row0
    row_weight = jnp.where(position < len_ref[0], weight_ref[0], 0.0)
    get_cot.wait()
    left_v[1] = (cot_v[...].astype(F32) * row_weight).astype(BF16)
    store(left_v, outs[0], 0)
    for shard in range(2):
        cols = slice(shard * hidden_units, (shard + 1) * hidden_units)
        if shard == 0:
            get_gu.wait()
            get_dw.wait()
            gate_w, up_w, down_w = gu_v[0], gu_v[1], dw_v[...]
        else:
            for copy in get_pb:
                copy.wait()
            gate_w, up_w, down_w = (
                pb_v[:, c * part : (c + 1) * part, :].reshape(width, hidden_units) for c in range(3)
            )
        gate = dot(left_v[0], gate_w)
        upper = dot(left_v[0], up_w)
        grad_hidden = dot(left_v[1], down_w, NT if shard == 0 else NN)
        sigma = jax.nn.sigmoid(gate)
        act = gate * sigma
        hidden = (act * upper).astype(BF16)
        grad_up = (grad_hidden * act).astype(BF16)
        grad_gate = (grad_hidden * upper * (sigma + act * (1.0 - sigma))).astype(BF16)
        act_v[0, :, cols] = grad_gate
        act_v[1, :, cols] = grad_up
        act_v[2, :, cols] = hidden
        grad = dot(grad_gate, gate_w, NT) + dot(grad_up, up_w, NT)
        term = dot(hidden, down_w, NN if shard == 0 else NT)
        if shard == 0:
            gn2_v[...] = grad
            if own:
                pending.pop(0).wait()
            ffn_v[...] = term
        else:
            low_v[0] = (gn2_v[...] + grad).astype(BF16)
            store(low_v.at[0], outs[2], 2)
            low_v[1] = (ffn_v[...] + term).astype(BF16)
            store(low_v.at[1], outs[3], 3)
    store(act_v, outs[1], 1)
    for copy in pending:
        copy.wait()


def feed_forward(slot, index, lengths, picked, atts, tokens, cotangent, out_full, gate_up, down, partner, gains):
    parts = len(atts)
    shares = len(partner) // 2
    rows, local = atts[0].shape
    width = tokens.shape[1]
    hidden = gate_up.shape[2]
    anywhere = pl.BlockSpec(memory_space=pl.ANY)
    out_shape = [
        sds((2, rows, width), BF16), sds((3, rows, 2 * hidden), BF16),
        sds((rows, width), BF16), sds((rows, width), BF16),
    ]
    if slot == 0:
        out_shape.append(sds((rows, width), F32))
    return call(
        functools.partial(ffn_kernel, parts, shares, slot),
        (1,),
        [smem(), smem(), whole(gains.shape)] + [anywhere] * (5 + parts + 2 * shares),
        [anywhere] * len(out_shape),
        out_shape,
        scratch=[
            pltpu.VMEM((rows, width), BF16),
            pltpu.VMEM((rows, width), BF16),
            pltpu.VMEM((parts, rows, local), BF16),
            pltpu.VMEM(out_full.shape, BF16),
            pltpu.VMEM(gate_up.shape, BF16),
            pltpu.VMEM(down.shape, BF16),
            pltpu.VMEM((shares, 2 * partner[0].shape[0], hidden), BF16),
            pltpu.VMEM((2, rows, width), BF16),
            pltpu.VMEM((3, rows, 2 * hidden), BF16),
            pltpu.VMEM((rows, width), F32),
            pltpu.VMEM((rows, width), F32),
            pltpu.VMEM((2, rows, width), BF16),
            pltpu.SemaphoreType.DMA((5 + parts + 2 * shares,)),
            pltpu.SemaphoreType.DMA((5,)),
        ],
        flops=2 * rows * width * (width + 12 * hidden),
        nbytes=rows * width * 30 + 12 * width * hidden,
        trans=rows * hidden * 2,
        prefetch=1,
    )(index, lengths, picked, gains, tokens, cotangent, out_full, gate_up, down, *atts, *partner)


def ffn_grad_kernel(sets, split, extra, idx_ref, *refs):
    left = refs[:sets]
    act = refs[sets : 2 * sets]
    refs = refs[2 * sets :]
    step = pl.program_id(0)

    def write(total, outs):
        part = outs[0].shape[-2]
        for out in outs:
            count = out.shape[0]
            for j in range(count):
                if len(outs) == 1:
                    out[j] = total[j * part : (j + 1) * part, :].astype(BF16)
        if len(outs) == 2:
            for keep in range(2):
                for bit in range(2):

                    @pl.when((idx_ref[3] & 1) == bit)
                    def _():
                        for j in range(outs[0].shape[0]):
                            d = 2 * j + (bit if keep else 1 - bit)
                            outs[keep][j] = total[d * part : (d + 1) * part, :].astype(BF16)

    outs = refs[2:] if extra else refs

    @pl.when(step < 3)
    def _():
        total = dot(left[0][0], act[0][0], TN)
        for e in range(1, sets):
            total = total + dot(left[e][0], act[e][0], TN)
        write(total, outs)

    if extra:

        @pl.when(step >= 3)
        def _():
            write(dot(refs[0][...], refs[1][...], TN), outs)


def ffn_grads(index, lefts, acts, shard, shares, split, grad_low=None, att_own=None):
    sets = len(lefts)
    _, rows, width = lefts[0].shape
    hidden = acts[0].shape[2] // 2
    part = width // shares
    extra = 0 if grad_low is None else att_own.shape[1] // hidden
    steps = 3 + extra
    specs = [pl.BlockSpec((1, rows, width), lambda c, idx: (jnp.minimum(c // 2, 1), 0, 0))] * sets
    specs += [pl.BlockSpec((1, rows, hidden), lambda c, idx: (jnp.minimum(c, 2), 0, shard))] * sets
    args = list(lefts) + list(acts)
    if extra:
        specs += [
            pl.BlockSpec(grad_low.shape, lambda c, idx: (0, 0)),
            pl.BlockSpec((att_own.shape[0], hidden), lambda c, idx: (0, jnp.maximum(c - 3, 0))),
        ]
        args += [grad_low, att_own]
    count = shares // 2 if split else shares
    out_spec = pl.BlockSpec((count, part, hidden), lambda c, idx: (0, c, 0))
    out_shape = sds((count, steps * part, hidden), BF16)
    outs = 2 if split else 1
    return call(
        functools.partial(ffn_grad_kernel, sets, split, extra),
        (steps,),
        specs,
        [out_spec] * outs,
        [out_shape] * outs,
        flops=2 * sets * rows * width * hidden * steps,
        nbytes=sets * rows * (2 * width + 3 * hidden) * 2 + steps * width * hidden * 2,
        prefetch=1,
    )(index, *args)


def resid_kernel(parts, members, idx_ref, len_ref, weight_ref, cot_ref, resid_ref, ow_ref, gain_ref, *refs):
    gn2_refs = refs[:members]
    att_refs = refs[members : members + parts]
    gr_ref, low_ref, cat_ref, sum_ref = refs[members + parts : members + parts + 4]
    g_refs = refs[members + parts + 4 :]
    rows, width = cot_ref.shape
    local = att_refs[0].shape[1]
    step = pl.program_id(0)
    first = (idx_ref[0] * pl.num_programs(0) + step) * rows
    slot = lax.broadcasted_iota(jnp.int32, (rows, 1), 0) + first
    row_weight = jnp.where(slot < len_ref[0], weight_ref[0], 0.0)
    gn2 = gn2_refs[0][...].astype(F32)
    for ref in gn2_refs[1:]:
        gn2 = gn2 + ref[...].astype(F32)
    resid = resid_ref[...]
    factor = rms(resid)
    unit = resid * factor
    grad = cot_ref[...].astype(F32) * row_weight + norm_back(gn2, gain_ref[1:2, :], unit, factor)
    gr_ref[...] = grad
    low = grad.astype(BF16)
    low_ref[...] = low

    @pl.when(step == 0)
    def _():
        sum_ref[...] = jnp.zeros_like(sum_ref)

    sum_ref[...] += jnp.sum((gn2 * unit).reshape(rows // 8, 8, width), axis=0)
    for d in range(parts):
        g_refs[d][...] = dot(low, ow_ref[:, d].reshape(local, width), NT).astype(BF16)
        cat_ref[:, d * local : (d + 1) * local] = att_refs[d][...]


def resid_back(index, lengths, picked, cotangent, resid, gn2s, out_full, gains, atts, block=256):
    share, width = resid.shape
    parts, members = len(atts), len(gn2s)
    local = atts[0].shape[1]
    steps = share // block
    row = lambda n: pl.BlockSpec((block, n), lambda i, idx: (i, 0))
    return call(
        functools.partial(resid_kernel, parts, members),
        (steps,),
        [
            smem(), smem(),
            pl.BlockSpec((block, width), lambda i, idx: (idx[0] * steps + i, 0)),
            row(width), whole(out_full.shape), whole(gains.shape),
        ]
        + [row(width)] * members
        + [row(local)] * parts,
        [row(width), row(width), row(parts * local), whole((8, width))] + [row(local)] * parts,
        [sds((share, width), F32), sds((share, width), BF16), sds((share, parts * local), BF16), sds((8, width), F32)]
        + [sds((share, local), BF16)] * parts,
        flops=2 * share * width * width,
        nbytes=share * width * 20,
        prefetch=1,
    )(index, lengths, picked, cotangent, resid, out_full, gains, *gn2s, *atts)


def attend_back_kernel(parts, idx_ref, q_ref, k_ref, v_ref, att_ref, cos_ref, sin_ref, *refs):
    grad_refs = refs[:parts]
    outs = refs[parts : 2 * parts]
    dk_acc, dv_acc = refs[2 * parts :]
    rows = q_ref.shape[1]
    step = pl.program_id(0)
    me = idx_ref[0]
    lane = lax.broadcasted_iota(jnp.int32, (rows, 128), 1)

    def table(ref, d):
        return ref[pl.ds(pl.multiple_of((me ^ d) * rows, rows), rows), :]

    def back(v, d, scale):
        return ((v * table(cos_ref, d) - swap_halves(v) * table(sin_ref, d)) * scale).astype(BF16)

    @pl.when(step == 0)
    def _():
        dk_acc[...] = jnp.zeros_like(dk_acc)
        dv_acc[...] = jnp.zeros_like(dv_acc)

    grad = grad_refs[0][...]
    for d in range(1, parts):
        grad = jnp.where(step == d, grad_refs[d][...], grad)
    prod = grad.astype(F32) * att_ref[...].astype(F32)
    zero = jnp.zeros((rows, 128), BF16)
    dqs = []
    for s in range(2):
        first = HD * (1 - s)
        own = (lane >= HD * s) & (lane < HD * (s + 1))
        delta = jnp.sum(jnp.where(own, prod, 0.0), axis=1, keepdims=True)
        hi, mid, low = split3(-delta)
        grad_own = jnp.where(own, grad, zero)
        grad_aug = jnp.where(lane == first + 2, low, grad_own)
        grad_aug = jnp.where(lane == first + 1, mid, grad_aug)
        grad_aug = jnp.where(lane == first, hi, grad_aug)
        q = q_ref[s]
        probs = jnp.exp2(dot(k_ref[s], q, NT))
        scores_grad = (probs * dot(v_ref[s], grad_aug, NT)).astype(BF16)
        dv_acc[...] += dot(probs.astype(BF16), grad_own)
        dk_acc[...] += dot(scores_grad, jnp.where(own, q, zero))
        dqs.append(dot(k_ref[s], scores_grad, TN).T)
    dq = jnp.where(lane < HD, dqs[0], dqs[1])
    for d in range(parts):

        @pl.when(step == d)
        def _():
            outs[d][0] = back(dq, d, FACTOR)

    @pl.when(step == parts - 1)
    def _():
        for d in range(parts):
            outs[d][1] = back(table(dk_acc, d), d, LN2)
            outs[d][2] = table(dv_acc, d).astype(BF16)


def attend_back(index, grads, q, k, v, att, cosine, sine, pair):
    parts = len(grads)
    share = grads[0].shape[0]
    rows = q.shape[1]
    keys = pl.BlockSpec((2, rows, 128), lambda i, idx: (pair, 0, 0), pipeline_mode=pl.Buffered(1))
    return call(
        functools.partial(attend_back_kernel, parts),
        (parts,),
        [
            pl.BlockSpec((2, share, 128), lambda i, idx: (pair, idx[0] ^ i, 0)),
            keys,
            keys,
            pl.BlockSpec((share, 128), lambda i, idx: (idx[0] ^ i, pair)),
            whole(cosine.shape),
            whole(sine.shape),
        ]
        + [pl.BlockSpec((share, 128), lambda i, idx: (0, pair))] * parts,
        [whole((3, share, 128))] * parts,
        [sds((3, share, 128), BF16)] * parts,
        scratch=[pltpu.VMEM((rows, 128), F32)] * 2,
        flops=2 * rows * rows * 128 * 10,
        nbytes=rows * 256 * 16,
        trans=2 * rows * rows,
        prefetch=1,
    )(index, q, k, v, att, cosine, sine, *grads)


def project_grad_kernel(parts, pairs, idx_ref, x_ref, w_ref, gain_ref, *refs):
    act_refs = refs[: parts * pairs]
    away_ref, keep_ref, sum_ref, acc = refs[parts * pairs :]
    step = pl.program_id(0)

    @pl.when(step == 0)
    def _():
        acc[...] = jnp.zeros_like(acc)

    x = x_ref[...].astype(F32)
    normed = (x * rms(x) * gain_ref[0:1, :]).astype(BF16)
    for d in range(parts):

        @pl.when(step == d)
        def _():
            acts = [act_refs[j * parts + d][c] for c in range(3) for j in range(pairs)]
            acc[...] += dot(normed, jnp.concatenate(acts, axis=1), TN)

    @pl.when(step == pl.num_programs(0) - 1)
    def _():
        count, part, _ = keep_ref.shape
        local = w_ref.shape[2]
        core = idx_ref[3] & 1
        for j in range(count):
            keep_ref[j] = acc[pl.ds(pl.multiple_of((2 * j + core) * part, part), part), :].astype(BF16)
            away_ref[j] = acc[pl.ds(pl.multiple_of((2 * j + 1 - core) * part, part), part), :].astype(BF16)
        gain_sum = acc[:, :local] * w_ref[0].astype(F32)
        for c in (1, 2):
            gain_sum += acc[:, c * local : (c + 1) * local] * w_ref[c].astype(F32)
        sum_ref[...] = jnp.broadcast_to(jnp.sum(gain_sum, axis=1, keepdims=True), sum_ref.shape)


def project_grads(index, tokens, acts, qkv_weight, gains, shares):
    width = tokens.shape[1]
    local = qkv_weight.shape[2]
    pairs, parts = len(acts), len(acts[0])
    share = acts[0][0].shape[1]
    flat = [a for group in acts for a in group]
    half = (shares // 2, width // shares, 3 * local)
    return call(
        functools.partial(project_grad_kernel, parts, pairs),
        (parts,),
        [
            pl.BlockSpec((share, width), lambda i, idx: (idx[0] ^ i, 0)),
            whole(qkv_weight.shape),
            whole(gains.shape),
        ]
        + [whole(a.shape) for a in flat],
        [whole(half), whole(half), whole((width, 128))],
        [sds(half, BF16), sds(half, BF16), sds((width, 128), F32)],
        scratch=[pltpu.VMEM((width, 3 * local), F32)],
        flops=2 * tokens.shape[0] * width * 3 * local,
        nbytes=tokens.size * 2 + 8 * width * local * 3,
        prefetch=1,
    )(index, tokens, qkv_weight, gains, *flat)


def token_grad_kernel(parts, pairs, idx_ref, x_ref, gr_ref, w_ref, gain_ref, *refs):
    act_refs = refs[: parts * pairs]
    out_ref = refs[-1]
    width = x_ref.shape[1]
    local = 128 * pairs
    grad = jnp.zeros(x_ref.shape, F32)
    for d in range(parts):
        for c in range(3):
            act = jnp.concatenate([act_refs[j * parts + d][c] for j in range(pairs)], axis=1)
            grad = grad + dot(act, w_ref[:, d, c].reshape(width, local), NT)
    x = x_ref[...].astype(F32)
    factor = rms(x)
    out_ref[...] = gr_ref[...] + norm_back(grad, gain_ref[0:1, :], x * factor, factor)


def token_grad(index, tokens, grad_resid, qkv_full, gains, acts, block=256):
    share, width = grad_resid.shape
    pairs, parts = len(acts), len(acts[0])
    flat = [a for group in acts for a in group]
    steps = share // block
    return call(
        functools.partial(token_grad_kernel, parts, pairs),
        (steps,),
        [
            pl.BlockSpec((block, width), lambda i, idx: (idx[0] * steps + i, 0)),
            pl.BlockSpec((block, width), lambda i, idx: (i, 0)),
            whole(qkv_full.shape),
            whole(gains.shape),
        ]
        + [pl.BlockSpec((3, block, 128), lambda i, idx: (0, i, 0))] * len(flat),
        pl.BlockSpec((block, width), lambda i, idx: (i, 0)),
        sds((share, width), F32),
        flops=2 * share * width * width * 3,
        nbytes=share * width * 10 + 6 * width * width,
        prefetch=1,
    )(index, tokens, grad_resid, qkv_full, gains, *flat)


def after(value, *others):
    return lax.optimization_barrier((value, *others))[0]


def body(
    tokens, qkv_weight, out_weight, gate_up_weight, down_weight, norm_gains,
    species_weight, species_ids, lengths, cotangent,
):
    rows, width = tokens.shape
    local = out_weight.shape[0]
    hidden = down_weight.shape[0]
    parts = lax.axis_size("tensor")
    members = parts // 2
    shares = lax.axis_size("dp")
    part = width // shares
    me = lax.axis_index("tensor")
    dp = lax.axis_index("dp")
    index = jnp.stack([me, me // members, me % members, dp]).astype(jnp.int32)
    cosine, sine = (jnp.asarray(t) for t in rotary_tables())
    pairs = local // 128
    valid = lengths[0] >= 0

    def region(f):
        shapes = jax.eval_shape(f)
        zeros = lambda: jax.tree.map(lambda a: jnp.zeros(a.shape, a.dtype), shapes)
        return lax.optimization_barrier(lax.cond(valid, f, zeros))

    def swap(a, d, name="tensor"):
        return lax.ppermute(a, name, [(i, i ^ d) for i in range(lax.axis_size(name))])

    def cut(a, start, size, axis=0):
        return lax.dynamic_slice_in_dim(a, start, size, axis)

    def exchange(pieces):
        return [swap(pieces[d], d) for d in range(1, parts)]

    def add(a, b):
        return (a.astype(F32) + b.astype(F32)).astype(BF16)

    bits = shares.bit_length() - 1

    def lanes_of(total):
        half = total.shape[1] // 2
        lead = list(range(bits - 1, 0, -1))
        shape = (2,) * (bits - 1) + (half, total.shape[2])
        return [
            (total[:, h * half : (h + 1) * half].reshape(shape), lead, order)
            for h, order in enumerate((lead, lead[::-1]))
        ]

    def halve(lanes, step):
        out = []
        for a, lead, order in lanes:
            bit = order[step]
            at = lead.index(bit)
            mine = (dp >> bit) & 1
            pick = lambda b: lax.dynamic_index_in_dim(a, b, at, keepdims=False)
            out.append((pick(mine), pick(1 - mine), [b for b in lead if b != bit], order, bit))
        return out

    def send(halves):
        return [swap(away, 1 << bit, "dp") for _, away, _, _, bit in halves]

    def merge(halves, got):
        return [(add(keep, g), lead, order) for (keep, _, lead, order, _), g in zip(halves, got)]

    def joined(lanes):
        return jnp.concatenate([a for a, _, _ in lanes], axis=0)

    matches = species_ids[:, None] == jnp.arange(species_weight.shape[0])[None, :]
    picked = jnp.sum(jnp.where(matches, species_weight[None, :], F32(0.0)), axis=1)

    chunks = cut_weights(index[3:], gate_up_weight, down_weight, shares)
    ow_cut = cut(out_weight, dp * (local // shares), local // shares)
    qkv_cut = cut(qkv_weight, dp * part, part, 1)

    def fan_out(a):
        return [swap(a, x, "dp") for x in range(2, shares, 2)]

    def cores(pieces):
        return [swap(a, 1, "dp") for a in pieces]

    def first():
        projected = project(lengths, tokens, qkv_weight, norm_gains, cosine, sine)
        ow = exchange([after(ow_cut, projected[0])] * parts)
        return jnp.stack([ow_cut] + ow), swap(chunks[0], members), projected

    ow, chunk_0, (q, k, v) = region(first)
    out_full = lax.all_gather(ow, "dp", axis=0)

    def second():
        return fan_out(chunk_0), swap(chunks[1], members), attend(index, q, k, v, parts)

    fan_0, chunk_1, (*att, att_nat, q_back) = region(second)
    slots = list(range(members - 1, -1, -1))
    rows_for = lambda e: exchange([att[d ^ e] for d in range(parts)])

    def third():
        fan_1 = fan_out(chunk_1)
        rows = rows_for(slots[0])
        return fan_1, cores([chunk_0] + fan_0), cores([chunk_1] + fan_1), rows

    fan_1, cores_0, cores_1, rows_now = region(third)
    even = [chunk_0, *fan_0, chunk_1, *fan_1]
    partner = [p for pair in zip(even, cores_0 + cores_1) for p in pair]

    lefts, acts, gn2s, terms, gn2_got = {}, {}, {}, {}, {}
    tied = tokens
    for e in slots:

        def feed():
            later = rows_for(e - 1) if e else []
            got = swap(gn2s[e + 1], e + 1) if e + 1 in gn2s else None
            qkv_all = exchange([qkv_cut] * parts) if e == 0 else None
            return later, got, qkv_all, feed_forward(
                e, index, lengths, picked, [att[e]] + rows_now, tied, cotangent, out_full,
                gate_up_weight, down_weight, partner, norm_gains
            )

        later, got, qkv_all, outs = region(feed)
        if got is not None:
            gn2_got[e + 1] = got
        if e:
            rows_now = later
        lefts[e], acts[e], gn2s[e], terms[e] = outs[:4]
        tied = after(tokens, gn2s[e])
    resid = outs[4]
    qkv_full = lax.all_gather(jnp.stack([qkv_cut] + qkv_all), "dp", axis=0)
    gn2_all = [gn2s[0]] + [gn2_got[e] for e in range(1, members)]
    grad_resid, grad_low, att_own, gain_two, *grads = resid_back(
        index, lengths, picked, cotangent, resid, gn2_all, out_full, norm_gains, [att[0]] + rows_now
    )
    lefts, acts = [lefts[e] for e in slots], [acts[e] for e in slots]

    def grads_partner():
        near = [swap(grads[d], d) for d in range(1, parts - 1)]
        return near, ffn_grads(index, lefts, acts, 1, shares, True)

    near, (away_b, keep_b) = region(grads_partner)

    def grads_own():
        far = swap(grads[parts - 1], parts - 1)
        got_b = swap(away_b, 1, "dp")
        (wg_a,) = ffn_grads(index, lefts, acts, 0, shares, False, grad_low, att_own)
        return far, got_b, wg_a

    far, got_b, wg_a = region(grads_own)
    sum_a = lax.psum_scatter(after(wg_a, qkv_full), "dp", scatter_dimension=0, tiled=True)[0]
    grads_all = [grads[0], *near, far]
    halves = halve(lanes_of(add(keep_b, got_b)), 0)

    def back(j):
        return attend_back(index, grads_all, q_back, k, v, att_nat, cosine, sine, j)

    def back_first():
        others = [swap(terms[e], e) for e in range(1, members)]
        return others, send(halves), back(0)

    others, got, group = region(back_first)
    out = resid + terms[0].astype(F32)
    for term in others:
        out = out + term.astype(F32)
    lanes = merge(halves, got)
    step = 1
    qkv_acts, acts_got = [group], []
    for j in range(1, pairs):
        halves = halve(lanes, step)

        def back_next():
            return exchange(group), send(halves), back(j)

        group_got, got, group = region(back_next)
        acts_got.append([qkv_acts[-1][0]] + group_got)
        qkv_acts.append(group)
        lanes = merge(halves, got)
        step += 1

    b_lanes = lanes
    for s in range(step, bits - 1):
        h = halve(b_lanes, s)
        b_lanes = merge(h, send(h))
    sum_b = joined(b_lanes)

    def finish():
        last = exchange(group)
        got_b = swap(sum_b, members)

        def inner():
            away_q, keep_q, gain_one = project_grads(index, tokens, qkv_acts, qkv_weight, norm_gains, shares)
            qkv_lanes = lanes_of(add(keep_q, swap(away_q, 1, "dp")))
            for s in range(bits - 1):
                h = halve(qkv_lanes, s)
                qkv_lanes = merge(h, send(h))
            gains_grad = jnp.stack([gain_one[:, 0] / norm_gains[0], jnp.sum(gain_two, axis=0)])
            for name, size in (("dp", shares), ("tensor", parts)):
                d = 1
                while d < size:
                    gains_grad = gains_grad + swap(gains_grad, d, name)
                    d *= 2
            return joined(qkv_lanes), gains_grad

        return last, got_b, region(inner)

    last, got_b, (qkv_sum, gains_grad) = region(finish)
    acts_got.append([group[0]] + last)
    op_sum = jnp.concatenate(
        [sum_a[(3 + c) * part : (4 + c) * part] for c in range(parts * local // hidden)], axis=1
    )

    def end():
        op_got = exchange([op_sum[:, d * local : (d + 1) * local] for d in range(parts)])
        return op_got, token_grad(index, tokens, grad_resid, qkv_full, norm_gains, acts_got)

    op_got, grad_tok = region(end)
    ffn_sum = sum_a[: 3 * part].astype(F32) + got_b.astype(F32)
    grad_op = op_sum[:, :local].astype(F32)
    for piece in op_got:
        grad_op = grad_op + piece.astype(F32)
    grad_gu = ffn_sum[: 2 * part].reshape(2, part, hidden)
    grad_down = ffn_sum[2 * part :].T
    qkv_sum = qkv_sum.astype(F32)
    grad_qkv = jnp.stack([qkv_sum[:, c * local : (c + 1) * local] for c in range(3)])
    return (out, grad_tok, grad_qkv, grad_op.T, grad_gu, grad_down, gains_grad)


def solution(mesh):
    in_specs = (
        P("dp", None),
        P(None, None, "tensor"),
        P("tensor", None),
        P(None, None, "tensor"),
        P("tensor", None),
        P(),
        P(),
        P("dp"),
        P("dp"),
        P("dp", None),
    )
    out_specs = (
        P(("dp", "tensor"), None),
        P(("dp", "tensor"), None),
        P(None, "dp", "tensor"),
        P("tensor", "dp"),
        P(None, "dp", "tensor"),
        P("tensor", "dp"),
        P(),
    )
    return jax.shard_map(body, mesh=mesh, in_specs=in_specs, out_specs=out_specs, check_vma=False)
```

```python
import functools
import math

import jax
import jax.numpy as jnp
import numpy as np
from jax import lax
from jax.experimental import pallas as pl
from jax.experimental.pallas import tpu as pltpu
from jax.sharding import PartitionSpec as P

HD = 64
WIN = 2048
EPSILON = 1e-05
NEG_FILL = -1e30
LOG2E = math.log2(math.e)
LN2 = math.log(2.0)
FACTOR = HD ** (-0.5)
VMEM = 60 * 2**20
F32 = jnp.float32
BF16 = jnp.bfloat16

NN = (((1,), (0,)), ((), ()))
NT = (((1,), (1,)), ((), ()))
TN = (((0,), (0,)), ((), ()))


def dot(a, b, dims=NN):
    return lax.dot_general(a, b, dims, preferred_element_type=F32)


def call(kernel, grid, in_specs, out_specs, out_shape, scratch=(), flops=0, nbytes=0, trans=0, prefetch=0):
    return pl.pallas_call(
        kernel,
        grid_spec=pltpu.PrefetchScalarGridSpec(
            num_scalar_prefetch=prefetch,
            grid=grid,
            in_specs=in_specs,
            out_specs=out_specs,
            scratch_shapes=list(scratch),
        ),
        out_shape=out_shape,
        compiler_params=pltpu.CompilerParams(vmem_limit_bytes=VMEM),
        cost_estimate=pl.CostEstimate(flops=flops, bytes_accessed=nbytes, transcendentals=trans),
    )


def whole(shape):
    return pl.BlockSpec(shape, lambda *_: (0,) * len(shape), pipeline_mode=pl.Buffered(1))


def smem():
    return pl.BlockSpec(memory_space=pltpu.SMEM)


def sds(shape, dtype):
    return jax.ShapeDtypeStruct(shape, dtype)


def rotary_tables():
    position = np.arange(WIN, dtype=np.float64)
    frequency = 10000.0 ** (-2.0 * np.arange(HD // 2, dtype=np.float64) / HD)
    angles = position[:, None] * frequency[None, :]
    cosine = np.cos(angles)
    sine = np.sin(angles)
    cos_full = np.tile(np.concatenate([cosine, cosine], axis=1), (1, 2))
    sin_full = np.tile(np.concatenate([-sine, sine], axis=1), (1, 2))
    return cos_full.astype(np.float32), sin_full.astype(np.float32)


def swap_halves(v):
    lane = lax.broadcasted_iota(jnp.int32, v.shape, 1)
    return jnp.where(lane % HD < HD // 2, pltpu.roll(v, 96, 1), pltpu.roll(v, 32, 1))


def rms(x):
    return lax.rsqrt(jnp.mean(x * x, axis=-1, keepdims=True) + EPSILON)


def split3(v):
    hi = v.astype(BF16)
    rest = v - hi.astype(F32)
    mid = rest.astype(BF16)
    low = (rest - mid.astype(F32)).astype(BF16)
    return hi, mid, low


def norm_back(grad_normed, gain, unit, factor):
    scaled = grad_normed * gain
    return factor * (scaled - unit * jnp.mean(scaled * unit, axis=-1, keepdims=True))


def qkv_kernel(len_ref, x_ref, w_ref, gain_ref, cos_ref, sin_ref, q_ref, k_ref, v_ref):
    rows = x_ref.shape[0]
    x = x_ref[...].astype(F32)
    normed = (x * rms(x) * gain_ref[0:1, :]).astype(BF16)
    cosine = cos_ref[...]
    sine = sin_ref[...]
    lane = lax.broadcasted_iota(jnp.int32, (rows, 128), 1)
    slot = lax.broadcasted_iota(jnp.int32, (rows, 128), 0) + pl.program_id(0) * rows
    masked = jnp.where(slot < len_ref[0], 0.0, NEG_FILL).astype(BF16)
    one = jnp.ones((rows, 128), BF16)
    zero = jnp.zeros((rows, 128), BF16)
    pairs = w_ref.shape[2] // 128
    for c in range(3):
        y = dot(normed, w_ref[c])
        for j in range(pairs):
            v = y[:, 128 * j : 128 * (j + 1)]
            if c < 2:
                v = v * cosine + swap_halves(v) * sine
            if c == 0:
                v = v * (FACTOR * LOG2E)
            v = v.astype(BF16)
            for s in range(2):
                first = HD * (1 - s)
                own = (lane >= HD * s) & (lane < HD * (s + 1))
                if c == 0:
                    q_ref[2 * j + s] = jnp.where(own, v, jnp.where(lane == first, one, zero))
                elif c == 1:
                    tail = jnp.where(
                        lane == first, masked, jnp.where(lane < first + 4, one, zero)
                    )
                    tail = jnp.where(lane < first, zero, tail)
                    k_ref[2 * j + s] = jnp.where(own, v, tail)
                else:
                    v_ref[2 * j + s] = jnp.where(own, v, one)


def project(lengths, tokens, qkv_weight, gains, cosine, sine, block=512):
    rows, width = tokens.shape
    local = qkv_weight.shape[2]
    heads = local // HD
    spec = pl.BlockSpec((heads, block, 128), lambda i: (0, i, 0))
    return call(
        qkv_kernel,
        (rows // block,),
        [
            smem(),
            pl.BlockSpec((block, width), lambda i: (i, 0)),
            whole(qkv_weight.shape),
            whole(gains.shape),
            pl.BlockSpec((block, 128), lambda i: (i, 0)),
            pl.BlockSpec((block, 128), lambda i: (i, 0)),
        ],
        [spec] * 3,
        [sds((heads, rows, 128), BF16)] * 3,
    )(lengths, tokens, qkv_weight, gains, cosine, sine)


def attend_kernel(sub, parts, done, idx_ref, q_ref, k_ref, v_ref, *refs):
    prev_refs = refs[:parts] if done else ()
    o_refs = refs[len(prev_refs) : len(prev_refs) + parts]
    nat_ref, qb_ref = refs[len(prev_refs) + parts :]
    rows = q_ref.shape[1]
    lane = lax.broadcasted_iota(jnp.int32, (sub, 128), 1)
    for r in range(rows // sub):
        part = slice(r * sub, (r + 1) * sub)
        outs = []
        for s in range(2):
            q = q_ref[s, part, :]
            scores = dot(q, k_ref[s], NT)
            peak = jnp.max(scores, axis=1, keepdims=True)
            expo = jnp.exp2(scores - peak).astype(BF16)
            acc = dot(expo, v_ref[s])
            outs.append(acc / pltpu.roll(acc, HD, 1))
            first = HD * (1 - s)
            total = jnp.where((lane >= first) & (lane < first + HD), acc, 1.0)
            hi, mid, low = split3(-(peak + jnp.log2(total)))
            tail = jnp.where(lane == first + 3, low, q)
            tail = jnp.where(lane == first + 2, mid, tail)
            qb_ref[s, part, :] = jnp.where(lane == first + 1, hi, tail)
        nat_ref[part, :] = jnp.where(lane < HD, outs[0], outs[1]).astype(BF16)
    for d in range(parts):

        @pl.when(pl.program_id(0) == d)
        def _():
            if done:
                o_refs[d][:, :done] = prev_refs[d][...]
            o_refs[d][:, done:] = nat_ref[...]


def attend(index, q, k, v, parts, pair, prev=(), sub=256):
    _, rows, _ = q.shape
    keys = k.shape[1]
    share = rows // parts
    cols = 128 * (pair + 1)
    return call(
        functools.partial(attend_kernel, min(sub, share), parts, 128 * pair),
        (parts,),
        [
            pl.BlockSpec((2, share, 128), lambda i, idx: (pair, idx[0] ^ i, 0)),
            pl.BlockSpec((2, keys, 128), lambda i, idx: (pair, 0, 0), pipeline_mode=pl.Buffered(1)),
            pl.BlockSpec((2, keys, 128), lambda i, idx: (pair, 0, 0), pipeline_mode=pl.Buffered(1)),
        ]
        + [whole(p.shape) for p in prev],
        [whole((share, cols))] * parts
        + [
            pl.BlockSpec((share, 128), lambda i, idx: (idx[0] ^ i, 0)),
            pl.BlockSpec((2, share, 128), lambda i, idx: (0, idx[0] ^ i, 0)),
        ],
        [sds((share, cols), BF16)] * parts + [sds((rows, 128), BF16), sds((2, rows, 128), BF16)],
        prefetch=1,
    )(index, q, k, v, *prev)


def cut_kernel(idx_ref, gu_ref, dw_ref, out_ref):
    part = gu_ref.shape[1]
    out_ref[:part, :] = gu_ref[0]
    out_ref[part : 2 * part, :] = gu_ref[1]
    out_ref[2 * part :, :] = dw_ref[...].T


def cut_weights(dp, gate_up, down, shares):
    _, width, hidden = gate_up.shape
    part = width // shares
    if part % 128:
        down = lax.dynamic_slice_in_dim(down, dp[0] * part, part, 1)
        spec = whole(down.shape)
    else:
        spec = pl.BlockSpec((hidden, part), lambda i, idx: (0, idx[0]))
    return call(
        cut_kernel,
        (1,),
        [pl.BlockSpec((2, part, hidden), lambda i, idx: (0, idx[0], 0)), spec],
        whole((3 * part, hidden)),
        sds((3 * part, hidden), BF16),
        nbytes=12 * part * hidden,
        prefetch=1,
    )(dp, gate_up, down)


def ffn_kernel(parts, shares, slot, idx_ref, len_ref, weight_ref, gain_ref, x_h, cot_h, gu_h, dw_h, pb_h, *refs):
    own = slot == 0
    att_h = refs[:parts]
    pieces_h = refs[parts : parts + shares]
    refs = refs[parts + shares :]
    count = 5 if own else 4
    outs, scratch = refs[:count], refs[count:]
    x_v, cot_v, att_v, ow_v, gu_v, dw_v, pb_v, left_v, act_v, ffn_v, gn2_v, low_v, sem_in, sem_out = scratch
    rows, width = x_v.shape
    local = att_v.shape[2]
    hidden_units = gu_v.shape[2]
    part = pb_v.shape[1] // 3
    row0 = pl.multiple_of((idx_ref[0] ^ slot) * rows, rows)
    mine = pl.ds(row0, rows)

    def fetch(src, dst, i):
        copy = pltpu.make_async_copy(src, dst, sem_in.at[i])
        copy.start()
        return copy

    pending = []

    def store(src, dst, i):
        copy = pltpu.make_async_copy(src, dst, sem_out.at[i])
        copy.start()
        pending.append(copy)

    get_x = fetch(x_h.at[mine], x_v, 0)
    get_ow = [fetch(pieces_h[x], ow_v.at[idx_ref[1] ^ x], 6 + parts + x) for x in range(shares)]
    get_att = [fetch(att_h[d], att_v.at[d], 2 + d) for d in range(parts)]
    get_cot = fetch(cot_h.at[mine], cot_v, 2 + parts)
    get_gu = fetch(gu_h, gu_v, 3 + parts)
    get_dw = fetch(dw_h, dw_v, 4 + parts)
    get_pb = fetch(pb_h, pb_v, 1)

    get_x.wait()
    for copy in get_ow:
        copy.wait()
    resid = x_v[...].astype(F32)
    for d in range(parts):
        get_att[d].wait()
        resid = resid + dot(att_v[d], ow_v[:, d].reshape(local, width))
    if own:
        ffn_v[...] = resid
        store(ffn_v, outs[4], 4)
    normed = (resid * rms(resid) * gain_ref[1:2, :]).astype(BF16)
    left_v[0] = normed
    position = lax.broadcasted_iota(jnp.int32, (rows, 1), 0) + row0
    row_weight = jnp.where(position < len_ref[0], weight_ref[0], 0.0)
    get_cot.wait()
    left_v[1] = (cot_v[...].astype(F32) * row_weight).astype(BF16)
    store(left_v, outs[0], 0)
    for shard in range(2):
        cols = slice(shard * hidden_units, (shard + 1) * hidden_units)
        if shard == 0:
            get_gu.wait()
            get_dw.wait()
            gate_w, up_w, down_w = gu_v[0], gu_v[1], dw_v[...]
        else:
            get_pb.wait()
            gate_w, up_w, down_w = (
                pb_v[:, c * part : (c + 1) * part, :].reshape(width, hidden_units) for c in range(3)
            )
        gate = dot(left_v[0], gate_w)
        upper = dot(left_v[0], up_w)
        grad_hidden = dot(left_v[1], down_w, NT if shard == 0 else NN)
        sigma = jax.nn.sigmoid(gate)
        act = gate * sigma
        hidden = (act * upper).astype(BF16)
        grad_up = (grad_hidden * act).astype(BF16)
        grad_gate = (grad_hidden * upper * (sigma + act * (1.0 - sigma))).astype(BF16)
        act_v[0, :, cols] = grad_gate
        act_v[1, :, cols] = grad_up
        act_v[2, :, cols] = hidden
        grad = dot(grad_gate, gate_w, NT) + dot(grad_up, up_w, NT)
        term = dot(hidden, down_w, NN if shard == 0 else NT)
        if shard == 0:
            gn2_v[...] = grad
            if own:
                pending.pop(0).wait()
            ffn_v[...] = term
        else:
            low_v[0] = (gn2_v[...] + grad).astype(BF16)
            store(low_v.at[0], outs[2], 2)
            low_v[1] = (ffn_v[...] + term).astype(BF16)
            store(low_v.at[1], outs[3], 3)
    store(act_v, outs[1], 1)
    for copy in pending:
        copy.wait()


def feed_forward(slot, index, lengths, picked, atts, tokens, cotangent, out_full, gate_up, down, partner, gains):
    parts = len(atts)
    shares = len(out_full)
    rows, local = atts[0].shape
    width = tokens.shape[1]
    hidden = gate_up.shape[2]
    anywhere = pl.BlockSpec(memory_space=pl.ANY)
    out_shape = [
        sds((2, rows, width), BF16), sds((3, rows, 2 * hidden), BF16),
        sds((rows, width), BF16), sds((rows, width), BF16),
    ]
    if slot == 0:
        out_shape.append(sds((rows, width), F32))
    return call(
        functools.partial(ffn_kernel, parts, shares, slot),
        (1,),
        [smem(), smem(), whole(gains.shape)] + [anywhere] * (5 + parts + shares),
        [anywhere] * len(out_shape),
        out_shape,
        scratch=[
            pltpu.VMEM((rows, width), BF16),
            pltpu.VMEM((rows, width), BF16),
            pltpu.VMEM((parts, rows, local), BF16),
            pltpu.VMEM((shares,) + out_full[0].shape, BF16),
            pltpu.VMEM(gate_up.shape, BF16),
            pltpu.VMEM(down.shape, BF16),
            pltpu.VMEM(partner.shape, BF16),
            pltpu.VMEM((2, rows, width), BF16),
            pltpu.VMEM((3, rows, 2 * hidden), BF16),
            pltpu.VMEM((rows, width), F32),
            pltpu.VMEM((rows, width), F32),
            pltpu.VMEM((2, rows, width), BF16),
            pltpu.SemaphoreType.DMA((6 + parts + shares,)),
            pltpu.SemaphoreType.DMA((5,)),
        ],
        flops=2 * rows * width * (width + 12 * hidden),
        nbytes=rows * width * 30 + 12 * width * hidden,
        trans=rows * hidden * 2,
        prefetch=1,
    )(index, lengths, picked, gains, tokens, cotangent, gate_up, down, partner, *atts, *out_full)


def ffn_grad_kernel(sets, split, extra, idx_ref, *refs):
    left = refs[:sets]
    act = refs[sets : 2 * sets]
    refs = refs[2 * sets :]
    step = pl.program_id(0)

    def write(total, outs):
        part = outs[0].shape[-2]
        for out in outs:
            count = out.shape[0]
            for j in range(count):
                if len(outs) == 1:
                    out[j] = total[j * part : (j + 1) * part, :].astype(BF16)
        if len(outs) == 2:
            for keep in range(2):
                for bit in range(2):

                    @pl.when((idx_ref[1] & 1) == bit)
                    def _():
                        for j in range(outs[0].shape[0]):
                            d = 2 * j + (bit if keep else 1 - bit)
                            outs[keep][j] = total[d * part : (d + 1) * part, :].astype(BF16)

    outs = refs[2:] if extra else refs

    @pl.when(step < 3)
    def _():
        total = dot(left[0][0], act[0][0], TN)
        for e in range(1, sets):
            total = total + dot(left[e][0], act[e][0], TN)
        write(total, outs)

    if extra:

        @pl.when(step >= 3)
        def _():
            write(dot(refs[0][...], refs[1][...], TN), outs)


def ffn_grads(index, lefts, acts, shard, shares, split, grad_low=None, att_own=None):
    sets = len(lefts)
    _, rows, width = lefts[0].shape
    hidden = acts[0].shape[2] // 2
    part = width // shares
    extra = 0 if grad_low is None else att_own.shape[1] // hidden
    steps = 3 + extra
    specs = [pl.BlockSpec((1, rows, width), lambda c, idx: (jnp.minimum(c // 2, 1), 0, 0))] * sets
    specs += [pl.BlockSpec((1, rows, hidden), lambda c, idx: (jnp.minimum(c, 2), 0, shard))] * sets
    args = list(lefts) + list(acts)
    if extra:
        specs += [
            pl.BlockSpec(grad_low.shape, lambda c, idx: (0, 0)),
            pl.BlockSpec((att_own.shape[0], hidden), lambda c, idx: (0, jnp.maximum(c - 3, 0))),
        ]
        args += [grad_low, att_own]
    count = shares // 2 if split else shares
    out_spec = pl.BlockSpec((count, part, hidden), lambda c, idx: (0, c, 0))
    out_shape = sds((count, steps * part, hidden), BF16)
    outs = 2 if split else 1
    return call(
        functools.partial(ffn_grad_kernel, sets, split, extra),
        (steps,),
        specs,
        [out_spec] * outs,
        [out_shape] * outs,
        flops=2 * sets * rows * width * hidden * steps,
        nbytes=sets * rows * (2 * width + 3 * hidden) * 2 + steps * width * hidden * 2,
        prefetch=1,
    )(index, *args)


def resid_kernel(parts, members, shares, idx_ref, len_ref, weight_ref, cot_ref, resid_ref, gain_ref, *refs):
    pieces, refs, ow_ref = refs[:shares], refs[shares:-1], refs[-1]
    gn2_refs = refs[:members]
    att_refs = refs[members : members + parts]
    gr_ref, low_ref, cat_ref, sum_ref = refs[members + parts : members + parts + 4]
    g_refs = refs[members + parts + 4 :]
    rows, width = cot_ref.shape
    local = att_refs[0].shape[1]
    step = pl.program_id(0)
    first = (idx_ref[0] * pl.num_programs(0) + step) * rows
    slot = lax.broadcasted_iota(jnp.int32, (rows, 1), 0) + first
    row_weight = jnp.where(slot < len_ref[0], weight_ref[0], 0.0)
    gn2 = gn2_refs[0][...].astype(F32)
    for ref in gn2_refs[1:]:
        gn2 = gn2 + ref[...].astype(F32)
    resid = resid_ref[...]
    factor = rms(resid)
    unit = resid * factor
    grad = cot_ref[...].astype(F32) * row_weight + norm_back(gn2, gain_ref[1:2, :], unit, factor)
    gr_ref[...] = grad
    low = grad.astype(BF16)
    low_ref[...] = low

    @pl.when(step == 0)
    def _():
        sum_ref[...] = jnp.zeros_like(sum_ref)
        for x in range(shares):
            ow_ref[idx_ref[1] ^ x] = pieces[x][...]

    sum_ref[...] += jnp.sum((gn2 * unit).reshape(rows // 8, 8, width), axis=0)
    for d in range(parts):
        g_refs[d][...] = dot(low, ow_ref[:, d].reshape(local, width), NT).astype(BF16)
        cat_ref[:, d * local : (d + 1) * local] = att_refs[d][...]


def resid_back(index, lengths, picked, cotangent, resid, gn2s, out_full, gains, atts, block=256):
    share, width = resid.shape
    parts, members = len(atts), len(gn2s)
    local = atts[0].shape[1]
    steps = share // block
    row = lambda n: pl.BlockSpec((block, n), lambda i, idx: (i, 0))
    return call(
        functools.partial(resid_kernel, parts, members, len(out_full)),
        (steps,),
        [
            smem(), smem(),
            pl.BlockSpec((block, width), lambda i, idx: (idx[0] * steps + i, 0)),
            row(width), whole(gains.shape),
        ]
        + [whole(p.shape) for p in out_full]
        + [row(width)] * members
        + [row(local)] * parts,
        [row(width), row(width), row(parts * local), whole((8, width))] + [row(local)] * parts,
        [sds((share, width), F32), sds((share, width), BF16), sds((share, parts * local), BF16), sds((8, width), F32)]
        + [sds((share, local), BF16)] * parts,
        scratch=[pltpu.VMEM((len(out_full),) + out_full[0].shape, BF16)],
        flops=2 * share * width * width,
        nbytes=share * width * 20,
        prefetch=1,
    )(index, lengths, picked, cotangent, resid, gains, *out_full, *gn2s, *atts)


def attend_back_kernel(parts, idx_ref, q_ref, k_ref, v_ref, att_ref, cos_ref, sin_ref, *refs):
    grad_refs = refs[:parts]
    outs = refs[parts : 2 * parts]
    dk_acc, dv_acc = refs[2 * parts :]
    rows = q_ref.shape[1]
    step = pl.program_id(0)
    me = idx_ref[0]
    lane = lax.broadcasted_iota(jnp.int32, (rows, 128), 1)

    def table(ref, d):
        return ref[pl.ds(pl.multiple_of((me ^ d) * rows, rows), rows), :]

    def back(v, d, scale):
        return ((v * table(cos_ref, d) - swap_halves(v) * table(sin_ref, d)) * scale).astype(BF16)

    @pl.when(step == 0)
    def _():
        dk_acc[...] = jnp.zeros_like(dk_acc)
        dv_acc[...] = jnp.zeros_like(dv_acc)

    grad = grad_refs[0][...]
    for d in range(1, parts):
        grad = jnp.where(step == d, grad_refs[d][...], grad)
    prod = grad.astype(F32) * att_ref[...].astype(F32)
    zero = jnp.zeros((rows, 128), BF16)
    dqs = []
    for s in range(2):
        first = HD * (1 - s)
        own = (lane >= HD * s) & (lane < HD * (s + 1))
        delta = jnp.sum(jnp.where(own, prod, 0.0), axis=1, keepdims=True)
        hi, mid, low = split3(-delta)
        grad_own = jnp.where(own, grad, zero)
        grad_aug = jnp.where(lane == first + 2, low, grad_own)
        grad_aug = jnp.where(lane == first + 1, mid, grad_aug)
        grad_aug = jnp.where(lane == first, hi, grad_aug)
        q = q_ref[s]
        probs = jnp.exp2(dot(k_ref[s], q, NT))
        scores_grad = (probs * dot(v_ref[s], grad_aug, NT)).astype(BF16)
        dv_acc[...] += dot(probs.astype(BF16), grad_own)
        dk_acc[...] += dot(scores_grad, jnp.where(own, q, zero))
        dqs.append(dot(k_ref[s], scores_grad, TN).T)
    dq = jnp.where(lane < HD, dqs[0], dqs[1])
    for d in range(parts):

        @pl.when(step == d)
        def _():
            outs[d][0] = back(dq, d, FACTOR)

    @pl.when(step == parts - 1)
    def _():
        for d in range(parts):
            outs[d][1] = back(table(dk_acc, d), d, LN2)
            outs[d][2] = table(dv_acc, d).astype(BF16)


def attend_back(index, grads, q, k, v, att, cosine, sine, pair):
    parts = len(grads)
    share = grads[0].shape[0]
    rows = q.shape[1]
    keys = pl.BlockSpec((2, rows, 128), lambda i, idx: (pair, 0, 0), pipeline_mode=pl.Buffered(1))
    return call(
        functools.partial(attend_back_kernel, parts),
        (parts,),
        [
            pl.BlockSpec((2, share, 128), lambda i, idx: (0, idx[0] ^ i, 0)),
            keys,
            keys,
            pl.BlockSpec((share, 128), lambda i, idx: (idx[0] ^ i, 0)),
            whole(cosine.shape),
            whole(sine.shape),
        ]
        + [pl.BlockSpec((share, 128), lambda i, idx: (0, pair))] * parts,
        [whole((3, share, 128))] * parts,
        [sds((3, share, 128), BF16)] * parts,
        scratch=[pltpu.VMEM((rows, 128), F32)] * 2,
        flops=2 * rows * rows * 128 * 10,
        nbytes=rows * 256 * 16,
        trans=2 * rows * rows,
        prefetch=1,
    )(index, q, k, v, att, cosine, sine, *grads)


def project_grad_kernel(parts, pairs, idx_ref, x_ref, w_ref, gain_ref, *refs):
    act_refs = refs[: parts * pairs]
    away_ref, keep_ref, sum_ref, acc = refs[parts * pairs :]
    step = pl.program_id(0)

    @pl.when(step == 0)
    def _():
        acc[...] = jnp.zeros_like(acc)

    x = x_ref[...].astype(F32)
    normed = (x * rms(x) * gain_ref[0:1, :]).astype(BF16)
    for d in range(parts):

        @pl.when(step == d)
        def _():
            acts = [act_refs[j * parts + d][c] for c in range(3) for j in range(pairs)]
            acc[...] += dot(normed, jnp.concatenate(acts, axis=1), TN)

    @pl.when(step == pl.num_programs(0) - 1)
    def _():
        count, part, _ = keep_ref.shape
        local = w_ref.shape[2]
        core = idx_ref[1] & 1
        for j in range(count):
            keep_ref[j] = acc[pl.ds(pl.multiple_of((2 * j + core) * part, part), part), :].astype(BF16)
            away_ref[j] = acc[pl.ds(pl.multiple_of((2 * j + 1 - core) * part, part), part), :].astype(BF16)
        gain_sum = acc[:, :local] * w_ref[0].astype(F32)
        for c in (1, 2):
            gain_sum += acc[:, c * local : (c + 1) * local] * w_ref[c].astype(F32)
        sum_ref[...] = jnp.broadcast_to(jnp.sum(gain_sum, axis=1, keepdims=True), sum_ref.shape)


def project_grads(index, tokens, acts, qkv_weight, gains, shares):
    width = tokens.shape[1]
    local = qkv_weight.shape[2]
    pairs, parts = len(acts), len(acts[0])
    share = acts[0][0].shape[1]
    flat = [a for group in acts for a in group]
    half = (shares // 2, width // shares, 3 * local)
    return call(
        functools.partial(project_grad_kernel, parts, pairs),
        (parts,),
        [
            pl.BlockSpec((share, width), lambda i, idx: (idx[0] ^ i, 0)),
            whole(qkv_weight.shape),
            whole(gains.shape),
        ]
        + [whole(a.shape) for a in flat],
        [whole(half), whole(half), whole((width, 128))],
        [sds(half, BF16), sds(half, BF16), sds((width, 128), F32)],
        scratch=[pltpu.VMEM((width, 3 * local), F32)],
        flops=2 * tokens.shape[0] * width * 3 * local,
        nbytes=tokens.size * 2 + 8 * width * local * 3,
        prefetch=1,
    )(index, tokens, qkv_weight, gains, *flat)


def token_grad_kernel(parts, pairs, idx_ref, x_ref, gr_ref, w_ref, gain_ref, own_ref, got_ref, *refs):
    act_refs = refs[: parts * pairs]
    out_ref, gu_ref, down_ref = refs[parts * pairs :]
    width = x_ref.shape[1]
    local = 128 * pairs
    grad = jnp.zeros(x_ref.shape, F32)
    for d in range(parts):
        for c in range(3):
            act = jnp.concatenate([act_refs[j * parts + d][c] for j in range(pairs)], axis=1)
            grad = grad + dot(act, w_ref[:, d, c].reshape(width, local), NT)
    x = x_ref[...].astype(F32)
    factor = rms(x)
    out_ref[...] = gr_ref[...] + norm_back(grad, gain_ref[0:1, :], x * factor, factor)

    @pl.when(pl.program_id(0) == 0)
    def _():
        part = gu_ref.shape[1]
        total = own_ref[: 3 * part, :].astype(F32) + got_ref[...].astype(F32)
        gu_ref[0] = total[:part]
        gu_ref[1] = total[part : 2 * part]
        down_ref[...] = total[2 * part :].T


def token_grad(index, tokens, grad_resid, qkv_full, gains, acts, ffn_own, ffn_got, block=256):
    share, width = grad_resid.shape
    pairs, parts = len(acts), len(acts[0])
    flat = [a for group in acts for a in group]
    steps = share // block
    part, hidden = ffn_got.shape[0] // 3, ffn_got.shape[1]
    return call(
        functools.partial(token_grad_kernel, parts, pairs),
        (steps,),
        [
            pl.BlockSpec((block, width), lambda i, idx: (idx[0] * steps + i, 0)),
            pl.BlockSpec((block, width), lambda i, idx: (i, 0)),
            whole(qkv_full.shape),
            whole(gains.shape),
            whole(ffn_own.shape),
            whole(ffn_got.shape),
        ]
        + [pl.BlockSpec((3, block, 128), lambda i, idx: (0, i, 0))] * len(flat),
        [
            pl.BlockSpec((block, width), lambda i, idx: (i, 0)),
            whole((2, part, hidden)),
            whole((hidden, part)),
        ],
        [sds((share, width), F32), sds((2, part, hidden), F32), sds((hidden, part), F32)],
        flops=2 * share * width * width * 3,
        nbytes=share * width * 10 + 6 * width * width,
        prefetch=1,
    )(index, tokens, grad_resid, qkv_full, gains, ffn_own, ffn_got, *flat)


def after(value, *others):
    return lax.optimization_barrier((value, *others))[0]


def body(
    tokens, qkv_weight, out_weight, gate_up_weight, down_weight, norm_gains,
    species_weight, species_ids, lengths, cotangent,
):
    rows, width = tokens.shape
    local = out_weight.shape[0]
    hidden = down_weight.shape[0]
    parts = lax.axis_size("tensor")
    members = parts // 2
    slots = list(range(members - 1, -1, -1))
    shares = lax.axis_size("dp")
    part = width // shares
    me = lax.axis_index("tensor")
    dp = lax.axis_index("dp")
    index = jnp.stack([me, dp]).astype(jnp.int32)
    cosine, sine = (jnp.asarray(t) for t in rotary_tables())
    pairs = local // 128
    valid = lengths[0] >= 0

    def region(f):
        shapes = jax.eval_shape(f)
        zeros = lambda: jax.tree.map(lambda a: jnp.zeros(a.shape, a.dtype), shapes)
        return lax.optimization_barrier(lax.cond(valid, f, zeros))

    def beside(sends, f, apart=False):
        return region(lambda: ([swap(*x) for x in sends], region(f) if apart else f()))

    def swap(a, d, name="tensor"):
        return lax.ppermute(a, name, [(i, i ^ d) for i in range(lax.axis_size(name))])

    def cut(a, start, size, axis=0):
        return lax.dynamic_slice_in_dim(a, start, size, axis)

    def outgoing(pieces):
        return [(pieces[d], d, "tensor") for d in range(1, parts)]

    def exchange(pieces):
        return [swap(*send) for send in outgoing(pieces)]

    def add(a, b):
        return (a.astype(F32) + b.astype(F32)).astype(BF16)

    bits = shares.bit_length() - 1

    def lanes_of(total):
        half = total.shape[1] // 2
        lead = list(range(bits - 1, 0, -1))
        shape = (2,) * (bits - 1) + (half, total.shape[2])
        return [
            (total[:, h * half : (h + 1) * half].reshape(shape), lead, order)
            for h, order in enumerate((lead, lead[::-1]))
        ]

    def halve(lanes, step):
        out = []
        for a, lead, order in lanes:
            bit = order[step]
            at = lead.index(bit)
            mine = (dp >> bit) & 1
            pick = lambda b: lax.dynamic_index_in_dim(a, b, at, keepdims=False)
            out.append((pick(mine), pick(1 - mine), [b for b in lead if b != bit], order, bit))
        return out

    def leaving(halves):
        return [(away, 1 << bit, "dp") for _, away, _, _, bit in halves]

    def merge(halves, got):
        return [(add(keep, g), lead, order) for (keep, _, lead, order, _), g in zip(halves, got)]

    def joined(lanes):
        return jnp.concatenate([a for a, _, _ in lanes], axis=0)

    matches = species_ids[:, None] == jnp.arange(species_weight.shape[0])[None, :]
    picked = jnp.sum(jnp.where(matches, species_weight[None, :], F32(0.0)), axis=1)

    mine = cut_weights(index[1:], gate_up_weight, down_weight, shares)
    ow_cut = cut(out_weight, dp * (local // shares), local // shares)
    qkv_cut = cut(qkv_weight, dp * part, part, 1)

    def first():
        projected = project(lengths, tokens, qkv_weight, norm_gains, cosine, sine)
        return projected, attend(index, *projected, parts, 0)

    (partner_cut,), ((q, k, v), heads) = beside([(mine, members, "tensor")], first)
    partner = lax.all_gather(partner_cut, "dp", axis=0)
    heads = [heads]

    def second():
        more = heads[:]
        for j in range(1, pairs):
            more.append(attend(index, q, k, v, parts, j, more[-1][:parts]))
        return more[1:]

    ow, more = beside(outgoing([after(ow_cut, partner_cut)] * parts), second)
    heads += more
    att = heads[-1][:parts]
    att_nat = [h[parts] for h in heads]
    q_back = [h[parts + 1] for h in heads]
    rows_for = lambda e: outgoing([att[d ^ e] for d in range(parts)])
    ow = jnp.stack([ow_cut] + ow)

    def third():
        even = [ow] + [swap(ow, x, "dp") for x in range(2, shares, 2)]
        return [p for a in even for p in (a, swap(a, 1, "dp"))][1:]

    def third_all():
        rows = [swap(*x) for x in rows_for(slots[0])]
        return rows, third()

    rows_now, ow_got = region(third_all)
    out_full = [ow] + ow_got

    lefts, acts, gn2s, terms, gn2_got, qkv_all = {}, {}, {}, {}, {}, {0: qkv_cut}
    tied = tokens
    for e in slots:

        def feed():
            return feed_forward(
                e, index, lengths, picked, [att[e]] + rows_now, tied, cotangent, out_full,
                gate_up_weight, down_weight, partner, norm_gains
            )

        later = rows_for(e - 1) if e else []
        sums = [(gn2s[e + 1], e + 1, "tensor")] if e + 1 in gn2s else []
        sent = [d for d in range(1, parts) if (d == 1) == (e == slots[0])] if e in (slots[0], 0) else []
        got, outs = beside(later + sums + [(qkv_cut, d, "tensor") for d in sent], feed)
        later, got = got[: len(later)], got[len(later) :]
        if sums:
            gn2_got[e + 1] = got.pop(0)
        qkv_all.update(zip(sent, got))
        if e:
            rows_now = later
        lefts[e], acts[e], gn2s[e], terms[e] = outs[:4]
        tied = after(tokens, gn2s[e])
    resid = outs[4]
    qkv_full = lax.all_gather(jnp.stack([qkv_all[d] for d in range(parts)]), "dp", axis=0)
    gn2_all = [gn2s[0]] + [gn2_got[e] for e in range(1, members)]
    grad_resid, grad_low, att_own, gain_two, *grads = resid_back(
        index, lengths, picked, cotangent, resid, gn2_all, out_full, norm_gains, [att[0]] + rows_now
    )
    lefts, acts = [lefts[e] for e in slots], [acts[e] for e in slots]

    near, (away_b, keep_b) = beside(
        [(grads[d], d, "tensor") for d in range(1, parts - 1)],
        lambda: ffn_grads(index, lefts, acts, 1, shares, True),
    )
    (far, got_b), (wg_a,) = beside(
        [(grads[parts - 1], parts - 1, "tensor"), (away_b, 1, "dp")],
        lambda: ffn_grads(index, lefts, acts, 0, shares, False, grad_low, att_own),
    )
    sum_a = lax.psum_scatter(after(wg_a, qkv_full), "dp", scatter_dimension=0, tiled=True)[0]
    grads_all = [grads[0], *near, far]
    halves = halve(lanes_of(add(keep_b, got_b)), 0)

    def back(j):
        return attend_back(index, grads_all, q_back[j], k, v, att_nat[j], cosine, sine, j)

    terms_out = [(terms[e], e, "tensor") for e in range(1, members)]
    got, group = beside(terms_out + leaving(halves), lambda: back(0))
    others, got = got[: len(terms_out)], got[len(terms_out) :]
    lanes = merge(halves, got)
    step = 1
    qkv_acts, acts_got = [group], []
    for j in range(1, pairs):
        halves = halve(lanes, step)

        got, group = beside(outgoing(group) + leaving(halves), lambda: back(j))
        group_got, got = got[: parts - 1], got[parts - 1 :]
        acts_got.append([qkv_acts[-1][0]] + group_got)
        qkv_acts.append(group)
        lanes = merge(halves, got)
        step += 1

    b_lanes = lanes
    for s in range(step, bits - 1):
        h = halve(b_lanes, s)
        b_lanes = merge(h, [swap(*x) for x in leaving(h)])
    sum_b = joined(b_lanes)

    def finish():
        away_q, keep_q, gain_one = project_grads(index, tokens, qkv_acts, qkv_weight, norm_gains, shares)
        total = add(keep_q, swap(away_q, 1, "dp"))
        one, two = lanes_of(total)
        for s in range(bits - 1):
            (h1,), (h2,) = halve([one], s), halve([two], s)
            g1 = swap(*leaving([h1])[0])
            g2 = swap(after(leaving([h2])[0][0], g1), 1 << h2[4], "dp")
            one, two = merge([h1, h2], [g1, g2])
        qkv_sum = joined([one, two]).astype(F32)
        grad_qkv = jnp.stack([qkv_sum[:, c * local : (c + 1) * local] for c in range(3)])
        gains_grad = after(jnp.stack([gain_one[:, 0] / norm_gains[0], jnp.sum(gain_two, axis=0)]), g2)
        for s in range(bits):
            gains_grad = gains_grad + swap(gains_grad, 1 << s, "dp")
        out = resid + terms[0].astype(F32)
        for term in others:
            out = out + term.astype(F32)
        return grad_qkv, gains_grad, out

    got, (grad_qkv, gains_grad, out) = beside(
        outgoing(group) + [(sum_b, members, "tensor")], finish, apart=True
    )
    *last, got_b = got
    acts_got.append([group[0]] + last)
    op_sum = jnp.concatenate(
        [sum_a[(3 + c) * part : (4 + c) * part] for c in range(parts * local // hidden)], axis=1
    )
    gains_low = jnp.concatenate([a.reshape(-1, local) for a in split3(gains_grad)])
    pieces = [jnp.concatenate([op_sum[:, d * local : (d + 1) * local], gains_low]) for d in range(parts)]
    got, (grad_tok, grad_gu, grad_down) = beside(
        outgoing(pieces),
        lambda: token_grad(index, tokens, grad_resid, qkv_full, norm_gains, acts_got, sum_a, got_b),
    )
    got = jnp.stack([pieces[0]] + got).astype(F32)
    grad_op = jnp.sum(got[:, :part], axis=0).T
    gains_all = got[:, part:].reshape(parts, 3, 2, width)
    gains_all = gains_all[:, 0] + gains_all[:, 1] + gains_all[:, 2]
    gains_grad = jnp.zeros_like(gains_all[0])
    for z in range(parts):
        gains_grad = gains_grad + lax.dynamic_index_in_dim(gains_all, me ^ z, 0, keepdims=False)
    return (out, grad_tok, grad_qkv, grad_op, grad_gu, grad_down, gains_grad)


def solution(mesh):
    in_specs = (
        P("dp", None),
        P(None, None, "tensor"),
        P("tensor", None),
        P(None, None, "tensor"),
        P("tensor", None),
        P(),
        P(),
        P("dp"),
        P("dp"),
        P("dp", None),
    )
    out_specs = (
        P(("dp", "tensor"), None),
        P(("dp", "tensor"), None),
        P(None, "dp", "tensor"),
        P("tensor", "dp"),
        P(None, "dp", "tensor"),
        P("tensor", "dp"),
        P(),
    )
    return jax.shard_map(body, mesh=mesh, in_specs=in_specs, out_specs=out_specs, check_vma=False)
```

```python
import functools
import math

import jax
import jax.numpy as jnp
import numpy as np
from jax import lax
from jax.experimental import pallas as pl
from jax.experimental.pallas import tpu as pltpu
from jax.sharding import PartitionSpec as P

HD = 64
WIN = 2048
EPSILON = 1e-05
NEG_FILL = -1e30
LOG2E = math.log2(math.e)
LN2 = math.log(2.0)
FACTOR = HD ** (-0.5)
VMEM = 60 * 2**20
F32 = jnp.float32
BF16 = jnp.bfloat16

NN = (((1,), (0,)), ((), ()))
NT = (((1,), (1,)), ((), ()))
TN = (((0,), (0,)), ((), ()))


def dot(a, b, dims=NN):
    return lax.dot_general(a, b, dims, preferred_element_type=F32)


def call(kernel, grid, in_specs, out_specs, out_shape, scratch=(), flops=0, nbytes=0, trans=0, prefetch=0):
    return pl.pallas_call(
        kernel,
        grid_spec=pltpu.PrefetchScalarGridSpec(
            num_scalar_prefetch=prefetch,
            grid=grid,
            in_specs=in_specs,
            out_specs=out_specs,
            scratch_shapes=list(scratch),
        ),
        out_shape=out_shape,
        compiler_params=pltpu.CompilerParams(vmem_limit_bytes=VMEM),
        cost_estimate=pl.CostEstimate(flops=flops, bytes_accessed=nbytes, transcendentals=trans),
    )


def whole(shape):
    return pl.BlockSpec(shape, lambda *_: (0,) * len(shape), pipeline_mode=pl.Buffered(1))


def smem():
    return pl.BlockSpec(memory_space=pltpu.SMEM)


def sds(shape, dtype):
    return jax.ShapeDtypeStruct(shape, dtype)


def rotary_tables():
    position = np.arange(WIN, dtype=np.float64)
    frequency = 10000.0 ** (-2.0 * np.arange(HD // 2, dtype=np.float64) / HD)
    angles = position[:, None] * frequency[None, :]
    cosine = np.cos(angles)
    sine = np.sin(angles)
    cos_full = np.tile(np.concatenate([cosine, cosine], axis=1), (1, 2))
    sin_full = np.tile(np.concatenate([-sine, sine], axis=1), (1, 2))
    return cos_full.astype(np.float32), sin_full.astype(np.float32)


def swap_halves(v):
    lane = lax.broadcasted_iota(jnp.int32, v.shape, 1)
    return jnp.where(lane % HD < HD // 2, pltpu.roll(v, 96, 1), pltpu.roll(v, 32, 1))


def rms(x):
    return lax.rsqrt(jnp.mean(x * x, axis=-1, keepdims=True) + EPSILON)


def split3(v):
    hi = v.astype(BF16)
    rest = v - hi.astype(F32)
    mid = rest.astype(BF16)
    low = (rest - mid.astype(F32)).astype(BF16)
    return hi, mid, low


def norm_back(grad_normed, gain, unit, factor):
    scaled = grad_normed * gain
    return factor * (scaled - unit * jnp.mean(scaled * unit, axis=-1, keepdims=True))


def qkv_kernel(len_ref, x_ref, w_ref, gain_ref, cos_ref, sin_ref, q_ref, k_ref, v_ref):
    rows = x_ref.shape[0]
    x = x_ref[...].astype(F32)
    normed = (x * rms(x) * gain_ref[0:1, :]).astype(BF16)
    cosine = cos_ref[...]
    sine = sin_ref[...]
    lane = lax.broadcasted_iota(jnp.int32, (rows, 128), 1)
    slot = lax.broadcasted_iota(jnp.int32, (rows, 128), 0) + pl.program_id(0) * rows
    masked = jnp.where(slot < len_ref[0], 0.0, NEG_FILL).astype(BF16)
    one = jnp.ones((rows, 128), BF16)
    zero = jnp.zeros((rows, 128), BF16)
    pairs = w_ref.shape[2] // 128
    for c in range(3):
        y = dot(normed, w_ref[c])
        for j in range(pairs):
            v = y[:, 128 * j : 128 * (j + 1)]
            if c < 2:
                v = v * cosine + swap_halves(v) * sine
            if c == 0:
                v = v * (FACTOR * LOG2E)
            v = v.astype(BF16)
            for s in range(2):
                first = HD * (1 - s)
                own = (lane >= HD * s) & (lane < HD * (s + 1))
                if c == 0:
                    q_ref[2 * j + s] = jnp.where(own, v, jnp.where(lane == first, one, zero))
                elif c == 1:
                    tail = jnp.where(
                        lane == first, masked, jnp.where(lane < first + 4, one, zero)
                    )
                    tail = jnp.where(lane < first, zero, tail)
                    k_ref[2 * j + s] = jnp.where(own, v, tail)
                else:
                    v_ref[2 * j + s] = jnp.where(own, v, one)


def project(lengths, tokens, qkv_weight, gains, cosine, sine, block=512):
    rows, width = tokens.shape
    local = qkv_weight.shape[2]
    heads = local // HD
    spec = pl.BlockSpec((heads, block, 128), lambda i: (0, i, 0))
    return call(
        qkv_kernel,
        (rows // block,),
        [
            smem(),
            pl.BlockSpec((block, width), lambda i: (i, 0)),
            whole(qkv_weight.shape),
            whole(gains.shape),
            pl.BlockSpec((block, 128), lambda i: (i, 0)),
            pl.BlockSpec((block, 128), lambda i: (i, 0)),
        ],
        [spec] * 3,
        [sds((heads, rows, 128), BF16)] * 3,
    )(lengths, tokens, qkv_weight, gains, cosine, sine)


def attend_kernel(sub, parts, idx_ref, q_ref, k_ref, v_ref, *refs):
    o_refs = refs[:parts]
    nat_ref, qb_ref = refs[parts:]
    rows = q_ref.shape[1]
    lane = lax.broadcasted_iota(jnp.int32, (sub, 128), 1)
    for r in range(rows // sub):
        part = slice(r * sub, (r + 1) * sub)
        outs = []
        for s in range(2):
            q = q_ref[s, part, :]
            scores = dot(q, k_ref[s], NT)
            peak = jnp.max(scores, axis=1, keepdims=True)
            expo = jnp.exp2(scores - peak).astype(BF16)
            acc = dot(expo, v_ref[s])
            outs.append(acc / pltpu.roll(acc, HD, 1))
            first = HD * (1 - s)
            total = jnp.where((lane >= first) & (lane < first + HD), acc, 1.0)
            hi, mid, low = split3(-(peak + jnp.log2(total)))
            tail = jnp.where(lane == first + 3, low, q)
            tail = jnp.where(lane == first + 2, mid, tail)
            qb_ref[s, part, :] = jnp.where(lane == first + 1, hi, tail)
        nat_ref[part, :] = jnp.where(lane < HD, outs[0], outs[1]).astype(BF16)
    for d in range(parts):

        @pl.when(pl.program_id(1) == d)
        def _():
            o_refs[d][...] = nat_ref[...]


def attend(index, q, k, v, parts, sub=256):
    heads, rows, _ = q.shape
    keys = k.shape[1]
    share = rows // parts
    local = heads * HD
    return call(
        functools.partial(attend_kernel, min(sub, share), parts),
        (heads // 2, parts),
        [
            pl.BlockSpec((2, share, 128), lambda j, i, idx: (j, idx[0] ^ i, 0)),
            pl.BlockSpec((2, keys, 128), lambda j, i, idx: (j, 0, 0)),
            pl.BlockSpec((2, keys, 128), lambda j, i, idx: (j, 0, 0)),
        ],
        [pl.BlockSpec((share, 128), lambda j, i, idx: (0, j))] * parts
        + [
            pl.BlockSpec((share, 128), lambda j, i, idx: (idx[0] ^ i, j)),
            pl.BlockSpec((2, share, 128), lambda j, i, idx: (j, idx[0] ^ i, 0)),
        ],
        [sds((share, local), BF16)] * parts + [sds((rows, local), BF16), sds((heads, rows, 128), BF16)],
        prefetch=1,
    )(index, q, k, v)


def cut_kernel(idx_ref, gu_ref, dw_ref, out_ref):
    part = gu_ref.shape[1]
    out_ref[:part, :] = gu_ref[0]
    out_ref[part : 2 * part, :] = gu_ref[1]
    out_ref[2 * part :, :] = dw_ref[...].T


def cut_weights(dp, gate_up, down, shares):
    _, width, hidden = gate_up.shape
    part = width // shares
    if part % 128:
        down = lax.dynamic_slice_in_dim(down, dp[0] * part, part, 1)
        spec = whole(down.shape)
    else:
        spec = pl.BlockSpec((hidden, part), lambda i, idx: (0, idx[0]))
    return call(
        cut_kernel,
        (1,),
        [pl.BlockSpec((2, part, hidden), lambda i, idx: (0, idx[0], 0)), spec],
        whole((3 * part, hidden)),
        sds((3 * part, hidden), BF16),
        nbytes=12 * part * hidden,
        prefetch=1,
    )(dp, gate_up, down)


def pack_kernel(*refs):
    out_ref, row = refs[-1], 0
    for ref in refs[:-1]:
        out_ref[row : row + ref.shape[0], :] = ref[...]
        row += ref.shape[0]


def pack(arrays):
    shape = (sum(a.shape[0] for a in arrays), arrays[0].shape[1])
    return call(pack_kernel, (1,), [whole(a.shape) for a in arrays], whole(shape), sds(shape, BF16))(*arrays)


def ffn_kernel(parts, ow_row, slot, idx_ref, len_ref, weight_ref, gain_ref, x_h, cot_h, gu_h, dw_h, pb_h, ow_h, *refs):
    own = slot == 0
    att_h = refs[:parts]
    refs = refs[parts:]
    count = 6 if own else 5
    outs, scratch = refs[:count], refs[count:]
    x_v, cot_v, att_v, ow_v, gu_v, dw_v, pb_v, left_v, act_v, ffn_v, gn2_v, low_v, sem_in, sem_out = scratch
    rows, width = x_v.shape
    local = att_v.shape[2]
    hidden_units = gu_v.shape[2]
    part = pb_v.shape[1] // 3
    row0 = pl.multiple_of((idx_ref[0] ^ slot) * rows, rows)
    mine = pl.ds(row0, rows)

    def fetch(src, dst, i):
        copy = pltpu.make_async_copy(src, dst, sem_in.at[i])
        copy.start()
        return copy

    pending = []

    def store(src, dst, i):
        copy = pltpu.make_async_copy(src, dst, sem_out.at[i])
        copy.start()
        pending.append(copy)

    get_x = fetch(x_h.at[mine], x_v, 0)
    get_ow = fetch(ow_h.at[:, pl.ds(ow_row, ow_v.shape[1])], ow_v, 6 + parts)
    get_att = [fetch(att_h[d], att_v.at[d], 2 + d) for d in range(parts)]
    get_cot = fetch(cot_h.at[mine], cot_v, 2 + parts)
    get_gu = fetch(gu_h, gu_v, 3 + parts)
    get_dw = fetch(dw_h, dw_v, 4 + parts)
    get_pb = fetch(pb_h.at[:, pl.ds(0, pb_v.shape[1])], pb_v, 1)

    get_x.wait()
    get_ow.wait()
    piece = ow_v.shape[1] // parts
    resid = x_v[...].astype(F32)
    for d in range(parts):
        get_att[d].wait()
        resid = resid + dot(att_v[d], ow_v[:, d * piece : (d + 1) * piece].reshape(local, width))
    if own:
        ffn_v[...] = resid
        store(ffn_v, outs[5], 4)
    normed = (resid * rms(resid) * gain_ref[1:2, :]).astype(BF16)
    left_v[0] = normed
    position = lax.broadcasted_iota(jnp.int32, (rows, 1), 0) + row0
    row_weight = jnp.where(position < len_ref[0], weight_ref[0], 0.0)
    get_cot.wait()
    left_v[1] = (cot_v[...].astype(F32) * row_weight).astype(BF16)
    store(left_v, outs[0], 0)
    for shard in range(2):
        cols = slice(shard * hidden_units, (shard + 1) * hidden_units)
        if shard == 0:
            get_gu.wait()
            get_dw.wait()
            gate_w, up_w, down_w = gu_v[0], gu_v[1], dw_v[...]
        else:
            get_pb.wait()
            gate_w, up_w, down_w = (
                pb_v[:, c * part : (c + 1) * part, :].reshape(width, hidden_units) for c in range(3)
            )
        gate = dot(left_v[0], gate_w)
        upper = dot(left_v[0], up_w)
        grad_hidden = dot(left_v[1], down_w, NT if shard == 0 else NN)
        sigma = 0.5 + 0.5 * jnp.tanh(0.5 * gate)
        act = gate * sigma
        hidden = (act * upper).astype(BF16)
        grad_up = (grad_hidden * act).astype(BF16)
        grad_gate = (grad_hidden * upper * (sigma + act * (1.0 - sigma))).astype(BF16)
        act_v[0, :, cols] = grad_gate
        act_v[1, :, cols] = grad_up
        act_v[2, :, cols] = hidden
        store(act_v.at[:, :, cols], outs[1].at[:, :, cols], 1 + 4 * shard)
        grad = dot(grad_gate, gate_w, NT) + dot(grad_up, up_w, NT)
        term = dot(hidden, down_w, NN if shard == 0 else NT)
        if shard == 0:
            gn2_v[...] = grad
            if own:
                pending.pop(0).wait()
            ffn_v[...] = term
        else:
            low_v[0] = (gn2_v[...] + grad).astype(BF16)
            store(low_v.at[0], outs[2], 2)
            low_v[1] = (ffn_v[...] + term).astype(BF16)
            cut = outs[3].shape[0]
            store(low_v.at[1, pl.ds(0, cut)], outs[3], 3)
            store(low_v.at[1, pl.ds(cut, rows - cut)], outs[4], 6)
    for copy in pending:
        copy.wait()


def feed_forward(slot, index, lengths, picked, atts, tokens, cotangent, out_full, gate_up, down, partner, gains):
    parts = len(atts)
    rows, local = atts[0].shape
    width = tokens.shape[1]
    hidden = gate_up.shape[2]
    early = rows * 5 // 8
    out_rows, ow_row = out_full
    shares = partner.shape[0]
    part = width // shares
    anywhere = pl.BlockSpec(memory_space=pl.ANY)
    out_shape = [
        sds((2, rows, width), BF16), sds((3, rows, 2 * hidden), BF16),
        sds((rows, width), BF16), sds((early, width), BF16), sds((rows - early, width), BF16),
    ]
    if slot == 0:
        out_shape.append(sds((rows, width), F32))
    return call(
        functools.partial(ffn_kernel, parts, ow_row, slot),
        (1,),
        [smem(), smem(), whole(gains.shape)] + [anywhere] * (6 + parts),
        [anywhere] * len(out_shape),
        out_shape,
        scratch=[
            pltpu.VMEM((rows, width), BF16),
            pltpu.VMEM((rows, width), BF16),
            pltpu.VMEM((parts, rows, local), BF16),
            pltpu.VMEM((shares, parts * local // shares, width), BF16),
            pltpu.VMEM(gate_up.shape, BF16),
            pltpu.VMEM(down.shape, BF16),
            pltpu.VMEM((shares, 3 * part, hidden), BF16),
            pltpu.VMEM((2, rows, width), BF16),
            pltpu.VMEM((3, rows, 2 * hidden), BF16),
            pltpu.VMEM((rows, width), F32),
            pltpu.VMEM((rows, width), F32),
            pltpu.VMEM((2, rows, width), BF16),
            pltpu.SemaphoreType.DMA((7 + parts,)),
            pltpu.SemaphoreType.DMA((7,)),
        ],
        prefetch=1,
    )(index, lengths, picked, gains, tokens, cotangent, gate_up, down, partner, out_rows, *atts)


def ffn_grad_kernel(sets, split, extra, cuts, idx_ref, *refs):
    left = refs[:sets]
    act = refs[sets : 2 * sets]
    refs = refs[2 * sets :]
    count = 2 if extra else 0
    op, folds, outs = refs[:count], refs[count : count + 2 * len(cuts)], refs[count + 2 * len(cuts) :]
    if cuts:
        fold_kernel(cuts, idx_ref, *folds, *outs[1:])
        outs = outs[:1]
    step = pl.program_id(0)

    def write(total):
        part = outs[0].shape[-2]
        if not split:
            for j in range(outs[0].shape[0]):
                outs[0][j] = total[j * part : (j + 1) * part, :].astype(BF16)
            return
        for keep in range(2):
            for bit in range(2):

                @pl.when((idx_ref[1] & 1) == bit)
                def _():
                    for j in range(outs[0].shape[0]):
                        d = 2 * j + (bit if keep else 1 - bit)
                        outs[keep][j] = total[d * part : (d + 1) * part, :].astype(BF16)

    @pl.when(step < 3)
    def _():
        total = dot(left[0][0], act[0][0], TN)
        for e in range(1, sets):
            total = total + dot(left[e][0], act[e][0], TN)
        write(total)

    if extra:

        @pl.when(step >= 3)
        def _():
            write(dot(op[0][...], op[1][...], TN))


def ffn_grads(index, lefts, acts, shard, shares, split, grad_low=None, att_own=None, lanes=()):
    sets = len(lefts)
    _, rows, width = lefts[0].shape
    hidden = acts[0].shape[2] // 2
    part = width // shares
    extra = 0 if grad_low is None else att_own.shape[1] // hidden
    steps = 3 + extra
    specs = [pl.BlockSpec((1, rows, width), lambda c, idx: (jnp.minimum(c // 2, 1), 0, 0))] * sets
    specs += [pl.BlockSpec((1, rows, hidden), lambda c, idx: (jnp.minimum(c, 2), 0, shard))] * sets
    args = list(lefts) + list(acts)
    if extra:
        specs += [
            pl.BlockSpec(grad_low.shape, lambda c, idx: (0, 0)),
            pl.BlockSpec((att_own.shape[0], hidden), lambda c, idx: (0, jnp.maximum(c - 3, 0))),
        ]
        args += [grad_low, att_own]
    count = shares // 2 if split else shares
    outs = 2 if split else 1
    out_specs = [pl.BlockSpec((count, part, hidden), lambda c, idx: (0, c, 0))] * outs
    out_shape = [sds((count, steps * part, hidden), BF16)] * outs
    cuts, info = [], []
    for n, (keep, got, lead, order) in enumerate(lanes):
        size, lane_rows, cols = keep.shape
        lane_rows //= len(lanes)
        block = lane_rows // 4 if lane_rows % 64 == 0 else lane_rows
        last = lane_rows // block - 1
        at = functools.partial(lambda n, last, c, idx: (0, n * (last + 1) + jnp.minimum(c, last), 0), n, last)
        here = functools.partial(lambda last, c, idx: (0, jnp.minimum(c, last), 0), last)
        specs += [pl.BlockSpec((size, block, cols), at)] * 2
        args += [keep, got]
        bit = order[0]
        cuts.append((len(lead) - 1 - lead.index(bit), bit))
        info.append(([b for b in lead if b != bit], order[1:], bit))
        out_specs += [pl.BlockSpec((size // 2, block, cols), here)] * 2
        out_shape += [sds((size // 2, lane_rows, cols), BF16)] * 2
    res = call(
        functools.partial(ffn_grad_kernel, sets, split, extra, cuts),
        (steps,),
        specs,
        out_specs,
        out_shape,
        prefetch=1,
    )(index, *args)
    if not lanes:
        return res
    return res[0], [(res[1 + 2 * n], res[2 + 2 * n]) + info[n] for n in range(len(lanes))]


def resid_kernel(parts, members, idx_ref, len_ref, weight_ref, cot_ref, resid_ref, ow_ref, gain_ref, *refs):
    gn2_refs = refs[:members]
    att_refs = refs[members : members + parts]
    gr_ref, low_ref, cat_ref, sum_ref = refs[members + parts : members + parts + 4]
    g_refs = refs[members + parts + 4 :]
    rows, width = cot_ref.shape
    local = att_refs[0].shape[1]
    step = pl.program_id(0)
    first = (idx_ref[0] * pl.num_programs(0) + step) * rows
    slot = lax.broadcasted_iota(jnp.int32, (rows, 1), 0) + first
    row_weight = jnp.where(slot < len_ref[0], weight_ref[0], 0.0)
    gn2 = gn2_refs[0][...].astype(F32)
    for ref in gn2_refs[1:]:
        gn2 = gn2 + ref[...].astype(F32)
    resid = resid_ref[...]
    factor = rms(resid)
    unit = resid * factor
    grad = cot_ref[...].astype(F32) * row_weight + norm_back(gn2, gain_ref[1:2, :], unit, factor)
    gr_ref[...] = grad
    low = grad.astype(BF16)
    low_ref[...] = low

    @pl.when(step == 0)
    def _():
        sum_ref[...] = jnp.zeros_like(sum_ref)

    sum_ref[...] += jnp.sum((gn2 * unit).reshape(rows // 8, 8, width), axis=0)
    for d in range(parts):
        piece = ow_ref.shape[1] // parts
        block = ow_ref[:, d * piece : (d + 1) * piece].reshape(local, width)
        g_refs[d][...] = dot(low, block, NT).astype(BF16)
        cat_ref[:, d * local : (d + 1) * local] = att_refs[d][...]


def resid_back(index, lengths, picked, cotangent, resid, gn2s, out_full, gains, atts, block=256):
    share, width = resid.shape
    parts, members = len(atts), len(gn2s)
    local = atts[0].shape[1]
    out_rows, ow_row = out_full
    ow_rows = parts * local // out_rows.shape[0]
    steps = share // block
    row = lambda n: pl.BlockSpec((block, n), lambda i, idx: (i, 0))
    return call(
        functools.partial(resid_kernel, parts, members),
        (steps,),
        [
            smem(), smem(),
            pl.BlockSpec((block, width), lambda i, idx: (idx[0] * steps + i, 0)),
            row(width),
            pl.BlockSpec((out_rows.shape[0], ow_rows, width), lambda *_: (0, ow_row // ow_rows, 0), pipeline_mode=pl.Buffered(1)),
            whole(gains.shape),
        ]
        + [row(width)] * members
        + [row(local)] * parts,
        [row(width), row(width), row(parts * local), whole((8, width))] + [row(local)] * parts,
        [sds((share, width), F32), sds((share, width), BF16), sds((share, parts * local), BF16), sds((8, width), F32)]
        + [sds((share, local), BF16)] * parts,
        prefetch=1,
    )(index, lengths, picked, cotangent, resid, out_rows, gains, *gn2s, *atts)


def attend_back_kernel(parts, idx_ref, q_ref, k_ref, v_ref, att_ref, cos_ref, sin_ref, *refs):
    grad_refs = refs[:parts]
    outs = refs[parts : 2 * parts]
    dk_acc, dv_acc = refs[2 * parts :]
    rows = q_ref.shape[1]
    step = pl.program_id(0)
    me = idx_ref[0]
    lane = lax.broadcasted_iota(jnp.int32, (rows, 128), 1)

    def table(ref, d):
        return ref[pl.ds(pl.multiple_of((me ^ d) * rows, rows), rows), :]

    def columns(ref, d):
        return ref[:, pl.ds(pl.multiple_of((me ^ d) * rows, rows), rows)].T

    def back(v, d, scale):
        return ((v * table(cos_ref, d) - swap_halves(v) * table(sin_ref, d)) * scale).astype(BF16)

    @pl.when(step == 0)
    def _():
        dk_acc[...] = jnp.zeros_like(dk_acc)
        dv_acc[...] = jnp.zeros_like(dv_acc)

    grad = grad_refs[0][...]
    for d in range(1, parts):
        grad = jnp.where(step == d, grad_refs[d][...], grad)
    prod = grad.astype(F32) * att_ref[...].astype(F32)
    zero = jnp.zeros((rows, 128), BF16)
    dqs, probs_all, scores_all, grads_own, queries_own = [], [], [], [], []
    for s in range(2):
        first = HD * (1 - s)
        own = (lane >= HD * s) & (lane < HD * (s + 1))
        delta = jnp.sum(jnp.where(own, prod, 0.0), axis=1, keepdims=True)
        hi, mid, low = split3(-delta)
        grad_own = jnp.where(own, grad, zero)
        grad_aug = jnp.where(lane == first + 2, low, grad_own)
        grad_aug = jnp.where(lane == first + 1, mid, grad_aug)
        grad_aug = jnp.where(lane == first, hi, grad_aug)
        q = q_ref[s]
        probs = jnp.exp2(dot(q, k_ref[s], NT))
        scores_grad = (probs * dot(grad_aug, v_ref[s], NT)).astype(BF16)
        probs_all.append(probs.astype(BF16))
        scores_all.append(scores_grad)
        grads_own.append(grad_own)
        queries_own.append(jnp.where(own, q, zero))
        dqs.append(dot(scores_grad, k_ref[s]))
    dv_acc[...] += dot(jnp.concatenate(grads_own, axis=0).T, jnp.concatenate(probs_all, axis=0))
    dk_acc[...] += dot(jnp.concatenate(queries_own, axis=0).T, jnp.concatenate(scores_all, axis=0))
    dq = jnp.where(lane < HD, dqs[0], dqs[1])
    for d in range(parts):

        @pl.when(step == d)
        def _():
            outs[d][0] = back(dq, d, FACTOR)

    @pl.when(step == parts - 1)
    def _():
        for d in range(parts):
            outs[d][1] = back(columns(dk_acc, d), d, LN2)
            outs[d][2] = columns(dv_acc, d).astype(BF16)


def attend_back(index, grads, q, k, v, att, cosine, sine, pair):
    parts = len(grads)
    share = grads[0].shape[0]
    rows = q.shape[1]
    keys = pl.BlockSpec((2, rows, 128), lambda i, idx: (pair, 0, 0), pipeline_mode=pl.Buffered(1))
    return call(
        functools.partial(attend_back_kernel, parts),
        (parts,),
        [
            pl.BlockSpec((2, share, 128), lambda i, idx: (pair, idx[0] ^ i, 0)),
            keys,
            keys,
            pl.BlockSpec((share, 128), lambda i, idx: (idx[0] ^ i, pair)),
            whole(cosine.shape),
            whole(sine.shape),
        ]
        + [pl.BlockSpec((share, 128), lambda i, idx: (0, pair))] * parts,
        [whole((3, share, 128))] * parts,
        [sds((3, share, 128), BF16)] * parts,
        scratch=[pltpu.VMEM((128, rows), F32)] * 2,
        flops=2 * rows * rows * 128 * 10,
        nbytes=rows * 256 * 16,
        trans=2 * rows * rows,
        prefetch=1,
    )(index, q, k, v, att, cosine, sine, *grads)


def project_grad_kernel(parts, pairs, idx_ref, x_ref, w_ref, gain_ref, *refs):
    act_refs = refs[: parts * pairs]
    away_ref, keep_ref, sum_ref, acc = refs[parts * pairs :]
    step = pl.program_id(0)

    @pl.when(step == 0)
    def _():
        acc[...] = jnp.zeros_like(acc)

    x = x_ref[...].astype(F32)
    normed = (x * rms(x) * gain_ref[0:1, :]).astype(BF16)
    for d in range(parts):

        @pl.when(step == d)
        def _():
            acts = [act_refs[j * parts + d][c] for c in range(3) for j in range(pairs)]
            acc[...] += dot(normed, jnp.concatenate(acts, axis=1), TN)

    @pl.when(step == pl.num_programs(0) - 1)
    def _():
        count, part, _ = keep_ref.shape
        local = w_ref.shape[2]
        core = idx_ref[1] & 1
        for j in range(count):
            keep_ref[j] = acc[pl.ds(pl.multiple_of((2 * j + core) * part, part), part), :].astype(BF16)
            away_ref[j] = acc[pl.ds(pl.multiple_of((2 * j + 1 - core) * part, part), part), :].astype(BF16)
        gain_sum = acc[:, :local] * w_ref[0].astype(F32)
        for c in (1, 2):
            gain_sum += acc[:, c * local : (c + 1) * local] * w_ref[c].astype(F32)
        sum_ref[...] = jnp.broadcast_to(jnp.sum(gain_sum, axis=1, keepdims=True), sum_ref.shape)


def project_grads(index, tokens, acts, qkv_weight, gains, shares):
    width = tokens.shape[1]
    local = qkv_weight.shape[2]
    pairs, parts = len(acts), len(acts[0])
    share = acts[0][0].shape[1]
    flat = [a for group in acts for a in group]
    half = (shares // 2, width // shares, 3 * local)
    return call(
        functools.partial(project_grad_kernel, parts, pairs),
        (parts,),
        [
            pl.BlockSpec((share, width), lambda i, idx: (idx[0] ^ i, 0)),
            whole(qkv_weight.shape),
            whole(gains.shape),
        ]
        + [whole(a.shape) for a in flat],
        [whole(half), whole(half), whole((width, 128))],
        [sds(half, BF16), sds(half, BF16), sds((width, 128), F32)],
        scratch=[pltpu.VMEM((width, 3 * local), F32)],
        flops=2 * tokens.shape[0] * width * 3 * local,
        nbytes=tokens.size * 2 + 8 * width * local * 3,
        prefetch=1,
    )(index, tokens, qkv_weight, gains, *flat)


def token_grad_kernel(order, pairs, idx_ref, x_ref, gr_ref, w_ref, gain_ref, own_ref, got_ref, *refs):
    parts = len(order)
    act_refs = refs[: parts * pairs]
    out_ref, gu_ref, down_ref = refs[parts * pairs :]
    width = x_ref.shape[1]
    local = 128 * pairs
    grad = jnp.zeros(x_ref.shape, F32)
    for d in range(parts):
        for c in range(3):
            act = jnp.concatenate([act_refs[j * parts + d][c] for j in range(pairs)], axis=1)
            grad = grad + dot(act, w_ref[:, order.index(d), c].reshape(width, local), NT)
    x = x_ref[...].astype(F32)
    factor = rms(x)
    out_ref[...] = gr_ref[...] + norm_back(grad, gain_ref[0:1, :], x * factor, factor)

    @pl.when(pl.program_id(0) == 0)
    def _():
        part = gu_ref.shape[1]
        total = own_ref[: 3 * part, :].astype(F32) + got_ref[...].astype(F32)
        gu_ref[0] = total[:part]
        gu_ref[1] = total[part : 2 * part]
        down_ref[...] = total[2 * part :].T


def token_grad(index, tokens, grad_resid, qkv_full, order, gains, acts, ffn_own, ffn_got, block=256):
    share, width = grad_resid.shape
    pairs, parts = len(acts), len(acts[0])
    part, hidden = ffn_got.shape[0] // 3, ffn_got.shape[1]
    flat = [a for group in acts for a in group]
    steps = share // block
    return call(
        functools.partial(token_grad_kernel, order, pairs),
        (steps,),
        [
            pl.BlockSpec((block, width), lambda i, idx: (idx[0] * steps + i, 0)),
            pl.BlockSpec((block, width), lambda i, idx: (i, 0)),
            whole(qkv_full.shape),
            whole(gains.shape),
            whole(ffn_own.shape),
            whole(ffn_got.shape),
        ]
        + [pl.BlockSpec((3, block, 128), lambda i, idx: (0, i, 0))] * len(flat),
        [pl.BlockSpec((block, width), lambda i, idx: (i, 0)), whole((2, part, hidden)), whole((hidden, part))],
        [sds((share, width), F32), sds((2, part, hidden), F32), sds((hidden, part), F32)],
        prefetch=1,
    )(index, tokens, grad_resid, qkv_full, gains, ffn_own, ffn_got, *flat)


def fold_kernel(cuts, idx_ref, *refs):
    ins, outs = list(refs[: 2 * len(cuts)]), list(refs[2 * len(cuts) :])
    row = 0
    for at in cuts:
        keep, got = ins.pop(0), ins.pop(0)
        if at is None:
            rows = keep.shape[1]
            outs[0][row : row + rows, :] = (keep[0].astype(F32) + got[0].astype(F32)).astype(BF16)
            row += rows
            continue
        place, bit = at
        mine = (idx_ref[1] >> bit) & 1
        targets = ((outs.pop(0), mine), (outs.pop(0), 1 - mine))
        for j in range(keep.shape[0] // 2):
            rest = ((j >> place) << (place + 1)) | (j & ((1 << place) - 1))
            for out, value in targets:
                k = rest | (value << place)
                out[j] = (keep[k].astype(F32) + got[k].astype(F32)).astype(BF16)


def fold(index, lanes, cut_rows=False):
    cuts, specs, args, out_shape, info, total = [], [], [], [], [], 0
    for n, (keep, got, lead, order) in enumerate(lanes):
        count, rows, cols = keep.shape
        rows = rows // len(lanes) if cut_rows else rows
        at = functools.partial(lambda n, i, idx: (0, n, 0), n if cut_rows else 0)
        specs += [pl.BlockSpec((count, rows, cols), at)] * 2
        args += [keep, got]
        total += rows
        if order:
            bit = order[0]
            cuts.append((len(lead) - 1 - lead.index(bit), bit))
            info.append(([b for b in lead if b != bit], order[1:], bit))
            out_shape += [sds((count // 2, rows, cols), BF16)] * 2
        else:
            cuts.append(None)
    if not info:
        out_shape = [sds((total, cols), BF16)]
    res = call(
        functools.partial(fold_kernel, cuts), (1,), specs, [whole(o.shape) for o in out_shape], out_shape, prefetch=1
    )(index, *args)
    if not info:
        return res[0]
    return [(res[2 * n], res[2 * n + 1]) + info[n] for n in range(len(lanes))]


def after(value, *others):
    return lax.optimization_barrier((value, *others))[0]


def body(
    tokens, qkv_weight, out_weight, gate_up_weight, down_weight, norm_gains,
    species_weight, species_ids, lengths, cotangent,
):
    rows, width = tokens.shape
    local = out_weight.shape[0]
    hidden = down_weight.shape[0]
    parts = lax.axis_size("tensor")
    slots = list(range(parts - 2, -1, -2))
    shares = lax.axis_size("dp")
    part = width // shares
    me = lax.axis_index("tensor")
    dp = lax.axis_index("dp")
    index = jnp.stack([me, dp]).astype(jnp.int32)
    cosine, sine = (jnp.asarray(t) for t in rotary_tables())
    pairs = local // 128
    valid = lengths[0] >= 0

    def region(f):
        shapes = jax.eval_shape(f)
        zeros = lambda: jax.tree.map(lambda a: jnp.zeros(a.shape, a.dtype), shapes)
        return lax.optimization_barrier(lax.cond(valid, f, zeros))

    def beside(sends, f, apart=False):
        return region(lambda: ([swap(*x) for x in sends], region(f) if apart else f()))

    def swap(a, d, name="tensor"):
        return lax.ppermute(a, name, [(i, i ^ d) for i in range(lax.axis_size(name))])

    def cut(a, start, size, axis=0):
        return lax.dynamic_slice_in_dim(a, start, size, axis)

    def outgoing(pieces):
        return [(pieces[d], d, "tensor") for d in range(1, parts)]

    bits = shares.bit_length() - 1
    lead = list(range(bits - 1, 0, -1))

    def fold_first(keep, got):
        return fold(index, [(keep, got, lead, lead), (keep, got, lead, lead[::-1])], cut_rows=True)

    def fold_next(halves, got):
        return fold(index, [(keep, g, left, order) for (keep, _, left, order, _), g in zip(halves, got)])

    def leaving(halves):
        return [(away, 1 << bit, "dp") for _, away, _, _, bit in halves]

    matches = species_ids[:, None] == jnp.arange(species_weight.shape[0])[None, :]
    picked = jnp.sum(jnp.where(matches, species_weight[None, :], F32(0.0)), axis=1)

    mine = cut_weights(index[1:], gate_up_weight, down_weight, shares)
    ow_cut = cut(out_weight, dp * (local // shares), local // shares)
    qkv_cut = cut(qkv_weight, dp * part, part, 1).reshape(3 * part, local)
    top = parts // 2

    (partner_cut, *ow), (q, k, v) = beside(
        [(mine, 1, "tensor")] + outgoing([ow_cut] * parts),
        lambda: project(lengths, tokens, qkv_weight, norm_gains, cosine, sine),
    )
    if hidden == width:
        partner = lax.all_gather(pack([partner_cut, ow_cut, *ow]), "dp", axis=0)
        out_full = (partner, 3 * part)
    else:
        partner = lax.all_gather(partner_cut, "dp", axis=0)
        out_full = (lax.all_gather(pack([ow_cut, *ow]), "dp", axis=0), 0)
    (qkv_got,), (*att, att_nat, q_back) = beside(
        [(after(qkv_cut, partner_cut), top, "tensor")], lambda: attend(index, q, k, v, parts)
    )
    qkv_stack, order = pack([qkv_cut, qkv_got]), [0, top]
    rows_for = lambda e: outgoing([att[d ^ e] for d in range(parts)])
    rows_now = region(lambda: [swap(*x) for x in rows_for(slots[0])])

    lefts, acts, gn2s, terms, gn2_got = {}, {}, {}, {}, {}
    tied = tokens
    for e in slots:

        def feed():
            outs = feed_forward(
                e, index, lengths, picked, [att[e]] + rows_now, tied, cotangent, out_full,
                gate_up_weight, down_weight, partner, norm_gains
            )
            if e:
                return outs
            away_b, keep_b = ffn_grads(
                index, [*lefts.values(), outs[0]], [*acts.values(), outs[1]], 1, shares, True
            )
            return outs, keep_b, away_b

        sends = rows_for(e - 2) if e else []
        if e + 2 in gn2s:
            sends.append((gn2s[e + 2], e + 2, "tensor"))
        if len(order) < parts:
            bit = parts // (2 * len(order))
            sends.append((qkv_stack, bit, "tensor"))
        got, outs = beside(sends, feed)
        if len(order) < parts:
            qkv_stack, order = pack([qkv_stack, got.pop()]), order + [d ^ bit for d in order]
            if len(order) == parts:
                qkv_stack = qkv_stack.reshape(parts, 3, part, local)
                qkv_full = lax.all_gather(qkv_stack, "dp", axis=0)
        if e + 2 in gn2s:
            gn2_got[e + 2] = got.pop()
        if e:
            rows_now = got
        else:
            outs, keep_b, away_b = outs
        lefts[e], acts[e], gn2s[e], *terms[e] = outs[:5]
        tied = after(tokens, gn2s[e])
    resid = outs[5]
    gn2_all = [gn2s[0]] + [gn2_got[e] for e in slots[:-1]]
    (got_b,), (grad_resid, grad_low, att_own, gain_two, *grads) = beside(
        [(away_b, 1, "dp")],
        lambda: resid_back(
            index, lengths, picked, cotangent, resid, gn2_all, out_full, norm_gains, [att[0]] + rows_now
        ),
    )
    lefts, acts = [lefts[e] for e in slots], [acts[e] for e in slots]
    start = [(keep_b, got_b, lead, lead), (keep_b, got_b, lead, lead[::-1])]
    ways = []

    def grads_own():
        wg_a, halves = ffn_grads(index, lefts, acts, 0, shares, False, grad_low, att_own, start)
        ways[:] = [h[2:] for h in halves]
        return wg_a, [h[:2] for h in halves]

    got, (wg_a, halves) = beside(outgoing(grads), grads_own)
    halves = [tuple(h) + way for h, way in zip(halves, ways)]
    grads_all = [grads[0]] + got
    sum_a = lax.psum_scatter(after(wg_a, qkv_full), "dp", scatter_dimension=0, tiled=True)[0]
    step = 0

    def back(j):
        return attend_back(index, grads_all, q_back, k, v, att_nat, cosine, sine, j)

    def terms_out(i):
        return [(terms[e][i], e, "tensor") for e in slots[:-1]]

    got, group = beside(terms_out(0) + leaving(halves), lambda: back(0))
    first_terms, got = got[: len(slots) - 1], got[len(slots) - 1 :]
    halves, step = fold_next(halves, got), step + 1
    qkv_acts, acts_got = [group], []
    for j in range(1, pairs):
        now = leaving(halves) if step < bits - 1 else []
        got, group = beside(outgoing(group) + now, lambda: back(j))
        acts_got.append([qkv_acts[-1][0]] + got[: parts - 1])
        qkv_acts.append(group)
        if now:
            halves, step = fold_next(halves, got[parts - 1 :]), step + 1
    while step < bits - 1:
        halves, step = fold_next(halves, [swap(*x) for x in leaving(halves)]), step + 1
    sum_b = halves

    def finish():
        away_q, keep_q, gain_one = project_grads(index, tokens, qkv_acts, qkv_weight, norm_gains, shares)
        halves = fold(index, [(keep_q, swap(away_q, 1, "dp"), lead, lead)])
        for s in range(bits - 2):
            halves = fold_next(halves, [swap(*x) for x in leaving(halves)])
        gains_grad = jnp.stack([gain_one[:, 0] / norm_gains[0], jnp.sum(gain_two, axis=0)])
        gains_grad = after(gains_grad, *[h[0] for h in halves])
        for s in range(bits):
            gains_grad = gains_grad + swap(gains_grad, 1 << s, "dp")
        ways[:] = [h[2:] for h in halves]
        return [h[:2] for h in halves], gains_grad

    got, (halves, gains_grad) = beside(outgoing(group) + [(sum_b, 1, "tensor")], finish, apart=True)
    halves = [tuple(h) + way for h, way in zip(halves, ways)]
    acts_got.append([group[0]] + got[: parts - 1])
    got_b = got[-1]
    op_sum = jnp.concatenate(
        [sum_a[(3 + c) * part : (4 + c) * part] for c in range(parts * local // hidden)], axis=1
    )
    gains_low = jnp.concatenate([a.reshape(-1, local) for a in split3(gains_grad)])
    pieces = [jnp.concatenate([op_sum[:, d * local : (d + 1) * local], gains_low]) for d in range(parts)]
    got, (grad_tok, grad_gu, grad_down) = beside(
        leaving(halves) + terms_out(1) + outgoing(pieces),
        lambda: token_grad(index, tokens, grad_resid, qkv_full, order, norm_gains, acts_got, sum_a, got_b),
    )
    qkv_sum = fold_next(halves, got[:1]).astype(F32)
    grad_qkv = jnp.stack([qkv_sum[:, c * local : (c + 1) * local] for c in range(3)])
    second_terms, got = got[1 : len(slots)], got[len(slots) :]
    got = jnp.stack([pieces[0]] + got).astype(F32)
    grad_op = jnp.sum(got[:, :part], axis=0).T
    gains_all = got[:, part:].reshape(parts, 3, 2, width)
    gains_all = gains_all[:, 0] + gains_all[:, 1] + gains_all[:, 2]
    gains_grad = jnp.zeros_like(gains_all[0])
    for z in range(parts):
        gains_grad = gains_grad + lax.dynamic_index_in_dim(gains_all, me ^ z, 0, keepdims=False)
    ffn_rows = [
        sum((t.astype(F32) for t in got), own.astype(F32))
        for own, got in zip(terms[0], (first_terms, second_terms))
    ]
    out = resid + jnp.concatenate(ffn_rows)
    return (out, grad_tok, grad_qkv, grad_op, grad_gu, grad_down, gains_grad)


def solution(mesh):
    in_specs = (
        P("dp", None),
        P(None, None, "tensor"),
        P("tensor", None),
        P(None, None, "tensor"),
        P("tensor", None),
        P(),
        P(),
        P("dp"),
        P("dp"),
        P("dp", None),
    )
    out_specs = (
        P(("dp", "tensor"), None),
        P(("dp", "tensor"), None),
        P(None, "dp", "tensor"),
        P("tensor", "dp"),
        P(None, "dp", "tensor"),
        P("tensor", "dp"),
        P(),
    )
    return jax.shard_map(body, mesh=mesh, in_specs=in_specs, out_specs=out_specs, check_vma=False)
```

```python
import functools
import math

import jax
import jax.numpy as jnp
import numpy as np
from jax import lax
from jax.experimental import pallas as pl
from jax.experimental.pallas import tpu as pltpu
from jax.sharding import PartitionSpec as P

HD = 64
WIN = 2048
EPSILON = 1e-05
NEG_FILL = -1e30
LOG2E = math.log2(math.e)
LN2 = math.log(2.0)
FACTOR = HD ** (-0.5)
VMEM = 60 * 2**20
F32 = jnp.float32
BF16 = jnp.bfloat16

NN = (((1,), (0,)), ((), ()))
NT = (((1,), (1,)), ((), ()))
TN = (((0,), (0,)), ((), ()))


def dot(a, b, dims=NN):
    return lax.dot_general(a, b, dims, preferred_element_type=F32)


def call(kernel, grid, in_specs, out_specs, out_shape, scratch=(), flops=0, nbytes=0, trans=0, prefetch=0):
    return pl.pallas_call(
        kernel,
        grid_spec=pltpu.PrefetchScalarGridSpec(
            num_scalar_prefetch=prefetch,
            grid=grid,
            in_specs=in_specs,
            out_specs=out_specs,
            scratch_shapes=list(scratch),
        ),
        out_shape=out_shape,
        compiler_params=pltpu.CompilerParams(vmem_limit_bytes=VMEM),
        cost_estimate=pl.CostEstimate(flops=flops, bytes_accessed=nbytes, transcendentals=trans),
    )


def whole(shape):
    return pl.BlockSpec(shape, lambda *_: (0,) * len(shape), pipeline_mode=pl.Buffered(1))


def smem():
    return pl.BlockSpec(memory_space=pltpu.SMEM)


def sds(shape, dtype):
    return jax.ShapeDtypeStruct(shape, dtype)


def rotary_tables():
    position = np.arange(WIN, dtype=np.float64)
    frequency = 10000.0 ** (-2.0 * np.arange(HD // 2, dtype=np.float64) / HD)
    angles = position[:, None] * frequency[None, :]
    cosine = np.cos(angles)
    sine = np.sin(angles)
    cos_full = np.tile(np.concatenate([cosine, cosine], axis=1), (1, 2))
    sin_full = np.tile(np.concatenate([-sine, sine], axis=1), (1, 2))
    return cos_full.astype(np.float32), sin_full.astype(np.float32)


def swap_halves(v):
    lane = lax.broadcasted_iota(jnp.int32, v.shape, 1)
    return jnp.where(lane % HD < HD // 2, pltpu.roll(v, 96, 1), pltpu.roll(v, 32, 1))


def rms(x):
    return lax.rsqrt(jnp.mean(x * x, axis=-1, keepdims=True) + EPSILON)


def split3(v):
    hi = v.astype(BF16)
    rest = v - hi.astype(F32)
    mid = rest.astype(BF16)
    low = (rest - mid.astype(F32)).astype(BF16)
    return hi, mid, low


def norm_back(grad_normed, gain, unit, factor):
    scaled = grad_normed * gain
    return factor * (scaled - unit * jnp.mean(scaled * unit, axis=-1, keepdims=True))


def qkv_kernel(len_ref, x_ref, w_ref, gain_ref, cos_ref, sin_ref, q_ref, k_ref, v_ref, normed_ref):
    rows = x_ref.shape[0]
    x = x_ref[...].astype(F32)
    normed = (x * rms(x) * gain_ref[0:1, :]).astype(BF16)
    normed_ref[...] = normed
    cosine = cos_ref[...]
    sine = sin_ref[...]
    lane = lax.broadcasted_iota(jnp.int32, (rows, 128), 1)
    slot = lax.broadcasted_iota(jnp.int32, (rows, 128), 0) + pl.program_id(0) * rows
    masked = jnp.where(slot < len_ref[0], 0.0, NEG_FILL).astype(BF16)
    one = jnp.ones((rows, 128), BF16)
    zero = jnp.zeros((rows, 128), BF16)
    pairs = w_ref.shape[2] // 128
    for c in range(3):
        y = dot(normed, w_ref[c])
        for j in range(pairs):
            v = y[:, 128 * j : 128 * (j + 1)]
            if c < 2:
                v = v * cosine + swap_halves(v) * sine
            if c == 0:
                v = v * (FACTOR * LOG2E)
            v = v.astype(BF16)
            for s in range(2):
                first = HD * (1 - s)
                own = (lane >= HD * s) & (lane < HD * (s + 1))
                if c == 0:
                    q_ref[2 * j + s] = jnp.where(own, v, jnp.where(lane == first, one, zero))
                elif c == 1:
                    tail = jnp.where(
                        lane == first, masked, jnp.where(lane < first + 4, one, zero)
                    )
                    tail = jnp.where(lane < first, zero, tail)
                    k_ref[2 * j + s] = jnp.where(own, v, tail)
                else:
                    v_ref[2 * j + s] = jnp.where(own, v, one)


def project(lengths, tokens, qkv_weight, gains, cosine, sine, block=512):
    rows, width = tokens.shape
    local = qkv_weight.shape[2]
    heads = local // HD
    spec = pl.BlockSpec((heads, block, 128), lambda i: (0, i, 0))
    return call(
        qkv_kernel,
        (rows // block,),
        [
            smem(),
            pl.BlockSpec((block, width), lambda i: (i, 0)),
            whole(qkv_weight.shape),
            whole(gains.shape),
            pl.BlockSpec((block, 128), lambda i: (i, 0)),
            pl.BlockSpec((block, 128), lambda i: (i, 0)),
        ],
        [spec] * 3 + [pl.BlockSpec((block, width), lambda i: (i, 0))],
        [sds((heads, rows, 128), BF16)] * 3 + [sds((rows, width), BF16)],
    )(lengths, tokens, qkv_weight, gains, cosine, sine)


def attend_kernel(sub, parts, idx_ref, q_ref, k_ref, v_ref, *refs):
    o_refs = refs[:parts]
    nat_ref, qb_ref = refs[parts:]
    rows = q_ref.shape[1]
    lane = lax.broadcasted_iota(jnp.int32, (sub, 128), 1)
    for r in range(rows // sub):
        part = slice(r * sub, (r + 1) * sub)
        outs = []
        for s in range(2):
            q = q_ref[s, part, :]
            scores = dot(q, k_ref[s], NT)
            peak = jnp.max(scores, axis=1, keepdims=True)
            expo = jnp.exp2(scores - peak).astype(BF16)
            acc = dot(expo, v_ref[s])
            outs.append(acc / pltpu.roll(acc, HD, 1))
            first = HD * (1 - s)
            total = jnp.where((lane >= first) & (lane < first + HD), acc, 1.0)
            hi, mid, low = split3(-(peak + jnp.log2(total)))
            tail = jnp.where(lane == first + 3, low, q)
            tail = jnp.where(lane == first + 2, mid, tail)
            qb_ref[s, part, :] = jnp.where(lane == first + 1, hi, tail)
        nat_ref[part, :] = jnp.where(lane < HD, outs[0], outs[1]).astype(BF16)
    for d in range(parts):

        @pl.when(pl.program_id(1) == d)
        def _():
            o_refs[d][...] = nat_ref[...]


def attend(index, q, k, v, parts, sub=256):
    heads, rows, _ = q.shape
    keys = k.shape[1]
    share = rows // parts
    local = heads * HD
    return call(
        functools.partial(attend_kernel, min(sub, share), parts),
        (heads // 2, parts),
        [
            pl.BlockSpec((2, share, 128), lambda j, i, idx: (j, idx[0] ^ i, 0)),
            pl.BlockSpec((2, keys, 128), lambda j, i, idx: (j, 0, 0)),
            pl.BlockSpec((2, keys, 128), lambda j, i, idx: (j, 0, 0)),
        ],
        [pl.BlockSpec((share, 128), lambda j, i, idx: (0, j))] * parts
        + [
            pl.BlockSpec((share, 128), lambda j, i, idx: (idx[0] ^ i, j)),
            pl.BlockSpec((2, share, 128), lambda j, i, idx: (j, idx[0] ^ i, 0)),
        ],
        [sds((share, local), BF16)] * parts + [sds((rows, local), BF16), sds((heads, rows, 128), BF16)],
        prefetch=1,
    )(index, q, k, v)


def cut_kernel(idx_ref, gu_ref, dw_ref, *refs):
    part = gu_ref.shape[1]
    out_ref = refs[-1]
    out_ref[:part, :] = gu_ref[0]
    out_ref[part : 2 * part, :] = gu_ref[1]
    out_ref[2 * part : 3 * part, :] = dw_ref[...].T
    if len(refs) > 1:
        out_ref[3 * part :, :] = refs[0][...]


def cut_weights(dp, gate_up, down, shares, more):
    _, width, hidden = gate_up.shape
    part = width // shares
    if part % 128:
        down = lax.dynamic_slice_in_dim(down, dp[0] * part, part, 1)
        spec = whole(down.shape)
    else:
        spec = pl.BlockSpec((hidden, part), lambda i, idx: (0, idx[0]))
    shape = (3 * part + sum(a.shape[0] for a in more), hidden)
    return call(
        cut_kernel,
        (1,),
        [pl.BlockSpec((2, part, hidden), lambda i, idx: (0, idx[0], 0)), spec] + [whole(a.shape) for a in more],
        whole(shape),
        sds(shape, BF16),
        prefetch=1,
    )(dp, gate_up, down, *more)


def pack_kernel(*refs):
    out_ref, row = refs[-1], 0
    for ref in refs[:-1]:
        out_ref[row : row + ref.shape[0], :] = ref[...]
        row += ref.shape[0]


def pack(arrays):
    shape = (sum(a.shape[0] for a in arrays), arrays[0].shape[1])
    return call(pack_kernel, (1,), [whole(a.shape) for a in arrays], whole(shape), sds(shape, BF16))(*arrays)


def ffn_kernel(parts, ow_row, ow_order, slot, idx_ref, len_ref, weight_ref, gain_ref, x_h, cot_h, gu_h, dw_h, pb_h, ow_h, *refs):
    own = slot == 0
    att_h = refs[:parts]
    refs = refs[parts:]
    count = 7 if own else 6
    outs, scratch = refs[:count], refs[count:]
    x_v, cot_v, att_v, ow_v, gu_v, dw_v, pb_v, left_v, act_v, ffn_v, gn2_v, low_v, sem_in, sem_out = scratch
    rows, width = x_v.shape
    local = att_v.shape[2]
    hidden_units = gu_v.shape[2]
    part = pb_v.shape[1] // 3
    row0 = pl.multiple_of((idx_ref[0] ^ slot) * rows, rows)
    mine = pl.ds(row0, rows)

    def fetch(src, dst, i):
        copy = pltpu.make_async_copy(src, dst, sem_in.at[i])
        copy.start()
        return copy

    pending = []

    def store(src, dst, i):
        copy = pltpu.make_async_copy(src, dst, sem_out.at[i])
        copy.start()
        pending.append(copy)

    get_x = fetch(x_h.at[mine], x_v, 0)
    get_ow = fetch(ow_h.at[:, pl.ds(ow_row, ow_v.shape[1])], ow_v, 6 + parts)
    get_att = [fetch(att_h[d], att_v.at[d], 2 + d) for d in range(parts)]
    get_cot = fetch(cot_h.at[mine], cot_v, 2 + parts)
    get_gu = fetch(gu_h, gu_v, 3 + parts)
    get_dw = fetch(dw_h, dw_v, 4 + parts)
    get_pb = fetch(pb_h.at[:, pl.ds(0, pb_v.shape[1])], pb_v, 1)

    get_x.wait()
    get_ow.wait()
    piece = ow_v.shape[1] // parts
    resid = x_v[...].astype(F32)
    for d in range(parts):
        get_att[d].wait()
        at = ow_order.index(d) * piece
        resid = resid + dot(att_v[d], ow_v[:, at : at + piece].reshape(local, width))
    if own:
        ffn_v[...] = resid
        store(ffn_v, outs[6], 4)
    normed = (resid * rms(resid) * gain_ref[1:2, :]).astype(BF16)
    left_v[0] = normed
    position = lax.broadcasted_iota(jnp.int32, (rows, 1), 0) + row0
    row_weight = jnp.where(position < len_ref[0], weight_ref[0], 0.0)
    get_cot.wait()
    left_v[1] = (cot_v[...].astype(F32) * row_weight).astype(BF16)
    store(left_v, outs[0], 0)
    for shard in range(2):
        cols = slice(shard * hidden_units, (shard + 1) * hidden_units)
        if shard == 0:
            get_gu.wait()
            get_dw.wait()
            gate_w, up_w, down_w = gu_v[0], gu_v[1], dw_v[...]
        else:
            get_pb.wait()
            gate_w, up_w, down_w = (
                pb_v[:, c * part : (c + 1) * part, :].reshape(width, hidden_units) for c in range(3)
            )
        gate = dot(left_v[0], gate_w)
        upper = dot(left_v[0], up_w)
        grad_hidden = dot(left_v[1], down_w, NT if shard == 0 else NN)
        sigma = 0.5 + 0.5 * jnp.tanh(0.5 * gate)
        act = gate * sigma
        hidden = (act * upper).astype(BF16)
        grad_up = (grad_hidden * act).astype(BF16)
        grad_gate = (grad_hidden * upper * (sigma + act * (1.0 - sigma))).astype(BF16)
        act_v[0, :, cols] = grad_gate
        act_v[1, :, cols] = grad_up
        act_v[2, :, cols] = hidden
        store(act_v.at[:, :, cols], outs[1].at[:, :, cols], 1 + 4 * shard)
        grad = dot(grad_gate, gate_w, NT) + dot(grad_up, up_w, NT)
        term = dot(hidden, down_w, NN if shard == 0 else NT)
        if shard == 0:
            gn2_v[...] = grad
            if own:
                pending.pop(0).wait()
            ffn_v[...] = term
        else:
            low_v[0] = (gn2_v[...] + grad).astype(BF16)
            store(low_v.at[0], outs[2], 2)
            low_v[1] = (ffn_v[...] + term).astype(BF16)
            row = 0
            for n in range(3):
                size = outs[3 + n].shape[0]
                store(low_v.at[1, pl.ds(row, size)], outs[3 + n], (3, 6, 7)[n])
                row += size
    for copy in pending:
        copy.wait()


def feed_forward(slot, index, lengths, picked, atts, tokens, cotangent, out_full, gate_up, down, partner, gains):
    parts = len(atts)
    rows, local = atts[0].shape
    width = tokens.shape[1]
    hidden = gate_up.shape[2]
    out_rows, ow_row, ow_order = out_full
    shares = partner.shape[0]
    part = width // shares
    anywhere = pl.BlockSpec(memory_space=pl.ANY)
    out_shape = [
        sds((2, rows, width), BF16), sds((3, rows, 2 * hidden), BF16),
        sds((rows, width), BF16),
    ]
    out_shape += [sds((rows * n // 16, width), BF16) for n in (2, 11, 3)]
    if slot == 0:
        out_shape.append(sds((rows, width), F32))
    return call(
        functools.partial(ffn_kernel, parts, ow_row, ow_order, slot),
        (1,),
        [smem(), smem(), whole(gains.shape)] + [anywhere] * (6 + parts),
        [anywhere] * len(out_shape),
        out_shape,
        scratch=[
            pltpu.VMEM((rows, width), BF16),
            pltpu.VMEM((rows, width), BF16),
            pltpu.VMEM((parts, rows, local), BF16),
            pltpu.VMEM((shares, parts * local // shares, width), BF16),
            pltpu.VMEM(gate_up.shape, BF16),
            pltpu.VMEM(down.shape, BF16),
            pltpu.VMEM((shares, 3 * part, hidden), BF16),
            pltpu.VMEM((2, rows, width), BF16),
            pltpu.VMEM((3, rows, 2 * hidden), BF16),
            pltpu.VMEM((rows, width), F32),
            pltpu.VMEM((rows, width), F32),
            pltpu.VMEM((2, rows, width), BF16),
            pltpu.SemaphoreType.DMA((7 + parts,)),
            pltpu.SemaphoreType.DMA((8,)),
        ],
        prefetch=1,
    )(index, lengths, picked, gains, tokens, cotangent, gate_up, down, partner, out_rows, *atts)


def ffn_grad_kernel(sets, split, extra, cuts, idx_ref, *refs):
    left = refs[:sets]
    act = refs[sets : 2 * sets]
    refs = refs[2 * sets :]
    count = 2 if extra else 0
    op, folds, outs = refs[:count], refs[count : count + 2 * len(cuts)], refs[count + 2 * len(cuts) :]
    if cuts:
        fold_kernel(cuts, idx_ref, *folds, *outs[1:])
        outs = outs[:1]
    step = pl.program_id(0)

    def write(total):
        part = outs[0].shape[-2]
        if not split:
            for j in range(outs[0].shape[0]):
                outs[0][j] = total[j * part : (j + 1) * part, :].astype(BF16)
            return
        for keep in range(2):
            for bit in range(2):

                @pl.when((idx_ref[1] & 1) == bit)
                def _():
                    for j in range(outs[0].shape[0]):
                        d = 2 * j + (bit if keep else 1 - bit)
                        outs[keep][j] = total[d * part : (d + 1) * part, :].astype(BF16)

    @pl.when(step < 3)
    def _():
        total = dot(left[0][0], act[0][0], TN)
        for e in range(1, sets):
            total = total + dot(left[e][0], act[e][0], TN)
        write(total)

    if extra:

        @pl.when(step >= 3)
        def _():
            write(dot(op[0][...], op[1][...], TN))


def ffn_grads(index, lefts, acts, shard, shares, split, grad_low=None, att_own=None, lanes=()):
    sets = len(lefts)
    _, rows, width = lefts[0].shape
    hidden = acts[0].shape[2] // 2
    part = width // shares
    extra = 0 if grad_low is None else att_own.shape[1] // hidden
    steps = 3 + extra
    specs = [pl.BlockSpec((1, rows, width), lambda c, idx: (jnp.minimum(c // 2, 1), 0, 0))] * sets
    specs += [pl.BlockSpec((1, rows, hidden), lambda c, idx: (jnp.minimum(c, 2), 0, shard))] * sets
    args = list(lefts) + list(acts)
    if extra:
        specs += [
            pl.BlockSpec(grad_low.shape, lambda c, idx: (0, 0)),
            pl.BlockSpec((att_own.shape[0], hidden), lambda c, idx: (0, jnp.maximum(c - 3, 0))),
        ]
        args += [grad_low, att_own]
    count = shares // 2 if split else shares
    outs = 2 if split else 1
    out_specs = [pl.BlockSpec((count, part, hidden), lambda c, idx: (0, c, 0))] * outs
    out_shape = [sds((count, steps * part, hidden), BF16)] * outs
    cuts, info = [], []
    for n, (keep, got, lead, order) in enumerate(lanes):
        size, lane_rows, cols = keep.shape
        lane_rows //= len(lanes)
        block = lane_rows // 4 if lane_rows % 64 == 0 else lane_rows
        last = lane_rows // block - 1
        at = functools.partial(lambda n, last, c, idx: (0, n * (last + 1) + jnp.minimum(c, last), 0), n, last)
        here = functools.partial(lambda last, c, idx: (0, jnp.minimum(c, last), 0), last)
        specs += [pl.BlockSpec((size, block, cols), at)] * 2
        args += [keep, got]
        bit = order[0]
        cuts.append((len(lead) - 1 - lead.index(bit), bit))
        info.append(([b for b in lead if b != bit], order[1:], bit))
        out_specs += [pl.BlockSpec((size // 2, block, cols), here)] * 2
        out_shape += [sds((size // 2, lane_rows, cols), BF16)] * 2
    res = call(
        functools.partial(ffn_grad_kernel, sets, split, extra, cuts),
        (steps,),
        specs,
        out_specs,
        out_shape,
        prefetch=1,
    )(index, *args)
    if not lanes:
        return res
    return res[0], [(res[1 + 2 * n], res[2 + 2 * n]) + info[n] for n in range(len(lanes))]


def resid_kernel(ow_order, members, idx_ref, len_ref, weight_ref, cot_ref, resid_ref, ow_ref, gain_ref, *refs):
    parts = len(ow_order)
    gn2_refs = refs[:members]
    att_refs = refs[members : members + parts]
    gr_ref, low_ref, cat_ref, sum_ref = refs[members + parts : members + parts + 4]
    g_refs = refs[members + parts + 4 :]
    rows, width = cot_ref.shape
    local = att_refs[0].shape[1]
    step = pl.program_id(0)
    first = (idx_ref[0] * pl.num_programs(0) + step) * rows
    slot = lax.broadcasted_iota(jnp.int32, (rows, 1), 0) + first
    row_weight = jnp.where(slot < len_ref[0], weight_ref[0], 0.0)
    gn2 = gn2_refs[0][...].astype(F32)
    for ref in gn2_refs[1:]:
        gn2 = gn2 + ref[...].astype(F32)
    resid = resid_ref[...]
    factor = rms(resid)
    unit = resid * factor
    grad = cot_ref[...].astype(F32) * row_weight + norm_back(gn2, gain_ref[1:2, :], unit, factor)
    gr_ref[...] = grad
    low = grad.astype(BF16)
    low_ref[...] = low

    @pl.when(step == 0)
    def _():
        sum_ref[...] = jnp.zeros_like(sum_ref)

    sum_ref[...] += jnp.sum((gn2 * unit).reshape(rows // 8, 8, width), axis=0)
    for d in range(parts):
        piece = ow_ref.shape[1] // parts
        at = ow_order.index(d) * piece
        block = ow_ref[:, at : at + piece].reshape(local, width)
        g_refs[d][...] = dot(low, block, NT).astype(BF16)
        cat_ref[:, d * local : (d + 1) * local] = att_refs[d][...]


def resid_back(index, lengths, picked, cotangent, resid, gn2s, out_full, gains, atts, block=256):
    share, width = resid.shape
    parts, members = len(atts), len(gn2s)
    local = atts[0].shape[1]
    out_rows, ow_row, ow_order = out_full
    ow_rows = parts * local // out_rows.shape[0]
    steps = share // block
    row = lambda n: pl.BlockSpec((block, n), lambda i, idx: (i, 0))
    return call(
        functools.partial(resid_kernel, ow_order, members),
        (steps,),
        [
            smem(), smem(),
            pl.BlockSpec((block, width), lambda i, idx: (idx[0] * steps + i, 0)),
            row(width),
            pl.BlockSpec((out_rows.shape[0], ow_rows, width), lambda *_: (0, ow_row // ow_rows, 0), pipeline_mode=pl.Buffered(1)),
            whole(gains.shape),
        ]
        + [row(width)] * members
        + [row(local)] * parts,
        [row(width), row(width), row(parts * local), whole((8, width))] + [row(local)] * parts,
        [sds((share, width), F32), sds((share, width), BF16), sds((share, parts * local), BF16), sds((8, width), F32)]
        + [sds((share, local), BF16)] * parts,
        prefetch=1,
    )(index, lengths, picked, cotangent, resid, out_rows, gains, *gn2s, *atts)


def attend_back_kernel(parts, idx_ref, q_ref, k_ref, v_ref, att_ref, cos_ref, sin_ref, *refs):
    grad_refs = refs[:parts]
    outs = refs[parts : 2 * parts]
    dk_acc, dv_acc = refs[2 * parts :]
    rows = q_ref.shape[1]
    step = pl.program_id(0)
    me = idx_ref[0]
    lane = lax.broadcasted_iota(jnp.int32, (rows, 128), 1)

    def table(ref, d):
        return ref[pl.ds(pl.multiple_of((me ^ d) * rows, rows), rows), :]

    def columns(ref, d):
        return ref[:, pl.ds(pl.multiple_of((me ^ d) * rows, rows), rows)].T

    def back(v, d, scale):
        return ((v * table(cos_ref, d) - swap_halves(v) * table(sin_ref, d)) * scale).astype(BF16)

    @pl.when(step == 0)
    def _():
        dk_acc[...] = jnp.zeros_like(dk_acc)
        dv_acc[...] = jnp.zeros_like(dv_acc)

    grad = grad_refs[0][...]
    for d in range(1, parts):
        grad = jnp.where(step == d, grad_refs[d][...], grad)
    prod = grad.astype(F32) * att_ref[...].astype(F32)
    zero = jnp.zeros((rows, 128), BF16)
    dqs, probs_all, scores_all, grads_own, queries_own = [], [], [], [], []
    for s in range(2):
        first = HD * (1 - s)
        own = (lane >= HD * s) & (lane < HD * (s + 1))
        delta = jnp.sum(jnp.where(own, prod, 0.0), axis=1, keepdims=True)
        hi, mid, low = split3(-delta)
        grad_own = jnp.where(own, grad, zero)
        grad_aug = jnp.where(lane == first + 2, low, grad_own)
        grad_aug = jnp.where(lane == first + 1, mid, grad_aug)
        grad_aug = jnp.where(lane == first, hi, grad_aug)
        q = q_ref[s]
        probs = jnp.exp2(dot(q, k_ref[s], NT))
        scores_grad = (probs * dot(grad_aug, v_ref[s], NT)).astype(BF16)
        probs_all.append(probs.astype(BF16))
        scores_all.append(scores_grad)
        grads_own.append(grad_own)
        queries_own.append(jnp.where(own, q, zero))
        dqs.append(dot(scores_grad, k_ref[s]))
    dv_acc[...] += dot(jnp.concatenate(grads_own, axis=0).T, jnp.concatenate(probs_all, axis=0))
    dk_acc[...] += dot(jnp.concatenate(queries_own, axis=0).T, jnp.concatenate(scores_all, axis=0))
    dq = jnp.where(lane < HD, dqs[0], dqs[1])
    for d in range(parts):

        @pl.when(step == d)
        def _():
            outs[d][0] = back(dq, d, FACTOR)

    @pl.when(step == parts - 1)
    def _():
        for d in range(parts):
            outs[d][1] = back(columns(dk_acc, d), d, LN2)
            outs[d][2] = columns(dv_acc, d).astype(BF16)


def attend_back(index, grads, q, k, v, att, cosine, sine, pair):
    parts = len(grads)
    share = grads[0].shape[0]
    rows = q.shape[1]
    keys = pl.BlockSpec((2, rows, 128), lambda i, idx: (pair, 0, 0), pipeline_mode=pl.Buffered(1))
    return call(
        functools.partial(attend_back_kernel, parts),
        (parts,),
        [
            pl.BlockSpec((2, share, 128), lambda i, idx: (pair, idx[0] ^ i, 0)),
            keys,
            keys,
            pl.BlockSpec((share, 128), lambda i, idx: (idx[0] ^ i, pair)),
            whole(cosine.shape),
            whole(sine.shape),
        ]
        + [pl.BlockSpec((share, 128), lambda i, idx: (0, pair))] * parts,
        [whole((3, share, 128))] * parts,
        [sds((3, share, 128), BF16)] * parts,
        scratch=[pltpu.VMEM((128, rows), F32)] * 2,
        flops=2 * rows * rows * 128 * 10,
        nbytes=rows * 256 * 16,
        trans=2 * rows * rows,
        prefetch=1,
    )(index, q, k, v, att, cosine, sine, *grads)


def project_grad_kernel(parts, pairs, idx_ref, n_ref, w_ref, *refs):
    act_refs = refs[: parts * pairs]
    away_ref, keep_ref, sum_ref = refs[parts * pairs :]
    share = act_refs[0].shape[1]
    me = idx_ref[0]
    total = None
    for d in range(parts):
        rows = n_ref[pl.ds(pl.multiple_of((me ^ d) * share, share), share), :]
        act = jnp.concatenate([act_refs[j * parts + d][0] for j in range(pairs)], axis=1)
        term = dot(rows, act, TN)
        total = term if total is None else total + term
    count, part, _ = keep_ref.shape
    for bit in range(2):

        @pl.when((idx_ref[1] & 1) == bit)
        def _():
            for j in range(count):
                keep, away = 2 * j + bit, 2 * j + 1 - bit
                keep_ref[j] = total[keep * part : (keep + 1) * part, :].astype(BF16)
                away_ref[j] = total[away * part : (away + 1) * part, :].astype(BF16)

    gain_sum = jnp.sum(total * w_ref[0].astype(F32), axis=1, keepdims=True)

    @pl.when(pl.program_id(0) == 0)
    def _():
        sum_ref[...] = jnp.broadcast_to(gain_sum, sum_ref.shape)

    @pl.when(pl.program_id(0) > 0)
    def _():
        sum_ref[...] += jnp.broadcast_to(gain_sum, sum_ref.shape)


def project_grads(index, normed, acts, qkv_weight, shares):
    width = normed.shape[1]
    local = qkv_weight.shape[2]
    pairs, parts = len(acts), len(acts[0])
    share = acts[0][0].shape[1]
    flat = [a for group in acts for a in group]
    half = (shares // 2, width // shares, 3 * local)
    out = pl.BlockSpec(half[:2] + (local,), lambda c, idx: (0, 0, c))
    return call(
        functools.partial(project_grad_kernel, parts, pairs),
        (3,),
        [whole(normed.shape), pl.BlockSpec((1, width, local), lambda c, idx: (c, 0, 0))]
        + [pl.BlockSpec((1, share, 128), lambda c, idx: (c, 0, 0))] * len(flat),
        [out, out, whole((width, 128))],
        [sds(half, BF16), sds(half, BF16), sds((width, 128), F32)],
        prefetch=1,
    )(index, normed, qkv_weight, *flat)


def token_grad_kernel(order, pairs, idx_ref, x_ref, gr_ref, w_ref, gain_ref, own_ref, got_ref, *refs):
    parts = len(order)
    act_refs = refs[: parts * pairs]
    out_ref, gu_ref, down_ref = refs[parts * pairs :]
    width = x_ref.shape[1]
    local = 128 * pairs
    grad = jnp.zeros(x_ref.shape, F32)
    for d in range(parts):
        for c in range(3):
            act = jnp.concatenate([act_refs[j * parts + d][c] for j in range(pairs)], axis=1)
            grad = grad + dot(act, w_ref[:, order.index(d), c].reshape(width, local), NT)
    x = x_ref[...].astype(F32)
    factor = rms(x)
    out_ref[...] = gr_ref[...] + norm_back(grad, gain_ref[0:1, :], x * factor, factor)

    @pl.when(pl.program_id(0) == 0)
    def _():
        part = gu_ref.shape[1]
        total = own_ref[: 3 * part, :].astype(F32) + got_ref[...].astype(F32)
        gu_ref[0] = total[:part]
        gu_ref[1] = total[part : 2 * part]
        down_ref[...] = total[2 * part :].T


def token_grad(index, tokens, grad_resid, qkv_full, order, gains, acts, ffn_own, ffn_got, block=256):
    share, width = grad_resid.shape
    pairs, parts = len(acts), len(acts[0])
    part, hidden = ffn_got.shape[0] // 3, ffn_got.shape[1]
    flat = [a for group in acts for a in group]
    steps = share // block
    return call(
        functools.partial(token_grad_kernel, order, pairs),
        (steps,),
        [
            pl.BlockSpec((block, width), lambda i, idx: (idx[0] * steps + i, 0)),
            pl.BlockSpec((block, width), lambda i, idx: (i, 0)),
            whole(qkv_full.shape),
            whole(gains.shape),
            whole(ffn_own.shape),
            whole(ffn_got.shape),
        ]
        + [pl.BlockSpec((3, block, 128), lambda i, idx: (0, i, 0))] * len(flat),
        [pl.BlockSpec((block, width), lambda i, idx: (i, 0)), whole((2, part, hidden)), whole((hidden, part))],
        [sds((share, width), F32), sds((2, part, hidden), F32), sds((hidden, part), F32)],
        prefetch=1,
    )(index, tokens, grad_resid, qkv_full, gains, ffn_own, ffn_got, *flat)


def fold_kernel(cuts, idx_ref, *refs):
    ins, outs = list(refs[: 2 * len(cuts)]), list(refs[2 * len(cuts) :])
    row = 0
    for at in cuts:
        keep, got = ins.pop(0), ins.pop(0)
        if at is None:
            rows = keep.shape[1]
            outs[0][row : row + rows, :] = (keep[0].astype(F32) + got[0].astype(F32)).astype(BF16)
            row += rows
            continue
        place, bit = at
        mine = (idx_ref[1] >> bit) & 1
        targets = ((outs.pop(0), mine), (outs.pop(0), 1 - mine))
        for j in range(keep.shape[0] // 2):
            rest = ((j >> place) << (place + 1)) | (j & ((1 << place) - 1))
            for out, value in targets:
                k = rest | (value << place)
                out[j] = (keep[k].astype(F32) + got[k].astype(F32)).astype(BF16)


def fold(index, lanes, cut_rows=False):
    cuts, specs, args, out_shape, info, total = [], [], [], [], [], 0
    for n, (keep, got, lead, order) in enumerate(lanes):
        count, rows, cols = keep.shape
        rows = rows // len(lanes) if cut_rows else rows
        at = functools.partial(lambda n, i, idx: (0, n, 0), n if cut_rows else 0)
        specs += [pl.BlockSpec((count, rows, cols), at)] * 2
        args += [keep, got]
        total += rows
        if order:
            bit = order[0]
            cuts.append((len(lead) - 1 - lead.index(bit), bit))
            info.append(([b for b in lead if b != bit], order[1:], bit))
            out_shape += [sds((count // 2, rows, cols), BF16)] * 2
        else:
            cuts.append(None)
    if not info:
        out_shape = [sds((total, cols), BF16)]
    res = call(
        functools.partial(fold_kernel, cuts), (1,), specs, [whole(o.shape) for o in out_shape], out_shape, prefetch=1
    )(index, *args)
    if not info:
        return res[0]
    return [(res[2 * n], res[2 * n + 1]) + info[n] for n in range(len(lanes))]


def pieces_kernel(first, part, op_ref, gains_ref, *outs):
    local = outs[0].shape[1]
    hidden = op_ref.shape[1]
    rows = (outs[0].shape[0] - part) // 3
    gains = gains_ref[...]
    wide = gains.shape[1] // local
    flat = jnp.concatenate(
        [gains[r // wide : r // wide + 1, (r % wide) * local : (r % wide + 1) * local] for r in range(rows)]
    )
    parts3 = jnp.concatenate(split3(flat))
    for d, out in enumerate(outs):
        block = d * local // hidden
        col = d * local % hidden
        row = first + block * part
        out[:part, :] = op_ref[row : row + part, col : col + local]
        out[part:, :] = parts3


def make_pieces(sum_a, gains, first, part, local, parts):
    shape = (part + 3 * gains.size // local, local)
    return call(
        functools.partial(pieces_kernel, first, part),
        (1,),
        [whole(sum_a.shape), whole(gains.shape)],
        [whole(shape)] * parts,
        [sds(shape, BF16)] * parts,
    )(sum_a, gains)


def finish_kernel(count, parts, resid_ref, keep_ref, got_ref, *refs):
    own, others, refs = refs[:3], refs[3 : 3 + 3 * count], refs[3 + 3 * count :]
    pieces, (out_ref, qkv_ref, op_ref, gains_ref) = refs[:parts], refs[parts:]
    row = 0
    for n in range(3):
        rows = own[n].shape[0]
        total = resid_ref[row : row + rows, :] + own[n][...].astype(F32)
        for e in range(count):
            total = total + others[n * count + e][...].astype(F32)
        out_ref[row : row + rows, :] = total
        row += rows
    local = qkv_ref.shape[2]
    qkv = keep_ref[0].astype(F32) + got_ref[0].astype(F32)
    for c in range(3):
        qkv_ref[c] = qkv[:, c * local : (c + 1) * local]
    part = op_ref.shape[1]
    rows = (pieces[0].shape[0] - part) // 3

    def gains_of(ref):
        hi, mid, low = (ref[part + n * rows : part + (n + 1) * rows, :].astype(F32) for n in range(3))
        return hi + mid + low

    ops = [ref[:part, :].astype(F32) for ref in pieces]
    gains = [gains_of(ref) for ref in pieces]
    while len(ops) > 1:
        ops = [ops[2 * n] + ops[2 * n + 1] for n in range(len(ops) // 2)]
        gains = [gains[2 * n] + gains[2 * n + 1] for n in range(len(gains) // 2)]
    op_ref[...] = ops[0].T
    wide = gains_ref.shape[1] // local
    for r in range(rows):
        gains_ref[r // wide : r // wide + 1, (r % wide) * local : (r % wide + 1) * local] = gains[0][r : r + 1, :]


def finish_outputs(resid, own, others, keep, got, pieces):
    parts, count = len(pieces), len(others[0])
    width = resid.shape[1]
    part, local = keep.shape[1], keep.shape[2] // 3
    args = [resid, keep, got, *own, *[a for group in others for a in group], *pieces]
    shapes = [resid.shape, (3, part, local), (local, part), (2, width)]
    return call(
        functools.partial(finish_kernel, count, parts),
        (1,),
        [whole(a.shape) for a in args],
        [whole(shape) for shape in shapes],
        [sds(shape, F32) for shape in shapes],
    )(*args)


def after(value, *others):
    return lax.optimization_barrier((value, *others))[0]


def body(
    tokens, qkv_weight, out_weight, gate_up_weight, down_weight, norm_gains,
    species_weight, species_ids, lengths, cotangent,
):
    rows, width = tokens.shape
    local = out_weight.shape[0]
    hidden = down_weight.shape[0]
    parts = lax.axis_size("tensor")
    slots = list(range(parts - 2, -1, -2))
    shares = lax.axis_size("dp")
    part = width // shares
    me = lax.axis_index("tensor")
    dp = lax.axis_index("dp")
    index = jnp.stack([me, dp]).astype(jnp.int32)
    cosine, sine = (jnp.asarray(t) for t in rotary_tables())
    pairs = local // 128
    valid = lengths[0] >= 0

    def region(f):
        shapes = jax.eval_shape(f)
        zeros = lambda: jax.tree.map(lambda a: jnp.zeros(a.shape, a.dtype), shapes)
        return lax.optimization_barrier(lax.cond(valid, f, zeros))

    def beside(sends, f, apart=False):
        return region(lambda: ([swap(*x) for x in sends], region(f) if apart else f()))

    def swap(a, d, name="tensor"):
        return lax.ppermute(a, name, [(i, i ^ d) for i in range(lax.axis_size(name))])

    def cut(a, start, size, axis=0):
        return lax.dynamic_slice_in_dim(a, start, size, axis)

    def outgoing(pieces):
        return [(pieces[d], d, "tensor") for d in range(1, parts)]

    bits = shares.bit_length() - 1
    lead = list(range(bits - 1, 0, -1))

    def fold_first(keep, got):
        return fold(index, [(keep, got, lead, lead), (keep, got, lead, lead[::-1])], cut_rows=True)

    def fold_next(halves, got):
        return fold(index, [(keep, g, left, order) for (keep, _, left, order, _), g in zip(halves, got)])

    def leaving(halves):
        return [(away, 1 << bit, "dp") for _, away, _, _, bit in halves]

    matches = species_ids[:, None] == jnp.arange(species_weight.shape[0])[None, :]
    picked = jnp.sum(jnp.where(matches, species_weight[None, :], F32(0.0)), axis=1)

    ow_cut = cut(out_weight, dp * (local // shares), local // shares)
    qkv_cut = cut(qkv_weight, dp * part, part, 1).reshape(3 * part, local)
    top = parts // 2
    together = hidden == width
    mine = cut_weights(index[1:], gate_up_weight, down_weight, shares, [ow_cut] if together else [])
    sends = [(ow_cut, d, "tensor") for d in range(2 if together else 1, parts)]

    (partner_cut, *ow), (q, k, v, normed) = beside(
        [(mine, 1, "tensor")] + sends,
        lambda: project(lengths, tokens, qkv_weight, norm_gains, cosine, sine),
    )
    if together:
        partner = lax.all_gather(pack([partner_cut, ow_cut, *ow]), "dp", axis=0)
        out_full = (partner, 3 * part, [1, 0] + list(range(2, parts)))
    else:
        partner = lax.all_gather(partner_cut, "dp", axis=0)
        out_full = (lax.all_gather(pack([ow_cut, *ow]), "dp", axis=0), 0, list(range(parts)))

    (qkv_got,), (*att, att_nat, q_back) = beside(
        [(after(qkv_cut, partner_cut), top, "tensor")], lambda: attend(index, q, k, v, parts)
    )
    qkv_stack, order = pack([qkv_cut, qkv_got]), [0, top]
    rows_for = lambda e: outgoing([att[d ^ e] for d in range(parts)])
    rows_now = region(lambda: [swap(*x) for x in rows_for(slots[0])])

    lefts, acts, gn2s, terms, gn2_got = {}, {}, {}, {}, {}
    tied = tokens
    for e in slots:

        def feed():
            outs = feed_forward(
                e, index, lengths, picked, [att[e]] + rows_now, tied, cotangent, out_full,
                gate_up_weight, down_weight, partner, norm_gains
            )
            if e:
                return outs
            away_b, keep_b = ffn_grads(
                index, [*lefts.values(), outs[0]], [*acts.values(), outs[1]], 1, shares, True
            )
            return outs, keep_b, away_b

        sends = rows_for(e - 2) if e else []
        if e + 2 in gn2s:
            sends.append((gn2s[e + 2], e + 2, "tensor"))
        if len(order) < parts:
            bit = parts // (2 * len(order))
            sends.append((qkv_stack, bit, "tensor"))
        got, outs = beside(sends, feed)
        if len(order) < parts:
            qkv_stack, order = pack([qkv_stack, got.pop()]), order + [d ^ bit for d in order]
            if len(order) == parts:
                qkv_stack = qkv_stack.reshape(parts, 3, part, local)
                qkv_full = lax.all_gather(qkv_stack, "dp", axis=0)
        if e + 2 in gn2s:
            gn2_got[e + 2] = got.pop()
        if e:
            rows_now = got
        else:
            outs, keep_b, away_b = outs
        lefts[e], acts[e], gn2s[e], *terms[e] = outs[:6]
        tied = after(tokens, gn2s[e])
    resid = outs[6]
    gn2_all = [gn2s[0]] + [gn2_got[e] for e in slots[:-1]]

    def terms_out(i):
        return [(terms[e][i], e, "tensor") for e in slots[:-1]]

    terms_got = []
    (got_b, *got), (grad_resid, grad_low, att_own, gain_two, *grads) = beside(
        [(away_b, 1, "dp")] + terms_out(0),
        lambda: resid_back(
            index, lengths, picked, cotangent, resid, gn2_all, out_full, norm_gains, [att[0]] + rows_now
        ),
    )
    lefts, acts = [lefts[e] for e in slots], [acts[e] for e in slots]
    terms_got.append(got)
    start = [(keep_b, got_b, lead, lead), (keep_b, got_b, lead, lead[::-1])]
    ways = []

    def grads_own():
        wg_a, halves = ffn_grads(index, lefts, acts, 0, shares, False, grad_low, att_own, start)
        ways[:] = [h[2:] for h in halves]
        return wg_a, [h[:2] for h in halves]

    got, (wg_a, halves) = beside(outgoing(grads), grads_own)
    halves = [tuple(h) + way for h, way in zip(halves, ways)]
    grads_all = [grads[0]] + got
    sum_a = lax.psum_scatter(after(wg_a, qkv_full), "dp", scatter_dimension=0, tiled=True)[0]
    step = 0

    def back(j):
        return attend_back(index, grads_all, q_back, k, v, att_nat, cosine, sine, j)

    got, group = beside(terms_out(1) + leaving(halves), lambda: back(0))
    terms_got.append(got[: len(slots) - 1])
    got = got[len(slots) - 1 :]
    halves, step = fold_next(halves, got), step + 1
    qkv_acts, acts_got = [group], []
    for j in range(1, pairs):
        now = leaving(halves) if step < bits - 1 else []
        got, group = beside(outgoing(group) + now, lambda: back(j))
        acts_got.append([qkv_acts[-1][0]] + got[: parts - 1])
        qkv_acts.append(group)
        if now:
            halves, step = fold_next(halves, got[parts - 1 :]), step + 1
    while step < bits - 1:
        halves, step = fold_next(halves, [swap(*x) for x in leaving(halves)]), step + 1
    sum_b = halves

    def finish():
        away_q, keep_q, gain_one = project_grads(index, normed, qkv_acts, qkv_weight, shares)
        halves = fold(index, [(keep_q, swap(away_q, 1, "dp"), lead, lead)])
        for s in range(bits - 2):
            halves = fold_next(halves, [swap(*x) for x in leaving(halves)])
        gains_grad = jnp.stack([gain_one[:, 0] / norm_gains[0], jnp.sum(gain_two, axis=0)])
        gains_grad = after(gains_grad, *[h[0] for h in halves])
        for s in range(bits):
            gains_grad = gains_grad + swap(gains_grad, 1 << s, "dp")
        ways[:] = [h[2:] for h in halves]
        return [h[:2] for h in halves], gains_grad

    got, (halves, gains_grad) = beside(outgoing(group) + [(sum_b, 1, "tensor")], finish, apart=True)
    halves = [tuple(h) + way for h, way in zip(halves, ways)]
    acts_got.append([group[0]] + got[: parts - 1])
    got_b = got[-1]
    pieces = make_pieces(sum_a, gains_grad, 3 * part, part, local, parts)
    got, (grad_tok, grad_gu, grad_down) = beside(
        leaving(halves) + terms_out(2) + outgoing(pieces),
        lambda: token_grad(index, tokens, grad_resid, qkv_full, order, norm_gains, acts_got, sum_a, got_b),
    )
    terms_got.append(got[1 : len(slots)])
    out, grad_qkv, grad_op, gains_grad = finish_outputs(
        resid, terms[0], terms_got, halves[0][0], got[0], [pieces[0]] + got[len(slots) :]
    )
    return (out, grad_tok, grad_qkv, grad_op, grad_gu, grad_down, gains_grad)


def solution(mesh):
    in_specs = (
        P("dp", None),
        P(None, None, "tensor"),
        P("tensor", None),
        P(None, None, "tensor"),
        P("tensor", None),
        P(),
        P(),
        P("dp"),
        P("dp"),
        P("dp", None),
    )
    out_specs = (
        P(("dp", "tensor"), None),
        P(("dp", "tensor"), None),
        P(None, "dp", "tensor"),
        P("tensor", "dp"),
        P(None, "dp", "tensor"),
        P("tensor", "dp"),
        P(),
    )
    return jax.shard_map(body, mesh=mesh, in_specs=in_specs, out_specs=out_specs, check_vma=False)
```

```python
import functools
import math

import jax
import jax.numpy as jnp
import numpy as np
from jax import lax
from jax.experimental import pallas as pl
from jax.experimental.pallas import tpu as pltpu
from jax.sharding import PartitionSpec as P

HD = 64
WIN = 2048
EPSILON = 1e-05
NEG_FILL = -1e30
LOG2E = math.log2(math.e)
LN2 = math.log(2.0)
FACTOR = HD ** (-0.5)
VMEM = 60 * 2**20
F32 = jnp.float32
BF16 = jnp.bfloat16

NN = (((1,), (0,)), ((), ()))
NT = (((1,), (1,)), ((), ()))
TN = (((0,), (0,)), ((), ()))


def dot(a, b, dims=NN):
    return lax.dot_general(a, b, dims, preferred_element_type=F32)


def call(kernel, grid, in_specs, out_specs, out_shape, scratch=(), flops=0, nbytes=0, trans=0, prefetch=0):
    return pl.pallas_call(
        kernel,
        grid_spec=pltpu.PrefetchScalarGridSpec(
            num_scalar_prefetch=prefetch,
            grid=grid,
            in_specs=in_specs,
            out_specs=out_specs,
            scratch_shapes=list(scratch),
        ),
        out_shape=out_shape,
        compiler_params=pltpu.CompilerParams(vmem_limit_bytes=VMEM),
        cost_estimate=pl.CostEstimate(flops=flops, bytes_accessed=nbytes, transcendentals=trans),
    )


def whole(shape):
    return pl.BlockSpec(shape, lambda *_: (0,) * len(shape), pipeline_mode=pl.Buffered(1))


def staged(body, index, smalls, ins, outs, stores, scratch=()):
    n_small, n_in, n_out = len(smalls), len(ins), len(outs)

    def kernel(idx_ref, *refs):
        refs = list(refs)
        take = lambda n: [refs.pop(0) for _ in range(n)]
        small, far_in, far_out = take(n_small), take(n_in), take(n_out)
        near_in, near_out, extra = take(n_in), take(n_out), take(len(scratch))
        sem_in, sem_out = refs
        copies = []
        for n, (_, _, pick) in enumerate(ins):
            part = pick(idx_ref, far_in[n]) if pick else far_in[n]
            copies.append(pltpu.make_async_copy(part, near_in[n], sem_in.at[n]))
            copies[n].start()
        there, sent = set(), []

        def get(n):
            if n not in there:
                copies[n].wait()
                there.add(n)
            return near_in[n]

        def put(n, part=None):
            src, dst = near_out[n], far_out[n]
            if part is not None:
                src, dst = src.at[part], dst.at[part]
            copy = pltpu.make_async_copy(src, dst, sem_out.at[len(sent)])
            copy.start()
            sent.append(copy)

        body(idx_ref, small, get, near_out, put, extra)
        for n in range(n_in):
            get(n)
        for copy in sent:
            copy.wait()

    anywhere = pl.BlockSpec(memory_space=pl.ANY)
    specs = [smem() if a.ndim == 1 else whole(a.shape) for a in smalls]
    return call(
        kernel,
        (1,),
        specs + [anywhere] * n_in,
        [anywhere] * n_out,
        [sds(shape, dtype) for shape, dtype in outs],
        scratch=[pltpu.VMEM(shape, a.dtype) for a, shape, _ in ins]
        + [pltpu.VMEM(shape, dtype) for shape, dtype in outs]
        + list(scratch)
        + [pltpu.SemaphoreType.DMA((n_in,)), pltpu.SemaphoreType.DMA((stores,))],
        prefetch=1,
    )(index, *smalls, *[a for a, _, _ in ins])


def smem():
    return pl.BlockSpec(memory_space=pltpu.SMEM)


def sds(shape, dtype):
    return jax.ShapeDtypeStruct(shape, dtype)


def rotary_tables():
    position = np.arange(WIN, dtype=np.float64)
    frequency = 10000.0 ** (-2.0 * np.arange(HD // 2, dtype=np.float64) / HD)
    angles = position[:, None] * frequency[None, :]
    cosine = np.cos(angles)
    sine = np.sin(angles)
    cos_full = np.tile(np.concatenate([cosine, cosine], axis=1), (1, 2))
    sin_full = np.tile(np.concatenate([-sine, sine], axis=1), (1, 2))
    return cos_full.astype(np.float32), sin_full.astype(np.float32)


def swap_halves(v):
    lane = lax.broadcasted_iota(jnp.int32, v.shape, 1)
    return jnp.where(lane % HD < HD // 2, pltpu.roll(v, 96, 1), pltpu.roll(v, 32, 1))


def rms(x):
    return lax.rsqrt(jnp.mean(x * x, axis=-1, keepdims=True) + EPSILON)


def split3(v):
    hi = v.astype(BF16)
    rest = v - hi.astype(F32)
    mid = rest.astype(BF16)
    low = (rest - mid.astype(F32)).astype(BF16)
    return hi, mid, low


def norm_back(grad_normed, gain, unit, factor):
    scaled = grad_normed * gain
    return factor * (scaled - unit * jnp.mean(scaled * unit, axis=-1, keepdims=True))


def qkv_kernel(len_ref, x_ref, w_ref, gain_ref, cos_ref, sin_ref, q_ref, k_ref, v_ref, normed_ref):
    rows = x_ref.shape[0]
    x = x_ref[...].astype(F32)
    normed = (x * rms(x) * gain_ref[0:1, :]).astype(BF16)
    normed_ref[...] = normed
    cosine = cos_ref[...]
    sine = sin_ref[...]
    lane = lax.broadcasted_iota(jnp.int32, (rows, 128), 1)
    slot = lax.broadcasted_iota(jnp.int32, (rows, 128), 0) + pl.program_id(0) * rows
    masked = jnp.where(slot < len_ref[0], 0.0, NEG_FILL).astype(BF16)
    one = jnp.ones((rows, 128), BF16)
    zero = jnp.zeros((rows, 128), BF16)
    pairs = w_ref.shape[2] // 128
    for c in range(3):
        y = dot(normed, w_ref[c])
        for j in range(pairs):
            v = y[:, 128 * j : 128 * (j + 1)]
            if c < 2:
                v = v * cosine + swap_halves(v) * sine
            if c == 0:
                v = v * (FACTOR * LOG2E)
            v = v.astype(BF16)
            for s in range(2):
                first = HD * (1 - s)
                own = (lane >= HD * s) & (lane < HD * (s + 1))
                if c == 0:
                    q_ref[2 * j + s] = jnp.where(own, v, jnp.where(lane == first, one, zero))
                elif c == 1:
                    tail = jnp.where(
                        lane == first, masked, jnp.where(lane < first + 4, one, zero)
                    )
                    tail = jnp.where(lane < first, zero, tail)
                    k_ref[2 * j + s] = jnp.where(own, v, tail)
                else:
                    v_ref[2 * j + s] = jnp.where(own, v, one)


def project(lengths, tokens, qkv_weight, gains, cosine, sine, block=512):
    rows, width = tokens.shape
    local = qkv_weight.shape[2]
    heads = local // HD
    spec = pl.BlockSpec((heads, block, 128), lambda i: (0, i, 0))
    return call(
        qkv_kernel,
        (rows // block,),
        [
            smem(),
            pl.BlockSpec((block, width), lambda i: (i, 0)),
            whole(qkv_weight.shape),
            whole(gains.shape),
            pl.BlockSpec((block, 128), lambda i: (i, 0)),
            pl.BlockSpec((block, 128), lambda i: (i, 0)),
        ],
        [spec] * 3 + [pl.BlockSpec((block, width), lambda i: (i, 0))],
        [sds((heads, rows, 128), BF16)] * 3 + [sds((rows, width), BF16)],
    )(lengths, tokens, qkv_weight, gains, cosine, sine)


def attend_kernel(sub, parts, idx_ref, q_ref, k_ref, v_ref, *refs):
    o_refs = refs[:parts]
    nat_ref, qb_ref = refs[parts:]
    rows = q_ref.shape[1]
    lane = lax.broadcasted_iota(jnp.int32, (sub, 128), 1)
    for r in range(rows // sub):
        part = slice(r * sub, (r + 1) * sub)
        outs = []
        for s in range(2):
            q = q_ref[s, part, :]
            scores = dot(q, k_ref[s], NT)
            peak = jnp.max(scores, axis=1, keepdims=True)
            expo = jnp.exp2(scores - peak).astype(BF16)
            acc = dot(expo, v_ref[s])
            outs.append(acc / pltpu.roll(acc, HD, 1))
            first = HD * (1 - s)
            total = jnp.where((lane >= first) & (lane < first + HD), acc, 1.0)
            hi, mid, low = split3(-(peak + jnp.log2(total)))
            tail = jnp.where(lane == first + 3, low, q)
            tail = jnp.where(lane == first + 2, mid, tail)
            qb_ref[s, part, :] = jnp.where(lane == first + 1, hi, tail)
        nat_ref[part, :] = jnp.where(lane < HD, outs[0], outs[1]).astype(BF16)
    for d in range(parts):

        @pl.when(pl.program_id(1) == d)
        def _():
            o_refs[d][...] = nat_ref[...]


def attend(index, q, k, v, parts, sub=256):
    heads, rows, _ = q.shape
    keys = k.shape[1]
    share = rows // parts
    local = heads * HD
    return call(
        functools.partial(attend_kernel, min(sub, share), parts),
        (heads // 2, parts),
        [
            pl.BlockSpec((2, share, 128), lambda j, i, idx: (j, idx[0] ^ i, 0)),
            pl.BlockSpec((2, keys, 128), lambda j, i, idx: (j, 0, 0)),
            pl.BlockSpec((2, keys, 128), lambda j, i, idx: (j, 0, 0)),
        ],
        [pl.BlockSpec((share, 128), lambda j, i, idx: (0, j))] * parts
        + [
            pl.BlockSpec((share, 128), lambda j, i, idx: (idx[0] ^ i, j)),
            pl.BlockSpec((2, share, 128), lambda j, i, idx: (j, idx[0] ^ i, 0)),
        ],
        [sds((share, local), BF16)] * parts + [sds((rows, local), BF16), sds((heads, rows, 128), BF16)],
        prefetch=1,
    )(index, q, k, v)


def cut_kernel(idx_ref, gu_ref, dw_ref, *refs):
    part = gu_ref.shape[1]
    out_ref = refs[-1]
    out_ref[:part, :] = gu_ref[0]
    out_ref[part : 2 * part, :] = gu_ref[1]
    out_ref[2 * part : 3 * part, :] = dw_ref[...].T
    if len(refs) > 1:
        out_ref[3 * part :, :] = refs[0][...]


def cut_weights(dp, gate_up, down, shares, more):
    _, width, hidden = gate_up.shape
    part = width // shares
    if part % 128:
        down = lax.dynamic_slice_in_dim(down, dp[0] * part, part, 1)
        spec = whole(down.shape)
    else:
        spec = pl.BlockSpec((hidden, part), lambda i, idx: (0, idx[0]))
    shape = (3 * part + sum(a.shape[0] for a in more), hidden)
    return call(
        cut_kernel,
        (1,),
        [pl.BlockSpec((2, part, hidden), lambda i, idx: (0, idx[0], 0)), spec] + [whole(a.shape) for a in more],
        whole(shape),
        sds(shape, BF16),
        prefetch=1,
    )(dp, gate_up, down, *more)


def pack_kernel(*refs):
    out_ref, row = refs[-1], 0
    for ref in refs[:-1]:
        out_ref[row : row + ref.shape[0], :] = ref[...]
        row += ref.shape[0]


def pack(arrays):
    shape = (sum(a.shape[0] for a in arrays), arrays[0].shape[1])
    return call(pack_kernel, (1,), [whole(a.shape) for a in arrays], whole(shape), sds(shape, BF16))(*arrays)


def ffn_kernel(parts, ow_row, ow_order, slot, idx_ref, len_ref, weight_ref, gain_ref, x_h, cot_h, gu_h, dw_h, pb_h, ow_h, *refs):
    own = slot == 0
    att_h = refs[:parts]
    refs = refs[parts:]
    count = 7 if own else 6
    outs, scratch = refs[:count], refs[count:]
    x_v, cot_v, att_v, ow_v, gu_v, dw_v, pb_v, left_v, act_v, ffn_v, gn2_v, low_v, sem_in, sem_out = scratch
    rows, width = x_v.shape
    local = att_v.shape[2]
    hidden_units = gu_v.shape[2]
    part = pb_v.shape[1] // 3
    row0 = pl.multiple_of((idx_ref[0] ^ slot) * rows, rows)
    mine = pl.ds(row0, rows)

    def fetch(src, dst, i):
        copy = pltpu.make_async_copy(src, dst, sem_in.at[i])
        copy.start()
        return copy

    pending = []

    def store(src, dst, i):
        copy = pltpu.make_async_copy(src, dst, sem_out.at[i])
        copy.start()
        pending.append(copy)

    get_x = fetch(x_h.at[mine], x_v, 0)
    get_ow = fetch(ow_h.at[:, pl.ds(ow_row, ow_v.shape[1])], ow_v, 6 + parts)
    get_att = [fetch(att_h[d], att_v.at[d], 2 + d) for d in range(parts)]
    get_cot = fetch(cot_h.at[mine], cot_v, 2 + parts)
    get_gu = fetch(gu_h, gu_v, 3 + parts)
    get_dw = fetch(dw_h, dw_v, 4 + parts)
    get_pb = fetch(pb_h.at[:, pl.ds(0, pb_v.shape[1])], pb_v, 1)

    get_x.wait()
    get_ow.wait()
    piece = ow_v.shape[1] // parts
    for copy in get_att:
        copy.wait()
    att = jnp.concatenate([att_v[d] for d in ow_order], axis=1)
    out_w = [ow_v[:, n * piece : (n + 1) * piece].reshape(local, width) for n in range(parts)]
    resid = x_v[...].astype(F32) + dot(att, jnp.concatenate(out_w, axis=0))
    if own:
        ffn_v[...] = resid
        store(ffn_v, outs[6], 4)
    normed = (resid * rms(resid) * gain_ref[1:2, :]).astype(BF16)
    left_v[0] = normed
    position = lax.broadcasted_iota(jnp.int32, (rows, 1), 0) + row0
    row_weight = jnp.where(position < len_ref[0], weight_ref[0], 0.0)
    get_cot.wait()
    left_v[1] = (cot_v[...].astype(F32) * row_weight).astype(BF16)
    store(left_v, outs[0], 0)
    for shard in range(2):
        cols = slice(shard * hidden_units, (shard + 1) * hidden_units)
        if shard == 0:
            get_gu.wait()
            get_dw.wait()
            gate_w, up_w, down_w = gu_v[0], gu_v[1], dw_v[...]
        else:
            get_pb.wait()
            gate_w, up_w, down_w = (
                pb_v[:, c * part : (c + 1) * part, :].reshape(width, hidden_units) for c in range(3)
            )
        gate = dot(left_v[0], gate_w)
        upper = dot(left_v[0], up_w)
        grad_hidden = dot(left_v[1], down_w, NT if shard == 0 else NN)
        sigma = 0.5 + 0.5 * jnp.tanh(0.5 * gate)
        act = gate * sigma
        hidden = (act * upper).astype(BF16)
        grad_up = (grad_hidden * act).astype(BF16)
        grad_gate = (grad_hidden * upper * (sigma + act * (1.0 - sigma))).astype(BF16)
        act_v[0, :, cols] = grad_gate
        act_v[1, :, cols] = grad_up
        act_v[2, :, cols] = hidden
        store(act_v.at[:, :, cols], outs[1].at[:, :, cols], 1 + 4 * shard)
        grad = dot(
            jnp.concatenate([grad_gate, grad_up], axis=1), jnp.concatenate([gate_w, up_w], axis=1), NT
        )
        term = dot(hidden, down_w, NN if shard == 0 else NT)
        if shard == 0:
            gn2_v[...] = grad
            if own:
                pending.pop(0).wait()
            ffn_v[...] = term
        else:
            low_v[0] = (gn2_v[...] + grad).astype(BF16)
            store(low_v.at[0], outs[2], 2)
            low_v[1] = (ffn_v[...] + term).astype(BF16)
            row = 0
            for n in range(3):
                size = outs[3 + n].shape[0]
                store(low_v.at[1, pl.ds(row, size)], outs[3 + n], (3, 6, 7)[n])
                row += size
    for copy in pending:
        copy.wait()


def feed_forward(slot, index, lengths, picked, atts, tokens, cotangent, out_full, gate_up, down, partner, gains):
    parts = len(atts)
    rows, local = atts[0].shape
    width = tokens.shape[1]
    hidden = gate_up.shape[2]
    out_rows, ow_row, ow_order = out_full
    shares = partner.shape[0]
    part = width // shares
    anywhere = pl.BlockSpec(memory_space=pl.ANY)
    out_shape = [
        sds((2, rows, width), BF16), sds((3, rows, 2 * hidden), BF16),
        sds((rows, width), BF16),
    ]
    out_shape += [sds((rows * n // 16, width), BF16) for n in (2, 10, 4)]
    if slot == 0:
        out_shape.append(sds((rows, width), F32))
    return call(
        functools.partial(ffn_kernel, parts, ow_row, ow_order, slot),
        (1,),
        [smem(), smem(), whole(gains.shape)] + [anywhere] * (6 + parts),
        [anywhere] * len(out_shape),
        out_shape,
        scratch=[
            pltpu.VMEM((rows, width), BF16),
            pltpu.VMEM((rows, width), BF16),
            pltpu.VMEM((parts, rows, local), BF16),
            pltpu.VMEM((shares, parts * local // shares, width), BF16),
            pltpu.VMEM(gate_up.shape, BF16),
            pltpu.VMEM(down.shape, BF16),
            pltpu.VMEM((shares, 3 * part, hidden), BF16),
            pltpu.VMEM((2, rows, width), BF16),
            pltpu.VMEM((3, rows, 2 * hidden), BF16),
            pltpu.VMEM((rows, width), F32),
            pltpu.VMEM((rows, width), F32),
            pltpu.VMEM((2, rows, width), BF16),
            pltpu.SemaphoreType.DMA((7 + parts,)),
            pltpu.SemaphoreType.DMA((8,)),
        ],
        prefetch=1,
    )(index, lengths, picked, gains, tokens, cotangent, gate_up, down, partner, out_rows, *atts)


def write_shares(out, total):
    part = out.shape[-2]
    for j in range(out.shape[0]):
        out[j] = total[j * part : (j + 1) * part, :].astype(BF16)


def ffn_grad_kernel(sets, *refs):
    left = refs[:sets]
    act = refs[sets : 2 * sets]
    total = dot(left[0][0], act[0][0], TN)
    for e in range(1, sets):
        total = total + dot(left[e][0], act[e][0], TN)
    write_shares(refs[-1], total)


def ffn_grads(lefts, acts, shares):
    sets = len(lefts)
    _, rows, width = lefts[0].shape
    hidden = acts[0].shape[2] // 2
    part = width // shares
    specs = [pl.BlockSpec((1, rows, width), lambda c: (c % 3 // 2, 0, 0))] * sets
    specs += [pl.BlockSpec((1, rows, hidden), lambda c: (c % 3, 0, c // 3))] * sets
    return call(
        functools.partial(ffn_grad_kernel, sets),
        (6,),
        specs,
        pl.BlockSpec((shares, part, hidden), lambda c: (0, c, 0)),
        sds((shares, 6 * part, hidden), BF16),
    )(*lefts, *acts)


def out_grad_kernel(low_ref, *refs):
    *att_refs, out = refs
    each = out.shape[2] // att_refs[0].shape[1]
    for c in range(len(att_refs) // each):

        @pl.when(pl.program_id(0) == c)
        def _():
            rows = jnp.concatenate([ref[...] for ref in att_refs[c * each : (c + 1) * each]], axis=1)
            write_shares(out, dot(low_ref[...], rows, TN))


def out_grads(grad_low, att_own, shares, hidden):
    width = grad_low.shape[1]
    part = width // shares
    steps = len(att_own) * att_own[0].shape[1] // hidden
    return call(
        out_grad_kernel,
        (steps,),
        [whole(a.shape) for a in (grad_low, *att_own)],
        pl.BlockSpec((shares, part, hidden), lambda c: (0, c, 0)),
        sds((shares, steps * part, hidden), BF16),
    )(grad_low, *att_own)


def resid_kernel(ow_order, members, idx_ref, len_ref, weight_ref, cot_ref, resid_ref, ow_ref, gain_ref, *refs):
    parts = len(ow_order)
    gn2_refs = refs[:members]
    gr_ref, low_ref, sum_ref = refs[members : members + 3]
    g_refs = refs[members + 3 :]
    rows, width = cot_ref.shape
    local = g_refs[0].shape[1]
    step = pl.program_id(0)
    first = (idx_ref[0] * pl.num_programs(0) + step) * rows
    slot = lax.broadcasted_iota(jnp.int32, (rows, 1), 0) + first
    row_weight = jnp.where(slot < len_ref[0], weight_ref[0], 0.0)
    gn2 = gn2_refs[0][...].astype(F32)
    for ref in gn2_refs[1:]:
        gn2 = gn2 + ref[...].astype(F32)
    resid = resid_ref[...]
    factor = rms(resid)
    unit = resid * factor
    grad = cot_ref[...].astype(F32) * row_weight + norm_back(gn2, gain_ref[1:2, :], unit, factor)
    gr_ref[...] = grad
    low = grad.astype(BF16)
    low_ref[...] = low

    @pl.when(step == 0)
    def _():
        sum_ref[...] = jnp.zeros_like(sum_ref)

    sum_ref[...] += jnp.sum((gn2 * unit).reshape(rows // 8, 8, width), axis=0)
    for d in range(parts):
        piece = ow_ref.shape[1] // parts
        at = ow_order.index(d) * piece
        block = ow_ref[:, at : at + piece].reshape(local, width)
        g_refs[d][...] = dot(low, block, NT).astype(BF16)


def resid_back(index, lengths, picked, cotangent, resid, gn2s, out_full, gains, local, block=256):
    share, width = resid.shape
    parts, members = width // local, len(gn2s)
    out_rows, ow_row, ow_order = out_full
    ow_rows = parts * local // out_rows.shape[0]
    steps = share // block
    row = lambda n: pl.BlockSpec((block, n), lambda i, idx: (i, 0))
    return call(
        functools.partial(resid_kernel, ow_order, members),
        (steps,),
        [
            smem(), smem(),
            pl.BlockSpec((block, width), lambda i, idx: (idx[0] * steps + i, 0)),
            row(width),
            pl.BlockSpec((out_rows.shape[0], ow_rows, width), lambda *_: (0, ow_row // ow_rows, 0), pipeline_mode=pl.Buffered(1)),
            whole(gains.shape),
        ]
        + [row(width)] * members,
        [row(width), row(width), whole((8, width))] + [row(local)] * parts,
        [sds((share, width), F32), sds((share, width), BF16), sds((8, width), F32)]
        + [sds((share, local), BF16)] * parts,
        prefetch=1,
    )(index, lengths, picked, cotangent, resid, out_rows, gains, *gn2s)


def attend_back_kernel(parts, idx_ref, q_ref, k_ref, v_ref, att_ref, cos_ref, sin_ref, *refs):
    grad_refs = refs[:parts]
    outs = refs[parts : 2 * parts]
    dk_acc, dv_acc = refs[2 * parts :]
    rows = q_ref.shape[1]
    step = pl.program_id(0)
    me = idx_ref[0]
    lane = lax.broadcasted_iota(jnp.int32, (rows, 128), 1)

    def table(ref, d):
        return ref[pl.ds(pl.multiple_of((me ^ d) * rows, rows), rows), :]

    def columns(ref, d):
        return ref[:, pl.ds(pl.multiple_of((me ^ d) * rows, rows), rows)].T

    def back(v, d, scale):
        return ((v * table(cos_ref, d) - swap_halves(v) * table(sin_ref, d)) * scale).astype(BF16)

    @pl.when(step == 0)
    def _():
        dk_acc[...] = jnp.zeros_like(dk_acc)
        dv_acc[...] = jnp.zeros_like(dv_acc)

    grad = grad_refs[0][...]
    for d in range(1, parts):
        grad = jnp.where(step == d, grad_refs[d][...], grad)
    prod = grad.astype(F32) * att_ref[...].astype(F32)
    zero = jnp.zeros((rows, 128), BF16)
    dqs, probs_all, scores_all, grads_own, queries_own = [], [], [], [], []
    for s in range(2):
        first = HD * (1 - s)
        own = (lane >= HD * s) & (lane < HD * (s + 1))
        delta = jnp.sum(jnp.where(own, prod, 0.0), axis=1, keepdims=True)
        hi, mid, low = split3(-delta)
        grad_own = jnp.where(own, grad, zero)
        grad_aug = jnp.where(lane == first + 2, low, grad_own)
        grad_aug = jnp.where(lane == first + 1, mid, grad_aug)
        grad_aug = jnp.where(lane == first, hi, grad_aug)
        q = q_ref[s]
        probs = jnp.exp2(dot(q, k_ref[s], NT))
        scores_grad = (probs * dot(grad_aug, v_ref[s], NT)).astype(BF16)
        probs_all.append(probs.astype(BF16))
        scores_all.append(scores_grad)
        grads_own.append(grad_own)
        queries_own.append(jnp.where(own, q, zero))
        dqs.append(dot(scores_grad, k_ref[s]))
    dv_acc[...] += dot(jnp.concatenate(grads_own, axis=0).T, jnp.concatenate(probs_all, axis=0))
    dk_acc[...] += dot(jnp.concatenate(queries_own, axis=0).T, jnp.concatenate(scores_all, axis=0))
    dq = jnp.where(lane < HD, dqs[0], dqs[1])
    for d in range(parts):

        @pl.when(step == d)
        def _():
            outs[d][0] = back(dq, d, FACTOR)

    @pl.when(step == parts - 1)
    def _():
        for d in range(parts):
            outs[d][1] = back(columns(dk_acc, d), d, LN2)
            outs[d][2] = columns(dv_acc, d).astype(BF16)


def attend_back(index, grads, q, k, v, att, cosine, sine, pair):
    parts = len(grads)
    share = grads[0].shape[0]
    rows = q.shape[1]
    keys = pl.BlockSpec((2, rows, 128), lambda i, idx: (pair, 0, 0), pipeline_mode=pl.Buffered(1))
    return call(
        functools.partial(attend_back_kernel, parts),
        (parts,),
        [
            pl.BlockSpec((2, share, 128), lambda i, idx: (pair, idx[0] ^ i, 0)),
            keys,
            keys,
            pl.BlockSpec((share, 128), lambda i, idx: (idx[0] ^ i, pair)),
            whole(cosine.shape),
            whole(sine.shape),
        ]
        + [pl.BlockSpec((share, 128), lambda i, idx: (0, pair))] * parts,
        [whole((3, share, 128))] * parts,
        [sds((3, share, 128), BF16)] * parts,
        scratch=[pltpu.VMEM((128, rows), F32)] * 2,
        flops=2 * rows * rows * 128 * 10,
        nbytes=rows * 256 * 16,
        trans=2 * rows * rows,
        prefetch=1,
    )(index, q, k, v, att, cosine, sine, *grads)


def project_grads(index, normed, acts, qkv_weight, shares, pair, prev=None):
    width = normed.shape[1]
    local = 128 * (pair + 1)
    parts = len(acts)
    share = acts[0].shape[1]
    part = width // shares
    half = (shares // 2, part, 3 * local)
    ins = []
    for d in range(parts):
        pick = functools.partial(
            lambda d, idx, ref: ref.at[pl.ds(pl.multiple_of((idx[0] ^ d) * share, share), share)], d
        )
        ins += [(normed, (share, width), pick), (acts[d], acts[d].shape, None)]
    weight_cols = pl.ds(128 * pair, 128)
    ins.append((qkv_weight, (3, width, 128), lambda idx, ref: ref.at[:, :, weight_cols]))
    if prev:
        ins += [(a, a.shape, None) for a in prev]

    def body(idx_ref, _, get, outs, put, scratch):
        away_ref, keep_ref, sum_ref = outs
        (acc,) = scratch
        for d in range(parts):
            act_ref = get(2 * d + 1)
            act = jnp.concatenate([act_ref[c] for c in range(3)], axis=1)
            term = dot(get(2 * d)[...], act, TN)
            acc[...] = acc[...] + term if d else term
        core = idx_ref[1] & 1
        before = local - 128
        for n, (ref, bit) in enumerate(((away_ref, 1 - core), (keep_ref, core))):
            for c in range(3):
                if prev:
                    ref[:, :, c * local : c * local + before] = get(2 * parts + 1 + n)[
                        :, :, c * before : (c + 1) * before
                    ]
                for j in range(shares // 2):
                    rows = pl.ds(pl.multiple_of((2 * j + bit) * part, part), part)
                    ref[j, :, c * local + before : (c + 1) * local] = acc[rows, c * 128 : (c + 1) * 128].astype(BF16)
            put(n)
        weight = get(2 * parts)
        gain_sum = acc[:, :128] * weight[0].astype(F32)
        for c in (1, 2):
            gain_sum += acc[:, c * 128 : (c + 1) * 128] * weight[c].astype(F32)
        total = jnp.broadcast_to(jnp.sum(gain_sum, axis=1, keepdims=True), sum_ref.shape)
        sum_ref[...] = total + get(2 * parts + 3)[...] if prev else total
        put(2)

    outs = [(half, BF16), (half, BF16), ((width, 128), F32)]
    return staged(body, index, [], ins, outs, 3, [pltpu.VMEM((width, 3 * 128), F32)])


def token_grad(index, tokens, grad_resid, qkv_weight, qkv_full, gains, acts, ffn_own, ffn_got):
    share, width = grad_resid.shape
    pairs, parts = len(acts), len(acts[0])
    part, hidden = ffn_got.shape[0] // 3, ffn_got.shape[1]
    local = qkv_weight.shape[2]
    ins = []
    for d in range(parts):
        ins += [(acts[j][d], acts[j][d].shape, None) for j in range(pairs)]
        if d:
            rows = pl.ds((d - 1) * 3 * part, 3 * part)
            pick = functools.partial(lambda rows, idx, ref: ref.at[:, rows], rows)
            ins.append((qkv_full, (qkv_full.shape[0], 3 * part, local), pick))
        else:
            ins.append((qkv_weight, qkv_weight.shape, None))
        if d == 0:
            ins.append((ffn_own, ffn_got.shape, lambda idx, ref: ref.at[pl.ds(0, 3 * part)]))
            ins.append((ffn_got, ffn_got.shape, None))
    ins.append((tokens, (share, width), lambda idx, ref: ref.at[pl.ds(pl.multiple_of(idx[0] * share, share), share)]))
    ins.append((grad_resid, grad_resid.shape, None))

    def body(idx_ref, smalls, get, outs, put, scratch):
        out_ref, gu_ref, down_ref = outs
        (acc,) = scratch
        at = 0
        for n in range(parts):
            group = [get(at + j) for j in range(pairs)]
            weight = get(at + pairs)
            at += pairs + 1
            act = jnp.concatenate([ref[c] for c in range(3) for ref in group], axis=1)
            cut = lambda c: weight[:, c * part : (c + 1) * part].reshape(width, local) if n else weight[c]
            weight_all = jnp.concatenate([cut(c) for c in range(3)], axis=1)
            term = dot(act, weight_all, NT)
            acc[...] = acc[...] + term if n else term
            if n == 0:
                total = get(at)[...].astype(F32) + get(at + 1)[...].astype(F32)
                at += 2
                gu_ref[0] = total[:part]
                gu_ref[1] = total[part : 2 * part]
                down_ref[...] = total[2 * part :].T
                put(1)
                put(2)
        x_ref, gr_ref = get(at), get(at + 1)
        half = share // 2
        for c in range(2):
            rows = slice(c * half, (c + 1) * half)
            x = x_ref[rows, :].astype(F32)
            factor = rms(x)
            out_ref[rows, :] = gr_ref[rows, :] + norm_back(acc[rows, :], smalls[0][0:1, :], x * factor, factor)
            put(0, pl.ds(c * half, half))

    outs = [((share, width), F32), ((2, part, hidden), F32), ((hidden, part), F32)]
    return staged(body, index, [gains], ins, outs, 4, [pltpu.VMEM((share, width), F32)])


def fold_kernel(cuts, idx_ref, *refs):
    ins, outs = list(refs[: 2 * len(cuts)]), list(refs[2 * len(cuts) :])
    for place, bit in cuts:
        keep, got = ins.pop(0), ins.pop(0)
        mine = (idx_ref[1] >> bit) & 1
        targets = ((outs.pop(0), mine), (outs.pop(0), 1 - mine))
        for j in range(keep.shape[0] // 2):
            rest = ((j >> place) << (place + 1)) | (j & ((1 << place) - 1))
            for out, value in targets:
                k = rest | (value << place)
                out[j] = (keep[k].astype(F32) + got[k].astype(F32)).astype(BF16)


def fold(index, lanes):
    ins, outs, info, total = [], [], [], 0
    for keep, got, lead, order in lanes:
        count, rows, cols = keep.shape
        ins += [(a, a.shape, None) for a in (keep, got)]
        if order:
            info.append((len(lead) - 1 - lead.index(order[0]), [b for b in lead if b != order[0]], order[1:], order[0]))
            outs += [((count // 2, rows, cols), BF16)] * 2
        total += rows
    if not info:
        outs = [((total, cols), BF16)]

    def body(idx_ref, _, get, out_refs, put, __):
        row = 0
        for n in range(len(lanes)):
            keep, got = get(2 * n), get(2 * n + 1)
            if info:
                place, _, _, bit = info[n]
                fold_kernel([(place, bit)], idx_ref, keep, got, *out_refs[2 * n : 2 * n + 2])
                put(2 * n)
                put(2 * n + 1)
            else:
                rows = keep.shape[1]
                out_refs[0][row : row + rows, :] = (keep[0].astype(F32) + got[0].astype(F32)).astype(BF16)
                put(0, pl.ds(row, rows))
                row += rows

    res = staged(body, index, [], ins, outs, max(len(outs), len(lanes)))
    if not info:
        return res[0]
    return [(res[2 * n], res[2 * n + 1]) + info[n][1:] for n in range(len(lanes))]


def pieces_kernel(part, op_ref, gains_ref, *outs):
    local = outs[0].shape[1]
    hidden = op_ref.shape[1]
    rows = (outs[0].shape[0] - part) // 3
    gains = gains_ref[...]
    wide = gains.shape[1] // local
    flat = jnp.concatenate(
        [gains[r // wide : r // wide + 1, (r % wide) * local : (r % wide + 1) * local] for r in range(rows)]
    )
    parts3 = jnp.concatenate(split3(flat))
    for d, out in enumerate(outs):
        block = d * local // hidden
        col = d * local % hidden
        row = block * part
        out[:part, :] = op_ref[row : row + part, col : col + local]
        out[part:, :] = parts3


def make_pieces(sum_op, gains, part, local, parts):
    shape = (part + 3 * gains.size // local, local)
    return call(
        functools.partial(pieces_kernel, part),
        (1,),
        [whole(sum_op.shape), whole(gains.shape)],
        [whole(shape)] * parts,
        [sds(shape, BF16)] * parts,
    )(sum_op, gains)


def finish_outputs(index, resid, own, others, keep, got, pieces):
    parts, count = len(pieces), len(others[0])
    width = resid.shape[1]
    part, local = keep.shape[1], keep.shape[2] // 3
    ins, row = [], 0
    for n, a in enumerate(own):
        rows = pl.ds(row, a.shape[0])
        ins.append((resid, a.shape, functools.partial(lambda rows, idx, ref: ref.at[rows], rows)))
        ins += [(b, a.shape, None) for b in (a, *others[n])]
        row += a.shape[0]
    ins += [(a, a.shape, None) for a in (keep, got, *pieces)]

    def body(idx_ref, _, get, outs, put, __):
        out_ref, qkv_ref, op_ref, gains_ref = outs
        at = row = 0
        for a in own:
            total = get(at)[...]
            for n in range(count + 1):
                total = total + get(at + 1 + n)[...].astype(F32)
            out_ref[row : row + a.shape[0], :] = total
            put(0, pl.ds(row, a.shape[0]))
            row += a.shape[0]
            at += count + 2
        qkv = get(at)[0].astype(F32) + get(at + 1)[0].astype(F32)
        for c in range(3):
            qkv_ref[c] = qkv[:, c * local : (c + 1) * local]
        put(1)
        piece_refs = [get(at + 2 + d) for d in range(parts)]
        rows = (piece_refs[0].shape[0] - part) // 3

        def gains_of(ref):
            hi, mid, low = (ref[part + n * rows : part + (n + 1) * rows, :].astype(F32) for n in range(3))
            return hi + mid + low

        ops = [ref[:part, :].astype(F32) for ref in piece_refs]
        gains = [gains_of(ref) for ref in piece_refs]
        while len(ops) > 1:
            ops = [ops[2 * n] + ops[2 * n + 1] for n in range(len(ops) // 2)]
            gains = [gains[2 * n] + gains[2 * n + 1] for n in range(len(gains) // 2)]
        op_ref[...] = ops[0].T
        put(2)
        wide = width // local
        for r in range(rows):
            cols = slice((r % wide) * local, (r % wide + 1) * local)
            gains_ref[r // wide : r // wide + 1, cols] = gains[0][r : r + 1, :]
        put(3)

    shapes = [resid.shape, (3, part, local), (local, part), (2, width)]
    return staged(body, index, [], ins, [(shape, F32) for shape in shapes], len(own) + 3)


def after(value, *others):
    return lax.optimization_barrier((value, *others))[0]


def body(
    tokens, qkv_weight, out_weight, gate_up_weight, down_weight, norm_gains,
    species_weight, species_ids, lengths, cotangent,
):
    rows, width = tokens.shape
    local = out_weight.shape[0]
    hidden = down_weight.shape[0]
    parts = lax.axis_size("tensor")
    slots = list(range(parts - 2, -1, -2))
    shares = lax.axis_size("dp")
    part = width // shares
    me = lax.axis_index("tensor")
    dp = lax.axis_index("dp")
    index = jnp.stack([me, dp]).astype(jnp.int32)
    cosine, sine = (jnp.asarray(t) for t in rotary_tables())
    pairs = local // 128
    valid = lengths[0] >= 0

    def region(f):
        shapes = jax.eval_shape(f)
        zeros = lambda: jax.tree.map(lambda a: jnp.zeros(a.shape, a.dtype), shapes)
        return lax.optimization_barrier(lax.cond(valid, f, zeros))

    def beside(sends, f, apart=False):
        return region(lambda: ([swap(*x) for x in sends], region(f) if apart else f()))

    def swap(a, d, name="tensor"):
        return lax.ppermute(a, name, [(i, i ^ d) for i in range(lax.axis_size(name))])

    def cut(a, start, size, axis=0):
        return lax.dynamic_slice_in_dim(a, start, size, axis)

    def outgoing(pieces):
        return [(pieces[d], d, "tensor") for d in range(1, parts)]

    bits = shares.bit_length() - 1
    lead = list(range(bits - 1, 0, -1))

    def fold_next(halves, got):
        return fold(index, [(keep, g, left, order) for (keep, _, left, order, _), g in zip(halves, got)])

    def leaving(halves):
        return [(away, 1 << bit, "dp") for _, away, _, _, bit in halves]

    matches = species_ids[:, None] == jnp.arange(species_weight.shape[0])[None, :]
    picked = jnp.sum(jnp.where(matches, species_weight[None, :], F32(0.0)), axis=1)

    ow_cut = cut(out_weight, dp * (local // shares), local // shares)
    qkv_cut = cut(qkv_weight, dp * part, part, 1).reshape(3 * part, local)
    together = hidden == width
    mine = cut_weights(index[1:], gate_up_weight, down_weight, shares, [ow_cut] if together else [])
    sends = [(ow_cut, d, "tensor") for d in range(2 if together else 1, parts)]

    (partner_cut, *ow), (q, k, v, normed) = beside(
        [(mine, 1, "tensor")] + sends,
        lambda: project(lengths, tokens, qkv_weight, norm_gains, cosine, sine),
    )
    if together:
        partner = lax.all_gather(pack([partner_cut, ow_cut, *ow]), "dp", axis=0)
        out_full = (partner, 3 * part, [1, 0] + list(range(2, parts)))
    else:
        partner = lax.all_gather(partner_cut, "dp", axis=0)
        out_full = (lax.all_gather(pack([ow_cut, *ow]), "dp", axis=0), 0, list(range(parts)))

    sends = [(after(qkv_cut, partner_cut, picked), d, "tensor") for d in range(1, parts)]
    qkv_got, (*att, att_nat, q_back) = beside(sends, lambda: attend(index, q, k, v, parts))
    rows_for = lambda e: outgoing([att[d ^ e] for d in range(parts)])
    rows_now, qkv_stack = beside(rows_for(slots[0]), lambda: pack(qkv_got))
    qkv_full = lax.all_gather(qkv_stack, "dp", axis=0)

    lefts, acts, gn2s, terms, gn2_got = {}, {}, {}, {}, {}
    tied = tokens
    for e in slots:

        def feed():
            outs = feed_forward(
                e, index, lengths, picked, [att[e]] + rows_now, tied, cotangent, out_full,
                gate_up_weight, down_weight, partner, norm_gains
            )
            if e:
                return outs
            return outs, ffn_grads([*lefts.values(), outs[0]], [*acts.values(), outs[1]], shares)

        sends = rows_for(e - 2) if e else []
        if e + 2 in gn2s:
            sends.append((gn2s[e + 2], e + 2, "tensor"))
        got, outs = beside(sends, feed)
        if e + 2 in gn2s:
            gn2_got[e + 2] = got.pop()
        if e:
            rows_now = got
        else:
            outs, wg_ffn = outs
        lefts[e], acts[e], gn2s[e], *terms[e] = outs[:6]
        tied = after(tokens, gn2s[e])
    resid = outs[6]
    gn2_all = [gn2s[0]] + [gn2_got[e] for e in slots[:-1]]

    def terms_out(i):
        return [(terms[e][i], e, "tensor") for e in slots[:-1]]

    terms_got = []
    got, (grad_resid, grad_low, gain_two, *grads) = beside(
        terms_out(0),
        lambda: resid_back(
            index, lengths, picked, cotangent, resid, gn2_all, out_full, norm_gains, local
        ),
    )
    terms_got.append(got)
    sum_ffn = lax.psum_scatter(wg_ffn, "dp", scatter_dimension=0, tiled=True)[0]
    got, wg_op = beside(outgoing(grads), lambda: out_grads(grad_low, [att[0]] + rows_now, shares, hidden))
    grads_all = [grads[0]] + got

    def back(j):
        return attend_back(index, grads_all, q_back, k, v, att_nat, cosine, sine, j)

    terms_got.append([swap(after(a, wg_op), *way) for a, *way in terms_out(1)])
    group = region(lambda: back(0))
    group = after(group, *terms_got[1])
    sum_op = lax.psum_scatter(after(wg_op, qkv_full), "dp", scatter_dimension=0, tiled=True)[0]
    qkv_acts, acts_got, qkv_sums = [group], [], None
    for j in range(1, pairs):

        def back_next():
            return back(j), project_grads(index, normed, qkv_acts[-1], qkv_weight, shares, j - 1, qkv_sums)

        got, (group, qkv_sums) = beside(outgoing(group), back_next)
        acts_got.append([qkv_acts[-1][0]] + got)
        qkv_acts.append(group)
    ways = []

    def finish():
        away_q, keep_q, gain_one = project_grads(
            index, normed, qkv_acts[-1], qkv_weight, shares, pairs - 1, qkv_sums
        )
        halves = fold(index, [(keep_q, swap(away_q, 1, "dp"), lead, lead)])
        for s in range(bits - 2):
            halves = fold_next(halves, [swap(*x) for x in leaving(halves)])
        gains_grad = jnp.stack([gain_one[:, 0] / norm_gains[0], jnp.sum(gain_two, axis=0)])
        gains_grad = after(gains_grad, *[h[0] for h in halves])
        for s in range(bits):
            gains_grad = gains_grad + swap(gains_grad, 1 << s, "dp")
        ways[:] = [h[2:] for h in halves]
        return [h[:2] for h in halves], gains_grad

    got, (halves, gains_grad) = beside(outgoing(group) + [(sum_ffn[3 * part :], 1, "tensor")], finish, apart=True)
    halves = [tuple(h) + way for h, way in zip(halves, ways)]
    acts_got.append([group[0]] + got[: parts - 1])
    got_b = got[-1]
    pieces = make_pieces(sum_op, gains_grad, part, local, parts)
    got, (grad_tok, grad_gu, grad_down) = beside(
        leaving(halves) + terms_out(2) + outgoing(pieces),
        lambda: token_grad(index, tokens, grad_resid, qkv_weight, qkv_full, norm_gains, acts_got, sum_ffn, got_b),
    )
    terms_got.append(got[1 : len(slots)])
    out, grad_qkv, grad_op, gains_grad = finish_outputs(
        index, resid, terms[0], terms_got, halves[0][0], got[0], [pieces[0]] + got[len(slots) :]
    )
    return (out, grad_tok, grad_qkv, grad_op, grad_gu, grad_down, gains_grad)


def solution(mesh):
    in_specs = (
        P("dp", None),
        P(None, None, "tensor"),
        P("tensor", None),
        P(None, None, "tensor"),
        P("tensor", None),
        P(),
        P(),
        P("dp"),
        P("dp"),
        P("dp", None),
    )
    out_specs = (
        P(("dp", "tensor"), None),
        P(("dp", "tensor"), None),
        P(None, "dp", "tensor"),
        P("tensor", "dp"),
        P(None, "dp", "tensor"),
        P("tensor", "dp"),
        P(),
    )
    return jax.shard_map(body, mesh=mesh, in_specs=in_specs, out_specs=out_specs, check_vma=False)
```

```python
import functools
import math

import jax
import jax.numpy as jnp
import numpy as np
from jax import lax
from jax.experimental import pallas as pl
from jax.experimental.pallas import tpu as pltpu
from jax.sharding import PartitionSpec as P

HD = 64
WIN = 2048
EPSILON = 1e-05
NEG_FILL = -1e30
LOG2E = math.log2(math.e)
LN2 = math.log(2.0)
FACTOR = HD ** (-0.5)
VMEM = 60 * 2**20
F32 = jnp.float32
BF16 = jnp.bfloat16

NN = (((1,), (0,)), ((), ()))
NT = (((1,), (1,)), ((), ()))
TN = (((0,), (0,)), ((), ()))


def dot(a, b, dims=NN):
    return lax.dot_general(a, b, dims, preferred_element_type=F32)


def call(kernel, grid, in_specs, out_specs, out_shape, scratch=(), flops=0, nbytes=0, trans=0, prefetch=0):
    return pl.pallas_call(
        kernel,
        grid_spec=pltpu.PrefetchScalarGridSpec(
            num_scalar_prefetch=prefetch,
            grid=grid,
            in_specs=in_specs,
            out_specs=out_specs,
            scratch_shapes=list(scratch),
        ),
        out_shape=out_shape,
        compiler_params=pltpu.CompilerParams(vmem_limit_bytes=VMEM),
        cost_estimate=pl.CostEstimate(flops=flops, bytes_accessed=nbytes, transcendentals=trans),
    )


def whole(shape):
    return pl.BlockSpec(shape, lambda *_: (0,) * len(shape), pipeline_mode=pl.Buffered(1))


def staged(body, index, smalls, ins, outs, stores, scratch=()):
    n_small, n_in, n_out = len(smalls), len(ins), len(outs)

    def kernel(idx_ref, *refs):
        refs = list(refs)
        take = lambda n: [refs.pop(0) for _ in range(n)]
        small, far_in, far_out = take(n_small), take(n_in), take(n_out)
        near_in, near_out, extra = take(n_in), take(n_out), take(len(scratch))
        sem_in, sem_out = refs
        copies = []
        for n, (_, _, pick) in enumerate(ins):
            part = pick(idx_ref, far_in[n]) if pick else far_in[n]
            copies.append(pltpu.make_async_copy(part, near_in[n], sem_in.at[n]))
            copies[n].start()
        there, sent = set(), []

        def get(n):
            if n not in there:
                copies[n].wait()
                there.add(n)
            return near_in[n]

        def put(n, part=None):
            src, dst = near_out[n], far_out[n]
            if part is not None:
                src, dst = src.at[part], dst.at[part]
            copy = pltpu.make_async_copy(src, dst, sem_out.at[len(sent)])
            copy.start()
            sent.append(copy)

        body(idx_ref, small, get, near_out, put, extra)
        for n in range(n_in):
            get(n)
        for copy in sent:
            copy.wait()

    anywhere = pl.BlockSpec(memory_space=pl.ANY)
    specs = [smem() if a.ndim == 1 else whole(a.shape) for a in smalls]
    return call(
        kernel,
        (1,),
        specs + [anywhere] * n_in,
        [anywhere] * n_out,
        [sds(shape, dtype) for shape, dtype in outs],
        scratch=[pltpu.VMEM(shape, a.dtype) for a, shape, _ in ins]
        + [pltpu.VMEM(shape, dtype) for shape, dtype in outs]
        + list(scratch)
        + [pltpu.SemaphoreType.DMA((n_in,)), pltpu.SemaphoreType.DMA((stores,))],
        prefetch=1,
    )(index, *smalls, *[a for a, _, _ in ins])


def smem():
    return pl.BlockSpec(memory_space=pltpu.SMEM)


def sds(shape, dtype):
    return jax.ShapeDtypeStruct(shape, dtype)


def rotary_tables():
    position = np.arange(WIN, dtype=np.float64)
    frequency = 10000.0 ** (-2.0 * np.arange(HD // 2, dtype=np.float64) / HD)
    angles = position[:, None] * frequency[None, :]
    cosine = np.cos(angles)
    sine = np.sin(angles)
    cos_full = np.tile(np.concatenate([cosine, cosine], axis=1), (1, 2))
    sin_full = np.tile(np.concatenate([-sine, sine], axis=1), (1, 2))
    return cos_full.astype(np.float32), sin_full.astype(np.float32)


def swap_halves(v):
    lane = lax.broadcasted_iota(jnp.int32, v.shape, 1)
    return jnp.where(lane % HD < HD // 2, pltpu.roll(v, 96, 1), pltpu.roll(v, 32, 1))


def rms(x):
    return lax.rsqrt(jnp.mean(x * x, axis=-1, keepdims=True) + EPSILON)


def split3(v):
    hi = v.astype(BF16)
    rest = v - hi.astype(F32)
    mid = rest.astype(BF16)
    low = (rest - mid.astype(F32)).astype(BF16)
    return hi, mid, low


def norm_back(grad_normed, gain, unit, factor):
    scaled = grad_normed * gain
    return factor * (scaled - unit * jnp.mean(scaled * unit, axis=-1, keepdims=True))


def qkv_kernel(len_ref, x_ref, w_ref, gain_ref, cos_ref, sin_ref, q_ref, k_ref, v_ref, normed_ref):
    rows = x_ref.shape[0]
    x = x_ref[...].astype(F32)
    normed = (x * rms(x) * gain_ref[0:1, :]).astype(BF16)
    normed_ref[...] = normed
    cosine = cos_ref[...]
    sine = sin_ref[...]
    lane = lax.broadcasted_iota(jnp.int32, (rows, 128), 1)
    slot = lax.broadcasted_iota(jnp.int32, (rows, 128), 0) + pl.program_id(0) * rows
    masked = jnp.where(slot < len_ref[0], 0.0, NEG_FILL).astype(BF16)
    one = jnp.ones((rows, 128), BF16)
    zero = jnp.zeros((rows, 128), BF16)
    pairs = w_ref.shape[2] // 128
    for c in range(3):
        y = dot(normed, w_ref[c])
        for j in range(pairs):
            v = y[:, 128 * j : 128 * (j + 1)]
            if c < 2:
                v = v * cosine + swap_halves(v) * sine
            if c == 0:
                v = v * (FACTOR * LOG2E)
            v = v.astype(BF16)
            for s in range(2):
                first = HD * (1 - s)
                own = (lane >= HD * s) & (lane < HD * (s + 1))
                if c == 0:
                    q_ref[2 * j + s] = jnp.where(own, v, jnp.where(lane == first, one, zero))
                elif c == 1:
                    tail = jnp.where(
                        lane == first, masked, jnp.where(lane < first + 4, one, zero)
                    )
                    tail = jnp.where(lane < first, zero, tail)
                    k_ref[2 * j + s] = jnp.where(own, v, tail)
                else:
                    v_ref[2 * j + s] = jnp.where(own, v, one)


def project(lengths, tokens, qkv_weight, gains, cosine, sine, block=512):
    rows, width = tokens.shape
    local = qkv_weight.shape[2]
    heads = local // HD
    spec = pl.BlockSpec((heads, block, 128), lambda i: (0, i, 0))
    return call(
        qkv_kernel,
        (rows // block,),
        [
            smem(),
            pl.BlockSpec((block, width), lambda i: (i, 0)),
            whole(qkv_weight.shape),
            whole(gains.shape),
            pl.BlockSpec((block, 128), lambda i: (i, 0)),
            pl.BlockSpec((block, 128), lambda i: (i, 0)),
        ],
        [spec] * 3 + [pl.BlockSpec((block, width), lambda i: (i, 0))],
        [sds((heads, rows, 128), BF16)] * 3 + [sds((rows, width), BF16)],
    )(lengths, tokens, qkv_weight, gains, cosine, sine)


def attend_kernel(sub, parts, idx_ref, q_ref, k_ref, v_ref, *refs):
    o_refs = refs[:parts]
    nat_ref, qb_ref = refs[parts:]
    rows = q_ref.shape[1]
    lane = lax.broadcasted_iota(jnp.int32, (sub, 128), 1)
    for r in range(rows // sub):
        part = slice(r * sub, (r + 1) * sub)
        outs = []
        for s in range(2):
            q = q_ref[s, part, :]
            scores = dot(q, k_ref[s], NT)
            peak = jnp.max(scores, axis=1, keepdims=True)
            expo = jnp.exp2(scores - peak).astype(BF16)
            acc = dot(expo, v_ref[s])
            outs.append(acc / pltpu.roll(acc, HD, 1))
            first = HD * (1 - s)
            total = jnp.where((lane >= first) & (lane < first + HD), acc, 1.0)
            hi, mid, low = split3(-(peak + jnp.log2(total)))
            tail = jnp.where(lane == first + 3, low, q)
            tail = jnp.where(lane == first + 2, mid, tail)
            qb_ref[s, part, :] = jnp.where(lane == first + 1, hi, tail)
        nat_ref[part, :] = jnp.where(lane < HD, outs[0], outs[1]).astype(BF16)
    for d in range(parts):

        @pl.when(pl.program_id(1) == d)
        def _():
            o_refs[d][...] = nat_ref[...]


def attend(index, q, k, v, parts, sub=256):
    heads, rows, _ = q.shape
    keys = k.shape[1]
    share = rows // parts
    local = heads * HD
    return call(
        functools.partial(attend_kernel, min(sub, share), parts),
        (heads // 2, parts),
        [
            pl.BlockSpec((2, share, 128), lambda j, i, idx: (j, idx[0] ^ i, 0)),
            pl.BlockSpec((2, keys, 128), lambda j, i, idx: (j, 0, 0)),
            pl.BlockSpec((2, keys, 128), lambda j, i, idx: (j, 0, 0)),
        ],
        [pl.BlockSpec((share, 128), lambda j, i, idx: (0, j))] * parts
        + [
            pl.BlockSpec((share, 128), lambda j, i, idx: (idx[0] ^ i, j)),
            pl.BlockSpec((2, share, 128), lambda j, i, idx: (j, idx[0] ^ i, 0)),
        ],
        [sds((share, local), BF16)] * parts + [sds((rows, local), BF16), sds((heads, rows, 128), BF16)],
        prefetch=1,
    )(index, q, k, v)


def cut_kernel(idx_ref, gu_ref, dw_ref, *refs):
    part = gu_ref.shape[1]
    out_ref = refs[-1]
    out_ref[:part, :] = gu_ref[0]
    out_ref[part : 2 * part, :] = gu_ref[1]
    out_ref[2 * part : 3 * part, :] = dw_ref[...].T
    if len(refs) > 1:
        out_ref[3 * part :, :] = refs[0][...]


def cut_weights(dp, gate_up, down, shares, more):
    _, width, hidden = gate_up.shape
    part = width // shares
    if part % 128:
        down = lax.dynamic_slice_in_dim(down, dp[0] * part, part, 1)
        spec = whole(down.shape)
    else:
        spec = pl.BlockSpec((hidden, part), lambda i, idx: (0, idx[0]))
    shape = (3 * part + sum(a.shape[0] for a in more), hidden)
    return call(
        cut_kernel,
        (1,),
        [pl.BlockSpec((2, part, hidden), lambda i, idx: (0, idx[0], 0)), spec] + [whole(a.shape) for a in more],
        whole(shape),
        sds(shape, BF16),
        prefetch=1,
    )(dp, gate_up, down, *more)


def pack_kernel(*refs):
    out_ref, row = refs[-1], 0
    for ref in refs[:-1]:
        out_ref[row : row + ref.shape[0], :] = ref[...]
        row += ref.shape[0]


def pack(arrays):
    shape = (sum(a.shape[0] for a in arrays), arrays[0].shape[1])
    return call(pack_kernel, (1,), [whole(a.shape) for a in arrays], whole(shape), sds(shape, BF16))(*arrays)


def ffn_kernel(parts, ow_row, ow_order, slot, idx_ref, len_ref, weight_ref, gain_ref, x_h, cot_h, gu_h, dw_h, pb_h, ow_h, *refs):
    own = slot == 0
    att_h = refs[:parts]
    refs = refs[parts:]
    count = 7 if own else 6
    outs, scratch = refs[:count], refs[count:]
    x_v, cot_v, att_v, ow_v, gu_v, dw_v, pb_v, left_v, act_v, ffn_v, gn2_v, low_v, sem_in, sem_out = scratch
    rows, width = x_v.shape
    local = att_v.shape[2]
    hidden_units = gu_v.shape[2]
    part = pb_v.shape[1] // 3
    row0 = pl.multiple_of((idx_ref[0] ^ slot) * rows, rows)
    mine = pl.ds(row0, rows)

    def fetch(src, dst, i):
        copy = pltpu.make_async_copy(src, dst, sem_in.at[i])
        copy.start()
        return copy

    pending = []

    def store(src, dst, i):
        copy = pltpu.make_async_copy(src, dst, sem_out.at[i])
        copy.start()
        pending.append(copy)

    get_x = fetch(x_h.at[mine], x_v, 0)
    get_ow = fetch(ow_h.at[:, pl.ds(ow_row, ow_v.shape[1])], ow_v, 6 + parts)
    get_att = [fetch(att_h[d], att_v.at[d], 2 + d) for d in range(parts)]
    get_cot = fetch(cot_h.at[mine], cot_v, 2 + parts)
    get_gu = fetch(gu_h, gu_v, 3 + parts)
    get_dw = fetch(dw_h, dw_v, 4 + parts)
    get_pb = fetch(pb_h.at[:, pl.ds(0, pb_v.shape[1])], pb_v, 1)

    get_x.wait()
    get_ow.wait()
    piece = ow_v.shape[1] // parts
    for copy in get_att:
        copy.wait()
    att = jnp.concatenate([att_v[d] for d in ow_order], axis=1)
    out_w = [ow_v[:, n * piece : (n + 1) * piece].reshape(local, width) for n in range(parts)]
    resid = x_v[...].astype(F32) + dot(att, jnp.concatenate(out_w, axis=0))
    if own:
        ffn_v[...] = resid
        store(ffn_v, outs[6], 4)
    normed = (resid * rms(resid) * gain_ref[1:2, :]).astype(BF16)
    left_v[0] = normed
    position = lax.broadcasted_iota(jnp.int32, (rows, 1), 0) + row0
    row_weight = jnp.where(position < len_ref[0], weight_ref[0], 0.0)
    get_cot.wait()
    left_v[1] = (cot_v[...].astype(F32) * row_weight).astype(BF16)
    store(left_v, outs[0], 0)
    for shard in range(2):
        cols = slice(shard * hidden_units, (shard + 1) * hidden_units)
        if shard == 0:
            get_gu.wait()
            get_dw.wait()
            gate_w, up_w, down_w = gu_v[0], gu_v[1], dw_v[...]
        else:
            get_pb.wait()
            gate_w, up_w, down_w = (
                pb_v[:, c * part : (c + 1) * part, :].reshape(width, hidden_units) for c in range(3)
            )
        gate = dot(left_v[0], gate_w)
        upper = dot(left_v[0], up_w)
        grad_hidden = dot(left_v[1], down_w, NT if shard == 0 else NN)
        sigma = 0.5 + 0.5 * jnp.tanh(0.5 * gate)
        act = gate * sigma
        hidden = (act * upper).astype(BF16)
        grad_up = (grad_hidden * act).astype(BF16)
        grad_gate = (grad_hidden * upper * (sigma + act * (1.0 - sigma))).astype(BF16)
        act_v[0, :, cols] = grad_gate
        act_v[1, :, cols] = grad_up
        act_v[2, :, cols] = hidden
        store(act_v.at[:, :, cols], outs[1].at[:, :, cols], 1 + 4 * shard)
        grad = dot(
            jnp.concatenate([grad_gate, grad_up], axis=1), jnp.concatenate([gate_w, up_w], axis=1), NT
        )
        term = dot(hidden, down_w, NN if shard == 0 else NT)
        if shard == 0:
            gn2_v[...] = grad
            if own:
                pending.pop(0).wait()
            ffn_v[...] = term
        else:
            low_v[0] = (gn2_v[...] + grad).astype(BF16)
            store(low_v.at[0], outs[2], 2)
            low_v[1] = (ffn_v[...] + term).astype(BF16)
            row = 0
            for n in range(3):
                size = outs[3 + n].shape[0]
                store(low_v.at[1, pl.ds(row, size)], outs[3 + n], (3, 6, 7)[n])
                row += size
    for copy in pending:
        copy.wait()


def feed_forward(slot, index, lengths, picked, atts, tokens, cotangent, out_full, gate_up, down, partner, gains):
    parts = len(atts)
    rows, local = atts[0].shape
    width = tokens.shape[1]
    hidden = gate_up.shape[2]
    out_rows, ow_row, ow_order = out_full
    shares = partner.shape[0]
    part = width // shares
    anywhere = pl.BlockSpec(memory_space=pl.ANY)
    out_shape = [
        sds((2, rows, width), BF16), sds((3, rows, 2 * hidden), BF16),
        sds((rows, width), BF16),
    ]
    out_shape += [sds((rows * n // 16, width), BF16) for n in (3, 10, 3)]
    if slot == 0:
        out_shape.append(sds((rows, width), F32))
    return call(
        functools.partial(ffn_kernel, parts, ow_row, ow_order, slot),
        (1,),
        [smem(), smem(), whole(gains.shape)] + [anywhere] * (6 + parts),
        [anywhere] * len(out_shape),
        out_shape,
        scratch=[
            pltpu.VMEM((rows, width), BF16),
            pltpu.VMEM((rows, width), BF16),
            pltpu.VMEM((parts, rows, local), BF16),
            pltpu.VMEM((shares, parts * local // shares, width), BF16),
            pltpu.VMEM(gate_up.shape, BF16),
            pltpu.VMEM(down.shape, BF16),
            pltpu.VMEM((shares, 3 * part, hidden), BF16),
            pltpu.VMEM((2, rows, width), BF16),
            pltpu.VMEM((3, rows, 2 * hidden), BF16),
            pltpu.VMEM((rows, width), F32),
            pltpu.VMEM((rows, width), F32),
            pltpu.VMEM((2, rows, width), BF16),
            pltpu.SemaphoreType.DMA((7 + parts,)),
            pltpu.SemaphoreType.DMA((8,)),
        ],
        prefetch=1,
    )(index, lengths, picked, gains, tokens, cotangent, gate_up, down, partner, out_rows, *atts)


def write_shares(out, total):
    part = out.shape[-2]
    for j in range(out.shape[0]):
        out[j] = total[j * part : (j + 1) * part, :].astype(BF16)


def ffn_grad_kernel(sets, *refs):
    left = refs[:sets]
    act = refs[sets : 2 * sets]
    total = dot(left[0][0], act[0][0], TN)
    for e in range(1, sets):
        total = total + dot(left[e][0], act[e][0], TN)
    write_shares(refs[-1], total)


def ffn_grads(lefts, acts, shares):
    sets = len(lefts)
    _, rows, width = lefts[0].shape
    hidden = acts[0].shape[2] // 2
    part = width // shares
    specs = [pl.BlockSpec((1, rows, width), lambda c: (c % 3 // 2, 0, 0))] * sets
    specs += [pl.BlockSpec((1, rows, hidden), lambda c: (c % 3, 0, c // 3))] * sets
    return call(
        functools.partial(ffn_grad_kernel, sets),
        (6,),
        specs,
        pl.BlockSpec((shares, part, hidden), lambda c: (0, c, 0)),
        sds((shares, 6 * part, hidden), BF16),
    )(*lefts, *acts)


def out_grad_kernel(low_ref, *refs):
    *att_refs, out = refs
    each = out.shape[2] // att_refs[0].shape[1]
    for c in range(len(att_refs) // each):

        @pl.when(pl.program_id(0) == c)
        def _():
            rows = jnp.concatenate([ref[...] for ref in att_refs[c * each : (c + 1) * each]], axis=1)
            write_shares(out, dot(low_ref[...], rows, TN))


def out_grads(grad_low, att_own, shares, hidden):
    width = grad_low.shape[1]
    part = width // shares
    steps = len(att_own) * att_own[0].shape[1] // hidden
    return call(
        out_grad_kernel,
        (steps,),
        [whole(a.shape) for a in (grad_low, *att_own)],
        pl.BlockSpec((shares, part, hidden), lambda c: (0, c, 0)),
        sds((shares, steps * part, hidden), BF16),
    )(grad_low, *att_own)


def resid_kernel(ow_order, members, idx_ref, len_ref, weight_ref, cot_ref, resid_ref, ow_ref, gain_ref, *refs):
    parts = len(ow_order)
    gn2_refs = refs[:members]
    gr_ref, low_ref, sum_ref = refs[members : members + 3]
    g_refs = refs[members + 3 :]
    rows, width = cot_ref.shape
    local = g_refs[0].shape[1]
    step = pl.program_id(0)
    first = (idx_ref[0] * pl.num_programs(0) + step) * rows
    slot = lax.broadcasted_iota(jnp.int32, (rows, 1), 0) + first
    row_weight = jnp.where(slot < len_ref[0], weight_ref[0], 0.0)
    gn2 = gn2_refs[0][...].astype(F32)
    for ref in gn2_refs[1:]:
        gn2 = gn2 + ref[...].astype(F32)
    resid = resid_ref[...]
    factor = rms(resid)
    unit = resid * factor
    grad = cot_ref[...].astype(F32) * row_weight + norm_back(gn2, gain_ref[1:2, :], unit, factor)
    gr_ref[...] = grad
    low = grad.astype(BF16)
    low_ref[...] = low

    @pl.when(step == 0)
    def _():
        sum_ref[...] = jnp.zeros_like(sum_ref)

    sum_ref[...] += jnp.sum((gn2 * unit).reshape(rows // 8, 8, width), axis=0)
    for d in range(parts):
        piece = ow_ref.shape[1] // parts
        at = ow_order.index(d) * piece
        block = ow_ref[:, at : at + piece].reshape(local, width)
        g_refs[d][...] = dot(low, block, NT).astype(BF16)


def resid_back(index, lengths, picked, cotangent, resid, gn2s, out_full, gains, local, block=256):
    share, width = resid.shape
    parts, members = width // local, len(gn2s)
    out_rows, ow_row, ow_order = out_full
    ow_rows = parts * local // out_rows.shape[0]
    steps = share // block
    row = lambda n: pl.BlockSpec((block, n), lambda i, idx: (i, 0))
    return call(
        functools.partial(resid_kernel, ow_order, members),
        (steps,),
        [
            smem(), smem(),
            pl.BlockSpec((block, width), lambda i, idx: (idx[0] * steps + i, 0)),
            row(width),
            pl.BlockSpec((out_rows.shape[0], ow_rows, width), lambda *_: (0, ow_row // ow_rows, 0), pipeline_mode=pl.Buffered(1)),
            whole(gains.shape),
        ]
        + [row(width)] * members,
        [row(width), row(width), whole((8, width))] + [row(local)] * parts,
        [sds((share, width), F32), sds((share, width), BF16), sds((8, width), F32)]
        + [sds((share, local), BF16)] * parts,
        prefetch=1,
    )(index, lengths, picked, cotangent, resid, out_rows, gains, *gn2s)


def back_rows(grad, att, q_ref, k_ref, v_ref):
    rows = grad.shape[0]
    lane = lax.broadcasted_iota(jnp.int32, (rows, 128), 1)
    prod = grad.astype(F32) * att.astype(F32)
    zero = jnp.zeros((rows, 128), BF16)
    dqs, probs_all, scores_all, grads_own, queries_own = [], [], [], [], []
    for s in range(2):
        first = HD * (1 - s)
        own = (lane >= HD * s) & (lane < HD * (s + 1))
        delta = jnp.sum(jnp.where(own, prod, 0.0), axis=1, keepdims=True)
        hi, mid, low = split3(-delta)
        grad_own = jnp.where(own, grad, zero)
        grad_aug = jnp.where(lane == first + 2, low, grad_own)
        grad_aug = jnp.where(lane == first + 1, mid, grad_aug)
        grad_aug = jnp.where(lane == first, hi, grad_aug)
        q = q_ref[s]
        probs = jnp.exp2(dot(q, k_ref[s], NT))
        scores_grad = (probs * dot(grad_aug, v_ref[s], NT)).astype(BF16)
        probs_all.append(probs.astype(BF16))
        scores_all.append(scores_grad)
        grads_own.append(grad_own)
        queries_own.append(jnp.where(own, q, zero))
        dqs.append(dot(scores_grad, k_ref[s]))
    dv = dot(jnp.concatenate(grads_own, axis=0).T, jnp.concatenate(probs_all, axis=0))
    dk = dot(jnp.concatenate(queries_own, axis=0).T, jnp.concatenate(scores_all, axis=0))
    return jnp.where(lane < HD, dqs[0], dqs[1]), dk, dv


def rotated_back(v, cosine, sine, scale):
    return ((v * cosine - swap_halves(v) * sine) * scale).astype(BF16)


def attend_back_own_kernel(idx_ref, q_ref, k_ref, v_ref, att_ref, cos_ref, sin_ref, grad_ref, dq_ref, dk_ref, dv_ref):
    dq, dk_ref[0], dv_ref[0] = back_rows(grad_ref[...], att_ref[...], q_ref, k_ref, v_ref)
    dq_ref[...] = rotated_back(dq, cos_ref[...], sin_ref[...], FACTOR)


def attend_back_own(index, grad, q, k, v, att, cosine, sine):
    share, local = grad.shape
    pairs, rows = local // 128, q.shape[1]
    keys = pl.BlockSpec((2, rows, 128), lambda j, idx: (j, 0, 0))
    table = pl.BlockSpec((share, 128), lambda j, idx: (idx[0], 0))
    sums = pl.BlockSpec((1, 128, rows), lambda j, idx: (j, 0, 0))
    return call(
        attend_back_own_kernel,
        (pairs,),
        [
            pl.BlockSpec((2, share, 128), lambda j, idx: (j, idx[0], 0)),
            keys,
            keys,
            pl.BlockSpec((share, 128), lambda j, idx: (idx[0], j)),
            table,
            table,
            pl.BlockSpec((share, 128), lambda j, idx: (0, j)),
        ],
        [pl.BlockSpec((share, 128), lambda j, idx: (0, j)), sums, sums],
        [sds((share, local), BF16)] + [sds((pairs, 128, rows), F32)] * 2,
        prefetch=1,
    )(index, q, k, v, att, cosine, sine, grad)


def attend_back_kernel(parts, idx_ref, q_ref, k_ref, v_ref, att_ref, cos_ref, sin_ref, dq_ref, dk_ref, dv_ref, *refs):
    grad_refs = refs[: parts - 1]
    outs = refs[parts - 1 : 2 * parts - 1]
    dk_acc, dv_acc = refs[2 * parts - 1 :]
    rows = q_ref.shape[1]
    step = pl.program_id(0)
    me = idx_ref[0]

    def span(d):
        return pl.ds(pl.multiple_of((me ^ d) * rows, rows), rows)

    def back(v, d, scale):
        return rotated_back(v, cos_ref[span(d), :], sin_ref[span(d), :], scale)

    grad = grad_refs[0][...]
    for d in range(1, parts - 1):
        grad = jnp.where(step == d, grad_refs[d][...], grad)
    dq, dk, dv = back_rows(grad, att_ref[...], q_ref, k_ref, v_ref)

    @pl.when(step == 0)
    def _():
        outs[0][0] = dq_ref[...]
        dk_acc[...] = dk_ref[0] + dk
        dv_acc[...] = dv_ref[0] + dv

    @pl.when(step > 0)
    def _():
        dk_acc[...] += dk
        dv_acc[...] += dv

    for d in range(1, parts):

        @pl.when(step == d - 1)
        def _():
            outs[d][0] = back(dq, d, FACTOR)

    @pl.when(step == parts - 2)
    def _():
        for d in range(parts):
            outs[d][1] = back(dk_acc[:, span(d)].T, d, LN2)
            outs[d][2] = dv_acc[:, span(d)].T.astype(BF16)


def attend_back(index, grads, own, q, k, v, att, cosine, sine, pair):
    parts = len(grads) + 1
    share = grads[0].shape[0]
    rows = q.shape[1]
    once = pl.Buffered(1)
    keys = pl.BlockSpec((2, rows, 128), lambda i, idx: (pair, 0, 0), pipeline_mode=once)
    sums = pl.BlockSpec((1, 128, rows), lambda i, idx: (pair, 0, 0), pipeline_mode=once)
    return call(
        functools.partial(attend_back_kernel, parts),
        (parts - 1,),
        [
            pl.BlockSpec((2, share, 128), lambda i, idx: (pair, idx[0] ^ (i + 1), 0)),
            keys,
            keys,
            pl.BlockSpec((share, 128), lambda i, idx: (idx[0] ^ (i + 1), pair)),
            whole(cosine.shape),
            whole(sine.shape),
            pl.BlockSpec((share, 128), lambda i, idx: (0, pair), pipeline_mode=once),
            sums,
            sums,
        ]
        + [pl.BlockSpec((share, 128), lambda i, idx: (0, pair))] * (parts - 1),
        [whole((3, share, 128))] * parts,
        [sds((3, share, 128), BF16)] * parts,
        scratch=[pltpu.VMEM((128, rows), F32)] * 2,
        flops=2 * rows * rows * 128 * 10,
        nbytes=rows * 256 * 16,
        trans=2 * rows * rows,
        prefetch=1,
    )(index, q, k, v, att, cosine, sine, *own, *grads)


def project_grads(index, normed, acts, qkv_weight, shares, pair, prev=None):
    width = normed.shape[1]
    local = 128 * (pair + 1)
    parts = len(acts)
    share = acts[0].shape[1]
    part = width // shares
    half = (shares // 2, part, 3 * local)
    ins = []
    for d in range(parts):
        pick = functools.partial(
            lambda d, idx, ref: ref.at[pl.ds(pl.multiple_of((idx[0] ^ d) * share, share), share)], d
        )
        ins += [(normed, (share, width), pick), (acts[d], acts[d].shape, None)]
    weight_cols = pl.ds(128 * pair, 128)
    ins.append((qkv_weight, (3, width, 128), lambda idx, ref: ref.at[:, :, weight_cols]))
    if prev:
        ins += [(a, a.shape, None) for a in prev]

    def body(idx_ref, _, get, outs, put, scratch):
        away_ref, keep_ref, sum_ref = outs
        (acc,) = scratch
        for d in range(parts):
            act_ref = get(2 * d + 1)
            act = jnp.concatenate([act_ref[c] for c in range(3)], axis=1)
            term = dot(get(2 * d)[...], act, TN)
            acc[...] = acc[...] + term if d else term
        core = idx_ref[1] & 1
        before = local - 128
        for n, (ref, bit) in enumerate(((away_ref, 1 - core), (keep_ref, core))):
            for c in range(3):
                if prev:
                    ref[:, :, c * local : c * local + before] = get(2 * parts + 1 + n)[
                        :, :, c * before : (c + 1) * before
                    ]
                for j in range(shares // 2):
                    rows = pl.ds(pl.multiple_of((2 * j + bit) * part, part), part)
                    ref[j, :, c * local + before : (c + 1) * local] = acc[rows, c * 128 : (c + 1) * 128].astype(BF16)
            put(n)
        weight = get(2 * parts)
        gain_sum = acc[:, :128] * weight[0].astype(F32)
        for c in (1, 2):
            gain_sum += acc[:, c * 128 : (c + 1) * 128] * weight[c].astype(F32)
        total = jnp.broadcast_to(jnp.sum(gain_sum, axis=1, keepdims=True), sum_ref.shape)
        sum_ref[...] = total + get(2 * parts + 3)[...] if prev else total
        put(2)

    outs = [(half, BF16), (half, BF16), ((width, 128), F32)]
    return staged(body, index, [], ins, outs, 3, [pltpu.VMEM((width, 3 * 128), F32)])


def token_grad(index, tokens, grad_resid, qkv_weight, qkv_full, gains, acts, ffn_own, ffn_got):
    share, width = grad_resid.shape
    pairs, parts = len(acts), len(acts[0])
    part, hidden = ffn_got.shape[0] // 3, ffn_got.shape[1]
    local = qkv_weight.shape[2]
    ins = []
    for d in range(parts):
        ins += [(acts[j][d], acts[j][d].shape, None) for j in range(pairs)]
        if d:
            rows = pl.ds((d - 1) * 3 * part, 3 * part)
            pick = functools.partial(lambda rows, idx, ref: ref.at[:, rows], rows)
            ins.append((qkv_full, (qkv_full.shape[0], 3 * part, local), pick))
        else:
            ins.append((qkv_weight, qkv_weight.shape, None))
        if d == 0:
            ins.append((ffn_own, ffn_got.shape, lambda idx, ref: ref.at[pl.ds(0, 3 * part)]))
            ins.append((ffn_got, ffn_got.shape, None))
    ins.append((tokens, (share, width), lambda idx, ref: ref.at[pl.ds(pl.multiple_of(idx[0] * share, share), share)]))
    ins.append((grad_resid, grad_resid.shape, None))

    def body(idx_ref, smalls, get, outs, put, scratch):
        out_ref, gu_ref, down_ref = outs
        (acc,) = scratch
        at = 0
        for n in range(parts):
            group = [get(at + j) for j in range(pairs)]
            weight = get(at + pairs)
            at += pairs + 1
            act = jnp.concatenate([ref[c] for c in range(3) for ref in group], axis=1)
            cut = lambda c: weight[:, c * part : (c + 1) * part].reshape(width, local) if n else weight[c]
            weight_all = jnp.concatenate([cut(c) for c in range(3)], axis=1)
            term = dot(act, weight_all, NT)
            acc[...] = acc[...] + term if n else term
            if n == 0:
                total = get(at)[...].astype(F32) + get(at + 1)[...].astype(F32)
                at += 2
                gu_ref[0] = total[:part]
                gu_ref[1] = total[part : 2 * part]
                down_ref[...] = total[2 * part :].T
                put(1)
                put(2)
        x_ref, gr_ref = get(at), get(at + 1)
        half = share // 2
        for c in range(2):
            rows = slice(c * half, (c + 1) * half)
            x = x_ref[rows, :].astype(F32)
            factor = rms(x)
            out_ref[rows, :] = gr_ref[rows, :] + norm_back(acc[rows, :], smalls[0][0:1, :], x * factor, factor)
            put(0, pl.ds(c * half, half))

    outs = [((share, width), F32), ((2, part, hidden), F32), ((hidden, part), F32)]
    return staged(body, index, [gains], ins, outs, 4, [pltpu.VMEM((share, width), F32)])


def fold_kernel(cuts, idx_ref, *refs):
    ins, outs = list(refs[: 2 * len(cuts)]), list(refs[2 * len(cuts) :])
    for place, bit in cuts:
        keep, got = ins.pop(0), ins.pop(0)
        mine = (idx_ref[1] >> bit) & 1
        targets = ((outs.pop(0), mine), (outs.pop(0), 1 - mine))
        for j in range(keep.shape[0] // 2):
            rest = ((j >> place) << (place + 1)) | (j & ((1 << place) - 1))
            for out, value in targets:
                k = rest | (value << place)
                out[j] = (keep[k].astype(F32) + got[k].astype(F32)).astype(BF16)


def fold(index, lanes):
    ins, outs, info, total = [], [], [], 0
    for keep, got, lead, order in lanes:
        count, rows, cols = keep.shape
        ins += [(a, a.shape, None) for a in (keep, got)]
        if order:
            info.append((len(lead) - 1 - lead.index(order[0]), [b for b in lead if b != order[0]], order[1:], order[0]))
            outs += [((count // 2, rows, cols), BF16)] * 2
        total += rows
    if not info:
        outs = [((total, cols), BF16)]

    def body(idx_ref, _, get, out_refs, put, __):
        row = 0
        for n in range(len(lanes)):
            keep, got = get(2 * n), get(2 * n + 1)
            if info:
                place, _, _, bit = info[n]
                fold_kernel([(place, bit)], idx_ref, keep, got, *out_refs[2 * n : 2 * n + 2])
                put(2 * n)
                put(2 * n + 1)
            else:
                rows = keep.shape[1]
                out_refs[0][row : row + rows, :] = (keep[0].astype(F32) + got[0].astype(F32)).astype(BF16)
                put(0, pl.ds(row, rows))
                row += rows

    res = staged(body, index, [], ins, outs, max(len(outs), len(lanes)))
    if not info:
        return res[0]
    return [(res[2 * n], res[2 * n + 1]) + info[n][1:] for n in range(len(lanes))]


def pieces_kernel(part, op_ref, gains_ref, *outs):
    local = outs[0].shape[1]
    hidden = op_ref.shape[1]
    rows = (outs[0].shape[0] - part) // 3
    gains = gains_ref[...]
    wide = gains.shape[1] // local
    flat = jnp.concatenate(
        [gains[r // wide : r // wide + 1, (r % wide) * local : (r % wide + 1) * local] for r in range(rows)]
    )
    parts3 = jnp.concatenate(split3(flat))
    for d, out in enumerate(outs):
        block = d * local // hidden
        col = d * local % hidden
        row = block * part
        out[:part, :] = op_ref[row : row + part, col : col + local]
        out[part:, :] = parts3


def make_pieces(sum_op, gains, part, local, parts):
    shape = (part + 3 * gains.size // local, local)
    return call(
        functools.partial(pieces_kernel, part),
        (1,),
        [whole(sum_op.shape), whole(gains.shape)],
        [whole(shape)] * parts,
        [sds(shape, BF16)] * parts,
    )(sum_op, gains)


def finish_outputs(index, resid, own, others, keep, got, pieces):
    parts, count = len(pieces), len(others[0])
    width = resid.shape[1]
    part, local = keep.shape[1], keep.shape[2] // 3
    ins, row = [], 0
    for n, a in enumerate(own):
        rows = pl.ds(row, a.shape[0])
        ins.append((resid, a.shape, functools.partial(lambda rows, idx, ref: ref.at[rows], rows)))
        ins += [(b, a.shape, None) for b in (a, *others[n])]
        row += a.shape[0]
    ins += [(a, a.shape, None) for a in (keep, got, *pieces)]

    def body(idx_ref, _, get, outs, put, __):
        out_ref, qkv_ref, op_ref, gains_ref = outs
        at = row = 0
        for a in own:
            total = get(at)[...]
            for n in range(count + 1):
                total = total + get(at + 1 + n)[...].astype(F32)
            out_ref[row : row + a.shape[0], :] = total
            put(0, pl.ds(row, a.shape[0]))
            row += a.shape[0]
            at += count + 2
        qkv = get(at)[0].astype(F32) + get(at + 1)[0].astype(F32)
        for c in range(3):
            qkv_ref[c] = qkv[:, c * local : (c + 1) * local]
        put(1)
        piece_refs = [get(at + 2 + d) for d in range(parts)]
        rows = (piece_refs[0].shape[0] - part) // 3

        def gains_of(ref):
            hi, mid, low = (ref[part + n * rows : part + (n + 1) * rows, :].astype(F32) for n in range(3))
            return hi + mid + low

        ops = [ref[:part, :].astype(F32) for ref in piece_refs]
        gains = [gains_of(ref) for ref in piece_refs]
        while len(ops) > 1:
            ops = [ops[2 * n] + ops[2 * n + 1] for n in range(len(ops) // 2)]
            gains = [gains[2 * n] + gains[2 * n + 1] for n in range(len(gains) // 2)]
        op_ref[...] = ops[0].T
        put(2)
        wide = width // local
        for r in range(rows):
            cols = slice((r % wide) * local, (r % wide + 1) * local)
            gains_ref[r // wide : r // wide + 1, cols] = gains[0][r : r + 1, :]
        put(3)

    shapes = [resid.shape, (3, part, local), (local, part), (2, width)]
    return staged(body, index, [], ins, [(shape, F32) for shape in shapes], len(own) + 3)


def after(value, *others):
    return lax.optimization_barrier((value, *others))[0]


def body(
    tokens, qkv_weight, out_weight, gate_up_weight, down_weight, norm_gains,
    species_weight, species_ids, lengths, cotangent,
):
    rows, width = tokens.shape
    local = out_weight.shape[0]
    hidden = down_weight.shape[0]
    parts = lax.axis_size("tensor")
    slots = list(range(parts - 2, -1, -2))
    shares = lax.axis_size("dp")
    part = width // shares
    me = lax.axis_index("tensor")
    dp = lax.axis_index("dp")
    index = jnp.stack([me, dp]).astype(jnp.int32)
    cosine, sine = (jnp.asarray(t) for t in rotary_tables())
    pairs = local // 128
    valid = lengths[0] >= 0

    def region(f):
        shapes = jax.eval_shape(f)
        zeros = lambda: jax.tree.map(lambda a: jnp.zeros(a.shape, a.dtype), shapes)
        return lax.optimization_barrier(lax.cond(valid, f, zeros))

    def beside(sends, f, apart=False):
        return region(lambda: ([swap(*x) for x in sends], region(f) if apart else f()))

    def swap(a, d, name="tensor"):
        return lax.ppermute(a, name, [(i, i ^ d) for i in range(lax.axis_size(name))])

    def cut(a, start, size, axis=0):
        return lax.dynamic_slice_in_dim(a, start, size, axis)

    def outgoing(pieces):
        return [(pieces[d], d, "tensor") for d in range(1, parts)]

    bits = shares.bit_length() - 1
    lead = list(range(bits - 1, 0, -1))

    def fold_next(halves, got):
        return fold(index, [(keep, g, left, order) for (keep, _, left, order, _), g in zip(halves, got)])

    def leaving(halves):
        return [(away, 1 << bit, "dp") for _, away, _, _, bit in halves]

    matches = species_ids[:, None] == jnp.arange(species_weight.shape[0])[None, :]
    picked = jnp.sum(jnp.where(matches, species_weight[None, :], F32(0.0)), axis=1)

    ow_cut = cut(out_weight, dp * (local // shares), local // shares)
    qkv_cut = cut(qkv_weight, dp * part, part, 1).reshape(3 * part, local)
    together = hidden == width
    mine = cut_weights(index[1:], gate_up_weight, down_weight, shares, [ow_cut] if together else [])
    sends = [(ow_cut, d, "tensor") for d in range(2 if together else 1, parts)]

    (partner_cut, *ow), (q, k, v, normed) = beside(
        [(mine, 1, "tensor")] + sends,
        lambda: project(lengths, tokens, qkv_weight, norm_gains, cosine, sine),
    )
    if together:
        partner = lax.all_gather(pack([partner_cut, ow_cut, *ow]), "dp", axis=0)
        out_full = (partner, 3 * part, [1, 0] + list(range(2, parts)))
    else:
        partner = lax.all_gather(partner_cut, "dp", axis=0)
        out_full = (lax.all_gather(pack([ow_cut, *ow]), "dp", axis=0), 0, list(range(parts)))

    sends = [(after(qkv_cut, partner_cut, picked), d, "tensor") for d in range(1, parts)]
    qkv_got, (*att, att_nat, q_back) = beside(sends, lambda: attend(index, q, k, v, parts))
    rows_for = lambda e: outgoing([att[d ^ e] for d in range(parts)])
    rows_now, qkv_stack = beside(rows_for(slots[0]), lambda: pack(qkv_got))
    qkv_full = lax.all_gather(qkv_stack, "dp", axis=0)

    lefts, acts, gn2s, terms, gn2_got = {}, {}, {}, {}, {}
    tied = tokens
    for e in slots:

        def feed():
            outs = feed_forward(
                e, index, lengths, picked, [att[e]] + rows_now, tied, cotangent, out_full,
                gate_up_weight, down_weight, partner, norm_gains
            )
            if e:
                return outs
            return outs, ffn_grads([*lefts.values(), outs[0]], [*acts.values(), outs[1]], shares)

        sends = rows_for(e - 2) if e else []
        if e + 2 in gn2s:
            sends.append((gn2s[e + 2], e + 2, "tensor"))
        got, outs = beside(sends, feed)
        if e + 2 in gn2s:
            gn2_got[e + 2] = got.pop()
        if e:
            rows_now = got
        else:
            outs, wg_ffn = outs
        lefts[e], acts[e], gn2s[e], *terms[e] = outs[:6]
        tied = after(tokens, gn2s[e])
    resid = outs[6]
    gn2_all = [gn2s[0]] + [gn2_got[e] for e in slots[:-1]]

    def terms_out(i):
        return [(terms[e][i], e, "tensor") for e in slots[:-1]]

    terms_got = []
    got, (grad_resid, grad_low, gain_two, *grads) = beside(
        terms_out(0),
        lambda: resid_back(
            index, lengths, picked, cotangent, resid, gn2_all, out_full, norm_gains, local
        ),
    )
    terms_got.append(got)
    sum_ffn = lax.psum_scatter(wg_ffn, "dp", scatter_dimension=0, tiled=True)[0]
    def own_rows():
        return (
            attend_back_own(index, grads[0], q_back, k, v, att_nat, cosine, sine),
            out_grads(grad_low, [att[0]] + rows_now, shares, hidden),
        )

    grads_got, (back_own, wg_op) = beside(outgoing(grads), own_rows)

    def back(j):
        return attend_back(index, grads_got, back_own, q_back, k, v, att_nat, cosine, sine, j)

    terms_got.append([swap(after(a, wg_op), *way) for a, *way in terms_out(1)])
    group = region(lambda: back(0))
    group = after(group, *terms_got[1])
    sum_op = lax.psum_scatter(after(wg_op, qkv_full), "dp", scatter_dimension=0, tiled=True)[0]
    qkv_acts, acts_got, qkv_sums = [group], [], None
    for j in range(1, pairs):

        def back_next():
            return back(j), project_grads(index, normed, qkv_acts[-1], qkv_weight, shares, j - 1, qkv_sums)

        got, (group, qkv_sums) = beside(outgoing(group), back_next)
        acts_got.append([qkv_acts[-1][0]] + got)
        qkv_acts.append(group)
    ways = []

    def finish():
        away_q, keep_q, gain_one = project_grads(
            index, normed, qkv_acts[-1], qkv_weight, shares, pairs - 1, qkv_sums
        )
        halves = fold(index, [(keep_q, swap(away_q, 1, "dp"), lead, lead)])
        for s in range(bits - 2):
            halves = fold_next(halves, [swap(*x) for x in leaving(halves)])
        gains_grad = jnp.stack([gain_one[:, 0] / norm_gains[0], jnp.sum(gain_two, axis=0)])
        gains_grad = after(gains_grad, *[h[0] for h in halves])
        for s in range(bits):
            gains_grad = gains_grad + swap(gains_grad, 1 << s, "dp")
        ways[:] = [h[2:] for h in halves]
        return [h[:2] for h in halves], gains_grad

    got, (halves, gains_grad) = beside(outgoing(group) + [(sum_ffn[3 * part :], 1, "tensor")], finish, apart=True)
    halves = [tuple(h) + way for h, way in zip(halves, ways)]
    acts_got.append([group[0]] + got[: parts - 1])
    got_b = got[-1]
    pieces = make_pieces(sum_op, gains_grad, part, local, parts)
    got, (grad_tok, grad_gu, grad_down) = beside(
        leaving(halves) + terms_out(2) + outgoing(pieces),
        lambda: token_grad(index, tokens, grad_resid, qkv_weight, qkv_full, norm_gains, acts_got, sum_ffn, got_b),
    )
    terms_got.append(got[1 : len(slots)])
    out, grad_qkv, grad_op, gains_grad = finish_outputs(
        index, resid, terms[0], terms_got, halves[0][0], got[0], [pieces[0]] + got[len(slots) :]
    )
    return (out, grad_tok, grad_qkv, grad_op, grad_gu, grad_down, gains_grad)


def solution(mesh):
    in_specs = (
        P("dp", None),
        P(None, None, "tensor"),
        P("tensor", None),
        P(None, None, "tensor"),
        P("tensor", None),
        P(),
        P(),
        P("dp"),
        P("dp"),
        P("dp", None),
    )
    out_specs = (
        P(("dp", "tensor"), None),
        P(("dp", "tensor"), None),
        P(None, "dp", "tensor"),
        P("tensor", "dp"),
        P(None, "dp", "tensor"),
        P("tensor", "dp"),
        P(),
    )
    return jax.shard_map(body, mesh=mesh, in_specs=in_specs, out_specs=out_specs, check_vma=False)
```

```python
import functools
import math

import jax
import jax.numpy as jnp
import numpy as np
from jax import lax
from jax.experimental import pallas as pl
from jax.experimental.pallas import tpu as pltpu
from jax.sharding import PartitionSpec as P

HD = 64
WIN = 2048
EPSILON = 1e-05
NEG_FILL = -1e30
LOG2E = math.log2(math.e)
LN2 = math.log(2.0)
FACTOR = HD ** (-0.5)
VMEM = 60 * 2**20
F32 = jnp.float32
BF16 = jnp.bfloat16

NN = (((1,), (0,)), ((), ()))
NT = (((1,), (1,)), ((), ()))
TN = (((0,), (0,)), ((), ()))


def dot(a, b, dims=NN):
    return lax.dot_general(a, b, dims, preferred_element_type=F32)


def call(kernel, grid, in_specs, out_specs, out_shape, scratch=(), flops=0, nbytes=0, trans=0, prefetch=0):
    return pl.pallas_call(
        kernel,
        grid_spec=pltpu.PrefetchScalarGridSpec(
            num_scalar_prefetch=prefetch,
            grid=grid,
            in_specs=in_specs,
            out_specs=out_specs,
            scratch_shapes=list(scratch),
        ),
        out_shape=out_shape,
        compiler_params=pltpu.CompilerParams(vmem_limit_bytes=VMEM),
        cost_estimate=pl.CostEstimate(flops=flops, bytes_accessed=nbytes, transcendentals=trans),
    )


def whole(shape):
    return pl.BlockSpec(shape, lambda *_: (0,) * len(shape), pipeline_mode=pl.Buffered(1))


def staged(body, index, smalls, ins, outs, stores, scratch=()):
    n_small, n_in, n_out = len(smalls), len(ins), len(outs)

    def kernel(idx_ref, *refs):
        refs = list(refs)
        take = lambda n: [refs.pop(0) for _ in range(n)]
        small, far_in, far_out = take(n_small), take(n_in), take(n_out)
        near_in, near_out, extra = take(n_in), take(n_out), take(len(scratch))
        sem_in, sem_out = refs
        copies = []
        for n, (_, _, pick) in enumerate(ins):
            part = pick(idx_ref, far_in[n]) if pick else far_in[n]
            copies.append(pltpu.make_async_copy(part, near_in[n], sem_in.at[n]))
            copies[n].start()
        there, sent = set(), []

        def get(n):
            if n not in there:
                copies[n].wait()
                there.add(n)
            return near_in[n]

        def put(n, part=None):
            src, dst = near_out[n], far_out[n]
            if part is not None:
                src, dst = src.at[part], dst.at[part]
            copy = pltpu.make_async_copy(src, dst, sem_out.at[len(sent)])
            copy.start()
            sent.append(copy)

        body(idx_ref, small, get, near_out, put, extra)
        for n in range(n_in):
            get(n)
        for copy in sent:
            copy.wait()

    anywhere = pl.BlockSpec(memory_space=pl.ANY)
    specs = [smem() if a.ndim == 1 else whole(a.shape) for a in smalls]
    return call(
        kernel,
        (1,),
        specs + [anywhere] * n_in,
        [anywhere] * n_out,
        [sds(shape, dtype) for shape, dtype in outs],
        scratch=[pltpu.VMEM(shape, a.dtype) for a, shape, _ in ins]
        + [pltpu.VMEM(shape, dtype) for shape, dtype in outs]
        + list(scratch)
        + [pltpu.SemaphoreType.DMA((n_in,)), pltpu.SemaphoreType.DMA((stores,))],
        prefetch=1,
    )(index, *smalls, *[a for a, _, _ in ins])


def smem():
    return pl.BlockSpec(memory_space=pltpu.SMEM)


def sds(shape, dtype):
    return jax.ShapeDtypeStruct(shape, dtype)


def rotary_tables():
    position = np.arange(WIN, dtype=np.float64)
    frequency = 10000.0 ** (-2.0 * np.arange(HD // 2, dtype=np.float64) / HD)
    angles = position[:, None] * frequency[None, :]
    cosine = np.cos(angles)
    sine = np.sin(angles)
    cos_full = np.tile(np.concatenate([cosine, cosine], axis=1), (1, 2))
    sin_full = np.tile(np.concatenate([-sine, sine], axis=1), (1, 2))
    return cos_full.astype(np.float32), sin_full.astype(np.float32)


def swap_halves(v):
    lane = lax.broadcasted_iota(jnp.int32, v.shape, 1)
    return jnp.where(lane % HD < HD // 2, pltpu.roll(v, 96, 1), pltpu.roll(v, 32, 1))


def rms(x):
    return lax.rsqrt(jnp.mean(x * x, axis=-1, keepdims=True) + EPSILON)


def split3(v):
    hi = v.astype(BF16)
    rest = v - hi.astype(F32)
    mid = rest.astype(BF16)
    low = (rest - mid.astype(F32)).astype(BF16)
    return hi, mid, low


def norm_back(grad_normed, gain, unit, factor):
    scaled = grad_normed * gain
    return factor * (scaled - unit * jnp.mean(scaled * unit, axis=-1, keepdims=True))


def qkv_kernel(len_ref, x_ref, w_ref, gain_ref, cos_ref, sin_ref, q_ref, k_ref, v_ref, normed_ref):
    rows = x_ref.shape[0]
    x = x_ref[...].astype(F32)
    normed = (x * rms(x) * gain_ref[0:1, :]).astype(BF16)
    normed_ref[...] = normed
    cosine = cos_ref[...]
    sine = sin_ref[...]
    lane = lax.broadcasted_iota(jnp.int32, (rows, 128), 1)
    slot = lax.broadcasted_iota(jnp.int32, (rows, 128), 0) + pl.program_id(0) * rows
    masked = jnp.where(slot < len_ref[0], 0.0, NEG_FILL).astype(BF16)
    one = jnp.ones((rows, 128), BF16)
    zero = jnp.zeros((rows, 128), BF16)
    pairs = w_ref.shape[2] // 128
    for c in range(3):
        y = dot(normed, w_ref[c])
        for j in range(pairs):
            v = y[:, 128 * j : 128 * (j + 1)]
            if c < 2:
                v = v * cosine + swap_halves(v) * sine
            if c == 0:
                v = v * (FACTOR * LOG2E)
            v = v.astype(BF16)
            for s in range(2):
                first = HD * (1 - s)
                own = (lane >= HD * s) & (lane < HD * (s + 1))
                if c == 0:
                    q_ref[2 * j + s] = jnp.where(own, v, jnp.where(lane == first, one, zero))
                elif c == 1:
                    tail = jnp.where(
                        lane == first, masked, jnp.where(lane < first + 4, one, zero)
                    )
                    tail = jnp.where(lane < first, zero, tail)
                    k_ref[2 * j + s] = jnp.where(own, v, tail)
                else:
                    v_ref[2 * j + s] = jnp.where(own, v, one)


def project(lengths, tokens, qkv_weight, gains, cosine, sine, block=512):
    rows, width = tokens.shape
    local = qkv_weight.shape[2]
    heads = local // HD
    spec = pl.BlockSpec((heads, block, 128), lambda i: (0, i, 0))
    return call(
        qkv_kernel,
        (rows // block,),
        [
            smem(),
            pl.BlockSpec((block, width), lambda i: (i, 0)),
            whole(qkv_weight.shape),
            whole(gains.shape),
            pl.BlockSpec((block, 128), lambda i: (i, 0)),
            pl.BlockSpec((block, 128), lambda i: (i, 0)),
        ],
        [spec] * 3 + [pl.BlockSpec((block, width), lambda i: (i, 0))],
        [sds((heads, rows, 128), BF16)] * 3 + [sds((rows, width), BF16)],
    )(lengths, tokens, qkv_weight, gains, cosine, sine)


def attend_kernel(sub, parts, idx_ref, q_ref, k_ref, v_ref, *refs):
    o_refs = refs[:parts]
    nat_ref, qb_ref = refs[parts:]
    rows = q_ref.shape[1]
    lane = lax.broadcasted_iota(jnp.int32, (sub, 128), 1)
    for r in range(rows // sub):
        part = slice(r * sub, (r + 1) * sub)
        outs = []
        for s in range(2):
            q = q_ref[s, part, :]
            scores = dot(q, k_ref[s], NT)
            peak = jnp.max(scores, axis=1, keepdims=True)
            expo = jnp.exp2(scores - peak).astype(BF16)
            acc = dot(expo, v_ref[s])
            outs.append(acc / pltpu.roll(acc, HD, 1))
            first = HD * (1 - s)
            total = jnp.where((lane >= first) & (lane < first + HD), acc, 1.0)
            hi, mid, low = split3(-(peak + jnp.log2(total)))
            tail = jnp.where(lane == first + 3, low, q)
            tail = jnp.where(lane == first + 2, mid, tail)
            qb_ref[s, part, :] = jnp.where(lane == first + 1, hi, tail)
        nat_ref[part, :] = jnp.where(lane < HD, outs[0], outs[1]).astype(BF16)
    for d in range(parts):

        @pl.when(pl.program_id(1) == d)
        def _():
            o_refs[d][...] = nat_ref[...]


def attend(index, q, k, v, parts, sub=256):
    heads, rows, _ = q.shape
    keys = k.shape[1]
    share = rows // parts
    local = heads * HD
    return call(
        functools.partial(attend_kernel, min(sub, share), parts),
        (heads // 2, parts),
        [
            pl.BlockSpec((2, share, 128), lambda j, i, idx: (j, idx[0] ^ i, 0)),
            pl.BlockSpec((2, keys, 128), lambda j, i, idx: (j, 0, 0)),
            pl.BlockSpec((2, keys, 128), lambda j, i, idx: (j, 0, 0)),
        ],
        [pl.BlockSpec((share, 128), lambda j, i, idx: (0, j))] * parts
        + [
            pl.BlockSpec((share, 128), lambda j, i, idx: (idx[0] ^ i, j)),
            pl.BlockSpec((2, share, 128), lambda j, i, idx: (j, idx[0] ^ i, 0)),
        ],
        [sds((share, local), BF16)] * parts + [sds((rows, local), BF16), sds((heads, rows, 128), BF16)],
        prefetch=1,
    )(index, q, k, v)


def cut_kernel(idx_ref, gu_ref, dw_ref, *refs):
    part = gu_ref.shape[1]
    out_ref = refs[-1]
    out_ref[:part, :] = gu_ref[0]
    out_ref[part : 2 * part, :] = gu_ref[1]
    out_ref[2 * part : 3 * part, :] = dw_ref[...].T
    if len(refs) > 1:
        out_ref[3 * part :, :] = refs[0][...]


def cut_weights(dp, gate_up, down, shares, more):
    _, width, hidden = gate_up.shape
    part = width // shares
    if part % 128:
        down = lax.dynamic_slice_in_dim(down, dp[0] * part, part, 1)
        spec = whole(down.shape)
    else:
        spec = pl.BlockSpec((hidden, part), lambda i, idx: (0, idx[0]))
    shape = (3 * part + sum(a.shape[0] for a in more), hidden)
    return call(
        cut_kernel,
        (1,),
        [pl.BlockSpec((2, part, hidden), lambda i, idx: (0, idx[0], 0)), spec] + [whole(a.shape) for a in more],
        whole(shape),
        sds(shape, BF16),
        prefetch=1,
    )(dp, gate_up, down, *more)


def pack_kernel(*refs):
    out_ref, row = refs[-1], 0
    for ref in refs[:-1]:
        out_ref[row : row + ref.shape[0], :] = ref[...]
        row += ref.shape[0]


def pack(arrays):
    shape = (sum(a.shape[0] for a in arrays), arrays[0].shape[1])
    return call(pack_kernel, (1,), [whole(a.shape) for a in arrays], whole(shape), sds(shape, BF16))(*arrays)


def ffn_kernel(parts, ow_row, ow_order, slot, idx_ref, len_ref, weight_ref, gain_ref, x_h, cot_h, gu_h, dw_h, pb_h, ow_h, *refs):
    own = slot == 0
    att_h = refs[:parts]
    refs = refs[parts:]
    count = 7 if own else 6
    outs, scratch = refs[:count], refs[count:]
    x_v, cot_v, att_v, ow_v, gu_v, dw_v, pb_v, left_v, act_v, ffn_v, gn2_v, low_v, sem_in, sem_out = scratch
    rows, width = x_v.shape
    local = att_v.shape[2]
    hidden_units = gu_v.shape[2]
    part = pb_v.shape[1] // 3
    row0 = pl.multiple_of((idx_ref[0] ^ slot) * rows, rows)
    mine = pl.ds(row0, rows)

    def fetch(src, dst, i):
        copy = pltpu.make_async_copy(src, dst, sem_in.at[i])
        copy.start()
        return copy

    pending = []

    def store(src, dst, i):
        copy = pltpu.make_async_copy(src, dst, sem_out.at[i])
        copy.start()
        pending.append(copy)

    get_x = fetch(x_h.at[mine], x_v, 0)
    get_ow = fetch(ow_h.at[:, pl.ds(ow_row, ow_v.shape[1])], ow_v, 6 + parts)
    get_att = [fetch(att_h[d], att_v.at[d], 2 + d) for d in range(parts)]
    get_cot = fetch(cot_h.at[mine], cot_v, 2 + parts)
    get_gu = fetch(gu_h, gu_v, 3 + parts)
    get_dw = fetch(dw_h, dw_v, 4 + parts)
    get_pb = fetch(pb_h.at[:, pl.ds(0, pb_v.shape[1])], pb_v, 1)

    get_x.wait()
    get_ow.wait()
    piece = ow_v.shape[1] // parts
    for copy in get_att:
        copy.wait()
    att = jnp.concatenate([att_v[d] for d in ow_order], axis=1)
    out_w = [ow_v[:, n * piece : (n + 1) * piece].reshape(local, width) for n in range(parts)]
    resid = x_v[...].astype(F32) + dot(att, jnp.concatenate(out_w, axis=0))
    if own:
        ffn_v[...] = resid
        store(ffn_v, outs[6], 4)
    normed = (resid * rms(resid) * gain_ref[1:2, :]).astype(BF16)
    left_v[0] = normed
    position = lax.broadcasted_iota(jnp.int32, (rows, 1), 0) + row0
    row_weight = jnp.where(position < len_ref[0], weight_ref[0], 0.0)
    get_cot.wait()
    left_v[1] = (cot_v[...].astype(F32) * row_weight).astype(BF16)
    store(left_v, outs[0], 0)
    for shard in range(2):
        cols = slice(shard * hidden_units, (shard + 1) * hidden_units)
        if shard == 0:
            get_gu.wait()
            get_dw.wait()
            gate_w, up_w, down_w = gu_v[0], gu_v[1], dw_v[...]
        else:
            get_pb.wait()
            gate_w, up_w, down_w = (
                pb_v[:, c * part : (c + 1) * part, :].reshape(width, hidden_units) for c in range(3)
            )
        gate = dot(left_v[0], gate_w)
        upper = dot(left_v[0], up_w)
        grad_hidden = dot(left_v[1], down_w, NT if shard == 0 else NN)
        sigma = 0.5 + 0.5 * jnp.tanh(0.5 * gate)
        act = gate * sigma
        hidden = (act * upper).astype(BF16)
        grad_up = (grad_hidden * act).astype(BF16)
        grad_gate = (grad_hidden * upper * (sigma + act * (1.0 - sigma))).astype(BF16)
        act_v[0, :, cols] = grad_gate
        act_v[1, :, cols] = grad_up
        act_v[2, :, cols] = hidden
        store(act_v.at[:, :, cols], outs[1].at[:, :, cols], 1 + 4 * shard)
        grad = dot(
            jnp.concatenate([grad_gate, grad_up], axis=1), jnp.concatenate([gate_w, up_w], axis=1), NT
        )
        term = dot(hidden, down_w, NN if shard == 0 else NT)
        if shard == 0:
            gn2_v[...] = grad
            if own:
                pending.pop(0).wait()
            ffn_v[...] = term
        else:
            low_v[0] = (gn2_v[...] + grad).astype(BF16)
            store(low_v.at[0], outs[2], 2)
            low_v[1] = (ffn_v[...] + term).astype(BF16)
            row = 0
            for n in range(3):
                size = outs[3 + n].shape[0]
                store(low_v.at[1, pl.ds(row, size)], outs[3 + n], (3, 6, 7)[n])
                row += size
    for copy in pending:
        copy.wait()


def feed_forward(slot, index, lengths, picked, atts, tokens, cotangent, out_full, gate_up, down, partner, gains):
    parts = len(atts)
    rows, local = atts[0].shape
    width = tokens.shape[1]
    hidden = gate_up.shape[2]
    out_rows, ow_row, ow_order = out_full
    shares = partner.shape[0]
    part = width // shares
    anywhere = pl.BlockSpec(memory_space=pl.ANY)
    out_shape = [
        sds((2, rows, width), BF16), sds((3, rows, 2 * hidden), BF16),
        sds((rows, width), BF16),
    ]
    out_shape += [sds((rows * n // 16, width), BF16) for n in (3, 10, 3)]
    if slot == 0:
        out_shape.append(sds((rows, width), F32))
    return call(
        functools.partial(ffn_kernel, parts, ow_row, ow_order, slot),
        (1,),
        [smem(), smem(), whole(gains.shape)] + [anywhere] * (6 + parts),
        [anywhere] * len(out_shape),
        out_shape,
        scratch=[
            pltpu.VMEM((rows, width), BF16),
            pltpu.VMEM((rows, width), BF16),
            pltpu.VMEM((parts, rows, local), BF16),
            pltpu.VMEM((shares, parts * local // shares, width), BF16),
            pltpu.VMEM(gate_up.shape, BF16),
            pltpu.VMEM(down.shape, BF16),
            pltpu.VMEM((shares, 3 * part, hidden), BF16),
            pltpu.VMEM((2, rows, width), BF16),
            pltpu.VMEM((3, rows, 2 * hidden), BF16),
            pltpu.VMEM((rows, width), F32),
            pltpu.VMEM((rows, width), F32),
            pltpu.VMEM((2, rows, width), BF16),
            pltpu.SemaphoreType.DMA((7 + parts,)),
            pltpu.SemaphoreType.DMA((8,)),
        ],
        prefetch=1,
    )(index, lengths, picked, gains, tokens, cotangent, gate_up, down, partner, out_rows, *atts)


def write_shares(out, total):
    part = out.shape[-2]
    for j in range(out.shape[0]):
        out[j] = total[j * part : (j + 1) * part, :].astype(BF16)


def ffn_grad_kernel(sets, *refs):
    left = refs[:sets]
    act = refs[sets : 2 * sets]
    total = dot(left[0][0], act[0][0], TN)
    for e in range(1, sets):
        total = total + dot(left[e][0], act[e][0], TN)
    write_shares(refs[-1], total)


def ffn_grads(lefts, acts, shares):
    sets = len(lefts)
    _, rows, width = lefts[0].shape
    hidden = acts[0].shape[2] // 2
    part = width // shares
    specs = [pl.BlockSpec((1, rows, width), lambda c: (c % 3 // 2, 0, 0))] * sets
    specs += [pl.BlockSpec((1, rows, hidden), lambda c: (c % 3, 0, c // 3))] * sets
    return call(
        functools.partial(ffn_grad_kernel, sets),
        (6,),
        specs,
        pl.BlockSpec((shares, part, hidden), lambda c: (0, c, 0)),
        sds((shares, 6 * part, hidden), BF16),
    )(*lefts, *acts)


def out_grad_kernel(low_ref, *refs):
    *att_refs, out = refs
    each = out.shape[2] // att_refs[0].shape[1]
    for c in range(len(att_refs) // each):

        @pl.when(pl.program_id(0) == c)
        def _():
            rows = jnp.concatenate([ref[...] for ref in att_refs[c * each : (c + 1) * each]], axis=1)
            write_shares(out, dot(low_ref[...], rows, TN))


def out_grads(grad_low, att_own, shares, hidden):
    width = grad_low.shape[1]
    part = width // shares
    steps = len(att_own) * att_own[0].shape[1] // hidden
    return call(
        out_grad_kernel,
        (steps,),
        [whole(a.shape) for a in (grad_low, *att_own)],
        pl.BlockSpec((shares, part, hidden), lambda c: (0, c, 0)),
        sds((shares, steps * part, hidden), BF16),
    )(grad_low, *att_own)


def resid_kernel(ow_order, members, idx_ref, len_ref, weight_ref, cot_ref, resid_ref, ow_ref, gain_ref, *refs):
    parts = len(ow_order)
    gn2_refs = refs[:members]
    gr_ref, low_ref, sum_ref = refs[members : members + 3]
    g_refs = refs[members + 3 :]
    rows, width = cot_ref.shape
    local = g_refs[0].shape[1]
    step = pl.program_id(0)
    first = (idx_ref[0] * pl.num_programs(0) + step) * rows
    slot = lax.broadcasted_iota(jnp.int32, (rows, 1), 0) + first
    row_weight = jnp.where(slot < len_ref[0], weight_ref[0], 0.0)
    gn2 = gn2_refs[0][...].astype(F32)
    for ref in gn2_refs[1:]:
        gn2 = gn2 + ref[...].astype(F32)
    resid = resid_ref[...]
    factor = rms(resid)
    unit = resid * factor
    grad = cot_ref[...].astype(F32) * row_weight + norm_back(gn2, gain_ref[1:2, :], unit, factor)
    gr_ref[...] = grad
    low = grad.astype(BF16)
    low_ref[...] = low

    @pl.when(step == 0)
    def _():
        sum_ref[...] = jnp.zeros_like(sum_ref)

    sum_ref[...] += jnp.sum((gn2 * unit).reshape(rows // 8, 8, width), axis=0)
    for d in range(parts):
        piece = ow_ref.shape[1] // parts
        at = ow_order.index(d) * piece
        block = ow_ref[:, at : at + piece].reshape(local, width)
        g_refs[d][...] = dot(low, block, NT).astype(BF16)


def resid_back(index, lengths, picked, cotangent, resid, gn2s, out_full, gains, local, block=256):
    share, width = resid.shape
    parts, members = width // local, len(gn2s)
    out_rows, ow_row, ow_order = out_full
    ow_rows = parts * local // out_rows.shape[0]
    steps = share // block
    row = lambda n: pl.BlockSpec((block, n), lambda i, idx: (i, 0))
    return call(
        functools.partial(resid_kernel, ow_order, members),
        (steps,),
        [
            smem(), smem(),
            pl.BlockSpec((block, width), lambda i, idx: (idx[0] * steps + i, 0)),
            row(width),
            pl.BlockSpec((out_rows.shape[0], ow_rows, width), lambda *_: (0, ow_row // ow_rows, 0), pipeline_mode=pl.Buffered(1)),
            whole(gains.shape),
        ]
        + [row(width)] * members,
        [row(width), row(width), whole((8, width))] + [row(local)] * parts,
        [sds((share, width), F32), sds((share, width), BF16), sds((8, width), F32)]
        + [sds((share, local), BF16)] * parts,
        prefetch=1,
    )(index, lengths, picked, cotangent, resid, out_rows, gains, *gn2s)


def back_rows(grad, att, q_ref, k_ref, v_ref):
    rows = grad.shape[0]
    lane = lax.broadcasted_iota(jnp.int32, (rows, 128), 1)
    prod = grad.astype(F32) * att.astype(F32)
    zero = jnp.zeros((rows, 128), BF16)
    dqs, probs_all, scores_all, grads_own, queries_own = [], [], [], [], []
    for s in range(2):
        first = HD * (1 - s)
        own = (lane >= HD * s) & (lane < HD * (s + 1))
        delta = jnp.sum(jnp.where(own, prod, 0.0), axis=1, keepdims=True)
        hi, mid, low = split3(-delta)
        grad_own = jnp.where(own, grad, zero)
        grad_aug = jnp.where(lane == first + 2, low, grad_own)
        grad_aug = jnp.where(lane == first + 1, mid, grad_aug)
        grad_aug = jnp.where(lane == first, hi, grad_aug)
        q = q_ref[s]
        probs = jnp.exp2(dot(q, k_ref[s], NT))
        scores_grad = (probs * dot(grad_aug, v_ref[s], NT)).astype(BF16)
        probs_all.append(probs.astype(BF16))
        scores_all.append(scores_grad)
        grads_own.append(grad_own)
        queries_own.append(jnp.where(own, q, zero))
        dqs.append(dot(scores_grad, k_ref[s]))
    dv = dot(jnp.concatenate(grads_own, axis=0).T, jnp.concatenate(probs_all, axis=0))
    dk = dot(jnp.concatenate(queries_own, axis=0).T, jnp.concatenate(scores_all, axis=0))
    return jnp.where(lane < HD, dqs[0], dqs[1]), dk, dv


def rotated_back(v, cosine, sine, scale):
    return ((v * cosine - swap_halves(v) * sine) * scale).astype(BF16)


def attend_back_own_kernel(idx_ref, q_ref, k_ref, v_ref, att_ref, cos_ref, sin_ref, grad_ref, dq_ref, dk_ref, dv_ref):
    dq, dk_ref[0], dv_ref[0] = back_rows(grad_ref[...], att_ref[...], q_ref, k_ref, v_ref)
    dq_ref[...] = rotated_back(dq, cos_ref[...], sin_ref[...], FACTOR)


def attend_back_own(index, grad, q, k, v, att, cosine, sine):
    share, local = grad.shape
    pairs, rows = local // 128, q.shape[1]
    keys = pl.BlockSpec((2, rows, 128), lambda j, idx: (j, 0, 0))
    table = pl.BlockSpec((share, 128), lambda j, idx: (idx[0], 0))
    sums = pl.BlockSpec((1, 128, rows), lambda j, idx: (j, 0, 0))
    return call(
        attend_back_own_kernel,
        (pairs,),
        [
            pl.BlockSpec((2, share, 128), lambda j, idx: (j, idx[0], 0)),
            keys,
            keys,
            pl.BlockSpec((share, 128), lambda j, idx: (idx[0], j)),
            table,
            table,
            pl.BlockSpec((share, 128), lambda j, idx: (0, j)),
        ],
        [pl.BlockSpec((share, 128), lambda j, idx: (0, j)), sums, sums],
        [sds((share, local), BF16)] + [sds((pairs, 128, rows), F32)] * 2,
        prefetch=1,
    )(index, q, k, v, att, cosine, sine, grad)


def attend_back_kernel(parts, idx_ref, q_ref, k_ref, v_ref, att_ref, cos_ref, sin_ref, dq_ref, dk_ref, dv_ref, *refs):
    grad_refs = refs[: parts - 1]
    outs = refs[parts - 1 : 2 * parts - 1]
    dk_acc, dv_acc = refs[2 * parts - 1 :]
    rows = q_ref.shape[1]
    step = pl.program_id(0)
    me = idx_ref[0]

    def span(d):
        return pl.ds(pl.multiple_of((me ^ d) * rows, rows), rows)

    def back(v, d, scale):
        return rotated_back(v, cos_ref[span(d), :], sin_ref[span(d), :], scale)

    grad = grad_refs[0][...]
    for d in range(1, parts - 1):
        grad = jnp.where(step == d, grad_refs[d][...], grad)
    dq, dk, dv = back_rows(grad, att_ref[...], q_ref, k_ref, v_ref)

    @pl.when(step == 0)
    def _():
        outs[0][0] = dq_ref[...]
        dk_acc[...] = dk_ref[0] + dk
        dv_acc[...] = dv_ref[0] + dv

    @pl.when(step > 0)
    def _():
        dk_acc[...] += dk
        dv_acc[...] += dv

    for d in range(1, parts):

        @pl.when(step == d - 1)
        def _():
            outs[d][0] = back(dq, d, FACTOR)

    @pl.when(step == parts - 2)
    def _():
        for d in range(parts):
            outs[d][1] = back(dk_acc[:, span(d)].T, d, LN2)
            outs[d][2] = dv_acc[:, span(d)].T.astype(BF16)


def attend_back(index, grads, own, q, k, v, att, cosine, sine, pair):
    parts = len(grads) + 1
    share = grads[0].shape[0]
    rows = q.shape[1]
    once = pl.Buffered(1)
    keys = pl.BlockSpec((2, rows, 128), lambda i, idx: (pair, 0, 0), pipeline_mode=once)
    sums = pl.BlockSpec((1, 128, rows), lambda i, idx: (pair, 0, 0), pipeline_mode=once)
    return call(
        functools.partial(attend_back_kernel, parts),
        (parts - 1,),
        [
            pl.BlockSpec((2, share, 128), lambda i, idx: (pair, idx[0] ^ (i + 1), 0)),
            keys,
            keys,
            pl.BlockSpec((share, 128), lambda i, idx: (idx[0] ^ (i + 1), pair)),
            whole(cosine.shape),
            whole(sine.shape),
            pl.BlockSpec((share, 128), lambda i, idx: (0, pair), pipeline_mode=once),
            sums,
            sums,
        ]
        + [pl.BlockSpec((share, 128), lambda i, idx: (0, pair))] * (parts - 1),
        [whole((3, share, 128))] * parts,
        [sds((3, share, 128), BF16)] * parts,
        scratch=[pltpu.VMEM((128, rows), F32)] * 2,
        flops=2 * rows * rows * 128 * 10,
        nbytes=rows * 256 * 16,
        trans=2 * rows * rows,
        prefetch=1,
    )(index, q, k, v, att, cosine, sine, *own, *grads)


def project_grads(index, normed, acts, qkv_weight, shares, pair, prev=None):
    width = normed.shape[1]
    local = 128 * (pair + 1)
    parts = len(acts)
    share = acts[0].shape[1]
    part = width // shares
    half = (shares // 2, part, 3 * local)
    ins = []
    for d in range(parts):
        pick = functools.partial(
            lambda d, idx, ref: ref.at[pl.ds(pl.multiple_of((idx[0] ^ d) * share, share), share)], d
        )
        ins += [(normed, (share, width), pick), (acts[d], acts[d].shape, None)]
    weight_cols = pl.ds(128 * pair, 128)
    ins.append((qkv_weight, (3, width, 128), lambda idx, ref: ref.at[:, :, weight_cols]))
    if prev:
        ins += [(a, a.shape, None) for a in prev]

    def body(idx_ref, _, get, outs, put, scratch):
        away_ref, keep_ref, sum_ref = outs
        (acc,) = scratch
        for d in range(parts):
            act_ref = get(2 * d + 1)
            act = jnp.concatenate([act_ref[c] for c in range(3)], axis=1)
            term = dot(get(2 * d)[...], act, TN)
            acc[...] = acc[...] + term if d else term
        core = idx_ref[1] & 1
        before = local - 128
        for n, (ref, bit) in enumerate(((away_ref, 1 - core), (keep_ref, core))):
            for c in range(3):
                if prev:
                    ref[:, :, c * local : c * local + before] = get(2 * parts + 1 + n)[
                        :, :, c * before : (c + 1) * before
                    ]
                for j in range(shares // 2):
                    rows = pl.ds(pl.multiple_of((2 * j + bit) * part, part), part)
                    ref[j, :, c * local + before : (c + 1) * local] = acc[rows, c * 128 : (c + 1) * 128].astype(BF16)
            put(n)
        weight = get(2 * parts)
        gain_sum = acc[:, :128] * weight[0].astype(F32)
        for c in (1, 2):
            gain_sum += acc[:, c * 128 : (c + 1) * 128] * weight[c].astype(F32)
        total = jnp.broadcast_to(jnp.sum(gain_sum, axis=1, keepdims=True), sum_ref.shape)
        sum_ref[...] = total + get(2 * parts + 3)[...] if prev else total
        put(2)

    outs = [(half, BF16), (half, BF16), ((width, 128), F32)]
    return staged(body, index, [], ins, outs, 3, [pltpu.VMEM((width, 3 * 128), F32)])


def token_grad(index, tokens, grad_resid, qkv_weight, qkv_full, gains, acts, ffn_own, ffn_got):
    share, width = grad_resid.shape
    pairs, parts = len(acts), len(acts[0])
    part, hidden = ffn_got.shape[0] // 3, ffn_got.shape[1]
    local = qkv_weight.shape[2]
    ins = []
    for d in range(parts):
        ins += [(acts[j][d], acts[j][d].shape, None) for j in range(pairs)]
        if d:
            rows = pl.ds((d - 1) * 3 * part, 3 * part)
            pick = functools.partial(lambda rows, idx, ref: ref.at[:, rows], rows)
            ins.append((qkv_full, (qkv_full.shape[0], 3 * part, local), pick))
        else:
            ins.append((qkv_weight, qkv_weight.shape, None))
        if d == 0:
            ins.append((ffn_own, ffn_got.shape, lambda idx, ref: ref.at[pl.ds(0, 3 * part)]))
            ins.append((ffn_got, ffn_got.shape, None))
    ins.append((tokens, (share, width), lambda idx, ref: ref.at[pl.ds(pl.multiple_of(idx[0] * share, share), share)]))
    ins.append((grad_resid, grad_resid.shape, None))

    def body(idx_ref, smalls, get, outs, put, scratch):
        out_ref, gu_ref, down_ref = outs
        (acc,) = scratch
        at = 0
        for n in range(parts):
            group = [get(at + j) for j in range(pairs)]
            weight = get(at + pairs)
            at += pairs + 1
            act = jnp.concatenate([ref[c] for c in range(3) for ref in group], axis=1)
            cut = lambda c: weight[:, c * part : (c + 1) * part].reshape(width, local) if n else weight[c]
            weight_all = jnp.concatenate([cut(c) for c in range(3)], axis=1)
            term = dot(act, weight_all, NT)
            acc[...] = acc[...] + term if n else term
            if n == 0:
                total = get(at)[...].astype(F32) + get(at + 1)[...].astype(F32)
                at += 2
                gu_ref[0] = total[:part]
                gu_ref[1] = total[part : 2 * part]
                down_ref[...] = total[2 * part :].T
                put(1)
                put(2)
        x_ref, gr_ref = get(at), get(at + 1)
        half = share // 2
        for c in range(2):
            rows = slice(c * half, (c + 1) * half)
            x = x_ref[rows, :].astype(F32)
            factor = rms(x)
            out_ref[rows, :] = gr_ref[rows, :] + norm_back(acc[rows, :], smalls[0][0:1, :], x * factor, factor)
            put(0, pl.ds(c * half, half))

    outs = [((share, width), F32), ((2, part, hidden), F32), ((hidden, part), F32)]
    return staged(body, index, [gains], ins, outs, 4, [pltpu.VMEM((share, width), F32)])


def fold_kernel(cuts, idx_ref, *refs):
    ins, outs = list(refs[: 2 * len(cuts)]), list(refs[2 * len(cuts) :])
    for place, bit in cuts:
        keep, got = ins.pop(0), ins.pop(0)
        mine = (idx_ref[1] >> bit) & 1
        targets = ((outs.pop(0), mine), (outs.pop(0), 1 - mine))
        for j in range(keep.shape[0] // 2):
            rest = ((j >> place) << (place + 1)) | (j & ((1 << place) - 1))
            for out, value in targets:
                k = rest | (value << place)
                out[j] = (keep[k].astype(F32) + got[k].astype(F32)).astype(BF16)


def fold(index, lanes):
    ins, outs, info, total = [], [], [], 0
    for keep, got, lead, order in lanes:
        count, rows, cols = keep.shape
        ins += [(a, a.shape, None) for a in (keep, got)]
        if order:
            info.append((len(lead) - 1 - lead.index(order[0]), [b for b in lead if b != order[0]], order[1:], order[0]))
            outs += [((count // 2, rows, cols), BF16)] * 2
        total += rows
    if not info:
        outs = [((total, cols), BF16)]

    def body(idx_ref, _, get, out_refs, put, __):
        row = 0
        for n in range(len(lanes)):
            keep, got = get(2 * n), get(2 * n + 1)
            if info:
                place, _, _, bit = info[n]
                fold_kernel([(place, bit)], idx_ref, keep, got, *out_refs[2 * n : 2 * n + 2])
                put(2 * n)
                put(2 * n + 1)
            else:
                rows = keep.shape[1]
                out_refs[0][row : row + rows, :] = (keep[0].astype(F32) + got[0].astype(F32)).astype(BF16)
                put(0, pl.ds(row, rows))
                row += rows

    res = staged(body, index, [], ins, outs, max(len(outs), len(lanes)))
    if not info:
        return res[0]
    return [(res[2 * n], res[2 * n + 1]) + info[n][1:] for n in range(len(lanes))]


def pieces_kernel(part, op_ref, gains_ref, *outs):
    local = outs[0].shape[1]
    hidden = op_ref.shape[1]
    rows = (outs[0].shape[0] - part) // 3
    gains = gains_ref[...]
    wide = gains.shape[1] // local
    flat = jnp.concatenate(
        [gains[r // wide : r // wide + 1, (r % wide) * local : (r % wide + 1) * local] for r in range(rows)]
    )
    parts3 = jnp.concatenate(split3(flat))
    for d, out in enumerate(outs):
        block = d * local // hidden
        col = d * local % hidden
        row = block * part
        out[:part, :] = op_ref[row : row + part, col : col + local]
        out[part:, :] = parts3


def make_pieces(sum_op, gains, part, local, parts):
    shape = (part + 3 * gains.size // local, local)
    return call(
        functools.partial(pieces_kernel, part),
        (1,),
        [whole(sum_op.shape), whole(gains.shape)],
        [whole(shape)] * parts,
        [sds(shape, BF16)] * parts,
    )(sum_op, gains)


def finish_outputs(index, resid, own, others, keep, got, pieces):
    parts, count = len(pieces), len(others[0])
    width = resid.shape[1]
    part, local = keep.shape[1], keep.shape[2] // 3
    ins, row = [], 0
    for n, a in enumerate(own):
        rows = pl.ds(row, a.shape[0])
        ins.append((resid, a.shape, functools.partial(lambda rows, idx, ref: ref.at[rows], rows)))
        ins += [(b, a.shape, None) for b in (a, *others[n])]
        row += a.shape[0]
    ins += [(a, a.shape, None) for a in (keep, got, *pieces)]

    def body(idx_ref, _, get, outs, put, __):
        out_ref, qkv_ref, op_ref, gains_ref = outs
        at = row = 0
        for a in own:
            total = get(at)[...]
            for n in range(count + 1):
                total = total + get(at + 1 + n)[...].astype(F32)
            out_ref[row : row + a.shape[0], :] = total
            put(0, pl.ds(row, a.shape[0]))
            row += a.shape[0]
            at += count + 2
        qkv = get(at)[0].astype(F32) + get(at + 1)[0].astype(F32)
        for c in range(3):
            qkv_ref[c] = qkv[:, c * local : (c + 1) * local]
        put(1)
        piece_refs = [get(at + 2 + d) for d in range(parts)]
        rows = (piece_refs[0].shape[0] - part) // 3

        def gains_of(ref):
            hi, mid, low = (ref[part + n * rows : part + (n + 1) * rows, :].astype(F32) for n in range(3))
            return hi + mid + low

        ops = [ref[:part, :].astype(F32) for ref in piece_refs]
        gains = [gains_of(ref) for ref in piece_refs]
        while len(ops) > 1:
            ops = [ops[2 * n] + ops[2 * n + 1] for n in range(len(ops) // 2)]
            gains = [gains[2 * n] + gains[2 * n + 1] for n in range(len(gains) // 2)]
        op_ref[...] = ops[0].T
        put(2)
        wide = width // local
        for r in range(rows):
            cols = slice((r % wide) * local, (r % wide + 1) * local)
            gains_ref[r // wide : r // wide + 1, cols] = gains[0][r : r + 1, :]
        put(3)

    shapes = [resid.shape, (3, part, local), (local, part), (2, width)]
    return staged(body, index, [], ins, [(shape, F32) for shape in shapes], len(own) + 3)


def after(value, *others):
    return lax.optimization_barrier((value, *others))[0]


def body(
    tokens, qkv_weight, out_weight, gate_up_weight, down_weight, norm_gains,
    species_weight, species_ids, lengths, cotangent,
):
    rows, width = tokens.shape
    local = out_weight.shape[0]
    hidden = down_weight.shape[0]
    parts = lax.axis_size("tensor")
    slots = list(range(parts - 2, -1, -2))
    shares = lax.axis_size("dp")
    part = width // shares
    me = lax.axis_index("tensor")
    dp = lax.axis_index("dp")
    index = jnp.stack([me, dp]).astype(jnp.int32)
    cosine, sine = (jnp.asarray(t) for t in rotary_tables())
    pairs = local // 128
    valid = lengths[0] >= 0

    def region(f):
        shapes = jax.eval_shape(f)
        zeros = lambda: jax.tree.map(lambda a: jnp.zeros(a.shape, a.dtype), shapes)
        return lax.optimization_barrier(lax.cond(valid, f, zeros))

    def beside(sends, f, apart=False):
        return region(lambda: ([swap(*x) for x in sends], region(f) if apart else f()))

    def swap(a, d, name="tensor"):
        return lax.ppermute(a, name, [(i, i ^ d) for i in range(lax.axis_size(name))])

    def cut(a, start, size, axis=0):
        return lax.dynamic_slice_in_dim(a, start, size, axis)

    def outgoing(pieces):
        return [(pieces[d], d, "tensor") for d in range(1, parts)]

    bits = shares.bit_length() - 1
    lead = list(range(bits - 1, 0, -1))

    def fold_next(halves, got):
        return fold(index, [(keep, g, left, order) for (keep, _, left, order, _), g in zip(halves, got)])

    def leaving(halves):
        return [(away, 1 << bit, "dp") for _, away, _, _, bit in halves]

    matches = species_ids[:, None] == jnp.arange(species_weight.shape[0])[None, :]
    picked = jnp.sum(jnp.where(matches, species_weight[None, :], F32(0.0)), axis=1)

    ow_cut = cut(out_weight, dp * (local // shares), local // shares)
    qkv_cut = cut(qkv_weight, dp * part, part, 1).reshape(3 * part, local)
    together = hidden == width
    mine = cut_weights(index[1:], gate_up_weight, down_weight, shares, [ow_cut] if together else [])
    sends = [(ow_cut, d, "tensor") for d in range(2 if together else 1, parts)]

    (partner_cut, *ow), (q, k, v, normed) = beside(
        [(mine, 1, "tensor")] + sends,
        lambda: project(lengths, tokens, qkv_weight, norm_gains, cosine, sine),
    )
    if together:
        partner = lax.all_gather(pack([partner_cut, ow_cut, *ow]), "dp", axis=0)
        out_full = (partner, 3 * part, [1, 0] + list(range(2, parts)))
    else:
        partner = lax.all_gather(partner_cut, "dp", axis=0)
        out_full = (lax.all_gather(pack([ow_cut, *ow]), "dp", axis=0), 0, list(range(parts)))

    sends = [(after(qkv_cut, partner_cut, picked), d, "tensor") for d in range(1, parts)]
    qkv_got, (*att, att_nat, q_back) = beside(sends, lambda: attend(index, q, k, v, parts))
    rows_for = lambda e: outgoing([att[d ^ e] for d in range(parts)])
    rows_now, qkv_stack = beside(rows_for(slots[0]), lambda: pack(qkv_got))
    qkv_full = lax.all_gather(qkv_stack, "dp", axis=0)

    lefts, acts, gn2s, terms, gn2_got = {}, {}, {}, {}, {}
    tied = tokens
    for e in slots:

        def feed():
            outs = feed_forward(
                e, index, lengths, picked, [att[e]] + rows_now, tied, cotangent, out_full,
                gate_up_weight, down_weight, partner, norm_gains
            )
            if e:
                return outs
            return outs, ffn_grads([*lefts.values(), outs[0]], [*acts.values(), outs[1]], shares)

        sends = rows_for(e - 2) if e else []
        if e + 2 in gn2s:
            sends.append((gn2s[e + 2], e + 2, "tensor"))
        got, outs = beside(sends, feed)
        if e + 2 in gn2s:
            gn2_got[e + 2] = got.pop()
        if e:
            rows_now = got
        else:
            outs, wg_ffn = outs
        lefts[e], acts[e], gn2s[e], *terms[e] = outs[:6]
        tied = after(tokens, gn2s[e])
    resid = outs[6]
    gn2_all = [gn2s[0]] + [gn2_got[e] for e in slots[:-1]]

    def terms_out(i):
        return [(terms[e][i], e, "tensor") for e in slots[:-1]]

    terms_got = []
    got, (grad_resid, grad_low, gain_two, *grads) = beside(
        terms_out(0),
        lambda: resid_back(
            index, lengths, picked, cotangent, resid, gn2_all, out_full, norm_gains, local
        ),
    )
    terms_got.append(got)
    sum_ffn = lax.psum_scatter(wg_ffn, "dp", scatter_dimension=0, tiled=True)[0]
    def own_rows():
        return (
            attend_back_own(index, grads[0], q_back, k, v, att_nat, cosine, sine),
            out_grads(grad_low, [att[0]] + rows_now, shares, hidden),
        )

    grads_got, (back_own, wg_op) = beside(outgoing(grads), own_rows)

    def back(j):
        return attend_back(index, grads_got, back_own, q_back, k, v, att_nat, cosine, sine, j)

    terms_got.append([swap(after(a, wg_op), *way) for a, *way in terms_out(1)])
    group = region(lambda: back(0))
    if pairs == 1:
        group = after(group, *terms_got[1])
    sum_op = lax.psum_scatter(after(wg_op, qkv_full), "dp", scatter_dimension=0, tiled=True)[0]
    qkv_acts, acts_got, qkv_sums = [group], [], None
    for j in range(1, pairs):

        def back_next():
            return back(j), project_grads(index, normed, qkv_acts[-1], qkv_weight, shares, j - 1, qkv_sums)

        got, (group, qkv_sums) = beside(outgoing(group), back_next)
        acts_got.append([qkv_acts[-1][0]] + got)
        if j == 1:
            group = after(group, *terms_got[1])
        qkv_acts.append(group)
    ways = []

    def finish():
        away_q, keep_q, gain_one = project_grads(
            index, normed, qkv_acts[-1], qkv_weight, shares, pairs - 1, qkv_sums
        )
        halves = fold(index, [(keep_q, swap(away_q, 1, "dp"), lead, lead)])
        for s in range(bits - 2):
            halves = fold_next(halves, [swap(*x) for x in leaving(halves)])
        gains_grad = jnp.stack([gain_one[:, 0] / norm_gains[0], jnp.sum(gain_two, axis=0)])
        gains_grad = after(gains_grad, *[h[0] for h in halves])
        for s in range(bits):
            gains_grad = gains_grad + swap(gains_grad, 1 << s, "dp")
        ways[:] = [h[2:] for h in halves]
        return [h[:2] for h in halves], gains_grad

    got, (halves, gains_grad) = beside(outgoing(group) + [(sum_ffn[3 * part :], 1, "tensor")], finish, apart=True)
    halves = [tuple(h) + way for h, way in zip(halves, ways)]
    acts_got.append([group[0]] + got[: parts - 1])
    got_b = got[-1]
    pieces = make_pieces(sum_op, gains_grad, part, local, parts)
    got, (grad_tok, grad_gu, grad_down) = beside(
        leaving(halves) + terms_out(2) + outgoing(pieces),
        lambda: token_grad(index, tokens, grad_resid, qkv_weight, qkv_full, norm_gains, acts_got, sum_ffn, got_b),
    )
    terms_got.append(got[1 : len(slots)])
    out, grad_qkv, grad_op, gains_grad = finish_outputs(
        index, resid, terms[0], terms_got, halves[0][0], got[0], [pieces[0]] + got[len(slots) :]
    )
    return (out, grad_tok, grad_qkv, grad_op, grad_gu, grad_down, gains_grad)


def solution(mesh):
    in_specs = (
        P("dp", None),
        P(None, None, "tensor"),
        P("tensor", None),
        P(None, None, "tensor"),
        P("tensor", None),
        P(),
        P(),
        P("dp"),
        P("dp"),
        P("dp", None),
    )
    out_specs = (
        P(("dp", "tensor"), None),
        P(("dp", "tensor"), None),
        P(None, "dp", "tensor"),
        P("tensor", "dp"),
        P(None, "dp", "tensor"),
        P("tensor", "dp"),
        P(),
    )
    return jax.shard_map(body, mesh=mesh, in_specs=in_specs, out_specs=out_specs, check_vma=False)
```

```python
import functools
import math

import jax
import jax.numpy as jnp
import numpy as np
from jax import lax
from jax.experimental import pallas as pl
from jax.experimental.pallas import tpu as pltpu
from jax.sharding import PartitionSpec as P

HD = 64
WIN = 2048
EPSILON = 1e-05
NEG_FILL = -1e30
LOG2E = math.log2(math.e)
LN2 = math.log(2.0)
FACTOR = HD ** (-0.5)
VMEM = 60 * 2**20
F32 = jnp.float32
BF16 = jnp.bfloat16

NN = (((1,), (0,)), ((), ()))
NT = (((1,), (1,)), ((), ()))
TN = (((0,), (0,)), ((), ()))


def dot(a, b, dims=NN):
    return lax.dot_general(a, b, dims, preferred_element_type=F32)


def call(kernel, grid, in_specs, out_specs, out_shape, scratch=(), flops=0, nbytes=0, trans=0, prefetch=0):
    return pl.pallas_call(
        kernel,
        grid_spec=pltpu.PrefetchScalarGridSpec(
            num_scalar_prefetch=prefetch,
            grid=grid,
            in_specs=in_specs,
            out_specs=out_specs,
            scratch_shapes=list(scratch),
        ),
        out_shape=out_shape,
        compiler_params=pltpu.CompilerParams(vmem_limit_bytes=VMEM),
        cost_estimate=pl.CostEstimate(flops=flops, bytes_accessed=nbytes, transcendentals=trans),
    )


def whole(shape):
    return pl.BlockSpec(shape, lambda *_: (0,) * len(shape), pipeline_mode=pl.Buffered(1))


def staged(body, index, smalls, ins, outs, stores, scratch=()):
    n_small, n_in, n_out = len(smalls), len(ins), len(outs)

    def kernel(idx_ref, *refs):
        refs = list(refs)
        take = lambda n: [refs.pop(0) for _ in range(n)]
        small, far_in, far_out = take(n_small), take(n_in), take(n_out)
        near_in, near_out, extra = take(n_in), take(n_out), take(len(scratch))
        sem_in, sem_out = refs
        copies = []
        for n, (_, _, pick) in enumerate(ins):
            part = pick(idx_ref, far_in[n]) if pick else far_in[n]
            copies.append(pltpu.make_async_copy(part, near_in[n], sem_in.at[n]))
            copies[n].start()
        there, sent = set(), []

        def get(n):
            if n not in there:
                copies[n].wait()
                there.add(n)
            return near_in[n]

        def put(n, part=None):
            src, dst = near_out[n], far_out[n]
            if part is not None:
                src, dst = src.at[part], dst.at[part]
            copy = pltpu.make_async_copy(src, dst, sem_out.at[len(sent)])
            copy.start()
            sent.append(copy)

        body(idx_ref, small, get, near_out, put, extra)
        for n in range(n_in):
            get(n)
        for copy in sent:
            copy.wait()

    anywhere = pl.BlockSpec(memory_space=pl.ANY)
    specs = [smem() if a.ndim == 1 else whole(a.shape) for a in smalls]
    return call(
        kernel,
        (1,),
        specs + [anywhere] * n_in,
        [anywhere] * n_out,
        [sds(shape, dtype) for shape, dtype in outs],
        scratch=[pltpu.VMEM(shape, a.dtype) for a, shape, _ in ins]
        + [pltpu.VMEM(shape, dtype) for shape, dtype in outs]
        + list(scratch)
        + [pltpu.SemaphoreType.DMA((n_in,)), pltpu.SemaphoreType.DMA((stores,))],
        prefetch=1,
    )(index, *smalls, *[a for a, _, _ in ins])


def smem():
    return pl.BlockSpec(memory_space=pltpu.SMEM)


def sds(shape, dtype):
    return jax.ShapeDtypeStruct(shape, dtype)


def rotary_tables():
    position = np.arange(WIN, dtype=np.float64)
    frequency = 10000.0 ** (-2.0 * np.arange(HD // 2, dtype=np.float64) / HD)
    angles = position[:, None] * frequency[None, :]
    cosine = np.cos(angles)
    sine = np.sin(angles)
    cos_full = np.tile(np.concatenate([cosine, cosine], axis=1), (1, 2))
    sin_full = np.tile(np.concatenate([-sine, sine], axis=1), (1, 2))
    return cos_full.astype(np.float32), sin_full.astype(np.float32)


def swap_halves(v):
    lane = lax.broadcasted_iota(jnp.int32, v.shape, 1)
    return jnp.where(lane % HD < HD // 2, pltpu.roll(v, 96, 1), pltpu.roll(v, 32, 1))


def rms(x):
    return lax.rsqrt(jnp.mean(x * x, axis=-1, keepdims=True) + EPSILON)


def split3(v):
    hi = v.astype(BF16)
    rest = v - hi.astype(F32)
    mid = rest.astype(BF16)
    low = (rest - mid.astype(F32)).astype(BF16)
    return hi, mid, low


def norm_back(grad_normed, gain, unit, factor):
    scaled = grad_normed * gain
    return factor * (scaled - unit * jnp.mean(scaled * unit, axis=-1, keepdims=True))


def qkv_kernel(len_ref, x_ref, w_ref, gain_ref, cos_ref, sin_ref, q_ref, k_ref, v_ref, normed_ref):
    rows = x_ref.shape[0]
    x = x_ref[...].astype(F32)
    normed = (x * rms(x) * gain_ref[0:1, :]).astype(BF16)
    normed_ref[...] = normed
    cosine = cos_ref[...]
    sine = sin_ref[...]
    lane = lax.broadcasted_iota(jnp.int32, (rows, 128), 1)
    slot = lax.broadcasted_iota(jnp.int32, (rows, 128), 0) + pl.program_id(0) * rows
    masked = jnp.where(slot < len_ref[0], 0.0, NEG_FILL).astype(BF16)
    one = jnp.ones((rows, 128), BF16)
    zero = jnp.zeros((rows, 128), BF16)
    pairs = w_ref.shape[2] // 128
    for c in range(3):
        y = dot(normed, w_ref[c])
        for j in range(pairs):
            v = y[:, 128 * j : 128 * (j + 1)]
            if c < 2:
                v = v * cosine + swap_halves(v) * sine
            if c == 0:
                v = v * (FACTOR * LOG2E)
            v = v.astype(BF16)
            for s in range(2):
                first = HD * (1 - s)
                own = (lane >= HD * s) & (lane < HD * (s + 1))
                if c == 0:
                    q_ref[2 * j + s] = jnp.where(own, v, jnp.where(lane == first, one, zero))
                elif c == 1:
                    tail = jnp.where(
                        lane == first, masked, jnp.where(lane < first + 4, one, zero)
                    )
                    tail = jnp.where(lane < first, zero, tail)
                    k_ref[2 * j + s] = jnp.where(own, v, tail)
                else:
                    v_ref[2 * j + s] = jnp.where(own, v, one)


def project(lengths, tokens, qkv_weight, gains, cosine, sine, block=512):
    rows, width = tokens.shape
    local = qkv_weight.shape[2]
    heads = local // HD
    spec = pl.BlockSpec((heads, block, 128), lambda i: (0, i, 0))
    return call(
        qkv_kernel,
        (rows // block,),
        [
            smem(),
            pl.BlockSpec((block, width), lambda i: (i, 0)),
            whole(qkv_weight.shape),
            whole(gains.shape),
            pl.BlockSpec((block, 128), lambda i: (i, 0)),
            pl.BlockSpec((block, 128), lambda i: (i, 0)),
        ],
        [spec] * 3 + [pl.BlockSpec((block, width), lambda i: (i, 0))],
        [sds((heads, rows, 128), BF16)] * 3 + [sds((rows, width), BF16)],
    )(lengths, tokens, qkv_weight, gains, cosine, sine)


def attend_kernel(sub, parts, idx_ref, q_ref, k_ref, v_ref, *refs):
    o_refs = refs[:parts]
    nat_ref, qb_ref = refs[parts:]
    rows = q_ref.shape[1]
    lane = lax.broadcasted_iota(jnp.int32, (sub, 128), 1)
    for r in range(rows // sub):
        part = slice(r * sub, (r + 1) * sub)
        outs = []
        for s in range(2):
            q = q_ref[s, part, :]
            scores = dot(q, k_ref[s], NT)
            peak = jnp.max(scores, axis=1, keepdims=True)
            expo = jnp.exp2(scores - peak).astype(BF16)
            acc = dot(expo, v_ref[s])
            outs.append(acc / pltpu.roll(acc, HD, 1))
            first = HD * (1 - s)
            total = jnp.where((lane >= first) & (lane < first + HD), acc, 1.0)
            hi, mid, low = split3(-(peak + jnp.log2(total)))
            tail = jnp.where(lane == first + 3, low, q)
            tail = jnp.where(lane == first + 2, mid, tail)
            qb_ref[s, part, :] = jnp.where(lane == first + 1, hi, tail)
        nat_ref[part, :] = jnp.where(lane < HD, outs[0], outs[1]).astype(BF16)
    for d in range(parts):

        @pl.when(pl.program_id(1) == d)
        def _():
            o_refs[d][...] = nat_ref[...]


def attend(index, q, k, v, parts, sub=256):
    heads, rows, _ = q.shape
    keys = k.shape[1]
    share = rows // parts
    local = heads * HD
    return call(
        functools.partial(attend_kernel, min(sub, share), parts),
        (heads // 2, parts),
        [
            pl.BlockSpec((2, share, 128), lambda j, i, idx: (j, idx[0] ^ i, 0)),
            pl.BlockSpec((2, keys, 128), lambda j, i, idx: (j, 0, 0)),
            pl.BlockSpec((2, keys, 128), lambda j, i, idx: (j, 0, 0)),
        ],
        [pl.BlockSpec((share, 128), lambda j, i, idx: (0, j))] * parts
        + [
            pl.BlockSpec((share, 128), lambda j, i, idx: (idx[0] ^ i, j)),
            pl.BlockSpec((2, share, 128), lambda j, i, idx: (j, idx[0] ^ i, 0)),
        ],
        [sds((share, local), BF16)] * parts + [sds((rows, local), BF16), sds((heads, rows, 128), BF16)],
        prefetch=1,
    )(index, q, k, v)


def cut_kernel(idx_ref, gu_ref, dw_ref, *refs):
    part = gu_ref.shape[1]
    out_ref = refs[-1]
    out_ref[:part, :] = gu_ref[0]
    out_ref[part : 2 * part, :] = gu_ref[1]
    out_ref[2 * part : 3 * part, :] = dw_ref[...].T
    if len(refs) > 1:
        out_ref[3 * part :, :] = refs[0][...]


def cut_weights(dp, gate_up, down, shares, more):
    _, width, hidden = gate_up.shape
    part = width // shares
    if part % 128:
        down = lax.dynamic_slice_in_dim(down, dp[0] * part, part, 1)
        spec = whole(down.shape)
    else:
        spec = pl.BlockSpec((hidden, part), lambda i, idx: (0, idx[0]))
    shape = (3 * part + sum(a.shape[0] for a in more), hidden)
    return call(
        cut_kernel,
        (1,),
        [pl.BlockSpec((2, part, hidden), lambda i, idx: (0, idx[0], 0)), spec] + [whole(a.shape) for a in more],
        whole(shape),
        sds(shape, BF16),
        prefetch=1,
    )(dp, gate_up, down, *more)


def pack_kernel(*refs):
    out_ref, row = refs[-1], 0
    for ref in refs[:-1]:
        out_ref[row : row + ref.shape[0], :] = ref[...]
        row += ref.shape[0]


def pack(arrays):
    shape = (sum(a.shape[0] for a in arrays), arrays[0].shape[1])
    return call(pack_kernel, (1,), [whole(a.shape) for a in arrays], whole(shape), sds(shape, BF16))(*arrays)


def ffn_kernel(parts, ow_row, ow_order, slot, idx_ref, len_ref, weight_ref, gain_ref, x_h, cot_h, gu_h, dw_h, pb_h, ow_h, *refs):
    own = slot == 0
    att_h = refs[:parts]
    refs = refs[parts:]
    count = 7 if own else 6
    outs, scratch = refs[:count], refs[count:]
    x_v, cot_v, att_v, ow_v, gu_v, dw_v, pb_v, left_v, act_v, ffn_v, gn2_v, low_v, sem_in, sem_out = scratch
    rows, width = x_v.shape
    local = att_v.shape[2]
    hidden_units = gu_v.shape[2]
    part = pb_v.shape[1] // 3
    row0 = pl.multiple_of((idx_ref[0] ^ slot) * rows, rows)
    mine = pl.ds(row0, rows)

    def fetch(src, dst, i):
        copy = pltpu.make_async_copy(src, dst, sem_in.at[i])
        copy.start()
        return copy

    pending = []

    def store(src, dst, i):
        copy = pltpu.make_async_copy(src, dst, sem_out.at[i])
        copy.start()
        pending.append(copy)

    get_x = fetch(x_h.at[mine], x_v, 0)
    get_ow = fetch(ow_h.at[:, pl.ds(ow_row, ow_v.shape[1])], ow_v, 6 + parts)
    get_att = [fetch(att_h[d], att_v.at[d], 2 + d) for d in range(parts)]
    get_cot = fetch(cot_h.at[mine], cot_v, 2 + parts)
    get_gu = fetch(gu_h, gu_v, 3 + parts)
    get_dw = fetch(dw_h, dw_v, 4 + parts)
    get_pb = fetch(pb_h.at[:, pl.ds(0, pb_v.shape[1])], pb_v, 1)

    get_x.wait()
    get_ow.wait()
    piece = ow_v.shape[1] // parts
    for copy in get_att:
        copy.wait()
    att = jnp.concatenate([att_v[d] for d in ow_order], axis=1)
    out_w = [ow_v[:, n * piece : (n + 1) * piece].reshape(local, width) for n in range(parts)]
    resid = x_v[...].astype(F32) + dot(att, jnp.concatenate(out_w, axis=0))
    if own:
        ffn_v[...] = resid
        store(ffn_v, outs[6], 4)
    normed = (resid * rms(resid) * gain_ref[1:2, :]).astype(BF16)
    left_v[0] = normed
    position = lax.broadcasted_iota(jnp.int32, (rows, 1), 0) + row0
    row_weight = jnp.where(position < len_ref[0], weight_ref[0], 0.0)
    get_cot.wait()
    left_v[1] = (cot_v[...].astype(F32) * row_weight).astype(BF16)
    store(left_v, outs[0], 0)
    for shard in range(2):
        cols = slice(shard * hidden_units, (shard + 1) * hidden_units)
        if shard == 0:
            get_gu.wait()
            get_dw.wait()
            gate_w, up_w, down_w = gu_v[0], gu_v[1], dw_v[...]
        else:
            get_pb.wait()
            gate_w, up_w, down_w = (
                pb_v[:, c * part : (c + 1) * part, :].reshape(width, hidden_units) for c in range(3)
            )
        gate = dot(left_v[0], gate_w)
        upper = dot(left_v[0], up_w)
        grad_hidden = dot(left_v[1], down_w, NT if shard == 0 else NN)
        sigma = 0.5 + 0.5 * jnp.tanh(0.5 * gate)
        act = gate * sigma
        hidden = (act * upper).astype(BF16)
        grad_up = (grad_hidden * act).astype(BF16)
        grad_gate = (grad_hidden * upper * (sigma + act * (1.0 - sigma))).astype(BF16)
        act_v[0, :, cols] = grad_gate
        act_v[1, :, cols] = grad_up
        act_v[2, :, cols] = hidden
        store(act_v.at[:, :, cols], outs[1].at[:, :, cols], 1 + 4 * shard)
        grad = dot(
            jnp.concatenate([grad_gate, grad_up], axis=1), jnp.concatenate([gate_w, up_w], axis=1), NT
        )
        term = dot(hidden, down_w, NN if shard == 0 else NT)
        if shard == 0:
            gn2_v[...] = grad
            if own:
                pending.pop(0).wait()
            ffn_v[...] = term
        else:
            low_v[0] = (gn2_v[...] + grad).astype(BF16)
            store(low_v.at[0], outs[2], 2)
            low_v[1] = (ffn_v[...] + term).astype(BF16)
            row = 0
            for n in range(3):
                size = outs[3 + n].shape[0]
                store(low_v.at[1, pl.ds(row, size)], outs[3 + n], (3, 6, 7)[n])
                row += size
    for copy in pending:
        copy.wait()


def feed_forward(slot, index, lengths, picked, atts, tokens, cotangent, out_full, gate_up, down, partner, gains):
    parts = len(atts)
    rows, local = atts[0].shape
    width = tokens.shape[1]
    hidden = gate_up.shape[2]
    out_rows, ow_row, ow_order = out_full
    shares = partner.shape[0]
    part = width // shares
    anywhere = pl.BlockSpec(memory_space=pl.ANY)
    out_shape = [
        sds((2, rows, width), BF16), sds((3, rows, 2 * hidden), BF16),
        sds((rows, width), BF16),
    ]
    out_shape += [sds((rows * n // 16, width), BF16) for n in (3, 10, 3)]
    if slot == 0:
        out_shape.append(sds((rows, width), F32))
    return call(
        functools.partial(ffn_kernel, parts, ow_row, ow_order, slot),
        (1,),
        [smem(), smem(), whole(gains.shape)] + [anywhere] * (6 + parts),
        [anywhere] * len(out_shape),
        out_shape,
        scratch=[
            pltpu.VMEM((rows, width), BF16),
            pltpu.VMEM((rows, width), BF16),
            pltpu.VMEM((parts, rows, local), BF16),
            pltpu.VMEM((shares, parts * local // shares, width), BF16),
            pltpu.VMEM(gate_up.shape, BF16),
            pltpu.VMEM(down.shape, BF16),
            pltpu.VMEM((shares, 3 * part, hidden), BF16),
            pltpu.VMEM((2, rows, width), BF16),
            pltpu.VMEM((3, rows, 2 * hidden), BF16),
            pltpu.VMEM((rows, width), F32),
            pltpu.VMEM((rows, width), F32),
            pltpu.VMEM((2, rows, width), BF16),
            pltpu.SemaphoreType.DMA((7 + parts,)),
            pltpu.SemaphoreType.DMA((8,)),
        ],
        prefetch=1,
    )(index, lengths, picked, gains, tokens, cotangent, gate_up, down, partner, out_rows, *atts)


def write_shares(out, total):
    part = out.shape[-2]
    for j in range(out.shape[0]):
        out[j] = total[j * part : (j + 1) * part, :].astype(BF16)


def ffn_grad_kernel(sets, *refs):
    left = refs[:sets]
    act = refs[sets : 2 * sets]
    total = dot(left[0][0], act[0][0], TN)
    for e in range(1, sets):
        total = total + dot(left[e][0], act[e][0], TN)
    write_shares(refs[-1], total)


def ffn_grads(lefts, acts, shares):
    sets = len(lefts)
    _, rows, width = lefts[0].shape
    hidden = acts[0].shape[2] // 2
    part = width // shares
    specs = [pl.BlockSpec((1, rows, width), lambda c: (c % 3 // 2, 0, 0))] * sets
    specs += [pl.BlockSpec((1, rows, hidden), lambda c: (c % 3, 0, c // 3))] * sets
    return call(
        functools.partial(ffn_grad_kernel, sets),
        (6,),
        specs,
        pl.BlockSpec((shares, part, hidden), lambda c: (0, c, 0)),
        sds((shares, 6 * part, hidden), BF16),
    )(*lefts, *acts)


def out_grad_kernel(low_ref, *refs):
    *att_refs, out = refs
    each = out.shape[2] // att_refs[0].shape[1]
    for c in range(len(att_refs) // each):

        @pl.when(pl.program_id(0) == c)
        def _():
            rows = jnp.concatenate([ref[...] for ref in att_refs[c * each : (c + 1) * each]], axis=1)
            write_shares(out, dot(low_ref[...], rows, TN))


def out_grads(grad_low, att_own, shares, hidden):
    width = grad_low.shape[1]
    part = width // shares
    steps = len(att_own) * att_own[0].shape[1] // hidden
    return call(
        out_grad_kernel,
        (steps,),
        [whole(a.shape) for a in (grad_low, *att_own)],
        pl.BlockSpec((shares, part, hidden), lambda c: (0, c, 0)),
        sds((shares, steps * part, hidden), BF16),
    )(grad_low, *att_own)


def resid_kernel(ow_order, members, idx_ref, len_ref, weight_ref, cot_ref, resid_ref, ow_ref, gain_ref, *refs):
    parts = len(ow_order)
    gn2_refs = refs[:members]
    gr_ref, low_ref, sum_ref = refs[members : members + 3]
    g_refs = refs[members + 3 :]
    rows, width = cot_ref.shape
    local = g_refs[0].shape[1]
    step = pl.program_id(0)
    first = (idx_ref[0] * pl.num_programs(0) + step) * rows
    slot = lax.broadcasted_iota(jnp.int32, (rows, 1), 0) + first
    row_weight = jnp.where(slot < len_ref[0], weight_ref[0], 0.0)
    gn2 = gn2_refs[0][...].astype(F32)
    for ref in gn2_refs[1:]:
        gn2 = gn2 + ref[...].astype(F32)
    resid = resid_ref[...]
    factor = rms(resid)
    unit = resid * factor
    grad = cot_ref[...].astype(F32) * row_weight + norm_back(gn2, gain_ref[1:2, :], unit, factor)
    gr_ref[...] = grad
    low = grad.astype(BF16)
    low_ref[...] = low

    @pl.when(step == 0)
    def _():
        sum_ref[...] = jnp.zeros_like(sum_ref)

    sum_ref[...] += jnp.sum((gn2 * unit).reshape(rows // 8, 8, width), axis=0)
    for d in range(parts):
        piece = ow_ref.shape[1] // parts
        at = ow_order.index(d) * piece
        block = ow_ref[:, at : at + piece].reshape(local, width)
        g_refs[d][...] = dot(low, block, NT).astype(BF16)


def resid_back(index, lengths, picked, cotangent, resid, gn2s, out_full, gains, local, block=256):
    share, width = resid.shape
    parts, members = width // local, len(gn2s)
    out_rows, ow_row, ow_order = out_full
    ow_rows = parts * local // out_rows.shape[0]
    steps = share // block
    row = lambda n: pl.BlockSpec((block, n), lambda i, idx: (i, 0))
    return call(
        functools.partial(resid_kernel, ow_order, members),
        (steps,),
        [
            smem(), smem(),
            pl.BlockSpec((block, width), lambda i, idx: (idx[0] * steps + i, 0)),
            row(width),
            pl.BlockSpec((out_rows.shape[0], ow_rows, width), lambda *_: (0, ow_row // ow_rows, 0), pipeline_mode=pl.Buffered(1)),
            whole(gains.shape),
        ]
        + [row(width)] * members,
        [row(width), row(width), whole((8, width))] + [row(local)] * parts,
        [sds((share, width), F32), sds((share, width), BF16), sds((8, width), F32)]
        + [sds((share, local), BF16)] * parts,
        prefetch=1,
    )(index, lengths, picked, cotangent, resid, out_rows, gains, *gn2s)


def back_rows(grad, att, q_ref, k_ref, v_ref):
    rows = grad.shape[0]
    lane = lax.broadcasted_iota(jnp.int32, (rows, 128), 1)
    prod = grad.astype(F32) * att.astype(F32)
    zero = jnp.zeros((rows, 128), BF16)
    dqs, probs_all, scores_all, grads_own, queries_own = [], [], [], [], []
    for s in range(2):
        first = HD * (1 - s)
        own = (lane >= HD * s) & (lane < HD * (s + 1))
        delta = jnp.sum(jnp.where(own, prod, 0.0), axis=1, keepdims=True)
        hi, mid, low = split3(-delta)
        grad_own = jnp.where(own, grad, zero)
        grad_aug = jnp.where(lane == first + 2, low, grad_own)
        grad_aug = jnp.where(lane == first + 1, mid, grad_aug)
        grad_aug = jnp.where(lane == first, hi, grad_aug)
        q = q_ref[s]
        probs = jnp.exp2(dot(q, k_ref[s], NT))
        scores_grad = (probs * dot(grad_aug, v_ref[s], NT)).astype(BF16)
        probs_all.append(probs.astype(BF16))
        scores_all.append(scores_grad)
        grads_own.append(grad_own)
        queries_own.append(jnp.where(own, q, zero))
        dqs.append(dot(scores_grad, k_ref[s]))
    dv = dot(jnp.concatenate(grads_own, axis=0).T, jnp.concatenate(probs_all, axis=0))
    dk = dot(jnp.concatenate(queries_own, axis=0).T, jnp.concatenate(scores_all, axis=0))
    return jnp.where(lane < HD, dqs[0], dqs[1]), dk, dv


def rotated_back(v, cosine, sine, scale):
    return ((v * cosine - swap_halves(v) * sine) * scale).astype(BF16)


def attend_back_own_kernel(idx_ref, q_ref, k_ref, v_ref, att_ref, cos_ref, sin_ref, grad_ref, dq_ref, dk_ref, dv_ref):
    dq, dk_ref[0], dv_ref[0] = back_rows(grad_ref[...], att_ref[...], q_ref, k_ref, v_ref)
    dq_ref[...] = rotated_back(dq, cos_ref[...], sin_ref[...], FACTOR)


def attend_back_own(index, grad, q, k, v, att, cosine, sine):
    share, local = grad.shape
    pairs, rows = local // 128, q.shape[1]
    keys = pl.BlockSpec((2, rows, 128), lambda j, idx: (j, 0, 0))
    table = pl.BlockSpec((share, 128), lambda j, idx: (idx[0], 0))
    sums = pl.BlockSpec((1, 128, rows), lambda j, idx: (j, 0, 0))
    return call(
        attend_back_own_kernel,
        (pairs,),
        [
            pl.BlockSpec((2, share, 128), lambda j, idx: (j, idx[0], 0)),
            keys,
            keys,
            pl.BlockSpec((share, 128), lambda j, idx: (idx[0], j)),
            table,
            table,
            pl.BlockSpec((share, 128), lambda j, idx: (0, j)),
        ],
        [pl.BlockSpec((share, 128), lambda j, idx: (0, j)), sums, sums],
        [sds((share, local), BF16)] + [sds((pairs, 128, rows), F32)] * 2,
        prefetch=1,
    )(index, q, k, v, att, cosine, sine, grad)


def attend_back_kernel(parts, idx_ref, q_ref, k_ref, v_ref, att_ref, cos_ref, sin_ref, dq_ref, dk_ref, dv_ref, *refs):
    grad_refs = refs[: parts - 1]
    outs = refs[parts - 1 : 2 * parts - 1]
    dk_acc, dv_acc = refs[2 * parts - 1 :]
    rows = q_ref.shape[1]
    step = pl.program_id(0)
    me = idx_ref[0]

    def span(d):
        return pl.ds(pl.multiple_of((me ^ d) * rows, rows), rows)

    def back(v, d, scale):
        return rotated_back(v, cos_ref[span(d), :], sin_ref[span(d), :], scale)

    grad = grad_refs[0][...]
    for d in range(1, parts - 1):
        grad = jnp.where(step == d, grad_refs[d][...], grad)
    dq, dk, dv = back_rows(grad, att_ref[...], q_ref, k_ref, v_ref)

    @pl.when(step == 0)
    def _():
        outs[0][0] = dq_ref[...]
        dk_acc[...] = dk_ref[0] + dk
        dv_acc[...] = dv_ref[0] + dv

    @pl.when(step > 0)
    def _():
        dk_acc[...] += dk
        dv_acc[...] += dv

    for d in range(1, parts):

        @pl.when(step == d - 1)
        def _():
            outs[d][0] = back(dq, d, FACTOR)

    @pl.when(step == parts - 2)
    def _():
        for d in range(parts):
            outs[d][1] = back(dk_acc[:, span(d)].T, d, LN2)
            outs[d][2] = dv_acc[:, span(d)].T.astype(BF16)


def attend_back(index, grads, own, q, k, v, att, cosine, sine, pair):
    parts = len(grads) + 1
    share = grads[0].shape[0]
    rows = q.shape[1]
    once = pl.Buffered(1)
    keys = pl.BlockSpec((2, rows, 128), lambda i, idx: (pair, 0, 0), pipeline_mode=once)
    sums = pl.BlockSpec((1, 128, rows), lambda i, idx: (pair, 0, 0), pipeline_mode=once)
    return call(
        functools.partial(attend_back_kernel, parts),
        (parts - 1,),
        [
            pl.BlockSpec((2, share, 128), lambda i, idx: (pair, idx[0] ^ (i + 1), 0)),
            keys,
            keys,
            pl.BlockSpec((share, 128), lambda i, idx: (idx[0] ^ (i + 1), pair)),
            whole(cosine.shape),
            whole(sine.shape),
            pl.BlockSpec((share, 128), lambda i, idx: (0, pair), pipeline_mode=once),
            sums,
            sums,
        ]
        + [pl.BlockSpec((share, 128), lambda i, idx: (0, pair))] * (parts - 1),
        [whole((3, share, 128))] * parts,
        [sds((3, share, 128), BF16)] * parts,
        scratch=[pltpu.VMEM((128, rows), F32)] * 2,
        flops=2 * rows * rows * 128 * 10,
        nbytes=rows * 256 * 16,
        trans=2 * rows * rows,
        prefetch=1,
    )(index, q, k, v, att, cosine, sine, *own, *grads)


def project_grads(index, normed, acts, qkv_weight, shares, pair, prev=None):
    width = normed.shape[1]
    local = 128 * (pair + 1)
    parts = len(acts)
    share = acts[0].shape[1]
    part = width // shares
    half = (shares // 2, part, 3 * local)
    ins = []
    for d in range(parts):
        pick = functools.partial(
            lambda d, idx, ref: ref.at[pl.ds(pl.multiple_of((idx[0] ^ d) * share, share), share)], d
        )
        ins += [(normed, (share, width), pick), (acts[d], acts[d].shape, None)]
    weight_cols = pl.ds(128 * pair, 128)
    ins.append((qkv_weight, (3, width, 128), lambda idx, ref: ref.at[:, :, weight_cols]))
    if prev:
        ins += [(a, a.shape, None) for a in prev]

    def body(idx_ref, _, get, outs, put, scratch):
        away_ref, keep_ref, sum_ref = outs
        (acc,) = scratch
        for d in range(parts):
            act_ref = get(2 * d + 1)
            act = jnp.concatenate([act_ref[c] for c in range(3)], axis=1)
            term = dot(get(2 * d)[...], act, TN)
            acc[...] = acc[...] + term if d else term
        core = idx_ref[1] & 1
        before = local - 128
        for n, (ref, bit) in enumerate(((away_ref, 1 - core), (keep_ref, core))):
            for c in range(3):
                if prev:
                    ref[:, :, c * local : c * local + before] = get(2 * parts + 1 + n)[
                        :, :, c * before : (c + 1) * before
                    ]
                for j in range(shares // 2):
                    rows = pl.ds(pl.multiple_of((2 * j + bit) * part, part), part)
                    ref[j, :, c * local + before : (c + 1) * local] = acc[rows, c * 128 : (c + 1) * 128].astype(BF16)
            put(n)
        weight = get(2 * parts)
        gain_sum = acc[:, :128] * weight[0].astype(F32)
        for c in (1, 2):
            gain_sum += acc[:, c * 128 : (c + 1) * 128] * weight[c].astype(F32)
        total = jnp.broadcast_to(jnp.sum(gain_sum, axis=1, keepdims=True), sum_ref.shape)
        sum_ref[...] = total + get(2 * parts + 3)[...] if prev else total
        put(2)

    outs = [(half, BF16), (half, BF16), ((width, 128), F32)]
    return staged(body, index, [], ins, outs, 3, [pltpu.VMEM((width, 3 * 128), F32)])


def token_grad(index, tokens, grad_resid, qkv_weight, qkv_full, gains, acts, ffn_own, ffn_got):
    share, width = grad_resid.shape
    pairs, parts = len(acts), len(acts[0])
    part, hidden = ffn_got.shape[0] // 3, ffn_got.shape[1]
    local = qkv_weight.shape[2]
    ins = []
    for d in range(parts):
        ins += [(acts[j][d], acts[j][d].shape, None) for j in range(pairs)]
        if d:
            rows = pl.ds((d - 1) * 3 * part, 3 * part)
            pick = functools.partial(lambda rows, idx, ref: ref.at[:, rows], rows)
            ins.append((qkv_full, (qkv_full.shape[0], 3 * part, local), pick))
        else:
            ins.append((qkv_weight, qkv_weight.shape, None))
        if d == 0:
            ins.append((ffn_own, ffn_got.shape, lambda idx, ref: ref.at[pl.ds(0, 3 * part)]))
            ins.append((ffn_got, ffn_got.shape, None))
    ins.append((tokens, (share, width), lambda idx, ref: ref.at[pl.ds(pl.multiple_of(idx[0] * share, share), share)]))
    ins.append((grad_resid, grad_resid.shape, None))

    def body(idx_ref, smalls, get, outs, put, scratch):
        out_ref, gu_ref, down_ref = outs
        (acc,) = scratch
        at = 0
        for n in range(parts):
            group = [get(at + j) for j in range(pairs)]
            weight = get(at + pairs)
            at += pairs + 1
            act = jnp.concatenate([ref[c] for c in range(3) for ref in group], axis=1)
            cut = lambda c: weight[:, c * part : (c + 1) * part].reshape(width, local) if n else weight[c]
            weight_all = jnp.concatenate([cut(c) for c in range(3)], axis=1)
            term = dot(act, weight_all, NT)
            acc[...] = acc[...] + term if n else term
            if n == 0:
                total = get(at)[...].astype(F32) + get(at + 1)[...].astype(F32)
                at += 2
                gu_ref[0] = total[:part]
                gu_ref[1] = total[part : 2 * part]
                down_ref[...] = total[2 * part :].T
                put(1)
                put(2)
        x_ref, gr_ref = get(at), get(at + 1)
        half = share // 2
        for c in range(2):
            rows = slice(c * half, (c + 1) * half)
            x = x_ref[rows, :].astype(F32)
            factor = rms(x)
            out_ref[rows, :] = gr_ref[rows, :] + norm_back(acc[rows, :], smalls[0][0:1, :], x * factor, factor)
            put(0, pl.ds(c * half, half))

    outs = [((share, width), F32), ((2, part, hidden), F32), ((hidden, part), F32)]
    return staged(body, index, [gains], ins, outs, 4, [pltpu.VMEM((share, width), F32)])


def fold_kernel(cuts, idx_ref, *refs):
    ins, outs = list(refs[: 2 * len(cuts)]), list(refs[2 * len(cuts) :])
    for place, bit in cuts:
        keep, got = ins.pop(0), ins.pop(0)
        mine = (idx_ref[1] >> bit) & 1
        targets = ((outs.pop(0), mine), (outs.pop(0), 1 - mine))
        for j in range(keep.shape[0] // 2):
            rest = ((j >> place) << (place + 1)) | (j & ((1 << place) - 1))
            for out, value in targets:
                k = rest | (value << place)
                out[j] = (keep[k].astype(F32) + got[k].astype(F32)).astype(BF16)


def fold(index, lanes):
    ins, outs, info, total = [], [], [], 0
    for keep, got, lead, order in lanes:
        count, rows, cols = keep.shape
        ins += [(a, a.shape, None) for a in (keep, got)]
        if order:
            info.append((len(lead) - 1 - lead.index(order[0]), [b for b in lead if b != order[0]], order[1:], order[0]))
            outs += [((count // 2, rows, cols), BF16)] * 2
        total += rows
    if not info:
        outs = [((total, cols), BF16)]

    def body(idx_ref, _, get, out_refs, put, __):
        row = 0
        for n in range(len(lanes)):
            keep, got = get(2 * n), get(2 * n + 1)
            if info:
                place, _, _, bit = info[n]
                fold_kernel([(place, bit)], idx_ref, keep, got, *out_refs[2 * n : 2 * n + 2])
                put(2 * n)
                put(2 * n + 1)
            else:
                rows = keep.shape[1]
                out_refs[0][row : row + rows, :] = (keep[0].astype(F32) + got[0].astype(F32)).astype(BF16)
                put(0, pl.ds(row, rows))
                row += rows

    res = staged(body, index, [], ins, outs, max(len(outs), len(lanes)))
    if not info:
        return res[0]
    return [(res[2 * n], res[2 * n + 1]) + info[n][1:] for n in range(len(lanes))]


def pieces_kernel(part, op_ref, gains_ref, *outs):
    local = outs[0].shape[1]
    hidden = op_ref.shape[1]
    rows = (outs[0].shape[0] - part) // 3
    gains = gains_ref[...]
    wide = gains.shape[1] // local
    flat = jnp.concatenate(
        [gains[r // wide : r // wide + 1, (r % wide) * local : (r % wide + 1) * local] for r in range(rows)]
    )
    parts3 = jnp.concatenate(split3(flat))
    for d, out in enumerate(outs):
        block = d * local // hidden
        col = d * local % hidden
        row = block * part
        out[:part, :] = op_ref[row : row + part, col : col + local]
        out[part:, :] = parts3


def make_pieces(sum_op, gains, part, local, parts):
    shape = (part + 3 * gains.size // local, local)
    return call(
        functools.partial(pieces_kernel, part),
        (1,),
        [whole(sum_op.shape), whole(gains.shape)],
        [whole(shape)] * parts,
        [sds(shape, BF16)] * parts,
    )(sum_op, gains)


def finish_outputs(index, resid, own, others, keep, got, pieces):
    parts, count = len(pieces), len(others[0])
    width = resid.shape[1]
    part, local = keep.shape[1], keep.shape[2] // 3
    ins, row = [], 0
    for n, a in enumerate(own):
        rows = pl.ds(row, a.shape[0])
        ins.append((resid, a.shape, functools.partial(lambda rows, idx, ref: ref.at[rows], rows)))
        ins += [(b, a.shape, None) for b in (a, *others[n])]
        row += a.shape[0]
    ins += [(a, a.shape, None) for a in (keep, got, *pieces)]

    def body(idx_ref, _, get, outs, put, __):
        out_ref, qkv_ref, op_ref, gains_ref = outs
        at = row = 0
        for a in own:
            total = get(at)[...]
            for n in range(count + 1):
                total = total + get(at + 1 + n)[...].astype(F32)
            out_ref[row : row + a.shape[0], :] = total
            put(0, pl.ds(row, a.shape[0]))
            row += a.shape[0]
            at += count + 2
        qkv = get(at)[0].astype(F32) + get(at + 1)[0].astype(F32)
        for c in range(3):
            qkv_ref[c] = qkv[:, c * local : (c + 1) * local]
        put(1)
        piece_refs = [get(at + 2 + d) for d in range(parts)]
        rows = (piece_refs[0].shape[0] - part) // 3

        def gains_of(ref):
            hi, mid, low = (ref[part + n * rows : part + (n + 1) * rows, :].astype(F32) for n in range(3))
            return hi + mid + low

        ops = [ref[:part, :].astype(F32) for ref in piece_refs]
        gains = [gains_of(ref) for ref in piece_refs]
        while len(ops) > 1:
            ops = [ops[2 * n] + ops[2 * n + 1] for n in range(len(ops) // 2)]
            gains = [gains[2 * n] + gains[2 * n + 1] for n in range(len(gains) // 2)]
        op_ref[...] = ops[0].T
        put(2)
        wide = width // local
        for r in range(rows):
            cols = slice((r % wide) * local, (r % wide + 1) * local)
            gains_ref[r // wide : r // wide + 1, cols] = gains[0][r : r + 1, :]
        put(3)

    shapes = [resid.shape, (3, part, local), (local, part), (2, width)]
    return staged(body, index, [], ins, [(shape, F32) for shape in shapes], len(own) + 3)


def after(value, *others):
    return lax.optimization_barrier((value, *others))[0]


def body(
    tokens, qkv_weight, out_weight, gate_up_weight, down_weight, norm_gains,
    species_weight, species_ids, lengths, cotangent,
):
    rows, width = tokens.shape
    local = out_weight.shape[0]
    hidden = down_weight.shape[0]
    parts = lax.axis_size("tensor")
    slots = list(range(parts - 2, -1, -2))
    shares = lax.axis_size("dp")
    part = width // shares
    me = lax.axis_index("tensor")
    dp = lax.axis_index("dp")
    index = jnp.stack([me, dp]).astype(jnp.int32)
    cosine, sine = (jnp.asarray(t) for t in rotary_tables())
    pairs = local // 128
    valid = lengths[0] >= 0

    def region(f):
        shapes = jax.eval_shape(f)
        zeros = lambda: jax.tree.map(lambda a: jnp.zeros(a.shape, a.dtype), shapes)
        return lax.optimization_barrier(lax.cond(valid, f, zeros))

    def beside(sends, f, apart=False):
        return region(lambda: ([swap(*x) for x in sends], region(f) if apart else f()))

    def swap(a, d, name="tensor"):
        return lax.ppermute(a, name, [(i, i ^ d) for i in range(lax.axis_size(name))])

    def cut(a, start, size, axis=0):
        return lax.dynamic_slice_in_dim(a, start, size, axis)

    def outgoing(pieces):
        return [(pieces[d], d, "tensor") for d in range(1, parts)]

    bits = shares.bit_length() - 1
    lead = list(range(bits - 1, 0, -1))

    def fold_next(halves, got):
        return fold(index, [(keep, g, left, order) for (keep, _, left, order, _), g in zip(halves, got)])

    def leaving(halves):
        return [(away, 1 << bit, "dp") for _, away, _, _, bit in halves]

    matches = species_ids[:, None] == jnp.arange(species_weight.shape[0])[None, :]
    picked = jnp.sum(jnp.where(matches, species_weight[None, :], F32(0.0)), axis=1)

    ow_cut = cut(out_weight, dp * (local // shares), local // shares)
    qkv_cut = cut(qkv_weight, dp * part, part, 1).reshape(3 * part, local)
    together = hidden == width
    mine = cut_weights(index[1:], gate_up_weight, down_weight, shares, [ow_cut] if together else [])
    sends = [(ow_cut, d, "tensor") for d in range(2 if together else 1, parts)]

    (partner_cut, *ow), (q, k, v, normed) = beside(
        [(mine, 1, "tensor")] + sends,
        lambda: project(lengths, tokens, qkv_weight, norm_gains, cosine, sine),
    )
    if together:
        partner = lax.all_gather(pack([partner_cut, ow_cut, *ow]), "dp", axis=0)
        out_full = (partner, 3 * part, [1, 0] + list(range(2, parts)))
    else:
        partner = lax.all_gather(partner_cut, "dp", axis=0)
        out_full = (lax.all_gather(pack([ow_cut, *ow]), "dp", axis=0), 0, list(range(parts)))

    sends = [(after(qkv_cut, partner_cut, picked), d, "tensor") for d in range(1, parts)]
    qkv_got, (*att, att_nat, q_back) = beside(sends, lambda: attend(index, q, k, v, parts))
    rows_for = lambda e: outgoing([att[d ^ e] for d in range(parts)])
    rows_now, qkv_stack = beside(rows_for(slots[0]), lambda: pack(qkv_got))
    qkv_full = lax.all_gather(qkv_stack, "dp", axis=0)

    lefts, acts, gn2s, terms, gn2_got = {}, {}, {}, {}, {}
    tied = tokens
    for e in slots:

        def feed():
            outs = feed_forward(
                e, index, lengths, picked, [att[e]] + rows_now, tied, cotangent, out_full,
                gate_up_weight, down_weight, partner, norm_gains
            )
            if e:
                return outs
            return outs, ffn_grads([*lefts.values(), outs[0]], [*acts.values(), outs[1]], shares)

        sends = rows_for(e - 2) if e else []
        if e + 2 in gn2s:
            sends.append((gn2s[e + 2], e + 2, "tensor"))
        got, outs = beside(sends, feed)
        if e + 2 in gn2s:
            gn2_got[e + 2] = got.pop()
        if e:
            rows_now = got
        else:
            outs, wg_ffn = outs
        lefts[e], acts[e], gn2s[e], *terms[e] = outs[:6]
        tied = after(tokens, gn2s[e])
    resid = outs[6]
    gn2_all = [gn2s[0]] + [gn2_got[e] for e in slots[:-1]]

    def terms_out(i):
        return [(terms[e][i], e, "tensor") for e in slots[:-1]]

    terms_got = []
    got, (grad_resid, grad_low, gain_two, *grads) = beside(
        terms_out(0),
        lambda: resid_back(
            index, lengths, picked, cotangent, resid, gn2_all, out_full, norm_gains, local
        ),
    )
    terms_got.append(got)
    sum_ffn = lax.psum_scatter(wg_ffn, "dp", scatter_dimension=0, tiled=True)[0]
    def own_rows():
        return (
            attend_back_own(index, grads[0], q_back, k, v, att_nat, cosine, sine),
            out_grads(grad_low, [att[0]] + rows_now, shares, hidden),
        )

    grads_got, (back_own, wg_op) = beside(outgoing(grads), own_rows)

    def back(j):
        return attend_back(index, grads_got, back_own, q_back, k, v, att_nat, cosine, sine, j)

    terms_got.append([swap(after(a, wg_op), *way) for a, *way in terms_out(1)])
    group = back(0)
    if pairs == 1:
        group = after(group, *terms_got[1])
    sum_op = lax.psum_scatter(after(wg_op, qkv_full), "dp", scatter_dimension=0, tiled=True)[0]
    qkv_acts, acts_got, qkv_sums = [group], [], None
    for j in range(1, pairs):

        def back_next():
            return back(j), project_grads(index, normed, qkv_acts[-1], qkv_weight, shares, j - 1, qkv_sums)

        got, (group, qkv_sums) = beside(outgoing(group), back_next)
        acts_got.append([qkv_acts[-1][0]] + got)
        if j == 1:
            group = after(group, *terms_got[1])
        qkv_acts.append(group)
    ways = []

    def finish():
        away_q, keep_q, gain_one = project_grads(
            index, normed, qkv_acts[-1], qkv_weight, shares, pairs - 1, qkv_sums
        )
        halves = fold(index, [(keep_q, swap(away_q, 1, "dp"), lead, lead)])
        for s in range(bits - 2):
            halves = fold_next(halves, [swap(*x) for x in leaving(halves)])
        gains_grad = jnp.stack([gain_one[:, 0] / norm_gains[0], jnp.sum(gain_two, axis=0)])
        gains_grad = after(gains_grad, *[h[0] for h in halves])
        for s in range(bits):
            gains_grad = gains_grad + swap(gains_grad, 1 << s, "dp")
        ways[:] = [h[2:] for h in halves]
        return [h[:2] for h in halves], gains_grad

    got, (halves, gains_grad) = beside(outgoing(group) + [(sum_ffn[3 * part :], 1, "tensor")], finish, apart=True)
    halves = [tuple(h) + way for h, way in zip(halves, ways)]
    acts_got.append([group[0]] + got[: parts - 1])
    got_b = got[-1]
    pieces = make_pieces(sum_op, gains_grad, part, local, parts)
    got, (grad_tok, grad_gu, grad_down) = beside(
        leaving(halves) + terms_out(2) + outgoing(pieces),
        lambda: token_grad(index, tokens, grad_resid, qkv_weight, qkv_full, norm_gains, acts_got, sum_ffn, got_b),
    )
    terms_got.append(got[1 : len(slots)])
    out, grad_qkv, grad_op, gains_grad = finish_outputs(
        index, resid, terms[0], terms_got, halves[0][0], got[0], [pieces[0]] + got[len(slots) :]
    )
    return (out, grad_tok, grad_qkv, grad_op, grad_gu, grad_down, gains_grad)


def solution(mesh):
    in_specs = (
        P("dp", None),
        P(None, None, "tensor"),
        P("tensor", None),
        P(None, None, "tensor"),
        P("tensor", None),
        P(),
        P(),
        P("dp"),
        P("dp"),
        P("dp", None),
    )
    out_specs = (
        P(("dp", "tensor"), None),
        P(("dp", "tensor"), None),
        P(None, "dp", "tensor"),
        P("tensor", "dp"),
        P(None, "dp", "tensor"),
        P("tensor", "dp"),
        P(),
    )
    return jax.shard_map(body, mesh=mesh, in_specs=in_specs, out_specs=out_specs, check_vma=False)
```
